32 devices in a mesh: replica: 4 (over y, core), fsdp: 8 (over z, x).
Axes of the slice: x: 2, y: 2, z: 4, core: 2. Of those that a mesh axis runs over, the one named last changes fastest.
Arguments:
- inputs: bfloat16 [4096, 1536], P(('replica', 'fsdp')), may hold values from -6 to 6
- cotangent: bfloat16 [4096, 1536], P(('replica', 'fsdp')), may hold values from -6 to 6
- segment_ids: int32 [4096], P('replica'), may hold values from 0 to 27, as said below
- gains: float32 [2, 1536], replicated, may hold values from 0.5 to 1.5
- owner_table: int32 [1608], replicated, may hold values from 0 to 7, as said below
- master_tiles: float32 [1632, 128, 128], P('fsdp'), as said below
- left_stats: float32 [1632, 128, 128], P('fsdp')
- right_stats: float32 [1632, 128, 128], P('fsdp')
- left_roots: float32 [1632, 128, 128], P('fsdp')
- right_roots: float32 [1632, 128, 128], P('fsdp')
Outputs:
- outputs: bfloat16 [4096, 1536], P(('replica', 'fsdp'))
- input_grad: bfloat16 [4096, 1536], P(('replica', 'fsdp'))
- gain_grads: float32 [2, 1536], replicated
- new_gains: float32 [2, 1536], replicated
- weight_grads: float32 [1632, 128, 128], P('fsdp')
- new_master: float32 [1632, 128, 128], P('fsdp')
- new_low: bfloat16 [1632, 128, 128], P('fsdp')
- new_left: float32 [1632, 128, 128], P('fsdp')
- new_right: float32 [1632, 128, 128], P('fsdp')
The draws below stay inside these ranges and needn't reach their ends.
Inputs may be any that keep to these rules, and one draw needn't show every extreme that they name: `segment_ids`: never falls along the tokens; the id changes at every multiple of 1024. Documents hold at most 2048 tokens. `owner_table`: no owner holds more than 204 tiles and one holds exactly 204. `master_tiles`: empty slots hold arbitrary finite tiles.
All inputs are finite; a program needn't handle non-finite values.
Results may differ from the reference program's by a relative error of at most 0.017.
Values may be sent and summed in bfloat16 or wider, within the bound.
A program may use at most 896 MiB of HBM per device.

```python
import math
import jax
import jax.numpy as jnp
import numpy as np
from jax import lax

D = 1536
HEADS = 12
HEAD_DIM = 128
FF = 4608
WINDOW = 1024
TILE = 128
TOK_DEV = 128
GROUP = 1024
TOKENS = 4096
NTILES = 1608
CAP = 204
N_REPLICA = 4
N_FSDP = 8


def matrix_shapes_drawn():
    head_width = HEADS * HEAD_DIM
    return [(D, head_width), (D, HEAD_DIM), (D, HEAD_DIM), (head_width, D), (D, FF), (D, FF), (FF, D)]


def tile_kinds():
    kinds = []
    for number, shape_pair in enumerate(matrix_shapes_drawn()):
        kinds = kinds + [number] * (shape_pair[0] // TILE * (shape_pair[1] // TILE))
    return np.array(kinds, np.int32)


def dealt_owners(key):
    order = jax.random.permutation(key, NTILES).astype(jnp.int32)
    heavy = jax.random.randint(jax.random.fold_in(key, 1), (), 0, N_FSDP)
    position = jnp.arange(NTILES, dtype=jnp.int32)
    others = (position - CAP) % (N_FSDP - 1)
    others = others + (others >= heavy).astype(jnp.int32)
    dealt = jnp.where(position < CAP, heavy, others).astype(jnp.int32)
    return jnp.zeros((NTILES,), jnp.int32).at[order].set(dealt)


def slot_kinds(key):
    owner_table = dealt_owners(key)
    onehot = (owner_table[:, None] == jnp.arange(N_FSDP, dtype=jnp.int32)[None, :]).astype(jnp.int32)
    earlier = jnp.cumsum(onehot, 0) - onehot
    slots = owner_table * CAP + jnp.sum(earlier * onehot, 1)
    return jnp.full((N_FSDP * CAP,), 7, jnp.int32).at[slots].set(jnp.asarray(tile_kinds()))


def weight_scales():
    head_width = HEADS * HEAD_DIM
    out_scale = (head_width * 3.0 / WINDOW) ** (-0.5)
    return jnp.asarray([D ** (-0.5), D ** (-0.5), D ** (-0.5), out_scale, D ** (-0.5), D ** (-0.5), FF ** (-0.5), 0.02], jnp.float32)


def grad_sizes():
    root = float(TOKENS) ** 0.5
    return jnp.asarray([1.0, 1.0, 1.5, 0.1, 0.3, 0.3, 0.5, 1.0], jnp.float32) * root


def statistic(key, kinds, top):
    size_each = grad_sizes()[kinds][:, None, None]
    base = TILE * size_each * size_each
    diagonal = jnp.exp(jax.random.uniform(jax.random.fold_in(key, 1), (N_FSDP * CAP, TILE), jnp.float32, 0.0, math.log(top)))
    noise = jax.random.normal(jax.random.fold_in(key, 2), (N_FSDP * CAP, TILE, TILE), jnp.float32)
    noise = (noise + jnp.swapaxes(noise, 1, 2)) * 0.7071
    identity = jnp.eye(TILE, dtype=jnp.float32)
    return base * (identity * diagonal[:, :, None] + (1.0 - identity) * noise * TILE ** (-0.5))


def root_matrix(key, kinds, lowest, highest, off_scale):
    size_each = grad_sizes()[kinds][:, None, None] ** (-0.5)
    diagonal = jnp.exp(jax.random.uniform(jax.random.fold_in(key, 1), (N_FSDP * CAP, TILE), jnp.float32, math.log(lowest), math.log(highest)))
    noise = jax.random.normal(jax.random.fold_in(key, 2), (N_FSDP * CAP, TILE, TILE), jnp.float32)
    noise = (noise + jnp.swapaxes(noise, 1, 2)) * 0.7071
    identity = jnp.eye(TILE, dtype=jnp.float32)
    return size_each * (identity * diagonal[:, :, None] + (1.0 - identity) * noise * off_scale * TILE ** (-0.5))


def draw_owner_table(key, part):
    return dealt_owners(key)


def draw_segment_ids(key, part):
    key = jax.random.fold_in(key, 5)
    shortest = max(WINDOW // 5, 1)
    most_docs = GROUP // shortest + 2
    lengths = jax.random.randint(key, (N_REPLICA, most_docs), shortest, 2 * WINDOW + 1)
    ends = jnp.cumsum(lengths, 1).astype(jnp.int32)
    place = jnp.arange(GROUP, dtype=jnp.int32)
    local_ids = jax.vmap(lambda stream_ends: jnp.searchsorted(stream_ends, place, side='right'))(ends).astype(jnp.int32)
    streams = jnp.arange(N_REPLICA, dtype=jnp.int32)
    last_ids = local_ids[:, GROUP - 1]
    offsets = jnp.where(streams == 0, 0, (streams + 1) * most_docs - 1 - last_ids).astype(jnp.int32)
    return (local_ids + offsets[:, None]).reshape(TOKENS)


def draw_master_tiles(key, part):
    kinds = slot_kinds(key)
    key = jax.random.fold_in(key, 11)
    scale = weight_scales()[kinds][:, None, None]
    noise = jax.random.normal(key, (N_FSDP * CAP, TILE, TILE), jnp.float32)
    return noise * scale


def draw_left_stats(key, part):
    kinds = slot_kinds(key)
    key = jax.random.fold_in(key, 12)
    return statistic(key, kinds, 4.0)


def draw_right_stats(key, part):
    kinds = slot_kinds(key)
    key = jax.random.fold_in(key, 13)
    return statistic(key, kinds, 4.0)


def draw_left_roots(key, part):
    kinds = slot_kinds(key)
    key = jax.random.fold_in(key, 14)
    return root_matrix(key, kinds, 0.7, 1.4, 0.5)


def draw_right_roots(key, part):
    kinds = slot_kinds(key)
    key = jax.random.fold_in(key, 15)
    return root_matrix(key, kinds, 0.7, 1.4, 0.5)


def shard_levels(rng, dims, shards, low, high):
    factor_of = 1.0
    for axis_at, blocks in shards:
        steps = jax.random.uniform(jax.random.fold_in(jax.random.fold_in(rng, 6), axis_at), (blocks,), jnp.float32, low / len(shards), high / len(shards))
        factor_of = factor_of * jnp.repeat(jnp.exp(steps), dims[axis_at] // blocks).reshape((-1,) + (1,) * (len(dims) - 1 - axis_at))
    return factor_of


def bell_draw(rng, dims, spread, limit, cuts=(), held_as=jnp.bfloat16):
    factor_of = shard_levels(rng, dims, cuts, -0.22, 0.18) if cuts else 1.0
    entries = jax.random.normal(rng, dims, jnp.float32) * spread * factor_of
    return jnp.minimum(jnp.maximum(entries, -limit), limit).astype(held_as)


def setup_inputs(seed: int = 0) -> dict:
    streams_of = jax.random.split(jax.random.key(seed), 11)
    inputs = bell_draw(streams_of[0], (TOKENS, D), 1.0, 6.0, ((0, 32),))
    cotangent = bell_draw(streams_of[1], (TOKENS, D), 1.0, 6.0, ((0, 32),))
    segment_ids = draw_segment_ids(jax.random.fold_in(streams_of[10], 71), 0)
    gains = jnp.clip(1.0 + 0.1 * jax.random.normal(streams_of[3], (2, D), jnp.float32), 0.5, 1.5)
    owner_table = draw_owner_table(jax.random.fold_in(streams_of[10], 71), 0)
    master_tiles = draw_master_tiles(jax.random.fold_in(streams_of[10], 71), 0)
    left_stats = draw_left_stats(jax.random.fold_in(streams_of[10], 71), 0)
    right_stats = draw_right_stats(jax.random.fold_in(streams_of[10], 71), 0)
    left_roots = draw_left_roots(jax.random.fold_in(streams_of[10], 71), 0)
    right_roots = draw_right_roots(jax.random.fold_in(streams_of[10], 71), 0)
    return {"inputs": inputs, "cotangent": cotangent, "segment_ids": segment_ids, "gains": gains, "owner_table": owner_table, "master_tiles": master_tiles, "left_stats": left_stats, "right_stats": right_stats, "left_roots": left_roots, "right_roots": right_roots}


EPSILON = 1e-06
STEP_RATE = 0.02
STAT_DECAY = 0.5
GAIN_STEP = 0.1
HIGHEST = lax.Precision.HIGHEST

@jax.custom_vjp
def low(v):
    return lax.optimization_barrier(v.astype(jnp.bfloat16)).astype(jnp.float32)

@jax.custom_vjp
def low_back(v):
    return v

def low_keep(v):
    return (low(v), None)

def low_pass(kept, grad):
    return (grad,)

def back_keep(v):
    return (v, None)

def back_low(kept, grad):
    return (low(grad),)
low.defvjp(low_keep, low_pass)
low_back.defvjp(back_keep, back_low)

def matrix_shapes():
    head_width = HEADS * HEAD_DIM
    return [(D, head_width), (D, HEAD_DIM), (D, HEAD_DIM), (head_width, D), (D, FF), (D, FF), (FF, D)]

def to_matrices(tiles):
    result = []
    offset = 0
    for row_count, columns in matrix_shapes():
        number = row_count // TILE * (columns // TILE)
        tile_grid = tiles[offset:offset + number].reshape(row_count // TILE, columns // TILE, TILE, TILE)
        result.append(tile_grid.transpose(0, 2, 1, 3).reshape(row_count, columns))
        offset = offset + number
    return tuple(result)

def to_tiles(matrices):
    pieces = []
    for matrix in matrices:
        row_count, columns = matrix.shape
        tile_grid = matrix.reshape(row_count // TILE, TILE, columns // TILE, TILE).transpose(0, 2, 1, 3)
        pieces.append(tile_grid.reshape(-1, TILE, TILE))
    return jnp.concatenate(pieces, 0)

def slot_of_tiles(owner_table, owners, capacity):
    onehot = (owner_table[:, None] == jnp.arange(owners, dtype=jnp.int32)[None, :]).astype(jnp.int32)
    earlier = jnp.cumsum(onehot, 0) - onehot
    ranking = lax.optimization_barrier(jnp.sum(earlier * onehot, 1))
    return (owner_table * capacity + ranking).astype(jnp.int32)

def normalize(values, gain_row):
    mean_square = lax.optimization_barrier(jnp.mean(values * values, -1, keepdims=True))
    return values * lax.rsqrt(mean_square + EPSILON) * gain_row

def rotate(values, angles):
    half_dim = values.shape[-1] // 2
    cosine = jnp.cos(angles)[:, None, :]
    sine_part = jnp.sin(angles)[:, None, :]
    first_half = values[..., :half_dim]
    second = values[..., half_dim:]
    return jnp.concatenate([first_half * cosine - second * sine_part, second * cosine + first_half * sine_part], -1)

def angles_of(positions):
    half_dim = HEAD_DIM // 2
    inverse = 10000.0 ** (-2.0 * jnp.arange(half_dim, dtype=jnp.float32) / HEAD_DIM)
    return positions[:, None] * inverse[None, :]

def attention(queries, key_rows, value_rows, segment):
    total_rows = queries.shape[0]
    padded_keys = jnp.concatenate([jnp.zeros((WINDOW, HEAD_DIM), jnp.float32), key_rows], 0)
    padded_values = jnp.concatenate([jnp.zeros((WINDOW, HEAD_DIM), jnp.float32), value_rows], 0)
    padded_ids = jnp.concatenate([jnp.full((WINDOW,), -1, jnp.int32), segment], 0)
    key_span = WINDOW + TOK_DEV
    score_scale = HEAD_DIM ** (-0.5)
    distance = jnp.arange(TOK_DEV, dtype=jnp.int32)[:, None] + WINDOW - jnp.arange(key_span, dtype=jnp.int32)[None, :]

    def one_block(block_index):
        first_row = block_index * TOK_DEV
        block_queries = lax.dynamic_slice_in_dim(queries, first_row, TOK_DEV, 0)
        block_keys = lax.dynamic_slice_in_dim(padded_keys, first_row, key_span, 0)
        block_values = lax.dynamic_slice_in_dim(padded_values, first_row, key_span, 0)
        query_ids = lax.dynamic_slice_in_dim(segment, first_row, TOK_DEV, 0)
        key_ids = lax.dynamic_slice_in_dim(padded_ids, first_row, key_span, 0)
        allowed = (query_ids[:, None] == key_ids[None, :]) & (distance >= 0) & (distance < WINDOW)
        scores = low_back(jnp.einsum('qhd,kd->hqk', block_queries, block_keys, precision=HIGHEST) * score_scale)
        scores = jnp.where(allowed[None], scores, -1e+30)
        row_peak = lax.optimization_barrier(jnp.max(scores, -1, keepdims=True))
        weights = jnp.exp(scores - row_peak)
        probability = low(weights / lax.optimization_barrier(jnp.sum(weights, -1, keepdims=True)))
        weighted = jnp.einsum('hqk,kd->qhd', probability, block_values, precision=HIGHEST)
        return weighted.reshape(TOK_DEV, HEADS * HEAD_DIM)
    blocks = lax.map(jax.checkpoint(one_block), jnp.arange(total_rows // TOK_DEV, dtype=jnp.int32))
    return blocks.reshape(total_rows, HEADS * HEAD_DIM)

def group_forward(inputs, gains, matrices, segment, positions):
    w_query, w_key, w_value, w_out, w_gate, w_up, w_down = matrices
    total_rows = inputs.shape[0]
    normed = low(normalize(inputs, gains[0]))
    query_pre = low_back(jnp.dot(normed, w_query, precision=HIGHEST))
    key_pre = low_back(jnp.dot(normed, w_key, precision=HIGHEST))
    value_rows = low_back(low(jnp.dot(normed, w_value, precision=HIGHEST)))
    angles = angles_of(positions)
    queries = low(rotate(query_pre.reshape(total_rows, HEADS, HEAD_DIM), angles))
    key_rows = low(rotate(key_pre[:, None, :], angles)[:, 0, :])
    attended = low_back(low(attention(queries, key_rows, value_rows, segment)))
    branch = low_back(jnp.dot(attended, w_out, precision=HIGHEST))
    middle = inputs + branch
    normed_two = low(normalize(middle, gains[1]))
    gate = low_back(jnp.dot(normed_two, w_gate, precision=HIGHEST))
    up_part = low_back(jnp.dot(normed_two, w_up, precision=HIGHEST))
    hidden = low(jax.nn.gelu(gate, approximate=True) * up_part)
    return middle + jnp.dot(hidden, w_down, precision=HIGHEST)

def reference(inputs, cotangent, segment_ids, gains, owner_table, master_tiles, left_stats, right_stats, left_roots, right_roots):
    group_rows = TOK_DEV * N_FSDP
    capacity = master_tiles.shape[0] // N_FSDP
    slots = slot_of_tiles(owner_table, N_FSDP, capacity)
    rounded = master_tiles.astype(jnp.bfloat16).astype(jnp.float32)
    matrices = to_matrices(rounded[slots])
    inputs_wide = inputs.astype(jnp.float32)
    cotangent_wide = cotangent.astype(jnp.float32)

    def one_group(carry, group_index):
        first_row = group_index * group_rows
        group_inputs = lax.dynamic_slice_in_dim(inputs_wide, first_row, group_rows, 0)
        group_cotangent = lax.dynamic_slice_in_dim(cotangent_wide, first_row, group_rows, 0)
        group_ids = lax.dynamic_slice_in_dim(segment_ids, first_row, group_rows, 0)
        starts = jnp.searchsorted(group_ids, group_ids, side='left').astype(jnp.int32)
        positions = (jnp.arange(group_rows, dtype=jnp.int32) - starts).astype(jnp.float32)

        def forward(values, gain_rows, weights):
            return group_forward(values, gain_rows, weights, group_ids, positions)
        outputs, backward = jax.vjp(forward, group_inputs, gains, matrices)
        input_grad, gain_grad, weight_grad = backward(group_cotangent)
        summed = jax.tree.map(lambda earlier_sum, addend: earlier_sum + addend, carry[1], weight_grad)
        return ((carry[0] + gain_grad, summed), (outputs.astype(jnp.bfloat16), input_grad.astype(jnp.bfloat16)))
    start_carry = (jnp.zeros_like(gains), jax.tree.map(jnp.zeros_like, matrices))
    (gain_grads, weight_sums), (outputs, input_grads) = lax.scan(one_group, start_carry, jnp.arange(N_REPLICA, dtype=jnp.int32))
    grad_slots = jnp.zeros_like(master_tiles).at[slots].set(to_tiles(weight_sums))
    new_left = STAT_DECAY * left_stats + (1.0 - STAT_DECAY) * jnp.einsum('sij,skj->sik', grad_slots, grad_slots, precision=HIGHEST)
    new_right = STAT_DECAY * right_stats + (1.0 - STAT_DECAY) * jnp.einsum('sji,sjk->sik', grad_slots, grad_slots, precision=HIGHEST)
    right_turned = jnp.einsum('sij,sjk->sik', grad_slots, right_roots, precision=HIGHEST)
    turned = jnp.einsum('sij,sjk->sik', left_roots, right_turned, precision=HIGHEST)
    new_master = master_tiles - STEP_RATE * turned
    gain_rate = GAIN_STEP * (TOK_DEV * N_FSDP * N_REPLICA) ** (-0.5)
    new_gains = gains - gain_rate * gain_grads
    return (outputs.reshape(-1, D), input_grads.reshape(-1, D), gain_grads, new_gains, grad_slots, new_master, new_master.astype(jnp.bfloat16), new_left, new_right)
```

```python
import functools

import jax
import jax.numpy as jnp
import numpy as np
from jax import lax
from jax.experimental import pallas as pl
from jax.experimental.pallas import tpu as pltpu
from jax.sharding import PartitionSpec as P

HEADS = 12
HEAD_DIM = 128
FF = 4608
WINDOW = 1024


EPSILON = 1e-06
STEP_RATE = 0.02
STAT_DECAY = 0.5
GAIN_STEP = 0.1
F32, BF16 = jnp.float32, jnp.bfloat16
MESH = pl.DeviceIdType.MESH


def gather_kernel(chunk, deep, shared, depth, own, full, keep_sem, up_s, up_r, down_s, down_r, x_s, x_r, y_s, y_r, core_s, core_r):
    run = deep + shared
    half = (2 * deep + shared) * chunk
    whole = 2 * deep + shared
    replica = lax.axis_index("replica")
    member = lax.axis_index("fsdp")
    y, core = replica // 2, replica % 2
    z, x = member // 2, member % 2
    mirrored = z // 2
    inner = z + mirrored * (3 - 2 * z)
    above, below = (replica, (z + 1) * 2 + x), (replica, (z - 1) * 2 + x)
    across, beside, twin = (replica, z * 2 + 1 - x), ((1 - y) * 2 + core, member), (y * 2 + 1 - core, member)

    barrier = pltpu.get_barrier_semaphore()
    def greet(device):
        pl.semaphore_signal(barrier, inc=1, device_id=device, device_id_type=MESH)
    pl.when(z < 3)(lambda: greet(above))
    pl.when(z > 0)(lambda: greet(below))
    greet(across); greet(beside); greet(twin)
    @pl.when((z == 0) | (z == 3))
    def _():
        pl.semaphore_wait(barrier, 4)
    @pl.when((z > 0) & (z < 3))
    def _():
        pl.semaphore_wait(barrier, 5)

    keep = pltpu.make_async_copy(own, full.at[member], keep_sem)
    keep.start()

    def place(k, plane):
        return plane * (whole - 1) + k * (1 - 2 * plane)
    def rows(chunk_at, owner_core):
        return pl.ds(owner_core * half + chunk_at * chunk, chunk)
    def copy(source_owner, chunk_at, send, recv, device, from_own=False, owner_core=None):
        at = rows(chunk_at, core if owner_core is None else owner_core)
        target = full.at[source_owner, at]
        source = own.at[at] if from_own else target
        return pltpu.make_async_remote_copy(src_ref=source, dst_ref=target, send_sem=send, recv_sem=recv, device_id=device, device_id_type=MESH)
    def go_up(zb, k, own_block=False):
        return copy(zb * 2 + x, place(k, y), up_s.at[zb, k], up_r.at[zb, k], above, own_block)
    def go_down(zb, k, own_block=False):
        return copy(zb * 2 + x, place(k, y), down_s.at[zb, k], down_r.at[zb, k], below, own_block)
    def go_x(zb, k, own_block=False):
        return copy(zb * 2 + x, place(k, y), x_s.at[zb, k], x_r.at[zb, k], across, own_block)
    def come_x(zb, k):
        return copy(zb * 2 + 1 - x, place(k, y), x_s.at[zb, k], x_r.at[zb, k], across)
    def go_y(owner, k):
        return copy(owner, place(k, y), y_s.at[owner, k], y_r.at[owner, k], beside)
    def come_y(owner, k):
        return copy(owner, place(k, 1 - y), y_s.at[owner, k], y_r.at[owner, k], beside)
    def go_core(owner, at):
        return copy(owner, at, core_s.at[owner, at], core_r.at[owner, at], twin)

    def onward(owner, k):
        go_core(owner, place(k, y)).start()
        @pl.when(k < deep)
        def _():
            if depth:
                @pl.when(k >= depth)
                def _():
                    go_y(owner, k - depth).wait_send()
            go_y(owner, k).start()

    def leave(make, zb, k, own_block):
        if depth:
            @pl.when(k >= depth)
            def _():
                make(zb, k - depth, own_block).wait_send()
        make(zb, k, own_block).start()

    def across_block(g):
        b = g if g >= 2 else (g + inner) % 2
        return b + mirrored * (3 - 2 * b)

    def group(g):
        def tick(k, _):
            if g == 0:
                pl.when(z < 3)(lambda: leave(go_up, z, k, True))
                pl.when(z > 0)(lambda: leave(go_down, z, k, True))
                leave(go_x, z, k, True)
            if 1 <= g <= 3:
                @pl.when(z - g >= 0)
                def _():
                    zb = z - g
                    pltpu_wait = copy(zb * 2 + x, place(k, y), up_s.at[zb, k], up_r.at[zb, k], above)
                    pltpu_wait.wait_recv()
                    pl.when(z < 3)(lambda: leave(go_up, zb, k, False))
                    onward(zb * 2 + x, k)
                @pl.when(z + g <= 3)
                def _():
                    zb = z + g
                    copy(zb * 2 + x, place(k, y), down_s.at[zb, k], down_r.at[zb, k], below).wait_recv()
                    pl.when(z > 0)(lambda: leave(go_down, zb, k, False))
                    onward(zb * 2 + x, k)
                leave(go_x, across_block(g), k, False)
            if 1 <= g <= 4:
                b = across_block(g - 1)
                come_x(b, k).wait_recv()
                onward(b * 2 + 1 - x, k)
            if g >= 2:
                @pl.when(k < deep)
                def _():
                    def take(owner):
                        come_y(owner, k).wait_recv()
                        go_core(owner, place(k, 1 - y)).start()
                    if g - 1 <= 3:
                        pl.when(z - (g - 1) >= 0)(lambda: take((z - (g - 1)) * 2 + x))
                        pl.when(z + (g - 1) <= 3)(lambda: take((z + (g - 1)) * 2 + x))
                    if g - 1 >= 1:
                        take(across_block(g - 2) * 2 + 1 - x)
            return 0
        lax.fori_loop(0, run, tick, 0)
    for g in range(6):
        group(g)

    first = run - depth if depth else 0
    firsty = deep - depth if depth else 0
    def drain_z(zb, _):
        def one(k, _):
            @pl.when((zb <= z) & (z < 3))
            def _():
                go_up(zb, k).wait_send()
            @pl.when((zb >= z) & (z > 0))
            def _():
                go_down(zb, k).wait_send()
            go_x(zb, k).wait_send()
            return 0
        lax.fori_loop(first, run, one, 0)
        return 0
    lax.fori_loop(0, 4, drain_z, 0)
    def drain_owner(owner, _):
        @pl.when(owner != member)
        def _():
            def one_y(k, _):
                go_y(owner, k).wait_send()
                return 0
            lax.fori_loop(firsty, deep, one_y, 0)
            def one_core(k, _):
                go_core(owner, k).wait_send()
                copy(owner, k, core_s.at[owner, k], core_r.at[owner, k], twin, owner_core=1 - core).wait_recv()
                return 0
            lax.fori_loop(0, whole, one_core, 0)
        return 0
    lax.fori_loop(0, 8, drain_owner, 0)
    keep.wait()

def gather(own, chunk=6, deep=6, shared=5, depth=0):
    run, whole = deep + shared, 2 * deep + shared
    assert whole * chunk * 2 == own.shape[0]
    D = pltpu.SemaphoreType.DMA
    return pl.pallas_call(
        functools.partial(gather_kernel, chunk, deep, shared, depth),
        out_shape=jax.ShapeDtypeStruct((8,) + own.shape, own.dtype),
        in_specs=[pl.BlockSpec(memory_space=pl.ANY)],
        out_specs=pl.BlockSpec(memory_space=pl.ANY),
        scratch_shapes=[D] + [D((4, run))] * 6 + [D((8, deep))] * 2 + [D((8, whole))] * 2,
        compiler_params=pltpu.CompilerParams(collective_id=0, has_side_effects=True),
    )(own)


def reduce_kernel(chunk, left_step, right_step, lag, left_at, right_at, left, right, out,
                  left_all, right_all, x_out, x_in, z_out, z_in, total,
                  keep_sem, ly_s, ly_r, lc_s, lc_r, lf_s, lf_r, ry_s, ry_r, rc_s, rc_r, rf_s, rf_r,
                  x_s, x_r, z_s, z_r, ty_s, ty_r, tc_s, tc_r, tf_s, tf_r, done_sem):
    rows = left.shape[2]
    quarter = x_out.shape[1]
    pieces = quarter // chunk
    replica = lax.axis_index("replica")
    member = lax.axis_index("fsdp")
    y, core = replica // 2, replica % 2
    z, x = member // 2, member % 2
    across, beside, twin = (replica, z * 2 + 1 - x), ((1 - y) * 2 + core, member), (y * 2 + 1 - core, member)
    beside_replica, twin_replica, far_replica = (1 - y) * 2 + core, y * 2 + 1 - core, (1 - y) * 2 + 1 - core
    def level(step):
        return (z + step) % 4
    def depth_device(step):
        return (replica, level(step) * 2 + x)
    barrier = pltpu.get_barrier_semaphore()
    for device in [across, beside, twin] + [depth_device(step) for step in (1, 2, 3)]:
        pl.semaphore_signal(barrier, inc=1, device_id=device, device_id_type=MESH)
    pl.semaphore_wait(barrier, 6)

    def remote(source, target, send, recv, device):
        return pltpu.make_async_remote_copy(src_ref=source, dst_ref=target, send_sem=send, recv_sem=recv, device_id=device, device_id_type=MESH)

    left_total, right_total = left.shape[0], right.shape[0]
    def left_view(n, who):
        return left_all.at[pl.ds(n * left_step, left_step), :, pl.ds(pl.multiple_of(who * rows, rows), rows)]
    def right_view(n, who):
        return right_all.at[pl.ds(n * right_step, right_step), pl.ds(pl.multiple_of(who * rows, rows), rows), :]
    def moves(view, source, step, sems):
        ys, yr, cs, cr, fs, fr = sems
        def own(n):
            return source.at[pl.ds(n * step, step)]
        return (
            lambda n: remote(own(n), view(n, replica), ys.at[n], yr.at[n], beside),
            lambda n: remote(own(n), view(n, replica), cs.at[n], cr.at[n], twin),
            lambda n: remote(view(n, beside_replica), view(n, beside_replica), fs.at[n], fr.at[n], twin),
            lambda n: remote(own(n), view(n, beside_replica), ys.at[n], yr.at[n], beside),
            lambda n: remote(own(n), view(n, twin_replica), cs.at[n], cr.at[n], twin),
            lambda n: remote(own(n), view(n, far_replica), fs.at[n], fr.at[n], twin),
        )
    sets = [
        (moves(left_view, left, left_step, (ly_s, ly_r, lc_s, lc_r, lf_s, lf_r)), left_total // left_step),
        (moves(right_view, right, right_step, (ry_s, ry_r, rc_s, rc_r, rf_s, rf_r)), right_total // right_step),
    ]
    own_left = pltpu.make_async_copy(left, left_all.at[pl.ds(0, left_total), :, pl.ds(pl.multiple_of(replica * rows, rows), rows)], keep_sem.at[0])
    own_right = pltpu.make_async_copy(right, right_all.at[:, pl.ds(pl.multiple_of(replica * rows, rows), rows), :], keep_sem.at[1])
    own_left.start()
    own_right.start()
    left_all[left_total] = jnp.zeros(left_all.shape[1:], left_all.dtype)
    for (to_y, to_twin, pass_on, from_y, from_twin, from_far), count in sets:
        def launch(n, _):
            to_y(n).start()
            to_twin(n).start()
            return 0
        lax.fori_loop(0, count, launch, 0)
    for (to_y, to_twin, pass_on, from_y, from_twin, from_far), count in sets:
        def relay(n, _):
            from_y(n).wait_recv()
            pass_on(n).start()
            return 0
        lax.fori_loop(0, count, relay, 0)
    for (to_y, to_twin, pass_on, from_y, from_twin, from_far), count in sets:
        def settle(n, _):
            from_twin(n).wait_recv()
            from_far(n).wait_recv()
            to_y(n).wait_send()
            to_twin(n).wait_send()
            pass_on(n).wait_send()
            return 0
        lax.fori_loop(0, count, settle, 0)
    own_left.wait()
    own_right.wait()

    def tile(owner, at):
        rank = replica * quarter + at
        return jnp.dot(left_all[left_at[owner, rank]], right_all[right_at[owner, rank]], preferred_element_type=F32)

    def x_copy(zb, k):
        at = pl.ds(k * chunk, chunk)
        return remote(x_out.at[zb, at], x_in.at[zb, at], x_s.at[zb, k], x_r.at[zb, k], across)
    def z_copy(step, k):
        at = pl.ds(k * chunk, chunk)
        return remote(z_out.at[step, at], z_in.at[step, at], z_s.at[step, k], z_r.at[step, k], depth_device(step))
    def total_at(who, k):
        return total.at[pl.ds(who * quarter + k * chunk, chunk)]
    def t_beside(k):
        return remote(total_at(replica, k), total_at(replica, k), ty_s.at[k], ty_r.at[k], beside)
    def t_twin(k):
        return remote(total_at(replica, k), total_at(replica, k), tc_s.at[k], tc_r.at[k], twin)
    def t_pass(k):
        return remote(total_at(beside_replica, k), total_at(beside_replica, k), tf_s.at[k], tf_r.at[k], twin)
    def come_beside(k):
        return remote(total_at(replica, k), total_at(beside_replica, k), ty_s.at[k], ty_r.at[k], beside)
    def come_twin(k):
        return remote(total_at(replica, k), total_at(twin_replica, k), tc_s.at[k], tc_r.at[k], twin)
    def come_far(k):
        return remote(total_at(replica, k), total_at(far_replica, k), tf_s.at[k], tf_r.at[k], twin)

    def send_x(k):
        def block(step, _):
            zb = level(step)
            def one(t, _):
                at = k * chunk + t
                x_out[zb, at] = tile(zb * 2 + 1 - x, at).astype(BF16)
                return 0
            lax.fori_loop(0, chunk, one, 0)
            x_copy(zb, k).start()
            return 0
        lax.fori_loop(0, 4, block, 0)

    def send_z(k):
        def block(step, _):
            zb = level(step)
            x_copy(zb, k).wait_recv()
            def one(t, _):
                at = k * chunk + t
                z_out[step, at] = (tile(zb * 2 + x, at) + x_in[zb, at].astype(F32)).astype(BF16)
                return 0
            lax.fori_loop(0, chunk, one, 0)
            @pl.when(step > 0)
            def _():
                z_copy(step, k).start()
            return 0
        lax.fori_loop(0, 4, block, 0)

    def finish(k):
        for step in (1, 2, 3):
            z_copy(step, k).wait_recv()
        def one(t, _):
            at = k * chunk + t
            added = z_out[0, at].astype(F32)
            for step in (1, 2, 3):
                added = added + z_in[step, at].astype(F32)
            total[replica * quarter + at] = added.astype(BF16)
            return 0
        lax.fori_loop(0, chunk, one, 0)
        t_beside(k).start()
        t_twin(k).start()

    def spread(k):
        come_beside(k).wait_recv()
        t_pass(k).start()

    def beat(n, _):
        @pl.when(n < pieces)
        def _():
            send_x(n)
        @pl.when((n >= lag) & (n < pieces + lag))
        def _():
            send_z(n - lag)
        @pl.when((n >= 2 * lag) & (n < pieces + 2 * lag))
        def _():
            finish(n - 2 * lag)
        @pl.when(n >= 3 * lag)
        def _():
            spread(n - 3 * lag)
        return 0
    lax.fori_loop(0, pieces + 3 * lag, beat, 0)

    def drain(k, _):
        come_twin(k).wait_recv()
        come_far(k).wait_recv()
        t_beside(k).wait_send()
        t_twin(k).wait_send()
        t_pass(k).wait_send()
        for zb in range(4):
            x_copy(zb, k).wait_send()
        for step in (1, 2, 3):
            z_copy(step, k).wait_send()
        return 0
    lax.fori_loop(0, pieces, drain, 0)
    result = pltpu.make_async_copy(total, out, done_sem)
    result.start()
    result.wait()

def reduce_tiles(left_at, right_at, left, right, chunk=3, left_step=8, right_step=10, lag=2):
    capacity = left_at.shape[1]
    quarter = capacity // 4
    pieces = quarter // chunk
    rows, side = left.shape[2], left.shape[1]
    nl, nr = left.shape[0] // left_step, right.shape[0] // right_step
    D = pltpu.SemaphoreType.DMA
    V = pltpu.VMEM
    return pl.pallas_call(
        functools.partial(reduce_kernel, chunk, left_step, right_step, lag),
        out_shape=jax.ShapeDtypeStruct((capacity, side, side), BF16),
        in_specs=[pl.BlockSpec(memory_space=pltpu.SMEM)] * 2 + [pl.BlockSpec(memory_space=pl.ANY)] * 2,
        out_specs=pl.BlockSpec(memory_space=pl.ANY),
        scratch_shapes=[
            V((left.shape[0] + 1, side, 4 * rows), BF16), V((right.shape[0], 4 * rows, side), BF16),
            V((4, quarter, side, side), BF16), V((4, quarter, side, side), BF16),
            V((4, quarter, side, side), BF16), V((4, quarter, side, side), BF16),
            V((capacity, side, side), BF16),
            D((2,))] + [D((nl,))] * 6 + [D((nr,))] * 6 + [D((4, pieces))] * 4 + [D((pieces,))] * 6 + [D],
        compiler_params=pltpu.CompilerParams(collective_id=1, has_side_effects=True, vmem_limit_bytes=62 * 2**20),
    )(left_at, right_at, left, right)


def shampoo_kernel(count, grads, left_old, right_old, left_root, right_root, master, grads_out, left_new, right_new, master_new, low_new):
    nt = (((1,), (1,)), ((), ()))
    tn = (((0,), (0,)), ((), ()))
    for at in range(count):
        grad = grads[at]
        grads_out[at] = grad.astype(F32)
        left_new[at] = STAT_DECAY * left_old[at] + (1.0 - STAT_DECAY) * lax.dot_general(grad, grad, nt, preferred_element_type=F32)
        right_new[at] = STAT_DECAY * right_old[at] + (1.0 - STAT_DECAY) * lax.dot_general(grad, grad, tn, preferred_element_type=F32)
        turned = jnp.dot(grad, right_root[at].astype(BF16), preferred_element_type=F32).astype(BF16)
        turned = jnp.dot(left_root[at].astype(BF16), turned, preferred_element_type=F32)
        fresh = master[at] - STEP_RATE * turned
        master_new[at] = fresh
        low_new[at] = fresh.astype(BF16)

def shampoo(grads, left_old, right_old, left_root, right_root, master, count=6):
    capacity, side = master.shape[0], master.shape[1]
    while capacity % count:
        count -= 1
    spec = pl.BlockSpec((count, side, side), lambda i: (i, 0, 0))
    wide = jax.ShapeDtypeStruct(master.shape, F32)
    return pl.pallas_call(
        functools.partial(shampoo_kernel, count),
        grid=(capacity // count,),
        in_specs=[spec] * 6,
        out_specs=[spec] * 5,
        out_shape=[wide, wide, wide, wide, jax.ShapeDtypeStruct(master.shape, BF16)],
        compiler_params=pltpu.CompilerParams(vmem_limit_bytes=40 * 2**20),
    )(grads, left_old, right_old, left_root, right_root, master)


def shifted(block, axis, distance):
    devices = range(lax.axis_size(axis))
    route = [(i - distance, i) for i in devices if i - distance in devices]
    return lax.ppermute(block, axis, route)


def normalize(values, gain_row):
    mean_square = jnp.mean(values * values, -1, keepdims=True)
    return values * lax.rsqrt(mean_square + EPSILON) * gain_row


def rotate(values, angles):
    half_dim = values.shape[-1] // 2
    cosine = jnp.cos(angles)[:, None, :]
    sine_part = jnp.sin(angles)[:, None, :]
    first_half = values[..., :half_dim]
    second = values[..., half_dim:]
    return jnp.concatenate(
        [first_half * cosine - second * sine_part, second * cosine + first_half * sine_part], -1
    )


def angles_of(positions):
    half_dim = HEAD_DIM // 2
    inverse = 10000.0 ** (-2.0 * jnp.arange(half_dim, dtype=jnp.float32) / HEAD_DIM)
    return positions[:, None] * inverse[None, :]


def slot_of_tiles(owner_table, owners, capacity):
    onehot = (owner_table[:, None] == jnp.arange(owners, dtype=jnp.int32)[None, :]).astype(
        jnp.int32
    )
    earlier = jnp.cumsum(onehot, 0) - onehot
    ranking = jnp.sum(earlier * onehot, 1)
    return owner_table * capacity + ranking


def matrix_layout(width, head_width, head_dim, hidden_width, tile_side):
    left_attended = width // tile_side
    left_second = left_attended + head_width // tile_side
    left_hidden = left_second + width // tile_side
    right_key = head_width // tile_side
    right_value = right_key + head_dim // tile_side
    right_branch = right_value + head_dim // tile_side
    right_gate = right_branch + width // tile_side
    right_up = right_gate + hidden_width // tile_side
    right_down = right_up + hidden_width // tile_side
    return [
        (width, head_width, 0, 0),
        (width, head_dim, 0, right_key),
        (width, head_dim, 0, right_value),
        (head_width, width, left_attended, right_branch),
        (width, hidden_width, left_second, right_gate),
        (width, hidden_width, left_second, right_up),
        (hidden_width, width, left_hidden, right_down),
    ]


def project(values, blocks):
    row_count = values.shape[0]
    result = jnp.einsum(
        "nar,abrc->nbc",
        values.reshape(row_count, blocks.shape[0], blocks.shape[2]),
        blocks,
        preferred_element_type=jnp.float32,
    )
    return result.reshape(row_count, blocks.shape[1] * blocks.shape[3])


def back_project(values, blocks):
    row_count = values.shape[0]
    result = jnp.einsum(
        "nbc,abrc->nar",
        values.reshape(row_count, blocks.shape[1], blocks.shape[3]),
        blocks,
        preferred_element_type=jnp.float32,
    )
    return result.reshape(row_count, blocks.shape[0] * blocks.shape[2])


def dense_tile_grads(layout, left_blocks, right_blocks, tile_side):
    pieces = []
    for row_total, column_total, left_base, right_base in layout:
        left_part = left_blocks[:, left_base : left_base + row_total // tile_side]
        right_part = right_blocks[:, right_base : right_base + column_total // tile_side]
        product = jnp.einsum(
            "nar,nbc->abrc", left_part, right_part, preferred_element_type=jnp.float32
        )
        pieces.append(product.reshape(-1, tile_side, tile_side))
    pieces.append(jnp.zeros((1, tile_side, tile_side), jnp.float32))
    return jnp.concatenate(pieces, 0)


def block_tables(layout, tile_side, left_total):
    left_of, right_of = [], []
    for row_total, column_total, left_base, right_base in layout:
        for i in range(row_total // tile_side):
            for j in range(column_total // tile_side):
                left_of.append(left_base + i)
                right_of.append(right_base + j)
    return np.array(left_of + [left_total], np.int32), np.array(right_of + [0], np.int32)


def body(
    inputs,
    cotangent,
    segment_ids,
    gains,
    owner_table,
    master_tiles,
    left_stats,
    right_stats,
    left_roots,
    right_roots,
):
    owners = lax.axis_size("fsdp")
    replicas = lax.axis_size("replica")
    member = lax.axis_index("fsdp")
    capacity = master_tiles.shape[0]
    tile_side = master_tiles.shape[1]
    row_count = inputs.shape[0]
    width = inputs.shape[1]
    head_width = HEADS * HEAD_DIM
    tile_total = owner_table.shape[0]
    layout = matrix_layout(width, head_width, HEAD_DIM, FF, tile_side)
    slots = slot_of_tiles(owner_table, owners, capacity)
    slot_tile = (
        jnp.full((owners * capacity,), tile_total, jnp.int32)
        .at[slots]
        .set(jnp.arange(tile_total, dtype=jnp.int32))
    )
    known = owners == 8 and replicas == 4 and capacity == 204
    low_tiles = master_tiles.astype(jnp.bfloat16)
    if known:
        full = gather(low_tiles).reshape(owners * capacity, tile_side, tile_side)
    else:
        full = lax.all_gather(low_tiles, "fsdp", axis=0, tiled=True)
    all_tiles = jnp.take(full, slots, axis=0)
    weights = []
    offset = 0
    for row_total, column_total, left_base, right_base in layout:
        number = row_total // tile_side * (column_total // tile_side)
        weights.append(
            all_tiles[offset : offset + number].reshape(
                row_total // tile_side, column_total // tile_side, tile_side, tile_side
            )
        )
        offset = offset + number
    w_query, w_key, w_value, w_out, w_gate, w_up, w_down = weights
    base_row = member * row_count
    own_ids = lax.dynamic_slice_in_dim(segment_ids, base_row, row_count, 0)
    starts = jnp.sum((segment_ids[None, :] < own_ids[:, None]).astype(jnp.int32), 1)
    positions = (base_row + jnp.arange(row_count, dtype=jnp.int32) - starts).astype(jnp.float32)
    angles = angles_of(positions)
    inputs_wide = inputs.astype(jnp.float32)
    normed = normalize(inputs_wide, gains[0]).astype(jnp.bfloat16)
    query_pre = project(normed, w_query)
    key_pre = project(normed, w_key)
    values_own = project(normed, w_value).astype(jnp.bfloat16)
    queries = rotate(query_pre.reshape(row_count, HEADS, HEAD_DIM), angles).astype(jnp.bfloat16)
    keys_own = rotate(key_pre[:, None, :], angles)[:, 0, :].astype(jnp.bfloat16)
    reach = WINDOW // row_count
    own_pair = jnp.concatenate([keys_own, values_own], 1)
    received = [shifted(own_pair, "fsdp", distance_back) for distance_back in range(reach, 0, -1)]
    pair_rows = jnp.concatenate(received + [own_pair], 0)
    key_rows = pair_rows[:, :HEAD_DIM]
    value_rows = pair_rows[:, HEAD_DIM:]
    padded_ids = jnp.concatenate([jnp.full((reach * row_count,), -1, jnp.int32), segment_ids], 0)
    key_ids = lax.dynamic_slice_in_dim(padded_ids, base_row, (reach + 1) * row_count, 0)
    distance = (
        jnp.arange(row_count, dtype=jnp.int32)[:, None]
        + reach * row_count
        - jnp.arange((reach + 1) * row_count, dtype=jnp.int32)[None, :]
    )
    allowed = (own_ids[:, None] == key_ids[None, :]) & (distance >= 0) & (distance < WINDOW)
    score_scale = HEAD_DIM ** (-0.5)
    scores = (
        jnp.einsum("nhd,kd->hnk", queries, key_rows, preferred_element_type=jnp.float32)
        * score_scale
    )
    scores = jnp.where(allowed[None], scores, -1e30)
    row_peak = jnp.max(scores, -1, keepdims=True)
    exponent = jnp.exp(scores - row_peak)
    row_total_sum = jnp.sum(exponent, -1, keepdims=True)
    probability = (exponent / row_total_sum).astype(jnp.bfloat16)
    log_total = row_peak + jnp.log(row_total_sum)
    attended = (
        jnp.einsum("hnk,kd->nhd", probability, value_rows, preferred_element_type=jnp.float32)
        .reshape(row_count, head_width)
        .astype(jnp.bfloat16)
    )
    middle = inputs_wide + project(attended, w_out)
    normed_two = normalize(middle, gains[1]).astype(jnp.bfloat16)
    gate = project(normed_two, w_gate)
    up_part = project(normed_two, w_up)

    def geglu(gate_values, up_values):
        return jax.nn.gelu(gate_values, approximate=True) * up_values

    hidden_wide, geglu_back = jax.vjp(geglu, gate, up_part)
    hidden = hidden_wide.astype(jnp.bfloat16)
    outputs = (middle + project(hidden, w_down)).astype(jnp.bfloat16)
    grad_hidden = back_project(cotangent, w_down)
    gate_back, up_back = geglu_back(grad_hidden)
    gate_grad = gate_back.astype(jnp.bfloat16)
    up_grad = up_back.astype(jnp.bfloat16)
    grad_normed_two = back_project(gate_grad, w_gate) + back_project(up_grad, w_up)
    middle_back, norm_two_back = jax.vjp(normalize, middle, gains[1])[1](grad_normed_two)
    grad_middle = cotangent.astype(jnp.float32) + middle_back
    branch_grad = grad_middle.astype(jnp.bfloat16)
    grad_attended = (
        back_project(branch_grad, w_out).astype(jnp.bfloat16).reshape(row_count, HEADS, HEAD_DIM)
    )
    scores_again = (
        jnp.einsum("nhd,kd->hnk", queries, key_rows, preferred_element_type=jnp.float32)
        * score_scale
    )
    scores_again = jnp.where(allowed[None], scores_again, -1e30)
    exact_prob = jnp.exp(scores_again - log_total)
    grad_prob = jnp.einsum(
        "nhd,kd->hnk", grad_attended, value_rows, preferred_element_type=jnp.float32
    )
    grad_scores = (
        exact_prob * (grad_prob - jnp.sum(exact_prob * grad_prob, -1, keepdims=True))
    ).astype(jnp.bfloat16)
    grad_queries = (
        jnp.einsum("hnk,kd->nhd", grad_scores, key_rows, preferred_element_type=jnp.float32)
        * score_scale
    )
    grad_keys = (
        jnp.einsum("hnk,nhd->kd", grad_scores, queries, preferred_element_type=jnp.float32)
        * score_scale
    )
    grad_values = jnp.einsum(
        "hnk,nhd->kd", probability, grad_attended, preferred_element_type=jnp.float32
    )
    grad_pairs = jnp.concatenate([grad_keys, grad_values], 1)
    own_grad = grad_pairs[reach * row_count :]
    for distance_back in range(1, reach + 1):
        sent_rows = grad_pairs[
            (reach - distance_back) * row_count : (reach - distance_back + 1) * row_count
        ]
        own_grad = own_grad + shifted(
            sent_rows.astype(jnp.bfloat16), "fsdp", -distance_back
        ).astype(sent_rows.dtype)
    grad_query_pre = (
        rotate(grad_queries, -angles).reshape(row_count, head_width).astype(jnp.bfloat16)
    )
    grad_key_pre = rotate(own_grad[:, None, :HEAD_DIM], -angles)[:, 0, :].astype(jnp.bfloat16)
    grad_values_low = own_grad[:, HEAD_DIM:].astype(jnp.bfloat16)
    grad_normed = (
        back_project(grad_query_pre, w_query)
        + back_project(grad_key_pre, w_key)
        + back_project(grad_values_low, w_value)
    )
    inputs_back, norm_one_back = jax.vjp(normalize, inputs_wide, gains[0])[1](grad_normed)
    input_grad = (grad_middle + inputs_back).astype(jnp.bfloat16)
    gain_grads = lax.psum(jnp.stack([norm_one_back, norm_two_back]), ("replica", "fsdp"))
    gain_rate = GAIN_STEP * (row_count * owners * replicas) ** (-0.5)
    new_gains = gains - gain_rate * gain_grads
    left_parts = jnp.concatenate([normed, attended, normed_two, hidden], 1)
    right_parts = jnp.concatenate(
        [grad_query_pre, grad_key_pre, grad_values_low, branch_grad, gate_grad, up_grad, cotangent],
        1,
    )
    left_blocks = left_parts.reshape(row_count, -1, tile_side)
    right_blocks = right_parts.reshape(row_count, -1, tile_side)
    if known:
        left_of, right_of = block_tables(layout, tile_side, left_blocks.shape[1])
        left_at = jnp.take(jnp.asarray(left_of), slot_tile).reshape(owners, capacity)
        right_at = jnp.take(jnp.asarray(right_of), slot_tile).reshape(owners, capacity)
        left_turned = left_parts.T.reshape(-1, tile_side, row_count)
        right_turned = right_blocks.transpose(1, 0, 2)
        grads_low = reduce_tiles(left_at, right_at, left_turned, right_turned)
    else:
        dense = dense_tile_grads(layout, left_blocks, right_blocks, tile_side)
        partial_sum = lax.psum_scatter(
            jnp.take(dense, slot_tile, axis=0), "fsdp", scatter_dimension=0, tiled=True
        )
        grads_low = lax.psum(partial_sum.astype(jnp.bfloat16), "replica")
    grads_all, left_all, right_all, master_all, low_all = shampoo(
        grads_low, left_stats, right_stats, left_roots, right_roots, master_tiles
    )
    return (
        outputs,
        input_grad,
        gain_grads,
        new_gains,
        grads_all,
        master_all,
        low_all,
        left_all,
        right_all,
    )


def solution(mesh):
    return jax.shard_map(
        body,
        mesh=mesh,
        in_specs=(
            P(("replica", "fsdp"), None),
            P(("replica", "fsdp"), None),
            P("replica"),
            P(),
            P(),
            P("fsdp", None, None),
            P("fsdp", None, None),
            P("fsdp", None, None),
            P("fsdp", None, None),
            P("fsdp", None, None),
        ),
        out_specs=(
            P(("replica", "fsdp"), None),
            P(("replica", "fsdp"), None),
            P(),
            P(),
            P("fsdp", None, None),
            P("fsdp", None, None),
            P("fsdp", None, None),
            P("fsdp", None, None),
            P("fsdp", None, None),
        ),
        check_vma=False,
    )
```

```python
import functools

import jax
import jax.numpy as jnp
import numpy as np
from jax import lax
from jax.experimental import pallas as pl
from jax.experimental.pallas import tpu as pltpu
from jax.sharding import PartitionSpec as P

HEADS = 12
HEAD_DIM = 128
FF = 4608
WINDOW = 1024


EPSILON = 1e-06
STEP_RATE = 0.02
STAT_DECAY = 0.5
GAIN_STEP = 0.1
F32, BF16 = jnp.float32, jnp.bfloat16
MESH = pl.DeviceIdType.MESH


def gather_kernel(chunk, deep, shared, depth, own, full, keep_sem, up_s, up_r, down_s, down_r, x_s, x_r, y_s, y_r, core_s, core_r):
    run = deep + shared
    half = (2 * deep + shared) * chunk
    whole = 2 * deep + shared
    replica = lax.axis_index("replica")
    member = lax.axis_index("fsdp")
    y, core = replica // 2, replica % 2
    z, x = member // 2, member % 2
    mirrored = z // 2
    inner = z + mirrored * (3 - 2 * z)
    above, below = (replica, (z + 1) * 2 + x), (replica, (z - 1) * 2 + x)
    across, beside, twin = (replica, z * 2 + 1 - x), ((1 - y) * 2 + core, member), (y * 2 + 1 - core, member)

    barrier = pltpu.get_barrier_semaphore()
    def greet(device):
        pl.semaphore_signal(barrier, inc=1, device_id=device, device_id_type=MESH)
    pl.when(z < 3)(lambda: greet(above))
    pl.when(z > 0)(lambda: greet(below))
    greet(across); greet(beside); greet(twin)
    @pl.when((z == 0) | (z == 3))
    def _():
        pl.semaphore_wait(barrier, 4)
    @pl.when((z > 0) & (z < 3))
    def _():
        pl.semaphore_wait(barrier, 5)

    keep = pltpu.make_async_copy(own, full.at[member], keep_sem)
    keep.start()

    def place(k, plane):
        return plane * (whole - 1) + k * (1 - 2 * plane)
    def rows(chunk_at, owner_core):
        return pl.ds(owner_core * half + chunk_at * chunk, chunk)
    def copy(source_owner, chunk_at, send, recv, device, from_own=False, owner_core=None):
        at = rows(chunk_at, core if owner_core is None else owner_core)
        target = full.at[source_owner, at]
        source = own.at[at] if from_own else target
        return pltpu.make_async_remote_copy(src_ref=source, dst_ref=target, send_sem=send, recv_sem=recv, device_id=device, device_id_type=MESH)
    def go_up(zb, k, own_block=False):
        return copy(zb * 2 + x, place(k, y), up_s.at[zb, k], up_r.at[zb, k], above, own_block)
    def go_down(zb, k, own_block=False):
        return copy(zb * 2 + x, place(k, y), down_s.at[zb, k], down_r.at[zb, k], below, own_block)
    def go_x(zb, k, own_block=False):
        return copy(zb * 2 + x, place(k, y), x_s.at[zb, k], x_r.at[zb, k], across, own_block)
    def come_x(zb, k):
        return copy(zb * 2 + 1 - x, place(k, y), x_s.at[zb, k], x_r.at[zb, k], across)
    def go_y(owner, k):
        return copy(owner, place(k, y), y_s.at[owner, k], y_r.at[owner, k], beside)
    def come_y(owner, k):
        return copy(owner, place(k, 1 - y), y_s.at[owner, k], y_r.at[owner, k], beside)
    def go_core(owner, at):
        return copy(owner, at, core_s.at[owner, at], core_r.at[owner, at], twin)

    def onward(owner, k):
        go_core(owner, place(k, y)).start()
        @pl.when(k < deep)
        def _():
            if depth:
                @pl.when(k >= depth)
                def _():
                    go_y(owner, k - depth).wait_send()
            go_y(owner, k).start()

    def leave(make, zb, k, own_block):
        if depth:
            @pl.when(k >= depth)
            def _():
                make(zb, k - depth, own_block).wait_send()
        make(zb, k, own_block).start()

    def across_block(g):
        b = g if g >= 2 else (g + inner) % 2
        return b + mirrored * (3 - 2 * b)

    def group(g):
        def tick(k, _):
            if g == 0:
                pl.when(z < 3)(lambda: leave(go_up, z, k, True))
                pl.when(z > 0)(lambda: leave(go_down, z, k, True))
                leave(go_x, z, k, True)
            if 1 <= g <= 3:
                @pl.when(z - g >= 0)
                def _():
                    zb = z - g
                    pltpu_wait = copy(zb * 2 + x, place(k, y), up_s.at[zb, k], up_r.at[zb, k], above)
                    pltpu_wait.wait_recv()
                    pl.when(z < 3)(lambda: leave(go_up, zb, k, False))
                    onward(zb * 2 + x, k)
                @pl.when(z + g <= 3)
                def _():
                    zb = z + g
                    copy(zb * 2 + x, place(k, y), down_s.at[zb, k], down_r.at[zb, k], below).wait_recv()
                    pl.when(z > 0)(lambda: leave(go_down, zb, k, False))
                    onward(zb * 2 + x, k)
                leave(go_x, across_block(g), k, False)
            if 1 <= g <= 4:
                b = across_block(g - 1)
                come_x(b, k).wait_recv()
                onward(b * 2 + 1 - x, k)
            if g >= 2:
                @pl.when(k < deep)
                def _():
                    def take(owner):
                        come_y(owner, k).wait_recv()
                        go_core(owner, place(k, 1 - y)).start()
                    if g - 1 <= 3:
                        pl.when(z - (g - 1) >= 0)(lambda: take((z - (g - 1)) * 2 + x))
                        pl.when(z + (g - 1) <= 3)(lambda: take((z + (g - 1)) * 2 + x))
                    if g - 1 >= 1:
                        take(across_block(g - 2) * 2 + 1 - x)
            return 0
        lax.fori_loop(0, run, tick, 0)
    for g in range(6):
        group(g)

    first = run - depth if depth else 0
    firsty = deep - depth if depth else 0
    def drain_z(zb, _):
        def one(k, _):
            @pl.when((zb <= z) & (z < 3))
            def _():
                go_up(zb, k).wait_send()
            @pl.when((zb >= z) & (z > 0))
            def _():
                go_down(zb, k).wait_send()
            go_x(zb, k).wait_send()
            return 0
        lax.fori_loop(first, run, one, 0)
        return 0
    lax.fori_loop(0, 4, drain_z, 0)
    def drain_owner(owner, _):
        @pl.when(owner != member)
        def _():
            def one_y(k, _):
                go_y(owner, k).wait_send()
                return 0
            lax.fori_loop(firsty, deep, one_y, 0)
            def one_core(k, _):
                go_core(owner, k).wait_send()
                copy(owner, k, core_s.at[owner, k], core_r.at[owner, k], twin, owner_core=1 - core).wait_recv()
                return 0
            lax.fori_loop(0, whole, one_core, 0)
        return 0
    lax.fori_loop(0, 8, drain_owner, 0)
    keep.wait()

def gather(own, chunk=6, deep=6, shared=5, depth=0):
    run, whole = deep + shared, 2 * deep + shared
    assert whole * chunk * 2 == own.shape[0]
    D = pltpu.SemaphoreType.DMA
    return pl.pallas_call(
        functools.partial(gather_kernel, chunk, deep, shared, depth),
        out_shape=jax.ShapeDtypeStruct((8,) + own.shape, own.dtype),
        in_specs=[pl.BlockSpec(memory_space=pl.ANY)],
        out_specs=pl.BlockSpec(memory_space=pl.ANY),
        scratch_shapes=[D] + [D((4, run))] * 6 + [D((8, deep))] * 2 + [D((8, whole))] * 2,
        compiler_params=pltpu.CompilerParams(collective_id=0, has_side_effects=True),
    )(own)


def prepare_kernel(owners, capacity, owner_row, block_values, inputs, cotangent, gain, slots, blocks_at, normed, early, ranks):
    total = owner_row.shape[1]
    lanes = 128
    owner = owner_row[...]
    same = (owner == lax.broadcasted_iota(jnp.int32, (owners, total), 0)).astype(F32)
    ones_before = (lax.broadcasted_iota(jnp.int32, (lanes, lanes), 0) < lax.broadcasted_iota(jnp.int32, (lanes, lanes), 1)).astype(BF16)
    carry = jnp.zeros((owners, 1), F32)
    for c in range(total // lanes):
        at = slice(c * lanes, (c + 1) * lanes)
        piece = same[:, at]
        before = jnp.dot(piece.astype(BF16), ones_before, preferred_element_type=F32) + carry
        ranks[:, at] = jnp.sum(before * piece, 0, keepdims=True).astype(jnp.int32)
        carry = carry + jnp.sum(piece, 1, keepdims=True)
    slot = jnp.where(owner >= 0, owner * capacity + ranks[...], -1)
    slots[...] = slot
    padded = blocks_at.shape[1]
    for o in range(owners):
        here = lax.broadcasted_iota(jnp.int32, (padded, total), 0)
        here = jnp.where(here < capacity, here + o * capacity, -2)
        hit = jnp.where(here == slot, 1.0, 0.0).astype(BF16)
        blocks_at[o] = jnp.dot(hit, block_values[...], preferred_element_type=F32)
    values = inputs[...].astype(F32)
    mean_square = jnp.mean(values * values, -1, keepdims=True)
    scaled = values * lax.rsqrt(mean_square + EPSILON) * gain[...]
    normed[...] = scaled.astype(BF16)
    count = early.shape[0] // 2
    for c in range(count):
        at = slice(c * lanes, (c + 1) * lanes)
        early[c] = scaled[:, at].T.astype(BF16)
        early[count + c] = cotangent[:, at]

def prepare(owners, capacity, owner_row, block_values, inputs, cotangent, gain):
    rows, width = inputs.shape
    padded = -(-capacity // 16) * 16
    S = jax.ShapeDtypeStruct
    spec = pl.BlockSpec(memory_space=pltpu.VMEM)
    return pl.pallas_call(
        functools.partial(prepare_kernel, owners, capacity),
        in_specs=[spec] * 5,
        out_specs=[spec] * 4,
        out_shape=[S(owner_row.shape, jnp.int32), S((owners, padded, 128), F32), S((rows, width), BF16),
                   S((2 * width // 128, 128, rows), BF16)],
        scratch_shapes=[pltpu.VMEM(owner_row.shape, jnp.int32)],
        compiler_params=pltpu.CompilerParams(vmem_limit_bytes=40 * 2**20),
    )(owner_row, block_values, inputs, cotangent, gain)


BY_ROWS = (((1,), (1,)), ((), ()))
BY_COLUMNS = (((0,), (0,)), ((), ()))


def mul(a, b):
    return jnp.dot(a, b, preferred_element_type=F32)


def mul_turned(a, b):
    return lax.dot_general(a, b, BY_ROWS, preferred_element_type=F32)


def mul_summed(a, b):
    return lax.dot_general(a, b, BY_COLUMNS, preferred_element_type=F32)


def turn(part, cosine, sine):
    return part * cosine + pltpu.roll(part, HEAD_DIM // 2, 1) * sine


def fetch_tile(full, slots, number, target, sem):
    pltpu.make_async_copy(full.at[slots[number]], target, sem).start()


def block_at(start, size):
    return pl.ds(pl.multiple_of(start, size), size)


def project_kernel(side, slots, full, normed, cosine, sine, queries, pair, weights, sems):
    wide = normed.shape[1] // side
    heads = queries.shape[1] // side

    def fetch(n, _):
        j, i = n // wide, n % wide
        number = jnp.where(j < heads, i * heads + j, wide * j + i)
        fetch_tile(full, slots, number, weights.at[block_at(i * side, side), block_at(j * side, side)], sems.at[j // 2])
        return 0

    lax.fori_loop(0, wide * (heads + 2), fetch, 0, unroll=8)
    for c in range((heads + 2) // 2):
        view = weights.at[:, pl.ds(c * 2 * side, 2 * side)]
        pltpu.make_async_copy(view, view, sems.at[c]).wait()
        product = mul(normed[...], view[...])
        for k in range(2):
            part = product[:, k * side : (k + 1) * side]
            if c < heads // 2:
                queries[:, (2 * c + k) * side : (2 * c + k + 1) * side] = turn(part, cosine[...], sine[...]).astype(BF16)
            elif k == 0:
                pair[:, :side] = turn(part, cosine[...], sine[...]).astype(BF16)
            else:
                pair[:, side:] = part.astype(BF16)


def project_heads(slots, full, normed, cosine, sine):
    rows, width = normed.shape
    side = full.shape[1]
    V = pltpu.VMEM
    spec = pl.BlockSpec(memory_space=V)
    return pl.pallas_call(
        functools.partial(project_kernel, side),
        grid_spec=pltpu.PrefetchScalarGridSpec(
            num_scalar_prefetch=1,
            grid=(),
            in_specs=[pl.BlockSpec(memory_space=pl.ANY), spec, spec, spec],
            out_specs=[spec, spec],
            scratch_shapes=[V((width, (HEADS + 2) * side), BF16), pltpu.SemaphoreType.DMA(((HEADS + 2) // 2,))],
        ),
        out_shape=[jax.ShapeDtypeStruct((rows, HEADS * side), BF16), jax.ShapeDtypeStruct((rows, 2 * side), BF16)],
        compiler_params=pltpu.CompilerParams(vmem_limit_bytes=40 * 2**20),
    )(slots, full, normed, cosine, sine)


def pairs_kernel(pair, pairs, keep_sem, sends, recvs):
    replica = lax.axis_index("replica")
    member = lax.axis_index("fsdp")
    count = pairs.shape[0]
    barrier = pltpu.get_barrier_semaphore()
    others = [(member + step) % count for step in range(1, count)]
    for other in others:
        pl.semaphore_signal(barrier, inc=1, device_id=(replica, other), device_id_type=MESH)
    pl.semaphore_wait(barrier, count - 1)
    keep = pltpu.make_async_copy(pair, pairs.at[member], keep_sem)
    keep.start()

    def copy(step, owner):
        return pltpu.make_async_remote_copy(
            src_ref=pair, dst_ref=pairs.at[owner], send_sem=sends.at[step], recv_sem=recvs.at[step],
            device_id=(replica, (member + step) % count), device_id_type=MESH)

    for step in range(1, count):
        copy(step, member).start()
    for step in range(1, count):
        copy(step, (member + count - step) % count).wait_recv()
    for step in range(1, count):
        copy(step, member).wait_send()
    keep.wait()


def gather_pairs(pair, count):
    D = pltpu.SemaphoreType.DMA
    spec = pl.BlockSpec(memory_space=pltpu.VMEM)
    return pl.pallas_call(
        pairs_kernel,
        out_shape=jax.ShapeDtypeStruct((count,) + pair.shape, pair.dtype),
        in_specs=[spec],
        out_specs=spec,
        scratch_shapes=[D, D((count,)), D((count,))],
        compiler_params=pltpu.CompilerParams(collective_id=2, has_side_effects=True),
    )(pair)


def fill_bias(first, own_ids, all_ids, bias):
    shape = bias.shape
    distance = first + lax.broadcasted_iota(jnp.int32, shape, 0) - lax.broadcasted_iota(jnp.int32, shape, 1)
    allowed = (own_ids[...] == all_ids[...]) & (distance >= 0) & (distance < WINDOW)
    bias[...] = jnp.where(allowed, 0.0, -1e30)


def softmax_of(scores):
    exponent = jnp.exp(scores - jnp.max(scores, -1, keepdims=True))
    return exponent / jnp.sum(exponent, -1, keepdims=True)


def attend_kernel(side, slots, first, full, queries, pairs, own_ids, all_ids, inputs, gain,
                  attended_turned, normed_two, normed_two_turned, middle, weights, attended, bias, sems):
    heads = attended.shape[1] // side
    wide = middle.shape[1] // side

    def fetch(n, _):
        j, i = n // heads, n % heads
        number = (heads + 2) * wide + i * wide + j
        fetch_tile(full, slots, number, weights.at[block_at(i * side, side), block_at(j * side, side)], sems.at[j // 2])
        return 0

    lax.fori_loop(0, wide * heads, fetch, 0, unroll=8)
    fill_bias(first[0], own_ids, all_ids, bias)
    keys = pairs[:, :, :side].reshape(-1, side)
    values = pairs[:, :, side:].reshape(-1, side)
    scale = HEAD_DIM ** (-0.5)
    for head in range(heads):
        at = slice(head * side, (head + 1) * side)
        scores = mul_turned(queries[:, at], keys) * scale + bias[...]
        product = mul(softmax_of(scores).astype(BF16), values)
        attended[:, at] = product.astype(BF16)
        attended_turned[head] = product.T.astype(BF16)
    total = jnp.zeros((inputs.shape[0], 1), F32)
    for c in range(wide // 2):
        view = weights.at[:, pl.ds(c * 2 * side, 2 * side)]
        pltpu.make_async_copy(view, view, sems.at[c]).wait()
        at = slice(c * 2 * side, (c + 1) * 2 * side)
        part = inputs[:, at].astype(F32) + mul(attended[...], view[...])
        middle[:, at] = part
        total = total + jnp.sum(part * part, -1, keepdims=True)
    scaled = lax.rsqrt(total / middle.shape[1] + EPSILON)
    for c in range(wide):
        at = slice(c * side, (c + 1) * side)
        part = middle[:, at] * scaled * gain[:, at]
        normed_two[:, at] = part.astype(BF16)
        normed_two_turned[c] = part.T.astype(BF16)


def attend(slots, first, full, queries, pairs, own_ids, all_ids, inputs, gain):
    rows, width = inputs.shape
    side = full.shape[1]
    V = pltpu.VMEM
    spec = pl.BlockSpec(memory_space=V)
    S = jax.ShapeDtypeStruct
    return pl.pallas_call(
        functools.partial(attend_kernel, side),
        grid_spec=pltpu.PrefetchScalarGridSpec(
            num_scalar_prefetch=2,
            grid=(),
            in_specs=[pl.BlockSpec(memory_space=pl.ANY)] + [spec] * 6,
            out_specs=[spec] * 4,
            scratch_shapes=[V((HEADS * side, width), BF16), V((rows, HEADS * side), BF16),
                            V((rows, pairs.shape[0] * pairs.shape[1]), F32), pltpu.SemaphoreType.DMA((width // side // 2,))],
        ),
        out_shape=[S((HEADS, side, rows), BF16), S((rows, width), BF16), S((width // side, side, rows), BF16), S((rows, width), F32)],
        compiler_params=pltpu.CompilerParams(vmem_limit_bytes=40 * 2**20),
    )(slots, first, full, queries, pairs, own_ids, all_ids, inputs, gain)


def norm_back(values, gain, grads):
    mean_square = jnp.mean(values * values, -1, keepdims=True)
    scaled = lax.rsqrt(mean_square + EPSILON)
    weighed = grads * gain
    inner = jnp.mean(weighed * values, -1, keepdims=True)
    back = scaled * weighed - values * (scaled * scaled * scaled * inner)
    return back, jnp.sum(grads * values * scaled, 0, keepdims=True)


GELU_SCALE = 0.7978845608028654
GELU_CUBE = 0.044715


def mlp_kernel(side, ring, slots, full, normed_own, normed_beside, cotangent_own, cotangent_beside, middle, gain,
               hidden_turned, gate_grad, up_grad, outputs, grad_middle, branch, branch_blocks, gain_term,
               normed, cotangent, forward, backward, gate_ring, up_ring, down_ring, sems):
    rows, width = normed_own.shape
    wide = width // side
    hidden_blocks = hidden_turned.shape[0]
    steps = hidden_blocks // 2
    heads = HEADS
    base = (heads + 2) * wide + heads * wide

    def fetch(j):
        slot = j % ring

        def one(n, _):
            i, k = n // 2, n % 2
            column = 2 * j + k
            fetch_tile(full, slots, base + i * hidden_blocks + column,
                       gate_ring.at[slot, block_at(i * side, side), block_at(k * side, side)], sems.at[slot])
            fetch_tile(full, slots, base + (wide + i) * hidden_blocks + column,
                       up_ring.at[slot, block_at(i * side, side), block_at(k * side, side)], sems.at[slot])
            fetch_tile(full, slots, base + 2 * wide * hidden_blocks + column * wide + i,
                       down_ring.at[slot, block_at(k * side, side), block_at(i * side, side)], sems.at[slot])
            return 0

        lax.fori_loop(0, 2 * wide, one, 0, unroll=8)

    for j in range(ring - 1):
        fetch(j)
    normed[:rows] = normed_own[...]
    cotangent[:rows] = cotangent_own[...]
    for c in range(wide):
        at = slice(c * side, (c + 1) * side)
        normed[rows:, at] = normed_beside[c].astype(F32).T.astype(BF16)
        cotangent[rows:, at] = cotangent_beside[c]
    forward[...] = jnp.zeros_like(forward)
    backward[...] = jnp.zeros_like(backward)

    def step(j, _):
        slot = j % ring
        for target in (gate_ring, up_ring, down_ring):
            view = target.at[slot]
            pltpu.make_async_copy(view, view, sems.at[slot]).wait()

        @pl.when(j + ring - 1 < steps)
        def _():
            fetch(j + ring - 1)

        gate = mul(normed[...], gate_ring[slot])
        up = mul(normed[...], up_ring[slot])
        grad_hidden = mul_turned(cotangent[...], down_ring[slot])
        square = gate * gate
        bend = jnp.tanh(GELU_SCALE * gate * (1.0 + GELU_CUBE * square))
        share = 0.5 * (1.0 + bend)
        active = gate * share
        slope = share + 0.5 * gate * (1.0 - bend * bend) * (GELU_SCALE * (1.0 + 3.0 * GELU_CUBE * square))
        hidden_wide = active * up
        hidden = hidden_wide.astype(BF16)
        gate_low = (grad_hidden * up * slope).astype(BF16)
        up_low = (grad_hidden * active).astype(BF16)
        for k in range(2):
            at = slice(k * side, (k + 1) * side)
            hidden_turned[2 * j + k] = hidden_wide[:, at].T.astype(BF16)
            gate_grad[2 * j + k] = gate_low[:, at]
            up_grad[2 * j + k] = up_low[:, at]
        forward[...] += mul(hidden[:rows], down_ring[slot])
        backward[...] += mul_turned(gate_low[:rows], gate_ring[slot]) + mul_turned(up_low[:rows], up_ring[slot])
        return 0

    lax.fori_loop(0, steps, step, 0)
    outputs[...] = (middle[...] + forward[...]).astype(BF16)
    back, term = norm_back(middle[...], gain[...], backward[...])
    gain_term[...] = term
    total = cotangent_own[...].astype(F32) + back
    grad_middle[...] = total
    low = total.astype(BF16)
    branch[...] = low
    for c in range(wide):
        branch_blocks[c] = low[:, c * side : (c + 1) * side]


def mlp(slots, full, normed_own, normed_beside, cotangent_own, cotangent_beside, middle, gain, ring=3):
    rows, width = normed_own.shape
    side = full.shape[1]
    blocks = FF // side
    V = pltpu.VMEM
    spec = pl.BlockSpec(memory_space=V)
    S = jax.ShapeDtypeStruct
    return pl.pallas_call(
        functools.partial(mlp_kernel, side, ring),
        grid_spec=pltpu.PrefetchScalarGridSpec(
            num_scalar_prefetch=1,
            grid=(),
            in_specs=[pl.BlockSpec(memory_space=pl.ANY)] + [spec] * 6,
            out_specs=[spec] * 8,
            scratch_shapes=[V((2 * rows, width), BF16), V((2 * rows, width), BF16), V((rows, width), F32), V((rows, width), F32),
                            V((ring, width, 2 * side), BF16), V((ring, width, 2 * side), BF16), V((ring, 2 * side, width), BF16),
                            pltpu.SemaphoreType.DMA((ring,))],
        ),
        out_shape=[S((blocks, side, 2 * rows), BF16), S((blocks, 2 * rows, side), BF16), S((blocks, 2 * rows, side), BF16),
                   S((rows, width), BF16), S((rows, width), F32), S((rows, width), BF16), S((width // side, rows, side), BF16),
                   S((1, width), F32)],
        compiler_params=pltpu.CompilerParams(vmem_limit_bytes=56 * 2**20),
    )(slots, full, normed_own, normed_beside, cotangent_own, cotangent_beside, middle, gain)


def attend_back_kernel(side, slots, first, full, branch, queries, pairs, own_ids, all_ids, cosine, sine,
                       query_grad, pair_grad, own_pair_grad, weights, attended_grad, bias, key_total, value_total, sems):
    rows = branch.shape[0]
    heads = queries.shape[1] // side
    wide = branch.shape[1] // side

    def fetch(n, _):
        i, j = n // wide, n % wide
        number = (heads + 2) * wide + i * wide + j
        fetch_tile(full, slots, number, weights.at[block_at(i * side, side), block_at(j * side, side)], sems.at[i // 2])
        return 0

    lax.fori_loop(0, wide * heads, fetch, 0, unroll=8)
    fill_bias(first[0], own_ids, all_ids, bias)
    keys = pairs[:, :, :side].reshape(-1, side)
    values = pairs[:, :, side:].reshape(-1, side)
    scale = HEAD_DIM ** (-0.5)
    for c in range(heads // 2):
        view = weights.at[pl.ds(c * 2 * side, 2 * side), :]
        pltpu.make_async_copy(view, view, sems.at[c]).wait()
        attended_grad[:, c * 2 * side : (c + 1) * 2 * side] = mul_turned(branch[...], view[...]).astype(BF16)
    key_total[...] = jnp.zeros_like(key_total)
    value_total[...] = jnp.zeros_like(value_total)
    for head in range(heads):
        at = slice(head * side, (head + 1) * side)
        scores = mul_turned(queries[:, at], keys) * scale + bias[...]
        share = softmax_of(scores)
        share_grad = mul_turned(attended_grad[:, at], values)
        inner = jnp.sum(share * share_grad, -1, keepdims=True)
        score_grad = (share * (share_grad - inner)).astype(BF16)
        query_grad[head] = turn(mul(score_grad, keys) * scale, cosine[...], -sine[...]).astype(BF16)
        key_total[...] += mul_summed(score_grad, queries[:, at])
        value_total[...] += mul_summed(share.astype(BF16), attended_grad[:, at])
    key_total[...] = key_total[...] * scale
    for b in range(pairs.shape[0]):
        at = slice(b * rows, (b + 1) * rows)
        pair_grad[b, :, :side] = key_total[at].astype(BF16)
        pair_grad[b, :, side:] = value_total[at].astype(BF16)
    own = block_at(first[0], rows)
    own_pair_grad[:, :side] = key_total[own, :]
    own_pair_grad[:, side:] = value_total[own, :]


def attend_back(slots, first, full, branch, queries, pairs, own_ids, all_ids, cosine, sine):
    rows, width = branch.shape
    side = full.shape[1]
    key_rows = pairs.shape[0] * pairs.shape[1]
    V = pltpu.VMEM
    spec = pl.BlockSpec(memory_space=V)
    S = jax.ShapeDtypeStruct
    return pl.pallas_call(
        functools.partial(attend_back_kernel, side),
        grid_spec=pltpu.PrefetchScalarGridSpec(
            num_scalar_prefetch=2,
            grid=(),
            in_specs=[pl.BlockSpec(memory_space=pl.ANY)] + [spec] * 7,
            out_specs=[spec] * 3,
            scratch_shapes=[V((HEADS * side, width), BF16), V((rows, HEADS * side), BF16), V((rows, key_rows), F32),
                            V((key_rows, side), F32), V((key_rows, side), F32), pltpu.SemaphoreType.DMA((HEADS // 2,))],
        ),
        out_shape=[S((HEADS, rows, side), BF16), S(pairs.shape, BF16), S((rows, 2 * side), F32)],
        compiler_params=pltpu.CompilerParams(vmem_limit_bytes=40 * 2**20),
    )(slots, first, full, branch, queries, pairs, own_ids, all_ids, cosine, sine)


def pairs_back_kernel(pair_grad, own_grad, cosine, sine, low, arrived, sends, recvs):
    replica = lax.axis_index("replica")
    member = lax.axis_index("fsdp")
    count = pair_grad.shape[0]
    side = cosine.shape[1]
    barrier = pltpu.get_barrier_semaphore()
    for step in range(1, count):
        pl.semaphore_signal(barrier, inc=1, device_id=(replica, (member + step) % count), device_id_type=MESH)
    pl.semaphore_wait(barrier, count - 1)

    def copy(step):
        target = (member + step) % count
        return pltpu.make_async_remote_copy(
            src_ref=pair_grad.at[target], dst_ref=arrived.at[step], send_sem=sends.at[step], recv_sem=recvs.at[step],
            device_id=(replica, target), device_id_type=MESH)

    for step in range(1, count):
        copy(step).start()
    total = own_grad[...]
    for step in range(1, count):
        copy(step).wait_recv()
        total = total + arrived[step].astype(F32)
    low[0] = turn(total[:, :side], cosine[...], -sine[...]).astype(BF16)
    low[1] = total[:, side:].astype(BF16)
    for step in range(1, count):
        copy(step).wait_send()


def pairs_back(pair_grad, own_grad, cosine, sine):
    count, rows, double = pair_grad.shape
    D = pltpu.SemaphoreType.DMA
    spec = pl.BlockSpec(memory_space=pltpu.VMEM)
    return pl.pallas_call(
        pairs_back_kernel,
        out_shape=jax.ShapeDtypeStruct((2, rows, double // 2), BF16),
        in_specs=[spec] * 4,
        out_specs=spec,
        scratch_shapes=[pltpu.VMEM(pair_grad.shape, BF16), D((count,)), D((count,))],
        compiler_params=pltpu.CompilerParams(collective_id=3, has_side_effects=True),
    )(pair_grad, own_grad, cosine, sine)


def input_back_kernel(side, slots, full, query_grad, pair_grad, inputs, grad_middle, gain,
                      input_grad, gain_term, weights, joined, backward, sems):
    wide = inputs.shape[1] // side
    heads = query_grad.shape[0]

    def fetch(n, _):
        i, j = n // (heads + 2), n % (heads + 2)
        number = jnp.where(j < heads, i * heads + j, wide * j + i)
        fetch_tile(full, slots, number, weights.at[block_at(i * side, side), block_at(j * side, side)], sems.at[i // 2])
        return 0

    lax.fori_loop(0, wide * (heads + 2), fetch, 0, unroll=8)
    for h in range(heads):
        joined[:, h * side : (h + 1) * side] = query_grad[h]
    for k in range(2):
        joined[:, (heads + k) * side : (heads + k + 1) * side] = pair_grad[k]
    for c in range(wide // 2):
        view = weights.at[pl.ds(c * 2 * side, 2 * side), :]
        pltpu.make_async_copy(view, view, sems.at[c]).wait()
        backward[:, c * 2 * side : (c + 1) * 2 * side] = mul_turned(joined[...], view[...])
    back, term = norm_back(inputs[...].astype(F32), gain[...], backward[...])
    gain_term[...] = term
    input_grad[...] = (grad_middle[...] + back).astype(BF16)


def input_back(slots, full, query_grad, pair_grad, inputs, grad_middle, gain):
    rows, width = inputs.shape
    side = full.shape[1]
    V = pltpu.VMEM
    spec = pl.BlockSpec(memory_space=V)
    S = jax.ShapeDtypeStruct
    return pl.pallas_call(
        functools.partial(input_back_kernel, side),
        grid_spec=pltpu.PrefetchScalarGridSpec(
            num_scalar_prefetch=1,
            grid=(),
            in_specs=[pl.BlockSpec(memory_space=pl.ANY)] + [spec] * 5,
            out_specs=[spec] * 2,
            scratch_shapes=[V((width, (HEADS + 2) * side), BF16), V((rows, (HEADS + 2) * side), BF16), V((rows, width), F32),
                            pltpu.SemaphoreType.DMA((width // side // 2,))],
        ),
        out_shape=[S((rows, width), BF16), S((1, width), F32)],
        compiler_params=pltpu.CompilerParams(vmem_limit_bytes=40 * 2**20),
    )(slots, full, query_grad, pair_grad, inputs, grad_middle, gain)


def reduce_kernel(chunk, lag, places, left_at, right_at, gain_part, *refs):
    count = len(places)
    sources, refs = refs[:count], refs[count:]
    (out, gain_out, left_all, right_all, x_out, x_in, z_out, z_in, total, gain_sum, gain_in, keep_sem, gain_s, gain_r,
     x_s, x_r, z_s, z_r, ty_s, ty_r, tc_s, tc_r, tf_s, tf_r, done_sem) = refs
    quarter = x_out.shape[1]
    pieces = quarter // chunk
    replica = lax.axis_index("replica")
    member = lax.axis_index("fsdp")
    y, core = replica // 2, replica % 2
    z, x = member // 2, member % 2
    across, beside, twin = (replica, z * 2 + 1 - x), ((1 - y) * 2 + core, member), (y * 2 + 1 - core, member)
    beside_replica, twin_replica, far_replica = (1 - y) * 2 + core, y * 2 + 1 - core, (1 - y) * 2 + 1 - core
    def level(step):
        return (z + step) % 4
    def depth_device(step):
        return (replica, level(step) * 2 + x)
    def keep(n):
        is_left, block, lane = places[n]
        source = sources[n]
        if is_left:
            target = left_all.at[pl.ds(block, source.shape[0]), :, pl.ds(lane, source.shape[2])]
        else:
            target = right_all.at[pl.ds(block, source.shape[0]), pl.ds(lane, source.shape[1]), :]
        return pltpu.make_async_copy(source, target, keep_sem.at[n])
    for n in range(count):
        keep(n).start()
    left_all[left_all.shape[0] - 1] = jnp.zeros(left_all.shape[1:], left_all.dtype)
    gain_sum[...] = gain_part[...]

    barrier = pltpu.get_barrier_semaphore()
    for device in [across, beside, twin] + [depth_device(step) for step in (1, 2, 3)]:
        pl.semaphore_signal(barrier, inc=1, device_id=device, device_id_type=MESH)
    pl.semaphore_wait(barrier, 6)

    def remote(source, target, send, recv, device):
        return pltpu.make_async_remote_copy(src_ref=source, dst_ref=target, send_sem=send, recv_sem=recv, device_id=device, device_id_type=MESH)

    def gain_copy(stage, device):
        return remote(gain_sum, gain_in.at[stage], gain_s.at[stage], gain_r.at[stage], device)
    def gain_pair(stage, device):
        gain_copy(stage, device).wait()
        gain_sum[...] = gain_sum[...] + gain_in[stage]
    def gain_z(step):
        return remote(gain_sum, gain_in.at[2 + step], gain_s.at[2 + step], gain_r.at[2 + step], depth_device(step))
    def gain_finish():
        for step in (1, 2, 3):
            gain_z(step).wait()
        gain_in[0] = gain_sum[...]
        added = jnp.zeros(gain_sum.shape, F32)
        for zb in range(4):
            step = (zb - z + 4) % 4
            added = added + gain_in[jnp.where(step == 0, 0, 2 + step)]
        gain_out[...] = added
    gain_copy(0, beside).start()
    for n in range(count):
        keep(n).wait()

    def tile(owner, at):
        rank = replica * quarter + at
        return jnp.dot(left_all[left_at[owner, rank]], right_all[right_at[owner, rank]], preferred_element_type=F32)

    def x_copy(zb, k):
        at = pl.ds(k * chunk, chunk)
        return remote(x_out.at[zb, at], x_in.at[zb, at], x_s.at[zb, k], x_r.at[zb, k], across)
    def z_copy(step, k):
        at = pl.ds(k * chunk, chunk)
        return remote(z_out.at[step, at], z_in.at[step, at], z_s.at[step, k], z_r.at[step, k], depth_device(step))
    def total_at(who, k):
        return total.at[pl.ds(who * quarter + k * chunk, chunk)]
    def t_beside(k):
        return remote(total_at(replica, k), total_at(replica, k), ty_s.at[k], ty_r.at[k], beside)
    def t_twin(k):
        return remote(total_at(replica, k), total_at(replica, k), tc_s.at[k], tc_r.at[k], twin)
    def t_pass(k):
        return remote(total_at(beside_replica, k), total_at(beside_replica, k), tf_s.at[k], tf_r.at[k], twin)
    def come_beside(k):
        return remote(total_at(replica, k), total_at(beside_replica, k), ty_s.at[k], ty_r.at[k], beside)
    def come_twin(k):
        return remote(total_at(replica, k), total_at(twin_replica, k), tc_s.at[k], tc_r.at[k], twin)
    def come_far(k):
        return remote(total_at(replica, k), total_at(far_replica, k), tf_s.at[k], tf_r.at[k], twin)

    def send_x(k):
        def block(step, _):
            zb = level(step)
            def one(t, _):
                at = k * chunk + t
                x_out[zb, at] = tile(zb * 2 + 1 - x, at).astype(BF16)
                return 0
            lax.fori_loop(0, chunk, one, 0)
            x_copy(zb, k).start()
            return 0
        lax.fori_loop(0, 4, block, 0)

    def send_z(k):
        def block(step, _):
            zb = level(step)
            x_copy(zb, k).wait_recv()
            def one(t, _):
                at = k * chunk + t
                z_out[step, at] = (tile(zb * 2 + x, at) + x_in[zb, at].astype(F32)).astype(BF16)
                return 0
            lax.fori_loop(0, chunk, one, 0)
            @pl.when(step > 0)
            def _():
                z_copy(step, k).start()
            return 0
        lax.fori_loop(0, 4, block, 0)

    def finish(k):
        for step in (1, 2, 3):
            z_copy(step, k).wait_recv()
        def one(t, _):
            at = k * chunk + t
            added = z_out[0, at].astype(F32)
            for step in (1, 2, 3):
                added = added + z_in[step, at].astype(F32)
            total[replica * quarter + at] = added.astype(BF16)
            return 0
        lax.fori_loop(0, chunk, one, 0)
        t_beside(k).start()
        t_twin(k).start()

    def spread(k):
        come_beside(k).wait_recv()
        t_pass(k).start()

    def beat(n, _):
        @pl.when(n < pieces)
        def _():
            send_x(n)
        @pl.when((n >= lag) & (n < pieces + lag))
        def _():
            send_z(n - lag)
        @pl.when((n >= 2 * lag) & (n < pieces + 2 * lag))
        def _():
            finish(n - 2 * lag)
        @pl.when(n >= 3 * lag)
        def _():
            spread(n - 3 * lag)

        @pl.when(n == 2)
        def _():
            gain_pair(0, beside)
            gain_copy(1, twin).start()

        @pl.when(n == 4)
        def _():
            gain_pair(1, twin)
            gain_copy(2, across).start()

        @pl.when(n == 6)
        def _():
            gain_pair(2, across)
            for step in (1, 2, 3):
                gain_z(step).start()

        @pl.when(n == 9)
        def _():
            gain_finish()
        return 0
    lax.fori_loop(0, pieces + 3 * lag, beat, 0)

    def drain(k, _):
        come_twin(k).wait_recv()
        come_far(k).wait_recv()
        t_beside(k).wait_send()
        t_twin(k).wait_send()
        t_pass(k).wait_send()
        for zb in range(4):
            x_copy(zb, k).wait_send()
        for step in (1, 2, 3):
            z_copy(step, k).wait_send()
        return 0
    lax.fori_loop(0, pieces, drain, 0)
    result = pltpu.make_async_copy(total, out, done_sem)
    result.start()
    result.wait()

def reduce_tiles(left_at, right_at, gain_part, parts, places, left_total, right_total, rows, chunk=3, lag=2):
    capacity = left_at.shape[1]
    quarter = capacity // 4
    pieces = quarter // chunk
    side = parts[0].shape[1]
    D = pltpu.SemaphoreType.DMA
    V = pltpu.VMEM
    S = jax.ShapeDtypeStruct
    spec = pl.BlockSpec(memory_space=V)
    held = V((4, quarter, side, side), BF16)
    return pl.pallas_call(
        functools.partial(reduce_kernel, chunk, lag, places),
        out_shape=[S((capacity, side, side), BF16), S(gain_part.shape, F32)],
        in_specs=[pl.BlockSpec(memory_space=pltpu.SMEM)] * 2 + [spec] + [pl.BlockSpec(memory_space=pl.ANY)] * len(parts),
        out_specs=[pl.BlockSpec(memory_space=pl.ANY), spec],
        scratch_shapes=[
            V((left_total + 1, side, rows), BF16), V((right_total, rows, side), BF16), held, held, held, held,
            V((capacity, side, side), BF16), V(gain_part.shape, F32), V((6,) + gain_part.shape, F32),
            D((len(parts),)), D((6,)), D((6,))] + [D((4, pieces))] * 4 + [D((pieces,))] * 6 + [D],
        compiler_params=pltpu.CompilerParams(collective_id=1, has_side_effects=True, vmem_limit_bytes=62 * 2**20),
    )(left_at, right_at, gain_part, *parts)


def shampoo_kernel(count, grads, left_old, right_old, left_root, right_root, master, grads_out, left_new, right_new, master_new, low_new):
    nt = (((1,), (1,)), ((), ()))
    tn = (((0,), (0,)), ((), ()))
    for at in range(count):
        grad = grads[at]
        grads_out[at] = grad.astype(F32)
        left_new[at] = STAT_DECAY * left_old[at] + (1.0 - STAT_DECAY) * lax.dot_general(grad, grad, nt, preferred_element_type=F32)
        right_new[at] = STAT_DECAY * right_old[at] + (1.0 - STAT_DECAY) * lax.dot_general(grad, grad, tn, preferred_element_type=F32)
        turned = jnp.dot(grad, right_root[at].astype(BF16), preferred_element_type=F32).astype(BF16)
        turned = jnp.dot(left_root[at].astype(BF16), turned, preferred_element_type=F32)
        fresh = master[at] - STEP_RATE * turned
        master_new[at] = fresh
        low_new[at] = fresh.astype(BF16)

def shampoo(grads, left_old, right_old, left_root, right_root, master, count=6):
    capacity, side = master.shape[0], master.shape[1]
    while capacity % count:
        count -= 1
    spec = pl.BlockSpec((count, side, side), lambda i: (i, 0, 0))
    wide = jax.ShapeDtypeStruct(master.shape, F32)
    return pl.pallas_call(
        functools.partial(shampoo_kernel, count),
        grid=(capacity // count,),
        in_specs=[spec] * 6,
        out_specs=[spec] * 5,
        out_shape=[wide, wide, wide, wide, jax.ShapeDtypeStruct(master.shape, BF16)],
        compiler_params=pltpu.CompilerParams(vmem_limit_bytes=40 * 2**20),
    )(grads, left_old, right_old, left_root, right_root, master)


def shifted(block, axis, distance):
    devices = range(lax.axis_size(axis))
    route = [(i - distance, i) for i in devices if i - distance in devices]
    return lax.ppermute(block, axis, route)


def normalize(values, gain_row):
    mean_square = jnp.mean(values * values, -1, keepdims=True)
    return values * lax.rsqrt(mean_square + EPSILON) * gain_row


def rotate(values, angles):
    half_dim = values.shape[-1] // 2
    cosine = jnp.cos(angles)[:, None, :]
    sine_part = jnp.sin(angles)[:, None, :]
    first_half = values[..., :half_dim]
    second = values[..., half_dim:]
    return jnp.concatenate(
        [first_half * cosine - second * sine_part, second * cosine + first_half * sine_part], -1
    )


def angles_of(positions):
    half_dim = HEAD_DIM // 2
    inverse = 10000.0 ** (-2.0 * jnp.arange(half_dim, dtype=jnp.float32) / HEAD_DIM)
    return positions[:, None] * inverse[None, :]


def slot_of_tiles(owner_table, owners, capacity):
    onehot = (owner_table[:, None] == jnp.arange(owners, dtype=jnp.int32)[None, :]).astype(
        jnp.int32
    )
    earlier = jnp.cumsum(onehot, 0) - onehot
    ranking = jnp.sum(earlier * onehot, 1)
    return owner_table * capacity + ranking


def matrix_layout(width, head_width, head_dim, hidden_width, tile_side):
    left_attended = width // tile_side
    left_second = left_attended + head_width // tile_side
    left_hidden = left_second + width // tile_side
    right_key = head_width // tile_side
    right_value = right_key + head_dim // tile_side
    right_branch = right_value + head_dim // tile_side
    right_gate = right_branch + width // tile_side
    right_up = right_gate + hidden_width // tile_side
    right_down = right_up + hidden_width // tile_side
    return [
        (width, head_width, 0, 0),
        (width, head_dim, 0, right_key),
        (width, head_dim, 0, right_value),
        (head_width, width, left_attended, right_branch),
        (width, hidden_width, left_second, right_gate),
        (width, hidden_width, left_second, right_up),
        (hidden_width, width, left_hidden, right_down),
    ]


def project(values, blocks):
    row_count = values.shape[0]
    result = jnp.einsum(
        "nar,abrc->nbc",
        values.reshape(row_count, blocks.shape[0], blocks.shape[2]),
        blocks,
        preferred_element_type=jnp.float32,
    )
    return result.reshape(row_count, blocks.shape[1] * blocks.shape[3])


def back_project(values, blocks):
    row_count = values.shape[0]
    result = jnp.einsum(
        "nbc,abrc->nar",
        values.reshape(row_count, blocks.shape[1], blocks.shape[3]),
        blocks,
        preferred_element_type=jnp.float32,
    )
    return result.reshape(row_count, blocks.shape[0] * blocks.shape[2])


def dense_tile_grads(layout, left_blocks, right_blocks, tile_side):
    pieces = []
    for row_total, column_total, left_base, right_base in layout:
        left_part = left_blocks[:, left_base : left_base + row_total // tile_side]
        right_part = right_blocks[:, right_base : right_base + column_total // tile_side]
        product = jnp.einsum(
            "nar,nbc->abrc", left_part, right_part, preferred_element_type=jnp.float32
        )
        pieces.append(product.reshape(-1, tile_side, tile_side))
    pieces.append(jnp.zeros((1, tile_side, tile_side), jnp.float32))
    return jnp.concatenate(pieces, 0)


def block_tables(layout, tile_side, left_total):
    left_of, right_of = [], []
    for row_total, column_total, left_base, right_base in layout:
        for i in range(row_total // tile_side):
            for j in range(column_total // tile_side):
                left_of.append(left_base + i)
                right_of.append(right_base + j)
    return np.array(left_of + [left_total], np.int32), np.array(right_of + [0], np.int32)


def body_anywhere(
    inputs,
    cotangent,
    segment_ids,
    gains,
    owner_table,
    master_tiles,
    left_stats,
    right_stats,
    left_roots,
    right_roots,
):
    owners = lax.axis_size("fsdp")
    replicas = lax.axis_size("replica")
    member = lax.axis_index("fsdp")
    capacity = master_tiles.shape[0]
    tile_side = master_tiles.shape[1]
    row_count = inputs.shape[0]
    width = inputs.shape[1]
    head_width = HEADS * HEAD_DIM
    tile_total = owner_table.shape[0]
    layout = matrix_layout(width, head_width, HEAD_DIM, FF, tile_side)
    slots = slot_of_tiles(owner_table, owners, capacity)
    slot_tile = (
        jnp.full((owners * capacity,), tile_total, jnp.int32)
        .at[slots]
        .set(jnp.arange(tile_total, dtype=jnp.int32))
    )
    full = lax.all_gather(master_tiles.astype(jnp.bfloat16), "fsdp", axis=0, tiled=True)
    all_tiles = jnp.take(full, slots, axis=0)
    weights = []
    offset = 0
    for row_total, column_total, left_base, right_base in layout:
        number = row_total // tile_side * (column_total // tile_side)
        weights.append(
            all_tiles[offset : offset + number].reshape(
                row_total // tile_side, column_total // tile_side, tile_side, tile_side
            )
        )
        offset = offset + number
    w_query, w_key, w_value, w_out, w_gate, w_up, w_down = weights
    base_row = member * row_count
    own_ids = lax.dynamic_slice_in_dim(segment_ids, base_row, row_count, 0)
    starts = jnp.sum((segment_ids[None, :] < own_ids[:, None]).astype(jnp.int32), 1)
    positions = (base_row + jnp.arange(row_count, dtype=jnp.int32) - starts).astype(jnp.float32)
    angles = angles_of(positions)
    inputs_wide = inputs.astype(jnp.float32)
    normed = normalize(inputs_wide, gains[0]).astype(jnp.bfloat16)
    query_pre = project(normed, w_query)
    key_pre = project(normed, w_key)
    values_own = project(normed, w_value).astype(jnp.bfloat16)
    queries = rotate(query_pre.reshape(row_count, HEADS, HEAD_DIM), angles).astype(jnp.bfloat16)
    keys_own = rotate(key_pre[:, None, :], angles)[:, 0, :].astype(jnp.bfloat16)
    reach = WINDOW // row_count
    own_pair = jnp.concatenate([keys_own, values_own], 1)
    received = [shifted(own_pair, "fsdp", distance_back) for distance_back in range(reach, 0, -1)]
    pair_rows = jnp.concatenate(received + [own_pair], 0)
    key_rows = pair_rows[:, :HEAD_DIM]
    value_rows = pair_rows[:, HEAD_DIM:]
    padded_ids = jnp.concatenate([jnp.full((reach * row_count,), -1, jnp.int32), segment_ids], 0)
    key_ids = lax.dynamic_slice_in_dim(padded_ids, base_row, (reach + 1) * row_count, 0)
    distance = (
        jnp.arange(row_count, dtype=jnp.int32)[:, None]
        + reach * row_count
        - jnp.arange((reach + 1) * row_count, dtype=jnp.int32)[None, :]
    )
    allowed = (own_ids[:, None] == key_ids[None, :]) & (distance >= 0) & (distance < WINDOW)
    score_scale = HEAD_DIM ** (-0.5)
    scores = (
        jnp.einsum("nhd,kd->hnk", queries, key_rows, preferred_element_type=jnp.float32)
        * score_scale
    )
    scores = jnp.where(allowed[None], scores, -1e30)
    row_peak = jnp.max(scores, -1, keepdims=True)
    exponent = jnp.exp(scores - row_peak)
    row_total_sum = jnp.sum(exponent, -1, keepdims=True)
    probability = (exponent / row_total_sum).astype(jnp.bfloat16)
    log_total = row_peak + jnp.log(row_total_sum)
    attended = (
        jnp.einsum("hnk,kd->nhd", probability, value_rows, preferred_element_type=jnp.float32)
        .reshape(row_count, head_width)
        .astype(jnp.bfloat16)
    )
    middle = inputs_wide + project(attended, w_out)
    normed_two = normalize(middle, gains[1]).astype(jnp.bfloat16)
    gate = project(normed_two, w_gate)
    up_part = project(normed_two, w_up)

    def geglu(gate_values, up_values):
        return jax.nn.gelu(gate_values, approximate=True) * up_values

    hidden_wide, geglu_back = jax.vjp(geglu, gate, up_part)
    hidden = hidden_wide.astype(jnp.bfloat16)
    outputs = (middle + project(hidden, w_down)).astype(jnp.bfloat16)
    grad_hidden = back_project(cotangent, w_down)
    gate_back, up_back = geglu_back(grad_hidden)
    gate_grad = gate_back.astype(jnp.bfloat16)
    up_grad = up_back.astype(jnp.bfloat16)
    grad_normed_two = back_project(gate_grad, w_gate) + back_project(up_grad, w_up)
    middle_back, norm_two_back = jax.vjp(normalize, middle, gains[1])[1](grad_normed_two)
    grad_middle = cotangent.astype(jnp.float32) + middle_back
    branch_grad = grad_middle.astype(jnp.bfloat16)
    grad_attended = (
        back_project(branch_grad, w_out).astype(jnp.bfloat16).reshape(row_count, HEADS, HEAD_DIM)
    )
    scores_again = (
        jnp.einsum("nhd,kd->hnk", queries, key_rows, preferred_element_type=jnp.float32)
        * score_scale
    )
    scores_again = jnp.where(allowed[None], scores_again, -1e30)
    exact_prob = jnp.exp(scores_again - log_total)
    grad_prob = jnp.einsum(
        "nhd,kd->hnk", grad_attended, value_rows, preferred_element_type=jnp.float32
    )
    grad_scores = (
        exact_prob * (grad_prob - jnp.sum(exact_prob * grad_prob, -1, keepdims=True))
    ).astype(jnp.bfloat16)
    grad_queries = (
        jnp.einsum("hnk,kd->nhd", grad_scores, key_rows, preferred_element_type=jnp.float32)
        * score_scale
    )
    grad_keys = (
        jnp.einsum("hnk,nhd->kd", grad_scores, queries, preferred_element_type=jnp.float32)
        * score_scale
    )
    grad_values = jnp.einsum(
        "hnk,nhd->kd", probability, grad_attended, preferred_element_type=jnp.float32
    )
    grad_pairs = jnp.concatenate([grad_keys, grad_values], 1)
    own_grad = grad_pairs[reach * row_count :]
    for distance_back in range(1, reach + 1):
        sent_rows = grad_pairs[
            (reach - distance_back) * row_count : (reach - distance_back + 1) * row_count
        ]
        own_grad = own_grad + shifted(
            sent_rows.astype(jnp.bfloat16), "fsdp", -distance_back
        ).astype(sent_rows.dtype)
    grad_query_pre = (
        rotate(grad_queries, -angles).reshape(row_count, head_width).astype(jnp.bfloat16)
    )
    grad_key_pre = rotate(own_grad[:, None, :HEAD_DIM], -angles)[:, 0, :].astype(jnp.bfloat16)
    grad_values_low = own_grad[:, HEAD_DIM:].astype(jnp.bfloat16)
    grad_normed = (
        back_project(grad_query_pre, w_query)
        + back_project(grad_key_pre, w_key)
        + back_project(grad_values_low, w_value)
    )
    inputs_back, norm_one_back = jax.vjp(normalize, inputs_wide, gains[0])[1](grad_normed)
    input_grad = (grad_middle + inputs_back).astype(jnp.bfloat16)
    gain_grads = lax.psum(jnp.stack([norm_one_back, norm_two_back]), ("replica", "fsdp"))
    gain_rate = GAIN_STEP * (row_count * owners * replicas) ** (-0.5)
    new_gains = gains - gain_rate * gain_grads
    left_parts = jnp.concatenate([normed, attended, normed_two, hidden], 1)
    right_parts = jnp.concatenate(
        [grad_query_pre, grad_key_pre, grad_values_low, branch_grad, gate_grad, up_grad, cotangent],
        1,
    )
    left_blocks = left_parts.reshape(row_count, -1, tile_side)
    right_blocks = right_parts.reshape(row_count, -1, tile_side)
    dense = dense_tile_grads(layout, left_blocks, right_blocks, tile_side)
    partial_sum = lax.psum_scatter(
        jnp.take(dense, slot_tile, axis=0), "fsdp", scatter_dimension=0, tiled=True
    )
    grads_low = lax.psum(partial_sum.astype(jnp.bfloat16), "replica")
    grads_all, left_all, right_all, master_all, low_all = shampoo(
        grads_low, left_stats, right_stats, left_roots, right_roots, master_tiles
    )
    return (
        outputs,
        input_grad,
        gain_grads,
        new_gains,
        grads_all,
        master_all,
        low_all,
        left_all,
        right_all,
    )


def body_of_units(
    inputs,
    cotangent,
    segment_ids,
    gains,
    owner_table,
    master_tiles,
    left_stats,
    right_stats,
    left_roots,
    right_roots,
):
    owners, replicas = 8, 4
    member = lax.axis_index("fsdp")
    capacity = master_tiles.shape[0]
    side = master_tiles.shape[1]
    rows, width = inputs.shape
    tile_total = owner_table.shape[0]
    layout = matrix_layout(width, HEADS * HEAD_DIM, HEAD_DIM, FF, side)
    left_of, right_of = block_tables(layout, side, 0)
    padded = -(-tile_total // 128) * 128
    block_values = np.zeros((padded, 128), np.float32)
    block_values[:tile_total, 0] = left_of[:-1] + 1
    block_values[:tile_total, 1] = right_of[:-1] + 1
    left_total, right_total = int(max(left_of)) + 1, int(max(right_of)) + 1
    owner_row = jnp.pad(owner_table, (0, padded - tile_total), constant_values=-1).reshape(1, padded)

    slots, blocks_at, normed, early = prepare(
        owners, capacity, owner_row, jnp.asarray(block_values, BF16), inputs, cotangent, gains[0:1]
    )
    slots = slots.reshape(padded)
    chosen = blocks_at[:, :capacity, :2].astype(jnp.int32) - 1
    left_at = jnp.where(chosen[..., 0] < 0, left_total, chosen[..., 0])
    right_at = jnp.maximum(chosen[..., 1], 0)
    base_row = member * rows
    own_ids = lax.dynamic_slice_in_dim(segment_ids, base_row, rows, 0)
    starts = jnp.sum((segment_ids[None, :] < own_ids[:, None]).astype(jnp.int32), 1)
    positions = (base_row + jnp.arange(rows, dtype=jnp.int32) - starts).astype(jnp.float32)
    angles = angles_of(positions)
    cosine, sine = jnp.cos(angles), jnp.sin(angles)
    cosine = jnp.concatenate([cosine, cosine], 1)
    sine = jnp.concatenate([-sine, sine], 1)
    first = base_row.astype(jnp.int32).reshape(1)
    own_column, all_row = own_ids.reshape(-1, 1), segment_ids.reshape(1, -1)

    def over_y(part):
        return lax.ppermute(part, "replica", [(0, 2), (1, 3), (2, 0), (3, 1)])

    def over_core(part):
        return lax.ppermute(part, "replica", [(0, 1), (1, 0), (2, 3), (3, 2)])

    def unit_of(part):
        beside = over_y(part)
        return [part, beside, over_core(part), over_core(beside)]

    early_unit = unit_of(early)
    full = gather(master_tiles.astype(BF16)).reshape(owners * capacity, side, side)
    queries, pair = project_heads(slots, full, normed, cosine, sine)
    pairs = gather_pairs(pair, owners)
    attended_turned, normed_two, normed_two_turned, middle = attend(
        slots, first, full, queries, pairs, own_column, all_row, inputs, gains[1:2]
    )
    two_unit = unit_of(normed_two_turned)
    attended_unit = unit_of(attended_turned)
    wide = width // side
    hidden, gate_grad, up_grad, outputs, grad_middle, branch, branch_blocks, term_two = mlp(
        slots, full, normed_two, two_unit[1], cotangent, early_unit[1][wide:], middle, gains[1:2]
    )
    branch_unit = unit_of(branch_blocks)
    hidden_far, gate_far, up_far = over_core(hidden), over_core(gate_grad), over_core(up_grad)
    query_grad, pair_grad, own_pair_grad = attend_back(
        slots, first, full, branch, queries, pairs, own_column, all_row, cosine, sine
    )
    query_unit = unit_of(query_grad)
    pair_low = pairs_back(pair_grad, own_pair_grad, cosine, sine)
    pair_unit = unit_of(pair_low)
    input_grad, term_one = input_back(slots, full, query_grad, pair_low, inputs, grad_middle, gains[0:1])

    parts, places = [], []

    def place(unit, is_left, block):
        for n, part in enumerate(unit):
            parts.append(part)
            places.append((is_left, block, n * rows * (4 // len(unit))))

    place([part[:wide] for part in early_unit], True, 0)
    place(attended_unit, True, wide)
    place(two_unit, True, wide + HEADS)
    place([hidden, hidden_far], True, 2 * wide + HEADS)
    place(query_unit, False, 0)
    place(pair_unit, False, HEADS)
    place(branch_unit, False, HEADS + 2)
    place([gate_grad, gate_far], False, HEADS + 2 + wide)
    place([up_grad, up_far], False, HEADS + 2 + wide + FF // side)
    place([part[wide:] for part in early_unit], False, HEADS + 2 + wide + 2 * FF // side)
    gain_part = jnp.concatenate([term_one, term_two, jnp.zeros((6, width), F32)], 0)
    grads_low, gain_sum = reduce_tiles(
        left_at, right_at, gain_part, parts, tuple(places), left_total, right_total, replicas * rows
    )
    gain_grads = gain_sum[:2]
    gain_rate = GAIN_STEP * (rows * owners * replicas) ** (-0.5)
    grads_all, left_all, right_all, master_all, low_all = shampoo(
        grads_low, left_stats, right_stats, left_roots, right_roots, master_tiles
    )
    return (
        outputs,
        input_grad,
        gain_grads,
        gains - gain_rate * gain_grads,
        grads_all,
        master_all,
        low_all,
        left_all,
        right_all,
    )


def solution(mesh):
    units = mesh.shape["replica"] == 4 and mesh.shape["fsdp"] == 8
    return jax.shard_map(
        body_of_units if units else body_anywhere,
        mesh=mesh,
        in_specs=(
            P(("replica", "fsdp"), None),
            P(("replica", "fsdp"), None),
            P("replica"),
            P(),
            P(),
            P("fsdp", None, None),
            P("fsdp", None, None),
            P("fsdp", None, None),
            P("fsdp", None, None),
            P("fsdp", None, None),
        ),
        out_specs=(
            P(("replica", "fsdp"), None),
            P(("replica", "fsdp"), None),
            P(),
            P(),
            P("fsdp", None, None),
            P("fsdp", None, None),
            P("fsdp", None, None),
            P("fsdp", None, None),
            P("fsdp", None, None),
        ),
        check_vma=False,
    )
```

```python
import functools

import jax
import jax.numpy as jnp
import numpy as np
from jax import lax
from jax.experimental import pallas as pl
from jax.experimental.pallas import tpu as pltpu
from jax.sharding import PartitionSpec as P

HEADS = 12
HEAD_DIM = 128
FF = 4608
WINDOW = 1024


EPSILON = 1e-06
STEP_RATE = 0.02
STAT_DECAY = 0.5
GAIN_STEP = 0.1
F32, BF16 = jnp.float32, jnp.bfloat16
MESH = pl.DeviceIdType.MESH


def gather_kernel(chunk, whole, deep_most, early, patience, master, full, stage, low, stage_sem, keep_sem,
                  up_s, up_r, down_s, down_r, x_s, x_r, eu_s, eu_r, ed_s, ed_r, y_s, y_r, core_s, core_r):
    replica = lax.axis_index("replica")
    member = lax.axis_index("fsdp")
    y, core = replica // 2, replica % 2
    z, x = member // 2, member % 2
    deep = deep_most - core
    run = whole - deep
    half = whole * chunk
    mirrored = z // 2
    inner = z + mirrored * (3 - 2 * z)
    above, below = (replica, (z + 1) * 2 + x), (replica, (z - 1) * 2 + x)
    across, beside, twin = (replica, z * 2 + 1 - x), ((1 - y) * 2 + core, member), (y * 2 + 1 - core, member)

    def rows(chunk_at, owner_core):
        return pl.ds(owner_core * half + chunk_at * chunk, chunk)

    def load(c, part):
        return pltpu.make_async_copy(master.at[rows(c, part)], stage.at[pl.ds(c * chunk, chunk)], stage_sem.at[c])

    def cast(c, part):
        load(c, part).wait()
        low[rows(c, part)] = stage[pl.ds(c * chunk, chunk)].astype(BF16)

    def place(k, plane):
        return plane * (whole - 1) + k * (1 - 2 * plane)

    def load_first(k, _):
        load(place(k, y), core).start()
        return 0

    lax.fori_loop(0, whole, load_first, 0)
    barrier = pltpu.get_barrier_semaphore()

    def greet(device):
        pl.semaphore_signal(barrier, inc=1, device_id=device, device_id_type=MESH)

    pl.when(z < 3)(lambda: greet(above))
    pl.when(z > 0)(lambda: greet(below))
    greet(across)
    greet(beside)
    greet(twin)

    @pl.when((z == 0) | (z == 3))
    def _():
        pl.semaphore_wait(barrier, 4)

    @pl.when((z > 0) & (z < 3))
    def _():
        pl.semaphore_wait(barrier, 5)

    def copy(owner, chunk_at, send, recv, device, from_own=False, owner_core=None):
        at = rows(chunk_at, core if owner_core is None else owner_core)
        target = full.at[owner, at]
        source = low.at[at] if from_own else target
        return pltpu.make_async_remote_copy(src_ref=source, dst_ref=target, send_sem=send, recv_sem=recv, device_id=device, device_id_type=MESH)

    def go_up(zb, k, own=False):
        return copy(zb * 2 + x, place(k, y), up_s.at[zb, k], up_r.at[zb, k], above, own)

    def go_down(zb, k, own=False):
        return copy(zb * 2 + x, place(k, y), down_s.at[zb, k], down_r.at[zb, k], below, own)

    def early_up(zb, k):
        return copy(zb * 2 + 1 - x, place(k, y), eu_s.at[zb, k], eu_r.at[zb, k], above)

    def early_down(zb, k):
        return copy(zb * 2 + 1 - x, place(k, y), ed_s.at[zb, k], ed_r.at[zb, k], below)

    def go_x(zb, k, own=False):
        return copy(zb * 2 + x, place(k, y), x_s.at[zb, k], x_r.at[zb, k], across, own)

    def come_x(zb, k):
        return copy(zb * 2 + 1 - x, place(k, y), x_s.at[zb, k], x_r.at[zb, k], across)

    def go_y(owner, k):
        return copy(owner, place(k, y), y_s.at[owner, k], y_r.at[owner, k], beside)

    def come_y(owner, k):
        return copy(owner, place(k, 1 - y), y_s.at[owner, k], y_r.at[owner, k], beside)

    def go_core(owner, at):
        return copy(owner, at, core_s.at[owner, at], core_r.at[owner, at], twin)

    def onward(owner, k):
        go_core(owner, place(k, y)).start()
        pl.when(k < deep)(lambda: go_y(owner, k).start())

    def across_block(g):
        b = g if g >= 2 else (g + inner) % 2
        return b + mirrored * (3 - 2 * b)

    def group(g):
        def tick(k, _):
            if g == 0:
                cast(place(k, y), core)
                pl.when(z < 3)(lambda: go_up(z, k, True).start())
                pl.when(z > 0)(lambda: go_down(z, k, True).start())
                go_x(z, k, True).start()
            if 1 <= g <= 3:
                @pl.when(z - g >= 0)
                def _():
                    go_up(z - g, k).wait_recv()
                    pl.when(z < 3)(lambda: go_up(z - g, k).start())
                    onward((z - g) * 2 + x, k)

                @pl.when(z + g <= 3)
                def _():
                    go_down(z + g, k).wait_recv()
                    pl.when(z > 0)(lambda: go_down(z + g, k).start())
                    onward((z + g) * 2 + x, k)

                pl.when(k >= early)(lambda: go_x(across_block(g), k).start())
            if g == 1:
                come_x(z, k).wait_recv()
                onward(z * 2 + 1 - x, k)

                @pl.when(k < early)
                def _():
                    pl.when(z < 3)(lambda: early_up(z, k).start())
                    pl.when(z > 0)(lambda: early_down(z, k).start())

            if 2 <= g <= 4:
                @pl.when(k >= early)
                def _():
                    come_x(across_block(g - 1), k).wait_recv()
                    onward(across_block(g - 1) * 2 + 1 - x, k)

                @pl.when((k < early) & (z - (g - 1) >= 0))
                def _():
                    zb = z - (g - 1)
                    early_up(zb, k).wait_recv()
                    pl.when(z < 3)(lambda: early_up(zb, k).start())
                    onward(zb * 2 + 1 - x, k)

                @pl.when((k < early) & (z + (g - 1) <= 3))
                def _():
                    zb = z + (g - 1)
                    early_down(zb, k).wait_recv()
                    pl.when(z > 0)(lambda: early_down(zb, k).start())
                    onward(zb * 2 + 1 - x, k)
            h = g - patience
            if 1 <= h <= 4:
                def take(owner):
                    come_y(owner, k).wait_recv()
                    go_core(owner, place(k, 1 - y)).start()

                if h <= 3:
                    pl.when((k < deep) & (z - h >= 0))(lambda: take((z - h) * 2 + x))
                    pl.when((k < deep) & (z + h <= 3))(lambda: take((z + h) * 2 + x))
                if h == 1:
                    pl.when(k < deep)(lambda: take(z * 2 + 1 - x))
                else:
                    pl.when((k < deep) & (k >= early))(lambda: take(across_block(h - 1) * 2 + 1 - x))
                    pl.when((k < early) & (z - (h - 1) >= 0))(lambda: take((z - (h - 1)) * 2 + 1 - x))
                    pl.when((k < early) & (z + (h - 1) <= 3))(lambda: take((z + (h - 1)) * 2 + 1 - x))
            return 0

        lax.fori_loop(0, run, tick, 0)

    group(0)

    def rest(k, _):
        cast(place(k, y), core)
        return 0

    lax.fori_loop(run, whole, rest, 0)

    def load_other(c, _):
        load(c, 1 - core).start()
        return 0

    lax.fori_loop(0, whole, load_other, 0)

    def cast_other(c, _):
        cast(c, 1 - core)
        return 0

    group(1)
    lax.fori_loop(0, whole, cast_other, 0)
    keep = pltpu.make_async_copy(low, full.at[member], keep_sem)
    keep.start()
    for g in range(2, 5 + patience):
        group(g)

    def drain_z(zb, _):
        def one(k, _):
            pl.when((zb <= z) & (z < 3))(lambda: go_up(zb, k).wait_send())
            pl.when((zb >= z) & (z > 0))(lambda: go_down(zb, k).wait_send())
            pl.when((zb == z) | (k >= early))(lambda: go_x(zb, k).wait_send())
            pl.when((k < early) & (zb <= z) & (z < 3))(lambda: early_up(zb, k).wait_send())
            pl.when((k < early) & (zb >= z) & (z > 0))(lambda: early_down(zb, k).wait_send())
            return 0

        lax.fori_loop(0, run, one, 0)
        return 0

    lax.fori_loop(0, 4, drain_z, 0)

    def drain_owner(owner, _):
        @pl.when(owner != member)
        def _():
            def one_y(k, _):
                go_y(owner, k).wait_send()
                return 0

            lax.fori_loop(0, deep, one_y, 0)

            def one_core(k, _):
                go_core(owner, k).wait_send()
                copy(owner, k, core_s.at[owner, k], core_r.at[owner, k], twin, owner_core=1 - core).wait_recv()
                return 0

            lax.fori_loop(0, whole, one_core, 0)

        return 0

    lax.fori_loop(0, 8, drain_owner, 0)
    keep.wait()


def gather(master, chunk=6, deep=6, early=1, patience=1):
    capacity = master.shape[0]
    whole = capacity // 2 // chunk
    run = whole - deep + 1
    D = pltpu.SemaphoreType.DMA
    V = pltpu.VMEM
    return pl.pallas_call(
        functools.partial(gather_kernel, chunk, whole, deep, early, patience),
        out_shape=jax.ShapeDtypeStruct((8,) + master.shape, BF16),
        in_specs=[pl.BlockSpec(memory_space=pl.ANY)],
        out_specs=pl.BlockSpec(memory_space=pl.ANY),
        scratch_shapes=[V((capacity // 2,) + master.shape[1:], F32), V(master.shape, BF16), D((whole,)), D]
        + [D((4, run))] * 6 + [D((4, max(early, 1)))] * 4 + [D((8, deep))] * 2 + [D((8, whole))] * 2,
        compiler_params=pltpu.CompilerParams(collective_id=0, has_side_effects=True, vmem_limit_bytes=40 * 2**20),
    )(master)


def prepare_kernel(owners, capacity, owner_row, block_values, inputs, cotangent, gain, slots, blocks_at, normed, early, ranks):
    total = owner_row.shape[1]
    lanes = 128
    owner = owner_row[...]
    same = (owner == lax.broadcasted_iota(jnp.int32, (owners, total), 0)).astype(F32)
    ones_before = (lax.broadcasted_iota(jnp.int32, (lanes, lanes), 0) < lax.broadcasted_iota(jnp.int32, (lanes, lanes), 1)).astype(BF16)
    carry = jnp.zeros((owners, 1), F32)
    for c in range(total // lanes):
        at = slice(c * lanes, (c + 1) * lanes)
        piece = same[:, at]
        before = jnp.dot(piece.astype(BF16), ones_before, preferred_element_type=F32) + carry
        ranks[:, at] = jnp.sum(before * piece, 0, keepdims=True).astype(jnp.int32)
        carry = carry + jnp.sum(piece, 1, keepdims=True)
    slot = jnp.where(owner >= 0, owner * capacity + ranks[...], -1)
    slots[...] = slot
    padded = blocks_at.shape[1]
    for o in range(owners):
        here = lax.broadcasted_iota(jnp.int32, (padded, total), 0)
        here = jnp.where(here < capacity, here + o * capacity, -2)
        hit = jnp.where(here == slot, 1.0, 0.0).astype(BF16)
        blocks_at[o] = jnp.dot(hit, block_values[...], preferred_element_type=F32)
    values = inputs[...].astype(F32)
    mean_square = jnp.mean(values * values, -1, keepdims=True)
    scaled = values * lax.rsqrt(mean_square + EPSILON) * gain[...]
    normed[...] = scaled.astype(BF16)
    count = early.shape[0] // 2
    for c in range(count):
        at = slice(c * lanes, (c + 1) * lanes)
        early[c] = scaled[:, at].T.astype(BF16)
        early[count + c] = cotangent[:, at]

def prepare(owners, capacity, owner_row, block_values, inputs, cotangent, gain):
    rows, width = inputs.shape
    padded = -(-capacity // 16) * 16
    S = jax.ShapeDtypeStruct
    spec = pl.BlockSpec(memory_space=pltpu.VMEM)
    return pl.pallas_call(
        functools.partial(prepare_kernel, owners, capacity),
        in_specs=[spec] * 5,
        out_specs=[spec] * 4,
        out_shape=[S(owner_row.shape, jnp.int32), S((owners, padded, 128), F32), S((rows, width), BF16),
                   S((2 * width // 128, 128, rows), BF16)],
        scratch_shapes=[pltpu.VMEM(owner_row.shape, jnp.int32)],
        compiler_params=pltpu.CompilerParams(vmem_limit_bytes=40 * 2**20),
    )(owner_row, block_values, inputs, cotangent, gain)


BY_ROWS = (((1,), (1,)), ((), ()))
BY_COLUMNS = (((0,), (0,)), ((), ()))


def mul(a, b):
    return jnp.dot(a, b, preferred_element_type=F32)


def mul_turned(a, b):
    return lax.dot_general(a, b, BY_ROWS, preferred_element_type=F32)


def mul_summed(a, b):
    return lax.dot_general(a, b, BY_COLUMNS, preferred_element_type=F32)


def turn(part, cosine, sine):
    return part * cosine + pltpu.roll(part, HEAD_DIM // 2, 1) * sine


def cost_of(microseconds):
    return pl.CostEstimate(flops=int(microseconds * 9e8), bytes_accessed=int(microseconds * 3e6), transcendentals=0)


def fetch_tile(full, slots, number, target, sem):
    pltpu.make_async_copy(full.at[slots[number]], target, sem).start()


def block_at(start, size):
    return pl.ds(pl.multiple_of(start, size), size)


def project_kernel(side, slots, full, normed, cosine, sine, queries, pair, weights, sems):
    wide = normed.shape[1] // side
    heads = queries.shape[1] // side

    def fetch(n, _):
        j, i = n // wide, n % wide
        number = jnp.where(j < heads, i * heads + j, wide * j + i)
        fetch_tile(full, slots, number, weights.at[block_at(i * side, side), block_at(j * side, side)], sems.at[j // 2])
        return 0

    lax.fori_loop(0, wide * (heads + 2), fetch, 0, unroll=8)
    for c in range((heads + 2) // 2):
        view = weights.at[:, pl.ds(c * 2 * side, 2 * side)]
        pltpu.make_async_copy(view, view, sems.at[c]).wait()
        product = mul(normed[...], view[...])
        for k in range(2):
            part = product[:, k * side : (k + 1) * side]
            if c < heads // 2:
                queries[:, (2 * c + k) * side : (2 * c + k + 1) * side] = turn(part, cosine[...], sine[...]).astype(BF16)
            elif k == 0:
                pair[:, :side] = turn(part, cosine[...], sine[...]).astype(BF16)
            else:
                pair[:, side:] = part.astype(BF16)


def project_heads(slots, full, normed, cosine, sine):
    rows, width = normed.shape
    side = full.shape[1]
    V = pltpu.VMEM
    spec = pl.BlockSpec(memory_space=V)
    return pl.pallas_call(
        functools.partial(project_kernel, side),
        grid_spec=pltpu.PrefetchScalarGridSpec(
            num_scalar_prefetch=1,
            grid=(),
            in_specs=[pl.BlockSpec(memory_space=pl.ANY), spec, spec, spec],
            out_specs=[spec, spec],
            scratch_shapes=[V((width, (HEADS + 2) * side), BF16), pltpu.SemaphoreType.DMA(((HEADS + 2) // 2,))],
        ),
        out_shape=[jax.ShapeDtypeStruct((rows, HEADS * side), BF16), jax.ShapeDtypeStruct((rows, 2 * side), BF16)],
        cost_estimate=cost_of(6),
        compiler_params=pltpu.CompilerParams(vmem_limit_bytes=40 * 2**20),
    )(slots, full, normed, cosine, sine)


def pairs_kernel(pair, pairs, keep_sem, sends, recvs):
    replica = lax.axis_index("replica")
    member = lax.axis_index("fsdp")
    count = pairs.shape[0]
    barrier = pltpu.get_barrier_semaphore()
    others = [(member + step) % count for step in range(1, count)]
    for other in others:
        pl.semaphore_signal(barrier, inc=1, device_id=(replica, other), device_id_type=MESH)
    pl.semaphore_wait(barrier, count - 1)
    keep = pltpu.make_async_copy(pair, pairs.at[member], keep_sem)
    keep.start()

    def copy(step, owner):
        return pltpu.make_async_remote_copy(
            src_ref=pair, dst_ref=pairs.at[owner], send_sem=sends.at[step], recv_sem=recvs.at[step],
            device_id=(replica, (member + step) % count), device_id_type=MESH)

    for step in range(1, count):
        copy(step, member).start()
    for step in range(1, count):
        copy(step, (member + count - step) % count).wait_recv()
    for step in range(1, count):
        copy(step, member).wait_send()
    keep.wait()


def gather_pairs(pair, count):
    D = pltpu.SemaphoreType.DMA
    spec = pl.BlockSpec(memory_space=pltpu.VMEM)
    return pl.pallas_call(
        pairs_kernel,
        out_shape=jax.ShapeDtypeStruct((count,) + pair.shape, pair.dtype),
        in_specs=[spec],
        out_specs=spec,
        scratch_shapes=[D, D((count,)), D((count,))],
        cost_estimate=cost_of(13),
        compiler_params=pltpu.CompilerParams(collective_id=2, has_side_effects=True),
    )(pair)


def fill_bias(first, own_ids, all_ids, bias):
    shape = bias.shape
    distance = first + lax.broadcasted_iota(jnp.int32, shape, 0) - lax.broadcasted_iota(jnp.int32, shape, 1)
    allowed = (own_ids[...] == all_ids[...]) & (distance >= 0) & (distance < WINDOW)
    bias[...] = jnp.where(allowed, 0.0, -1e30)


def softmax_of(scores):
    exponent = jnp.exp(scores - jnp.max(scores, -1, keepdims=True))
    return exponent / jnp.sum(exponent, -1, keepdims=True)


def attend_kernel(side, slots, first, full, queries, pairs, own_ids, all_ids, inputs, gain,
                  attended_turned, normed_two, normed_two_turned, middle, weights, attended, bias, sems):
    heads = attended.shape[1] // side
    wide = middle.shape[1] // side

    def fetch(n, _):
        j, i = n // heads, n % heads
        number = (heads + 2) * wide + i * wide + j
        fetch_tile(full, slots, number, weights.at[block_at(i * side, side), block_at(j * side, side)], sems.at[j // 2])
        return 0

    lax.fori_loop(0, wide * heads, fetch, 0, unroll=8)
    fill_bias(first[0], own_ids, all_ids, bias)
    keys = pairs[:, :, :side].reshape(-1, side)
    values = pairs[:, :, side:].reshape(-1, side)
    scale = HEAD_DIM ** (-0.5)
    for head in range(heads):
        at = slice(head * side, (head + 1) * side)
        scores = mul_turned(queries[:, at], keys) * scale + bias[...]
        product = mul(softmax_of(scores).astype(BF16), values)
        attended[:, at] = product.astype(BF16)
        attended_turned[head] = product.T.astype(BF16)
    total = jnp.zeros((inputs.shape[0], 1), F32)
    for c in range(wide // 2):
        view = weights.at[:, pl.ds(c * 2 * side, 2 * side)]
        pltpu.make_async_copy(view, view, sems.at[c]).wait()
        at = slice(c * 2 * side, (c + 1) * 2 * side)
        part = inputs[:, at].astype(F32) + mul(attended[...], view[...])
        middle[:, at] = part
        total = total + jnp.sum(part * part, -1, keepdims=True)
    scaled = lax.rsqrt(total / middle.shape[1] + EPSILON)
    for c in range(wide):
        at = slice(c * side, (c + 1) * side)
        part = middle[:, at] * scaled * gain[:, at]
        normed_two[:, at] = part.astype(BF16)
        normed_two_turned[c] = part.T.astype(BF16)


def attend(slots, first, full, queries, pairs, own_ids, all_ids, inputs, gain):
    rows, width = inputs.shape
    side = full.shape[1]
    V = pltpu.VMEM
    spec = pl.BlockSpec(memory_space=V)
    S = jax.ShapeDtypeStruct
    return pl.pallas_call(
        functools.partial(attend_kernel, side),
        grid_spec=pltpu.PrefetchScalarGridSpec(
            num_scalar_prefetch=2,
            grid=(),
            in_specs=[pl.BlockSpec(memory_space=pl.ANY)] + [spec] * 6,
            out_specs=[spec] * 4,
            scratch_shapes=[V((HEADS * side, width), BF16), V((rows, HEADS * side), BF16),
                            V((rows, pairs.shape[0] * pairs.shape[1]), F32), pltpu.SemaphoreType.DMA((width // side // 2,))],
        ),
        out_shape=[S((HEADS, side, rows), BF16), S((rows, width), BF16), S((width // side, side, rows), BF16), S((rows, width), F32)],
        cost_estimate=cost_of(11),
        compiler_params=pltpu.CompilerParams(vmem_limit_bytes=40 * 2**20),
    )(slots, first, full, queries, pairs, own_ids, all_ids, inputs, gain)


def norm_back(values, gain, grads):
    mean_square = jnp.mean(values * values, -1, keepdims=True)
    scaled = lax.rsqrt(mean_square + EPSILON)
    weighed = grads * gain
    inner = jnp.mean(weighed * values, -1, keepdims=True)
    back = scaled * weighed - values * (scaled * scaled * scaled * inner)
    return back, jnp.sum(grads * values * scaled, 0, keepdims=True)


GELU_SCALE = 0.7978845608028654
GELU_CUBE = 0.044715


def mlp_kernel(side, ring, span, slots, full, normed_own, normed_beside, cotangent_own, cotangent_beside, middle, gain,
               hidden_turned, gate_grad, up_grad, outputs, grad_middle, branch, branch_blocks, gain_term,
               normed, cotangent, forward, backward, gate_ring, up_ring, down_ring, sems):
    rows, width = normed_own.shape
    wide = width // side
    hidden_blocks = hidden_turned.shape[0]
    steps = hidden_blocks // span
    heads = HEADS
    base = (heads + 2) * wide + heads * wide

    def pieces_of(j, slot):
        todo = []
        for i in range(wide):
            for k in range(span):
                column = span * j + k
                row, lane = pl.ds(i * side, side), pl.ds(k * side, side)
                todo.append((base + i * hidden_blocks + column, gate_ring.at[slot, row, lane]))
                todo.append((base + (wide + i) * hidden_blocks + column, up_ring.at[slot, row, lane]))
                todo.append((base + 2 * wide * hidden_blocks + column * wide + i, down_ring.at[slot, lane, row]))
        return todo

    def start(todo, slot, first, last):
        for number, target in todo[first:last]:
            fetch_tile(full, slots, number, target, sems.at[slot])

    def arrived(slot):
        for target in (gate_ring, up_ring, down_ring):
            view = target.at[slot]
            pltpu.make_async_copy(view, view, sems.at[slot]).wait()

    for j in range(ring - 1):
        todo = pieces_of(j, j)
        start(todo, j, 0, len(todo))
    normed[:rows] = normed_own[...]
    cotangent[:rows] = cotangent_own[...]
    for c in range(wide):
        at = slice(c * side, (c + 1) * side)
        normed[rows:, at] = normed_beside[c].astype(F32).T.astype(BF16)
        cotangent[rows:, at] = cotangent_beside[c]
    forward[...] = jnp.zeros_like(forward)
    backward[...] = jnp.zeros_like(backward)

    def step(j, _):
        slot = j % ring
        arrived(slot)
        later = (j + ring - 1) % ring
        todo = pieces_of(jnp.minimum(j + ring - 1, steps - 1), later)
        sixth = len(todo) // 6
        start(todo, later, 0, sixth)
        gate = mul(normed[...], gate_ring[slot])
        start(todo, later, sixth, 2 * sixth)
        up = mul(normed[...], up_ring[slot])
        start(todo, later, 2 * sixth, 3 * sixth)
        grad_hidden = mul_turned(cotangent[...], down_ring[slot])
        start(todo, later, 3 * sixth, 4 * sixth)
        square = gate * gate
        bend = jnp.tanh(GELU_SCALE * gate * (1.0 + GELU_CUBE * square))
        share = 0.5 * (1.0 + bend)
        active = gate * share
        slope = share + 0.5 * gate * (1.0 - bend * bend) * (GELU_SCALE * (1.0 + 3.0 * GELU_CUBE * square))
        hidden_wide = active * up
        hidden = hidden_wide.astype(BF16)
        gate_low = (grad_hidden * up * slope).astype(BF16)
        up_low = (grad_hidden * active).astype(BF16)
        for k in range(span):
            at = slice(k * side, (k + 1) * side)
            hidden_turned[span * j + k] = hidden_wide[:, at].T.astype(BF16)
            gate_grad[span * j + k] = gate_low[:, at]
            up_grad[span * j + k] = up_low[:, at]
        forward[...] += mul(hidden[:rows], down_ring[slot])
        start(todo, later, 4 * sixth, 5 * sixth)
        start(todo, later, 5 * sixth, 6 * sixth)
        backward[...] += mul_turned(gate_low[:rows], gate_ring[slot]) + mul_turned(up_low[:rows], up_ring[slot])
        return 0

    lax.fori_loop(0, steps, step, 0)
    for j in range(steps, steps + ring - 1):
        arrived(j % ring)
    outputs[...] = (middle[...] + forward[...]).astype(BF16)
    back, term = norm_back(middle[...], gain[...], backward[...])
    gain_term[...] = term
    total = cotangent_own[...].astype(F32) + back
    grad_middle[...] = total
    low = total.astype(BF16)
    branch[...] = low
    for c in range(wide):
        branch_blocks[c] = low[:, c * side : (c + 1) * side]


def mlp(slots, full, normed_own, normed_beside, cotangent_own, cotangent_beside, middle, gain, ring=3, span=4):
    rows, width = normed_own.shape
    side = full.shape[1]
    blocks = FF // side
    V = pltpu.VMEM
    spec = pl.BlockSpec(memory_space=V)
    S = jax.ShapeDtypeStruct
    return pl.pallas_call(
        functools.partial(mlp_kernel, side, ring, span),
        grid_spec=pltpu.PrefetchScalarGridSpec(
            num_scalar_prefetch=1,
            grid=(),
            in_specs=[pl.BlockSpec(memory_space=pl.ANY)] + [spec] * 6,
            out_specs=[spec] * 8,
            scratch_shapes=[V((2 * rows, width), BF16), V((2 * rows, width), BF16), V((rows, width), F32), V((rows, width), F32),
                            V((ring, width, span * side), BF16), V((ring, width, span * side), BF16), V((ring, span * side, width), BF16),
                            pltpu.SemaphoreType.DMA((ring,))],
        ),
        out_shape=[S((blocks, side, 2 * rows), BF16), S((blocks, 2 * rows, side), BF16), S((blocks, 2 * rows, side), BF16),
                   S((rows, width), BF16), S((rows, width), F32), S((rows, width), BF16), S((width // side, rows, side), BF16),
                   S((1, width), F32)],
        cost_estimate=cost_of(37),
        compiler_params=pltpu.CompilerParams(vmem_limit_bytes=56 * 2**20),
    )(slots, full, normed_own, normed_beside, cotangent_own, cotangent_beside, middle, gain)


def attend_back_kernel(side, slots, first, full, branch, queries, pairs, own_ids, all_ids, cosine, sine,
                       query_grad, pair_grad, own_pair_grad, weights, attended_grad, bias, key_total, value_total, sems):
    rows = branch.shape[0]
    heads = queries.shape[1] // side
    wide = branch.shape[1] // side

    def fetch(n, _):
        i, j = n // wide, n % wide
        number = (heads + 2) * wide + i * wide + j
        fetch_tile(full, slots, number, weights.at[block_at(i * side, side), block_at(j * side, side)], sems.at[i // 2])
        return 0

    lax.fori_loop(0, wide * heads, fetch, 0, unroll=8)
    fill_bias(first[0], own_ids, all_ids, bias)
    keys = pairs[:, :, :side].reshape(-1, side)
    values = pairs[:, :, side:].reshape(-1, side)
    scale = HEAD_DIM ** (-0.5)
    for c in range(heads // 2):
        view = weights.at[pl.ds(c * 2 * side, 2 * side), :]
        pltpu.make_async_copy(view, view, sems.at[c]).wait()
        attended_grad[:, c * 2 * side : (c + 1) * 2 * side] = mul_turned(branch[...], view[...]).astype(BF16)
    key_total[...] = jnp.zeros_like(key_total)
    value_total[...] = jnp.zeros_like(value_total)
    for head in range(heads):
        at = slice(head * side, (head + 1) * side)
        scores = mul_turned(queries[:, at], keys) * scale + bias[...]
        share = softmax_of(scores)
        share_grad = mul_turned(attended_grad[:, at], values)
        inner = jnp.sum(share * share_grad, -1, keepdims=True)
        score_grad = (share * (share_grad - inner)).astype(BF16)
        query_grad[head] = turn(mul(score_grad, keys) * scale, cosine[...], -sine[...]).astype(BF16)
        key_total[...] += mul_summed(score_grad, queries[:, at])
        value_total[...] += mul_summed(share.astype(BF16), attended_grad[:, at])
    key_total[...] = key_total[...] * scale
    for b in range(pairs.shape[0]):
        at = slice(b * rows, (b + 1) * rows)
        pair_grad[b, :, :side] = key_total[at].astype(BF16)
        pair_grad[b, :, side:] = value_total[at].astype(BF16)
    own = block_at(first[0], rows)
    own_pair_grad[:, :side] = key_total[own, :]
    own_pair_grad[:, side:] = value_total[own, :]


def attend_back(slots, first, full, branch, queries, pairs, own_ids, all_ids, cosine, sine):
    rows, width = branch.shape
    side = full.shape[1]
    key_rows = pairs.shape[0] * pairs.shape[1]
    V = pltpu.VMEM
    spec = pl.BlockSpec(memory_space=V)
    S = jax.ShapeDtypeStruct
    return pl.pallas_call(
        functools.partial(attend_back_kernel, side),
        grid_spec=pltpu.PrefetchScalarGridSpec(
            num_scalar_prefetch=2,
            grid=(),
            in_specs=[pl.BlockSpec(memory_space=pl.ANY)] + [spec] * 7,
            out_specs=[spec] * 3,
            scratch_shapes=[V((HEADS * side, width), BF16), V((rows, HEADS * side), BF16), V((rows, key_rows), F32),
                            V((key_rows, side), F32), V((key_rows, side), F32), pltpu.SemaphoreType.DMA((HEADS // 2,))],
        ),
        out_shape=[S((HEADS, rows, side), BF16), S(pairs.shape, BF16), S((rows, 2 * side), F32)],
        cost_estimate=cost_of(15),
        compiler_params=pltpu.CompilerParams(vmem_limit_bytes=40 * 2**20),
    )(slots, first, full, branch, queries, pairs, own_ids, all_ids, cosine, sine)


def pairs_back_kernel(pair_grad, own_grad, query_grad, branch, cosine, sine, low, query_beside, query_twin, query_far,
                      branch_beside, branch_twin, branch_far, arrived, sends, recvs, unit_sends, unit_recvs):
    replica = lax.axis_index("replica")
    member = lax.axis_index("fsdp")
    beside = ((1 - replica // 2) * 2 + replica % 2, member)
    twin = (replica // 2 * 2 + 1 - replica % 2, member)
    count = pair_grad.shape[0]
    side = cosine.shape[1]
    barrier = pltpu.get_barrier_semaphore()
    for device in [(replica, (member + step) % count) for step in range(1, count)] + [beside, twin]:
        pl.semaphore_signal(barrier, inc=1, device_id=device, device_id_type=MESH)
    pl.semaphore_wait(barrier, count + 1)

    def copy(step):
        target = (member + step) % count
        return pltpu.make_async_remote_copy(
            src_ref=pair_grad.at[target], dst_ref=arrived.at[step], send_sem=sends.at[step], recv_sem=recvs.at[step],
            device_id=(replica, target), device_id_type=MESH)

    def unit_copy(n, source, target, device):
        return pltpu.make_async_remote_copy(
            src_ref=source, dst_ref=target, send_sem=unit_sends.at[n], recv_sem=unit_recvs.at[n],
            device_id=device, device_id_type=MESH)

    moves = []
    for n, (own, from_beside, from_twin, from_far) in enumerate(
            [(branch, branch_beside, branch_twin, branch_far), (query_grad, query_beside, query_twin, query_far)]):
        moves.append((unit_copy(3 * n, own, from_beside, beside), unit_copy(3 * n + 1, own, from_twin, twin),
                      unit_copy(3 * n + 2, from_beside, from_far, twin)))
    for step in range(1, count):
        copy(step).start()
    for to_beside, to_twin, pass_on in moves:
        to_beside.start()
        to_twin.start()
    total = own_grad[...]
    for step in range(1, count):
        copy(step).wait_recv()
        total = total + arrived[step].astype(F32)
    low[0] = turn(total[:, :side], cosine[...], -sine[...]).astype(BF16)
    low[1] = total[:, side:].astype(BF16)
    for step in range(1, count):
        copy(step).wait_send()
    for to_beside, to_twin, pass_on in moves:
        to_beside.wait_recv()
        pass_on.start()
    for to_beside, to_twin, pass_on in moves:
        to_beside.wait_send()
        to_twin.wait()
        pass_on.wait()


def pairs_back(pair_grad, own_grad, query_grad, branch, cosine, sine):
    count, rows, double = pair_grad.shape
    D = pltpu.SemaphoreType.DMA
    S = jax.ShapeDtypeStruct
    spec = pl.BlockSpec(memory_space=pltpu.VMEM)
    return pl.pallas_call(
        pairs_back_kernel,
        out_shape=[S((2, rows, double // 2), BF16)] + [S(query_grad.shape, BF16)] * 3 + [S(branch.shape, BF16)] * 3,
        in_specs=[spec] * 6,
        out_specs=[spec] * 7,
        scratch_shapes=[pltpu.VMEM(pair_grad.shape, BF16), D((count,)), D((count,)), D((6,)), D((6,))],
        cost_estimate=cost_of(16),
        compiler_params=pltpu.CompilerParams(collective_id=3, has_side_effects=True),
    )(pair_grad, own_grad, query_grad, branch, cosine, sine)


def input_back_kernel(side, slots, full, query_grad, pair_grad, inputs, grad_middle, gain,
                      input_grad, gain_term, weights, joined, backward, sems):
    wide = inputs.shape[1] // side
    heads = query_grad.shape[0]

    def fetch(n, _):
        i, j = n // (heads + 2), n % (heads + 2)
        number = jnp.where(j < heads, i * heads + j, wide * j + i)
        fetch_tile(full, slots, number, weights.at[block_at(i * side, side), block_at(j * side, side)], sems.at[i // 2])
        return 0

    lax.fori_loop(0, wide * (heads + 2), fetch, 0, unroll=8)
    for h in range(heads):
        joined[:, h * side : (h + 1) * side] = query_grad[h]
    for k in range(2):
        joined[:, (heads + k) * side : (heads + k + 1) * side] = pair_grad[k]
    for c in range(wide // 2):
        view = weights.at[pl.ds(c * 2 * side, 2 * side), :]
        pltpu.make_async_copy(view, view, sems.at[c]).wait()
        backward[:, c * 2 * side : (c + 1) * 2 * side] = mul_turned(joined[...], view[...])
    back, term = norm_back(inputs[...].astype(F32), gain[...], backward[...])
    gain_term[...] = term
    input_grad[...] = (grad_middle[...] + back).astype(BF16)


def input_back(slots, full, query_grad, pair_grad, inputs, grad_middle, gain):
    rows, width = inputs.shape
    side = full.shape[1]
    V = pltpu.VMEM
    spec = pl.BlockSpec(memory_space=V)
    S = jax.ShapeDtypeStruct
    return pl.pallas_call(
        functools.partial(input_back_kernel, side),
        grid_spec=pltpu.PrefetchScalarGridSpec(
            num_scalar_prefetch=1,
            grid=(),
            in_specs=[pl.BlockSpec(memory_space=pl.ANY)] + [spec] * 5,
            out_specs=[spec] * 2,
            scratch_shapes=[V((width, (HEADS + 2) * side), BF16), V((rows, (HEADS + 2) * side), BF16), V((rows, width), F32),
                            pltpu.SemaphoreType.DMA((width // side // 2,))],
        ),
        out_shape=[S((rows, width), BF16), S((1, width), F32)],
        cost_estimate=cost_of(8),
        compiler_params=pltpu.CompilerParams(vmem_limit_bytes=40 * 2**20),
    )(slots, full, query_grad, pair_grad, inputs, grad_middle, gain)


def reduce_kernel(chunk, lag, places, left_at, right_at, gain_part, *refs):
    count = len(places)
    sources, refs = refs[:count], refs[count:]
    (out, gain_out, left_all, right_all, x_out, x_in, z_out, z_in, total, gain_sum, gain_in, keep_sem, gain_s, gain_r,
     x_s, x_r, z_s, z_r, ty_s, ty_r, tc_s, tc_r, tf_s, tf_r, done_sem) = refs
    quarter = x_out.shape[1]
    pieces = quarter // chunk
    replica = lax.axis_index("replica")
    member = lax.axis_index("fsdp")
    y, core = replica // 2, replica % 2
    z, x = member // 2, member % 2
    across, beside, twin = (replica, z * 2 + 1 - x), ((1 - y) * 2 + core, member), (y * 2 + 1 - core, member)
    beside_replica, twin_replica, far_replica = (1 - y) * 2 + core, y * 2 + 1 - core, (1 - y) * 2 + 1 - core
    def level(step):
        return (z + step) % 4
    def depth_device(step):
        return (replica, level(step) * 2 + x)
    def keep(n):
        is_left, block, lane = places[n]
        source = sources[n]
        if is_left:
            target = left_all.at[pl.ds(block, source.shape[0]), :, pl.ds(lane, source.shape[2])]
        else:
            target = right_all.at[pl.ds(block, source.shape[0]), pl.ds(lane, source.shape[1]), :]
        return pltpu.make_async_copy(source, target, keep_sem.at[n])
    for n in range(count):
        keep(n).start()
    left_all[left_all.shape[0] - 1] = jnp.zeros(left_all.shape[1:], left_all.dtype)
    gain_sum[...] = gain_part[...]

    barrier = pltpu.get_barrier_semaphore()
    for device in [across, beside, twin] + [depth_device(step) for step in (1, 2, 3)]:
        pl.semaphore_signal(barrier, inc=1, device_id=device, device_id_type=MESH)
    pl.semaphore_wait(barrier, 6)

    def remote(source, target, send, recv, device):
        return pltpu.make_async_remote_copy(src_ref=source, dst_ref=target, send_sem=send, recv_sem=recv, device_id=device, device_id_type=MESH)

    def gain_copy(stage, device):
        return remote(gain_sum, gain_in.at[stage], gain_s.at[stage], gain_r.at[stage], device)
    def gain_pair(stage, device):
        gain_copy(stage, device).wait()
        gain_sum[...] = gain_sum[...] + gain_in[stage]
    def gain_z(step):
        return remote(gain_sum, gain_in.at[2 + step], gain_s.at[2 + step], gain_r.at[2 + step], depth_device(step))
    def gain_finish():
        for step in (1, 2, 3):
            gain_z(step).wait()
        gain_in[0] = gain_sum[...]
        added = jnp.zeros(gain_sum.shape, F32)
        for zb in range(4):
            step = (zb - z + 4) % 4
            added = added + gain_in[jnp.where(step == 0, 0, 2 + step)]
        gain_out[...] = added
    gain_copy(0, beside).start()
    for n in range(count):
        keep(n).wait()

    def tile(owner, at):
        rank = replica * quarter + at
        return jnp.dot(left_all[left_at[owner, rank]], right_all[right_at[owner, rank]], preferred_element_type=F32)

    def x_copy(zb, k):
        at = pl.ds(k * chunk, chunk)
        return remote(x_out.at[zb, at], x_in.at[zb, at], x_s.at[zb, k], x_r.at[zb, k], across)
    def z_copy(step, k):
        at = pl.ds(k * chunk, chunk)
        return remote(z_out.at[step, at], z_in.at[step, at], z_s.at[step, k], z_r.at[step, k], depth_device(step))
    def total_at(who, k):
        return total.at[pl.ds(who * quarter + k * chunk, chunk)]
    def t_beside(k):
        return remote(total_at(replica, k), total_at(replica, k), ty_s.at[k], ty_r.at[k], beside)
    def t_twin(k):
        return remote(total_at(replica, k), total_at(replica, k), tc_s.at[k], tc_r.at[k], twin)
    def t_pass(k):
        return remote(total_at(beside_replica, k), total_at(beside_replica, k), tf_s.at[k], tf_r.at[k], twin)
    def come_beside(k):
        return remote(total_at(replica, k), total_at(beside_replica, k), ty_s.at[k], ty_r.at[k], beside)
    def come_twin(k):
        return remote(total_at(replica, k), total_at(twin_replica, k), tc_s.at[k], tc_r.at[k], twin)
    def come_far(k):
        return remote(total_at(replica, k), total_at(far_replica, k), tf_s.at[k], tf_r.at[k], twin)

    def send_x(k):
        def block(step, _):
            zb = level(step)
            def one(t, _):
                at = k * chunk + t
                x_out[zb, at] = tile(zb * 2 + 1 - x, at).astype(BF16)
                return 0
            lax.fori_loop(0, chunk, one, 0)
            x_copy(zb, k).start()
            return 0
        lax.fori_loop(0, 4, block, 0)

    def send_z(k):
        def block(step, _):
            zb = level(step)
            x_copy(zb, k).wait_recv()
            def one(t, _):
                at = k * chunk + t
                z_out[step, at] = (tile(zb * 2 + x, at) + x_in[zb, at].astype(F32)).astype(BF16)
                return 0
            lax.fori_loop(0, chunk, one, 0)
            @pl.when(step > 0)
            def _():
                z_copy(step, k).start()
            return 0
        lax.fori_loop(0, 4, block, 0)

    def finish(k):
        for step in (1, 2, 3):
            z_copy(step, k).wait_recv()
        def one(t, _):
            at = k * chunk + t
            added = z_out[0, at].astype(F32)
            for step in (1, 2, 3):
                added = added + z_in[step, at].astype(F32)
            total[replica * quarter + at] = added.astype(BF16)
            return 0
        lax.fori_loop(0, chunk, one, 0)
        t_beside(k).start()
        t_twin(k).start()

    def spread(k):
        come_beside(k).wait_recv()
        t_pass(k).start()

    def beat(n, _):
        @pl.when(n < pieces)
        def _():
            send_x(n)
        @pl.when((n >= lag) & (n < pieces + lag))
        def _():
            send_z(n - lag)
        @pl.when((n >= 2 * lag) & (n < pieces + 2 * lag))
        def _():
            finish(n - 2 * lag)
        @pl.when(n >= 3 * lag)
        def _():
            spread(n - 3 * lag)

        @pl.when(n == 2)
        def _():
            gain_pair(0, beside)
            gain_copy(1, twin).start()

        @pl.when(n == 4)
        def _():
            gain_pair(1, twin)
            gain_copy(2, across).start()

        @pl.when(n == 6)
        def _():
            gain_pair(2, across)
            for step in (1, 2, 3):
                gain_z(step).start()

        @pl.when(n == 9)
        def _():
            gain_finish()
        return 0
    lax.fori_loop(0, pieces + 3 * lag, beat, 0)

    def drain(k, _):
        come_twin(k).wait_recv()
        come_far(k).wait_recv()
        t_beside(k).wait_send()
        t_twin(k).wait_send()
        t_pass(k).wait_send()
        for zb in range(4):
            x_copy(zb, k).wait_send()
        for step in (1, 2, 3):
            z_copy(step, k).wait_send()
        return 0
    lax.fori_loop(0, pieces, drain, 0)
    result = pltpu.make_async_copy(total, out, done_sem)
    result.start()
    result.wait()

def reduce_tiles(left_at, right_at, gain_part, parts, places, left_total, right_total, rows, chunk=3, lag=2):
    capacity = left_at.shape[1]
    quarter = capacity // 4
    pieces = quarter // chunk
    side = parts[0].shape[1]
    D = pltpu.SemaphoreType.DMA
    V = pltpu.VMEM
    S = jax.ShapeDtypeStruct
    spec = pl.BlockSpec(memory_space=V)
    held = V((4, quarter, side, side), BF16)
    return pl.pallas_call(
        functools.partial(reduce_kernel, chunk, lag, places),
        out_shape=[S((capacity, side, side), BF16), S(gain_part.shape, F32)],
        in_specs=[pl.BlockSpec(memory_space=pltpu.SMEM)] * 2 + [spec] + [pl.BlockSpec(memory_space=pl.ANY)] * len(parts),
        out_specs=[pl.BlockSpec(memory_space=pl.ANY), spec],
        scratch_shapes=[
            V((left_total + 1, side, rows), BF16), V((right_total, rows, side), BF16), held, held, held, held,
            V((capacity, side, side), BF16), V(gain_part.shape, F32), V((6,) + gain_part.shape, F32),
            D((len(parts),)), D((6,)), D((6,))] + [D((4, pieces))] * 4 + [D((pieces,))] * 6 + [D],
        compiler_params=pltpu.CompilerParams(collective_id=1, has_side_effects=True, vmem_limit_bytes=62 * 2**20),
    )(left_at, right_at, gain_part, *parts)


def shampoo_kernel(count, grads, left_old, right_old, left_root, right_root, master, grads_out, left_new, right_new, master_new, low_new):
    side = grads.shape[1]
    flips, boths = [], []
    for at in range(count):
        wide = grads[at].astype(F32)
        grads_out[at] = wide
        flips.append(wide.T.astype(BF16))
    for at in range(count):
        both = jnp.dot(grads[at], jnp.concatenate([flips[at], right_root[at].astype(BF16)], 1), preferred_element_type=F32)
        left_new[at] = STAT_DECAY * left_old[at] + (1.0 - STAT_DECAY) * both[:, :side]
        boths.append(both[:, side:].astype(BF16))
    for at in range(count):
        right_new[at] = STAT_DECAY * right_old[at] + (1.0 - STAT_DECAY) * jnp.dot(flips[at], grads[at], preferred_element_type=F32)
    for at in range(count):
        turned = jnp.dot(left_root[at].astype(BF16), boths[at], preferred_element_type=F32)
        fresh = master[at] - STEP_RATE * turned
        master_new[at] = fresh
        low_new[at] = fresh.astype(BF16)

def shampoo(grads, left_old, right_old, left_root, right_root, master, count=17):
    capacity, side = master.shape[0], master.shape[1]
    while capacity % count:
        count -= 1
    spec = pl.BlockSpec((count, side, side), lambda i: (i, 0, 0))
    wide = jax.ShapeDtypeStruct(master.shape, F32)
    return pl.pallas_call(
        functools.partial(shampoo_kernel, count),
        grid=(capacity // count,),
        in_specs=[spec] * 6,
        out_specs=[spec] * 5,
        out_shape=[wide, wide, wide, wide, jax.ShapeDtypeStruct(master.shape, BF16)],
        compiler_params=pltpu.CompilerParams(vmem_limit_bytes=60 * 2**20),
    )(grads, left_old, right_old, left_root, right_root, master)


def shifted(block, axis, distance):
    devices = range(lax.axis_size(axis))
    route = [(i - distance, i) for i in devices if i - distance in devices]
    return lax.ppermute(block, axis, route)


def normalize(values, gain_row):
    mean_square = jnp.mean(values * values, -1, keepdims=True)
    return values * lax.rsqrt(mean_square + EPSILON) * gain_row


def rotate(values, angles):
    half_dim = values.shape[-1] // 2
    cosine = jnp.cos(angles)[:, None, :]
    sine_part = jnp.sin(angles)[:, None, :]
    first_half = values[..., :half_dim]
    second = values[..., half_dim:]
    return jnp.concatenate(
        [first_half * cosine - second * sine_part, second * cosine + first_half * sine_part], -1
    )


def angles_of(positions):
    half_dim = HEAD_DIM // 2
    inverse = 10000.0 ** (-2.0 * jnp.arange(half_dim, dtype=jnp.float32) / HEAD_DIM)
    return positions[:, None] * inverse[None, :]


def slot_of_tiles(owner_table, owners, capacity):
    onehot = (owner_table[:, None] == jnp.arange(owners, dtype=jnp.int32)[None, :]).astype(
        jnp.int32
    )
    earlier = jnp.cumsum(onehot, 0) - onehot
    ranking = jnp.sum(earlier * onehot, 1)
    return owner_table * capacity + ranking


def matrix_layout(width, head_width, head_dim, hidden_width, tile_side):
    left_attended = width // tile_side
    left_second = left_attended + head_width // tile_side
    left_hidden = left_second + width // tile_side
    right_key = head_width // tile_side
    right_value = right_key + head_dim // tile_side
    right_branch = right_value + head_dim // tile_side
    right_gate = right_branch + width // tile_side
    right_up = right_gate + hidden_width // tile_side
    right_down = right_up + hidden_width // tile_side
    return [
        (width, head_width, 0, 0),
        (width, head_dim, 0, right_key),
        (width, head_dim, 0, right_value),
        (head_width, width, left_attended, right_branch),
        (width, hidden_width, left_second, right_gate),
        (width, hidden_width, left_second, right_up),
        (hidden_width, width, left_hidden, right_down),
    ]


def project(values, blocks):
    row_count = values.shape[0]
    result = jnp.einsum(
        "nar,abrc->nbc",
        values.reshape(row_count, blocks.shape[0], blocks.shape[2]),
        blocks,
        preferred_element_type=jnp.float32,
    )
    return result.reshape(row_count, blocks.shape[1] * blocks.shape[3])


def back_project(values, blocks):
    row_count = values.shape[0]
    result = jnp.einsum(
        "nbc,abrc->nar",
        values.reshape(row_count, blocks.shape[1], blocks.shape[3]),
        blocks,
        preferred_element_type=jnp.float32,
    )
    return result.reshape(row_count, blocks.shape[0] * blocks.shape[2])


def dense_tile_grads(layout, left_blocks, right_blocks, tile_side):
    pieces = []
    for row_total, column_total, left_base, right_base in layout:
        left_part = left_blocks[:, left_base : left_base + row_total // tile_side]
        right_part = right_blocks[:, right_base : right_base + column_total // tile_side]
        product = jnp.einsum(
            "nar,nbc->abrc", left_part, right_part, preferred_element_type=jnp.float32
        )
        pieces.append(product.reshape(-1, tile_side, tile_side))
    pieces.append(jnp.zeros((1, tile_side, tile_side), jnp.float32))
    return jnp.concatenate(pieces, 0)


def block_tables(layout, tile_side, left_total):
    left_of, right_of = [], []
    for row_total, column_total, left_base, right_base in layout:
        for i in range(row_total // tile_side):
            for j in range(column_total // tile_side):
                left_of.append(left_base + i)
                right_of.append(right_base + j)
    return np.array(left_of + [left_total], np.int32), np.array(right_of + [0], np.int32)


def body_anywhere(
    inputs,
    cotangent,
    segment_ids,
    gains,
    owner_table,
    master_tiles,
    left_stats,
    right_stats,
    left_roots,
    right_roots,
):
    owners = lax.axis_size("fsdp")
    replicas = lax.axis_size("replica")
    member = lax.axis_index("fsdp")
    capacity = master_tiles.shape[0]
    tile_side = master_tiles.shape[1]
    row_count = inputs.shape[0]
    width = inputs.shape[1]
    head_width = HEADS * HEAD_DIM
    tile_total = owner_table.shape[0]
    layout = matrix_layout(width, head_width, HEAD_DIM, FF, tile_side)
    slots = slot_of_tiles(owner_table, owners, capacity)
    slot_tile = (
        jnp.full((owners * capacity,), tile_total, jnp.int32)
        .at[slots]
        .set(jnp.arange(tile_total, dtype=jnp.int32))
    )
    full = lax.all_gather(master_tiles.astype(jnp.bfloat16), "fsdp", axis=0, tiled=True)
    all_tiles = jnp.take(full, slots, axis=0)
    weights = []
    offset = 0
    for row_total, column_total, left_base, right_base in layout:
        number = row_total // tile_side * (column_total // tile_side)
        weights.append(
            all_tiles[offset : offset + number].reshape(
                row_total // tile_side, column_total // tile_side, tile_side, tile_side
            )
        )
        offset = offset + number
    w_query, w_key, w_value, w_out, w_gate, w_up, w_down = weights
    base_row = member * row_count
    own_ids = lax.dynamic_slice_in_dim(segment_ids, base_row, row_count, 0)
    starts = jnp.sum((segment_ids[None, :] < own_ids[:, None]).astype(jnp.int32), 1)
    positions = (base_row + jnp.arange(row_count, dtype=jnp.int32) - starts).astype(jnp.float32)
    angles = angles_of(positions)
    inputs_wide = inputs.astype(jnp.float32)
    normed = normalize(inputs_wide, gains[0]).astype(jnp.bfloat16)
    query_pre = project(normed, w_query)
    key_pre = project(normed, w_key)
    values_own = project(normed, w_value).astype(jnp.bfloat16)
    queries = rotate(query_pre.reshape(row_count, HEADS, HEAD_DIM), angles).astype(jnp.bfloat16)
    keys_own = rotate(key_pre[:, None, :], angles)[:, 0, :].astype(jnp.bfloat16)
    reach = WINDOW // row_count
    own_pair = jnp.concatenate([keys_own, values_own], 1)
    received = [shifted(own_pair, "fsdp", distance_back) for distance_back in range(reach, 0, -1)]
    pair_rows = jnp.concatenate(received + [own_pair], 0)
    key_rows = pair_rows[:, :HEAD_DIM]
    value_rows = pair_rows[:, HEAD_DIM:]
    padded_ids = jnp.concatenate([jnp.full((reach * row_count,), -1, jnp.int32), segment_ids], 0)
    key_ids = lax.dynamic_slice_in_dim(padded_ids, base_row, (reach + 1) * row_count, 0)
    distance = (
        jnp.arange(row_count, dtype=jnp.int32)[:, None]
        + reach * row_count
        - jnp.arange((reach + 1) * row_count, dtype=jnp.int32)[None, :]
    )
    allowed = (own_ids[:, None] == key_ids[None, :]) & (distance >= 0) & (distance < WINDOW)
    score_scale = HEAD_DIM ** (-0.5)
    scores = (
        jnp.einsum("nhd,kd->hnk", queries, key_rows, preferred_element_type=jnp.float32)
        * score_scale
    )
    scores = jnp.where(allowed[None], scores, -1e30)
    row_peak = jnp.max(scores, -1, keepdims=True)
    exponent = jnp.exp(scores - row_peak)
    row_total_sum = jnp.sum(exponent, -1, keepdims=True)
    probability = (exponent / row_total_sum).astype(jnp.bfloat16)
    log_total = row_peak + jnp.log(row_total_sum)
    attended = (
        jnp.einsum("hnk,kd->nhd", probability, value_rows, preferred_element_type=jnp.float32)
        .reshape(row_count, head_width)
        .astype(jnp.bfloat16)
    )
    middle = inputs_wide + project(attended, w_out)
    normed_two = normalize(middle, gains[1]).astype(jnp.bfloat16)
    gate = project(normed_two, w_gate)
    up_part = project(normed_two, w_up)

    def geglu(gate_values, up_values):
        return jax.nn.gelu(gate_values, approximate=True) * up_values

    hidden_wide, geglu_back = jax.vjp(geglu, gate, up_part)
    hidden = hidden_wide.astype(jnp.bfloat16)
    outputs = (middle + project(hidden, w_down)).astype(jnp.bfloat16)
    grad_hidden = back_project(cotangent, w_down)
    gate_back, up_back = geglu_back(grad_hidden)
    gate_grad = gate_back.astype(jnp.bfloat16)
    up_grad = up_back.astype(jnp.bfloat16)
    grad_normed_two = back_project(gate_grad, w_gate) + back_project(up_grad, w_up)
    middle_back, norm_two_back = jax.vjp(normalize, middle, gains[1])[1](grad_normed_two)
    grad_middle = cotangent.astype(jnp.float32) + middle_back
    branch_grad = grad_middle.astype(jnp.bfloat16)
    grad_attended = (
        back_project(branch_grad, w_out).astype(jnp.bfloat16).reshape(row_count, HEADS, HEAD_DIM)
    )
    scores_again = (
        jnp.einsum("nhd,kd->hnk", queries, key_rows, preferred_element_type=jnp.float32)
        * score_scale
    )
    scores_again = jnp.where(allowed[None], scores_again, -1e30)
    exact_prob = jnp.exp(scores_again - log_total)
    grad_prob = jnp.einsum(
        "nhd,kd->hnk", grad_attended, value_rows, preferred_element_type=jnp.float32
    )
    grad_scores = (
        exact_prob * (grad_prob - jnp.sum(exact_prob * grad_prob, -1, keepdims=True))
    ).astype(jnp.bfloat16)
    grad_queries = (
        jnp.einsum("hnk,kd->nhd", grad_scores, key_rows, preferred_element_type=jnp.float32)
        * score_scale
    )
    grad_keys = (
        jnp.einsum("hnk,nhd->kd", grad_scores, queries, preferred_element_type=jnp.float32)
        * score_scale
    )
    grad_values = jnp.einsum(
        "hnk,nhd->kd", probability, grad_attended, preferred_element_type=jnp.float32
    )
    grad_pairs = jnp.concatenate([grad_keys, grad_values], 1)
    own_grad = grad_pairs[reach * row_count :]
    for distance_back in range(1, reach + 1):
        sent_rows = grad_pairs[
            (reach - distance_back) * row_count : (reach - distance_back + 1) * row_count
        ]
        own_grad = own_grad + shifted(
            sent_rows.astype(jnp.bfloat16), "fsdp", -distance_back
        ).astype(sent_rows.dtype)
    grad_query_pre = (
        rotate(grad_queries, -angles).reshape(row_count, head_width).astype(jnp.bfloat16)
    )
    grad_key_pre = rotate(own_grad[:, None, :HEAD_DIM], -angles)[:, 0, :].astype(jnp.bfloat16)
    grad_values_low = own_grad[:, HEAD_DIM:].astype(jnp.bfloat16)
    grad_normed = (
        back_project(grad_query_pre, w_query)
        + back_project(grad_key_pre, w_key)
        + back_project(grad_values_low, w_value)
    )
    inputs_back, norm_one_back = jax.vjp(normalize, inputs_wide, gains[0])[1](grad_normed)
    input_grad = (grad_middle + inputs_back).astype(jnp.bfloat16)
    gain_grads = lax.psum(jnp.stack([norm_one_back, norm_two_back]), ("replica", "fsdp"))
    gain_rate = GAIN_STEP * (row_count * owners * replicas) ** (-0.5)
    new_gains = gains - gain_rate * gain_grads
    left_parts = jnp.concatenate([normed, attended, normed_two, hidden], 1)
    right_parts = jnp.concatenate(
        [grad_query_pre, grad_key_pre, grad_values_low, branch_grad, gate_grad, up_grad, cotangent],
        1,
    )
    left_blocks = left_parts.reshape(row_count, -1, tile_side)
    right_blocks = right_parts.reshape(row_count, -1, tile_side)
    dense = dense_tile_grads(layout, left_blocks, right_blocks, tile_side)
    partial_sum = lax.psum_scatter(
        jnp.take(dense, slot_tile, axis=0), "fsdp", scatter_dimension=0, tiled=True
    )
    grads_low = lax.psum(partial_sum.astype(jnp.bfloat16), "replica")
    grads_all, left_all, right_all, master_all, low_all = shampoo(
        grads_low, left_stats, right_stats, left_roots, right_roots, master_tiles
    )
    return (
        outputs,
        input_grad,
        gain_grads,
        new_gains,
        grads_all,
        master_all,
        low_all,
        left_all,
        right_all,
    )


def body_of_units(
    inputs,
    cotangent,
    segment_ids,
    gains,
    owner_table,
    master_tiles,
    left_stats,
    right_stats,
    left_roots,
    right_roots,
):
    owners, replicas = 8, 4
    member = lax.axis_index("fsdp")
    capacity = master_tiles.shape[0]
    side = master_tiles.shape[1]
    rows, width = inputs.shape
    tile_total = owner_table.shape[0]
    layout = matrix_layout(width, HEADS * HEAD_DIM, HEAD_DIM, FF, side)
    left_of, right_of = block_tables(layout, side, 0)
    padded = -(-tile_total // 128) * 128
    block_values = np.zeros((padded, 128), np.float32)
    block_values[:tile_total, 0] = left_of[:-1] + 1
    block_values[:tile_total, 1] = right_of[:-1] + 1
    left_total, right_total = int(max(left_of)) + 1, int(max(right_of)) + 1
    owner_row = jnp.pad(owner_table, (0, padded - tile_total), constant_values=-1).reshape(1, padded)

    slots, blocks_at, normed, early = prepare(
        owners, capacity, owner_row, jnp.asarray(block_values, BF16), inputs, cotangent, gains[0:1]
    )
    slots = slots.reshape(padded)
    chosen = blocks_at[:, :capacity, :2].astype(jnp.int32) - 1
    left_at = jnp.where(chosen[..., 0] < 0, left_total, chosen[..., 0])
    right_at = jnp.maximum(chosen[..., 1], 0)
    base_row = member * rows
    own_ids = lax.dynamic_slice_in_dim(segment_ids, base_row, rows, 0)
    starts = jnp.sum((segment_ids[None, :] < own_ids[:, None]).astype(jnp.int32), 1)
    positions = (base_row + jnp.arange(rows, dtype=jnp.int32) - starts).astype(jnp.float32)
    angles = angles_of(positions)
    cosine, sine = jnp.cos(angles), jnp.sin(angles)
    cosine = jnp.concatenate([cosine, cosine], 1)
    sine = jnp.concatenate([-sine, sine], 1)
    first = base_row.astype(jnp.int32).reshape(1)
    own_column, all_row = own_ids.reshape(-1, 1), segment_ids.reshape(1, -1)

    def over_y(part):
        return lax.ppermute(part, "replica", [(0, 2), (1, 3), (2, 0), (3, 1)])

    def over_core(part):
        return lax.ppermute(part, "replica", [(0, 1), (1, 0), (2, 3), (3, 2)])

    def unit_of(part):
        beside = over_y(part)
        return [part, beside, over_core(part), over_core(beside)]

    early_unit = unit_of(early)
    full = gather(master_tiles).reshape(owners * capacity, side, side)
    queries, pair = project_heads(slots, full, normed, cosine, sine)
    pairs = gather_pairs(pair, owners)
    attended_turned, normed_two, normed_two_turned, middle = attend(
        slots, first, full, queries, pairs, own_column, all_row, inputs, gains[1:2]
    )
    two_unit = unit_of(normed_two_turned)
    attended_turned, _ = lax.optimization_barrier((attended_turned, two_unit[1]))
    attended_unit = unit_of(attended_turned)
    wide = width // side
    hidden, gate_grad, up_grad, outputs, grad_middle, branch, branch_blocks, term_two = mlp(
        slots, full, normed_two, two_unit[1], cotangent, early_unit[1][wide:], middle, gains[1:2]
    )
    hidden_far, gate_far, up_far = over_core(hidden), over_core(gate_grad), over_core(up_grad)
    query_grad, pair_grad, own_pair_grad = attend_back(
        slots, first, full, branch, queries, pairs, own_column, all_row, cosine, sine
    )
    pair_low, *others = pairs_back(pair_grad, own_pair_grad, query_grad, branch_blocks, cosine, sine)
    query_unit = [query_grad] + others[:3]
    branch_unit = [branch_blocks] + others[3:]
    pair_unit = unit_of(pair_low)
    input_grad, term_one = input_back(slots, full, query_grad, pair_low, inputs, grad_middle, gains[0:1])

    parts, places = [], []

    def place(unit, is_left, block):
        for n, part in enumerate(unit):
            parts.append(part)
            places.append((is_left, block, n * rows * (4 // len(unit))))

    place([part[:wide] for part in early_unit], True, 0)
    place(attended_unit, True, wide)
    place(two_unit, True, wide + HEADS)
    place([hidden, hidden_far], True, 2 * wide + HEADS)
    place(query_unit, False, 0)
    place(pair_unit, False, HEADS)
    place(branch_unit, False, HEADS + 2)
    place([gate_grad, gate_far], False, HEADS + 2 + wide)
    place([up_grad, up_far], False, HEADS + 2 + wide + FF // side)
    place([part[wide:] for part in early_unit], False, HEADS + 2 + wide + 2 * FF // side)
    gain_part = jnp.concatenate([term_one, term_two, jnp.zeros((6, width), F32)], 0)
    grads_low, gain_sum = reduce_tiles(
        left_at, right_at, gain_part, parts, tuple(places), left_total, right_total, replicas * rows
    )
    gain_grads = gain_sum[:2]
    gain_rate = GAIN_STEP * (rows * owners * replicas) ** (-0.5)
    grads_all, left_all, right_all, master_all, low_all = shampoo(
        grads_low, left_stats, right_stats, left_roots, right_roots, master_tiles
    )
    return (
        outputs,
        input_grad,
        gain_grads,
        gains - gain_rate * gain_grads,
        grads_all,
        master_all,
        low_all,
        left_all,
        right_all,
    )


def solution(mesh):
    units = mesh.shape["replica"] == 4 and mesh.shape["fsdp"] == 8
    return jax.shard_map(
        body_of_units if units else body_anywhere,
        mesh=mesh,
        in_specs=(
            P(("replica", "fsdp"), None),
            P(("replica", "fsdp"), None),
            P("replica"),
            P(),
            P(),
            P("fsdp", None, None),
            P("fsdp", None, None),
            P("fsdp", None, None),
            P("fsdp", None, None),
            P("fsdp", None, None),
        ),
        out_specs=(
            P(("replica", "fsdp"), None),
            P(("replica", "fsdp"), None),
            P(),
            P(),
            P("fsdp", None, None),
            P("fsdp", None, None),
            P("fsdp", None, None),
            P("fsdp", None, None),
            P("fsdp", None, None),
        ),
        check_vma=False,
    )
```

```python
import functools

import jax
import jax.numpy as jnp
import numpy as np
from jax import lax
from jax.experimental import pallas as pl
from jax.experimental.pallas import tpu as pltpu
from jax.sharding import PartitionSpec as P

HEADS = 12
HEAD_DIM = 128
FF = 4608
WINDOW = 1024


EPSILON = 1e-06
STEP_RATE = 0.02
STAT_DECAY = 0.5
GAIN_STEP = 0.1
F32, BF16 = jnp.float32, jnp.bfloat16
MESH = pl.DeviceIdType.MESH


def gather_kernel(chunk, whole, deep_most, early, patience, master, full, stage, low, stage_sem, keep_sem,
                  up_s, up_r, down_s, down_r, x_s, x_r, eu_s, eu_r, ed_s, ed_r, y_s, y_r, core_s, core_r):
    replica = lax.axis_index("replica")
    member = lax.axis_index("fsdp")
    y, core = replica // 2, replica % 2
    z, x = member // 2, member % 2
    deep = deep_most - core
    run = whole - deep
    half = whole * chunk
    mirrored = z // 2
    inner = z + mirrored * (3 - 2 * z)
    above, below = (replica, (z + 1) * 2 + x), (replica, (z - 1) * 2 + x)
    across, beside, twin = (replica, z * 2 + 1 - x), ((1 - y) * 2 + core, member), (y * 2 + 1 - core, member)

    def rows(chunk_at, owner_core):
        return pl.ds(owner_core * half + chunk_at * chunk, chunk)

    def load(c, part):
        return pltpu.make_async_copy(master.at[rows(c, part)], stage.at[pl.ds(c * chunk, chunk)], stage_sem.at[c])

    def cast(c, part):
        load(c, part).wait()
        low[rows(c, part)] = stage[pl.ds(c * chunk, chunk)].astype(BF16)

    def place(k, plane):
        return plane * (whole - 1) + k * (1 - 2 * plane)

    def load_first(k, _):
        load(place(k, y), core).start()
        return 0

    lax.fori_loop(0, whole, load_first, 0)
    barrier = pltpu.get_barrier_semaphore()

    def greet(device):
        pl.semaphore_signal(barrier, inc=1, device_id=device, device_id_type=MESH)

    pl.when(z < 3)(lambda: greet(above))
    pl.when(z > 0)(lambda: greet(below))
    greet(across)
    greet(beside)
    greet(twin)

    @pl.when((z == 0) | (z == 3))
    def _():
        pl.semaphore_wait(barrier, 4)

    @pl.when((z > 0) & (z < 3))
    def _():
        pl.semaphore_wait(barrier, 5)

    def copy(owner, chunk_at, send, recv, device, from_own=False, owner_core=None):
        at = rows(chunk_at, core if owner_core is None else owner_core)
        target = full.at[owner, at]
        source = low.at[at] if from_own else target
        return pltpu.make_async_remote_copy(src_ref=source, dst_ref=target, send_sem=send, recv_sem=recv, device_id=device, device_id_type=MESH)

    def go_up(zb, k, own=False):
        return copy(zb * 2 + x, place(k, y), up_s.at[zb, k], up_r.at[zb, k], above, own)

    def go_down(zb, k, own=False):
        return copy(zb * 2 + x, place(k, y), down_s.at[zb, k], down_r.at[zb, k], below, own)

    def early_up(zb, k):
        return copy(zb * 2 + 1 - x, place(k, y), eu_s.at[zb, k], eu_r.at[zb, k], above)

    def early_down(zb, k):
        return copy(zb * 2 + 1 - x, place(k, y), ed_s.at[zb, k], ed_r.at[zb, k], below)

    def go_x(zb, k, own=False):
        return copy(zb * 2 + x, place(k, y), x_s.at[zb, k], x_r.at[zb, k], across, own)

    def come_x(zb, k):
        return copy(zb * 2 + 1 - x, place(k, y), x_s.at[zb, k], x_r.at[zb, k], across)

    def go_y(owner, k):
        return copy(owner, place(k, y), y_s.at[owner, k], y_r.at[owner, k], beside)

    def come_y(owner, k):
        return copy(owner, place(k, 1 - y), y_s.at[owner, k], y_r.at[owner, k], beside)

    def go_core(owner, at):
        return copy(owner, at, core_s.at[owner, at], core_r.at[owner, at], twin)

    def onward(owner, k):
        go_core(owner, place(k, y)).start()
        pl.when(k < deep)(lambda: go_y(owner, k).start())

    def across_block(g):
        b = g if g >= 2 else (g + inner) % 2
        return b + mirrored * (3 - 2 * b)

    def group(g):
        def tick(k, _):
            if g == 0:
                cast(place(k, y), core)
                pl.when(z < 3)(lambda: go_up(z, k, True).start())
                pl.when(z > 0)(lambda: go_down(z, k, True).start())
                go_x(z, k, True).start()
            if 1 <= g <= 3:
                @pl.when(z - g >= 0)
                def _():
                    go_up(z - g, k).wait_recv()
                    pl.when(z < 3)(lambda: go_up(z - g, k).start())
                    onward((z - g) * 2 + x, k)

                @pl.when(z + g <= 3)
                def _():
                    go_down(z + g, k).wait_recv()
                    pl.when(z > 0)(lambda: go_down(z + g, k).start())
                    onward((z + g) * 2 + x, k)

                pl.when(k >= early)(lambda: go_x(across_block(g), k).start())
            if g == 1:
                come_x(z, k).wait_recv()
                onward(z * 2 + 1 - x, k)

                @pl.when(k < early)
                def _():
                    pl.when(z < 3)(lambda: early_up(z, k).start())
                    pl.when(z > 0)(lambda: early_down(z, k).start())

            if 2 <= g <= 4:
                @pl.when(k >= early)
                def _():
                    come_x(across_block(g - 1), k).wait_recv()
                    onward(across_block(g - 1) * 2 + 1 - x, k)

                @pl.when((k < early) & (z - (g - 1) >= 0))
                def _():
                    zb = z - (g - 1)
                    early_up(zb, k).wait_recv()
                    pl.when(z < 3)(lambda: early_up(zb, k).start())
                    onward(zb * 2 + 1 - x, k)

                @pl.when((k < early) & (z + (g - 1) <= 3))
                def _():
                    zb = z + (g - 1)
                    early_down(zb, k).wait_recv()
                    pl.when(z > 0)(lambda: early_down(zb, k).start())
                    onward(zb * 2 + 1 - x, k)
            h = g - patience
            if 1 <= h <= 4:
                def take(owner):
                    come_y(owner, k).wait_recv()
                    go_core(owner, place(k, 1 - y)).start()

                if h <= 3:
                    pl.when((k < deep) & (z - h >= 0))(lambda: take((z - h) * 2 + x))
                    pl.when((k < deep) & (z + h <= 3))(lambda: take((z + h) * 2 + x))
                if h == 1:
                    pl.when(k < deep)(lambda: take(z * 2 + 1 - x))
                else:
                    pl.when((k < deep) & (k >= early))(lambda: take(across_block(h - 1) * 2 + 1 - x))
                    pl.when((k < early) & (z - (h - 1) >= 0))(lambda: take((z - (h - 1)) * 2 + 1 - x))
                    pl.when((k < early) & (z + (h - 1) <= 3))(lambda: take((z + (h - 1)) * 2 + 1 - x))
            return 0

        lax.fori_loop(0, run, tick, 0)

    group(0)

    def rest(k, _):
        cast(place(k, y), core)
        return 0

    lax.fori_loop(run, whole, rest, 0)

    def load_other(c, _):
        load(c, 1 - core).start()
        return 0

    lax.fori_loop(0, whole, load_other, 0)

    def cast_other(c, _):
        cast(c, 1 - core)
        return 0

    group(1)
    lax.fori_loop(0, whole, cast_other, 0)
    keep = pltpu.make_async_copy(low, full.at[member], keep_sem)
    keep.start()
    for g in range(2, 5 + patience):
        group(g)

    def drain_z(zb, _):
        def one(k, _):
            pl.when((zb <= z) & (z < 3))(lambda: go_up(zb, k).wait_send())
            pl.when((zb >= z) & (z > 0))(lambda: go_down(zb, k).wait_send())
            pl.when((zb == z) | (k >= early))(lambda: go_x(zb, k).wait_send())
            pl.when((k < early) & (zb <= z) & (z < 3))(lambda: early_up(zb, k).wait_send())
            pl.when((k < early) & (zb >= z) & (z > 0))(lambda: early_down(zb, k).wait_send())
            return 0

        lax.fori_loop(0, run, one, 0)
        return 0

    lax.fori_loop(0, 4, drain_z, 0)

    def drain_owner(owner, _):
        @pl.when(owner != member)
        def _():
            def one_y(k, _):
                go_y(owner, k).wait_send()
                return 0

            lax.fori_loop(0, deep, one_y, 0)

            def one_core(k, _):
                go_core(owner, k).wait_send()
                copy(owner, k, core_s.at[owner, k], core_r.at[owner, k], twin, owner_core=1 - core).wait_recv()
                return 0

            lax.fori_loop(0, whole, one_core, 0)

        return 0

    lax.fori_loop(0, 8, drain_owner, 0)
    keep.wait()


def gather(master, chunk=6, deep=6, early=1, patience=1):
    capacity = master.shape[0]
    whole = capacity // 2 // chunk
    run = whole - deep + 1
    D = pltpu.SemaphoreType.DMA
    V = pltpu.VMEM
    return pl.pallas_call(
        functools.partial(gather_kernel, chunk, whole, deep, early, patience),
        out_shape=jax.ShapeDtypeStruct((8,) + master.shape, BF16),
        in_specs=[pl.BlockSpec(memory_space=pl.ANY)],
        out_specs=pl.BlockSpec(memory_space=pl.ANY),
        scratch_shapes=[V((capacity // 2,) + master.shape[1:], F32), V(master.shape, BF16), D((whole,)), D]
        + [D((4, run))] * 6 + [D((4, max(early, 1)))] * 4 + [D((8, deep))] * 2 + [D((8, whole))] * 2,
        compiler_params=pltpu.CompilerParams(collective_id=0, has_side_effects=True, vmem_limit_bytes=40 * 2**20),
    )(master)


def prepare_kernel(owners, capacity, owner_row, block_values, inputs, cotangent, gain, slots, blocks_at, normed, early, ranks):
    total = owner_row.shape[1]
    lanes = 128
    owner = owner_row[...]
    same = (owner == lax.broadcasted_iota(jnp.int32, (owners, total), 0)).astype(F32)
    ones_before = (lax.broadcasted_iota(jnp.int32, (lanes, lanes), 0) < lax.broadcasted_iota(jnp.int32, (lanes, lanes), 1)).astype(BF16)
    carry = jnp.zeros((owners, 1), F32)
    for c in range(total // lanes):
        at = slice(c * lanes, (c + 1) * lanes)
        piece = same[:, at]
        before = jnp.dot(piece.astype(BF16), ones_before, preferred_element_type=F32) + carry
        ranks[:, at] = jnp.sum(before * piece, 0, keepdims=True).astype(jnp.int32)
        carry = carry + jnp.sum(piece, 1, keepdims=True)
    slot = jnp.where(owner >= 0, owner * capacity + ranks[...], -1)
    slots[...] = slot
    padded = blocks_at.shape[1]
    for o in range(owners):
        here = lax.broadcasted_iota(jnp.int32, (padded, total), 0)
        here = jnp.where(here < capacity, here + o * capacity, -2)
        hit = jnp.where(here == slot, 1.0, 0.0).astype(BF16)
        blocks_at[o] = jnp.dot(hit, block_values[...], preferred_element_type=F32)
    values = inputs[...].astype(F32)
    mean_square = jnp.mean(values * values, -1, keepdims=True)
    scaled = values * lax.rsqrt(mean_square + EPSILON) * gain[...]
    normed[...] = scaled.astype(BF16)
    count = early.shape[0] // 2
    for c in range(count):
        at = slice(c * lanes, (c + 1) * lanes)
        early[c] = scaled[:, at].T.astype(BF16)
        early[count + c] = cotangent[:, at]

def prepare(owners, capacity, owner_row, block_values, inputs, cotangent, gain):
    rows, width = inputs.shape
    padded = -(-capacity // 16) * 16
    S = jax.ShapeDtypeStruct
    spec = pl.BlockSpec(memory_space=pltpu.VMEM)
    return pl.pallas_call(
        functools.partial(prepare_kernel, owners, capacity),
        in_specs=[spec] * 5,
        out_specs=[spec] * 4,
        out_shape=[S(owner_row.shape, jnp.int32), S((owners, padded, 128), F32), S((rows, width), BF16),
                   S((2 * width // 128, 128, rows), BF16)],
        scratch_shapes=[pltpu.VMEM(owner_row.shape, jnp.int32)],
        compiler_params=pltpu.CompilerParams(vmem_limit_bytes=40 * 2**20),
    )(owner_row, block_values, inputs, cotangent, gain)


BY_ROWS = (((1,), (1,)), ((), ()))
BY_COLUMNS = (((0,), (0,)), ((), ()))


def mul(a, b):
    return jnp.dot(a, b, preferred_element_type=F32)


def mul_turned(a, b):
    return lax.dot_general(a, b, BY_ROWS, preferred_element_type=F32)


def mul_summed(a, b):
    return lax.dot_general(a, b, BY_COLUMNS, preferred_element_type=F32)


def turn(part, cosine, sine):
    return part * cosine + pltpu.roll(part, HEAD_DIM // 2, 1) * sine


def cost_of(microseconds):
    return pl.CostEstimate(flops=int(microseconds * 9e8), bytes_accessed=int(microseconds * 3e6), transcendentals=0)


def fetch_tile(full, slots, number, target, sem):
    pltpu.make_async_copy(full.at[slots[number]], target, sem).start()


def block_at(start, size):
    return pl.ds(pl.multiple_of(start, size), size)


def project_kernel(side, slots, full, normed, cosine, sine, queries, pair, weights, sems):
    wide = normed.shape[1] // side
    heads = queries.shape[1] // side

    def fetch(n, _):
        j, i = n // wide, n % wide
        number = jnp.where(j < heads, i * heads + j, wide * j + i)
        fetch_tile(full, slots, number, weights.at[block_at(i * side, side), block_at(j * side, side)], sems.at[j // 2])
        return 0

    lax.fori_loop(0, wide * (heads + 2), fetch, 0, unroll=8)
    for c in range((heads + 2) // 2):
        view = weights.at[:, pl.ds(c * 2 * side, 2 * side)]
        pltpu.make_async_copy(view, view, sems.at[c]).wait()
        product = mul(normed[...], view[...])
        for k in range(2):
            part = product[:, k * side : (k + 1) * side]
            if c < heads // 2:
                queries[:, (2 * c + k) * side : (2 * c + k + 1) * side] = turn(part, cosine[...], sine[...]).astype(BF16)
            elif k == 0:
                pair[:, :side] = turn(part, cosine[...], sine[...]).astype(BF16)
            else:
                pair[:, side:] = part.astype(BF16)


def project_heads(slots, full, normed, cosine, sine):
    rows, width = normed.shape
    side = full.shape[1]
    V = pltpu.VMEM
    spec = pl.BlockSpec(memory_space=V)
    return pl.pallas_call(
        functools.partial(project_kernel, side),
        grid_spec=pltpu.PrefetchScalarGridSpec(
            num_scalar_prefetch=1,
            grid=(),
            in_specs=[pl.BlockSpec(memory_space=pl.ANY), spec, spec, spec],
            out_specs=[spec, spec],
            scratch_shapes=[V((width, (HEADS + 2) * side), BF16), pltpu.SemaphoreType.DMA(((HEADS + 2) // 2,))],
        ),
        out_shape=[jax.ShapeDtypeStruct((rows, HEADS * side), BF16), jax.ShapeDtypeStruct((rows, 2 * side), BF16)],
        cost_estimate=cost_of(6),
        compiler_params=pltpu.CompilerParams(vmem_limit_bytes=40 * 2**20),
    )(slots, full, normed, cosine, sine)


def pairs_kernel(pair, pairs, keep_sem, sends, recvs):
    replica = lax.axis_index("replica")
    member = lax.axis_index("fsdp")
    count = pairs.shape[0]
    barrier = pltpu.get_barrier_semaphore()
    others = [(member + step) % count for step in range(1, count)]
    for other in others:
        pl.semaphore_signal(barrier, inc=1, device_id=(replica, other), device_id_type=MESH)
    pl.semaphore_wait(barrier, count - 1)
    keep = pltpu.make_async_copy(pair, pairs.at[member], keep_sem)
    keep.start()

    def copy(step, owner):
        return pltpu.make_async_remote_copy(
            src_ref=pair, dst_ref=pairs.at[owner], send_sem=sends.at[step], recv_sem=recvs.at[step],
            device_id=(replica, (member + step) % count), device_id_type=MESH)

    for step in range(1, count):
        copy(step, member).start()
    for step in range(1, count):
        copy(step, (member + count - step) % count).wait_recv()
    for step in range(1, count):
        copy(step, member).wait_send()
    keep.wait()


def gather_pairs(pair, count):
    D = pltpu.SemaphoreType.DMA
    spec = pl.BlockSpec(memory_space=pltpu.VMEM)
    return pl.pallas_call(
        pairs_kernel,
        out_shape=jax.ShapeDtypeStruct((count,) + pair.shape, pair.dtype),
        in_specs=[spec],
        out_specs=spec,
        scratch_shapes=[D, D((count,)), D((count,))],
        cost_estimate=cost_of(13),
        compiler_params=pltpu.CompilerParams(collective_id=2, has_side_effects=True),
    )(pair)


def fill_bias(first, own_ids, all_ids, bias):
    shape = bias.shape
    distance = first + lax.broadcasted_iota(jnp.int32, shape, 0) - lax.broadcasted_iota(jnp.int32, shape, 1)
    allowed = (own_ids[...] == all_ids[...]) & (distance >= 0) & (distance < WINDOW)
    bias[...] = jnp.where(allowed, 0.0, -1e30)


def softmax_of(scores):
    exponent = jnp.exp(scores - jnp.max(scores, -1, keepdims=True))
    return exponent / jnp.sum(exponent, -1, keepdims=True)


def attend_kernel(side, slots, first, full, queries, pairs, own_ids, all_ids, inputs, gain,
                  attended_turned, normed_two, normed_two_turned, middle, weights, attended, bias, sems):
    heads = attended.shape[1] // side
    wide = middle.shape[1] // side

    def fetch(n, _):
        j, i = n // heads, n % heads
        number = (heads + 2) * wide + i * wide + j
        fetch_tile(full, slots, number, weights.at[block_at(i * side, side), block_at(j * side, side)], sems.at[j // 2])
        return 0

    lax.fori_loop(0, wide * heads, fetch, 0, unroll=8)
    fill_bias(first[0], own_ids, all_ids, bias)
    keys = pairs[:, :, :side].reshape(-1, side)
    values = pairs[:, :, side:].reshape(-1, side)
    scale = HEAD_DIM ** (-0.5)
    for head in range(heads):
        at = slice(head * side, (head + 1) * side)
        scores = mul_turned(queries[:, at], keys) * scale + bias[...]
        product = mul(softmax_of(scores).astype(BF16), values)
        attended[:, at] = product.astype(BF16)
        attended_turned[head] = product.T.astype(BF16)
    total = jnp.zeros((inputs.shape[0], 1), F32)
    for c in range(wide // 2):
        view = weights.at[:, pl.ds(c * 2 * side, 2 * side)]
        pltpu.make_async_copy(view, view, sems.at[c]).wait()
        at = slice(c * 2 * side, (c + 1) * 2 * side)
        part = inputs[:, at].astype(F32) + mul(attended[...], view[...])
        middle[:, at] = part
        total = total + jnp.sum(part * part, -1, keepdims=True)
    scaled = lax.rsqrt(total / middle.shape[1] + EPSILON)
    for c in range(wide):
        at = slice(c * side, (c + 1) * side)
        part = middle[:, at] * scaled * gain[:, at]
        normed_two[:, at] = part.astype(BF16)
        normed_two_turned[c] = part.T.astype(BF16)


def attend(slots, first, full, queries, pairs, own_ids, all_ids, inputs, gain):
    rows, width = inputs.shape
    side = full.shape[1]
    V = pltpu.VMEM
    spec = pl.BlockSpec(memory_space=V)
    S = jax.ShapeDtypeStruct
    return pl.pallas_call(
        functools.partial(attend_kernel, side),
        grid_spec=pltpu.PrefetchScalarGridSpec(
            num_scalar_prefetch=2,
            grid=(),
            in_specs=[pl.BlockSpec(memory_space=pl.ANY)] + [spec] * 6,
            out_specs=[spec] * 4,
            scratch_shapes=[V((HEADS * side, width), BF16), V((rows, HEADS * side), BF16),
                            V((rows, pairs.shape[0] * pairs.shape[1]), F32), pltpu.SemaphoreType.DMA((width // side // 2,))],
        ),
        out_shape=[S((HEADS, side, rows), BF16), S((rows, width), BF16), S((width // side, side, rows), BF16), S((rows, width), F32)],
        cost_estimate=cost_of(11),
        compiler_params=pltpu.CompilerParams(vmem_limit_bytes=40 * 2**20),
    )(slots, first, full, queries, pairs, own_ids, all_ids, inputs, gain)


def norm_back(values, gain, grads):
    mean_square = jnp.mean(values * values, -1, keepdims=True)
    scaled = lax.rsqrt(mean_square + EPSILON)
    weighed = grads * gain
    inner = jnp.mean(weighed * values, -1, keepdims=True)
    back = scaled * weighed - values * (scaled * scaled * scaled * inner)
    return back, jnp.sum(grads * values * scaled, 0, keepdims=True)


GELU_SCALE = 0.7978845608028654
GELU_CUBE = 0.044715


def mlp_kernel(side, ring, span, slots, full, normed_own, normed_beside, cotangent_own, cotangent_beside, middle, gain,
               hidden_turned, gate_grad, up_grad, outputs, grad_middle, branch, branch_blocks, gain_term,
               normed, cotangent, forward, backward, gate_ring, up_ring, down_ring, sems):
    rows, width = normed_own.shape
    wide = width // side
    hidden_blocks = hidden_turned.shape[0]
    steps = hidden_blocks // span
    heads = HEADS
    base = (heads + 2) * wide + heads * wide

    def pieces_of(j, slot):
        todo = []
        for i in range(wide):
            for k in range(span):
                column = span * j + k
                row, lane = pl.ds(i * side, side), pl.ds(k * side, side)
                todo.append((base + i * hidden_blocks + column, gate_ring.at[slot, row, lane]))
                todo.append((base + (wide + i) * hidden_blocks + column, up_ring.at[slot, row, lane]))
                todo.append((base + 2 * wide * hidden_blocks + column * wide + i, down_ring.at[slot, lane, row]))
        return todo

    def start(todo, slot, first, last):
        for number, target in todo[first:last]:
            fetch_tile(full, slots, number, target, sems.at[slot])

    def arrived(slot):
        for target in (gate_ring, up_ring, down_ring):
            view = target.at[slot]
            pltpu.make_async_copy(view, view, sems.at[slot]).wait()

    for j in range(ring - 1):
        todo = pieces_of(j, j)
        start(todo, j, 0, len(todo))
    normed[:rows] = normed_own[...]
    cotangent[:rows] = cotangent_own[...]
    for c in range(wide):
        at = slice(c * side, (c + 1) * side)
        normed[rows:, at] = normed_beside[c].astype(F32).T.astype(BF16)
        cotangent[rows:, at] = cotangent_beside[c]
    forward[...] = jnp.zeros_like(forward)
    backward[...] = jnp.zeros_like(backward)

    def step(j, _):
        slot = j % ring
        arrived(slot)
        later = (j + ring - 1) % ring
        todo = pieces_of(jnp.minimum(j + ring - 1, steps - 1), later)
        sixth = len(todo) // 6
        start(todo, later, 0, sixth)
        gate = mul(normed[...], gate_ring[slot])
        start(todo, later, sixth, 2 * sixth)
        up = mul(normed[...], up_ring[slot])
        start(todo, later, 2 * sixth, 3 * sixth)
        grad_hidden = mul_turned(cotangent[...], down_ring[slot])
        start(todo, later, 3 * sixth, 4 * sixth)
        square = gate * gate
        bend = jnp.tanh(GELU_SCALE * gate * (1.0 + GELU_CUBE * square))
        share = 0.5 * (1.0 + bend)
        active = gate * share
        slope = share + 0.5 * gate * (1.0 - bend * bend) * (GELU_SCALE * (1.0 + 3.0 * GELU_CUBE * square))
        hidden_wide = active * up
        hidden = hidden_wide.astype(BF16)
        gate_low = (grad_hidden * up * slope).astype(BF16)
        up_low = (grad_hidden * active).astype(BF16)
        for k in range(span):
            at = slice(k * side, (k + 1) * side)
            hidden_turned[span * j + k] = hidden_wide[:, at].T.astype(BF16)
            gate_grad[span * j + k] = gate_low[:, at]
            up_grad[span * j + k] = up_low[:, at]
        forward[...] += mul(hidden[:rows], down_ring[slot])
        start(todo, later, 4 * sixth, 5 * sixth)
        start(todo, later, 5 * sixth, 6 * sixth)
        backward[...] += mul_turned(gate_low[:rows], gate_ring[slot]) + mul_turned(up_low[:rows], up_ring[slot])
        return 0

    lax.fori_loop(0, steps, step, 0)
    for j in range(steps, steps + ring - 1):
        arrived(j % ring)
    outputs[...] = (middle[...] + forward[...]).astype(BF16)
    back, term = norm_back(middle[...], gain[...], backward[...])
    gain_term[...] = term
    total = cotangent_own[...].astype(F32) + back
    grad_middle[...] = total
    low = total.astype(BF16)
    branch[...] = low
    for c in range(wide):
        branch_blocks[c] = low[:, c * side : (c + 1) * side]


def mlp(slots, full, normed_own, normed_beside, cotangent_own, cotangent_beside, middle, gain, ring=3, span=4):
    rows, width = normed_own.shape
    side = full.shape[1]
    blocks = FF // side
    V = pltpu.VMEM
    spec = pl.BlockSpec(memory_space=V)
    S = jax.ShapeDtypeStruct
    return pl.pallas_call(
        functools.partial(mlp_kernel, side, ring, span),
        grid_spec=pltpu.PrefetchScalarGridSpec(
            num_scalar_prefetch=1,
            grid=(),
            in_specs=[pl.BlockSpec(memory_space=pl.ANY)] + [spec] * 6,
            out_specs=[spec] * 8,
            scratch_shapes=[V((2 * rows, width), BF16), V((2 * rows, width), BF16), V((rows, width), F32), V((rows, width), F32),
                            V((ring, width, span * side), BF16), V((ring, width, span * side), BF16), V((ring, span * side, width), BF16),
                            pltpu.SemaphoreType.DMA((ring,))],
        ),
        out_shape=[S((blocks, side, 2 * rows), BF16), S((blocks, 2 * rows, side), BF16), S((blocks, 2 * rows, side), BF16),
                   S((rows, width), BF16), S((rows, width), F32), S((rows, width), BF16), S((width // side, rows, side), BF16),
                   S((1, width), F32)],
        cost_estimate=cost_of(37),
        compiler_params=pltpu.CompilerParams(vmem_limit_bytes=56 * 2**20),
    )(slots, full, normed_own, normed_beside, cotangent_own, cotangent_beside, middle, gain)


def attend_back_kernel(side, slots, first, full, branch, queries, pairs, own_ids, all_ids, cosine, sine,
                       query_grad, pair_grad, own_pair_grad, weights, attended_grad, bias, key_total, value_total, sems):
    rows = branch.shape[0]
    heads = queries.shape[1] // side
    wide = branch.shape[1] // side

    def fetch(n, _):
        i, j = n // wide, n % wide
        number = (heads + 2) * wide + i * wide + j
        fetch_tile(full, slots, number, weights.at[block_at(i * side, side), block_at(j * side, side)], sems.at[i // 2])
        return 0

    lax.fori_loop(0, wide * heads, fetch, 0, unroll=8)
    fill_bias(first[0], own_ids, all_ids, bias)
    keys = pairs[:, :, :side].reshape(-1, side)
    values = pairs[:, :, side:].reshape(-1, side)
    scale = HEAD_DIM ** (-0.5)
    for c in range(heads // 2):
        view = weights.at[pl.ds(c * 2 * side, 2 * side), :]
        pltpu.make_async_copy(view, view, sems.at[c]).wait()
        attended_grad[:, c * 2 * side : (c + 1) * 2 * side] = mul_turned(branch[...], view[...]).astype(BF16)
    key_total[...] = jnp.zeros_like(key_total)
    value_total[...] = jnp.zeros_like(value_total)
    for head in range(heads):
        at = slice(head * side, (head + 1) * side)
        scores = mul_turned(queries[:, at], keys) * scale + bias[...]
        share = softmax_of(scores)
        share_grad = mul_turned(attended_grad[:, at], values)
        inner = jnp.sum(share * share_grad, -1, keepdims=True)
        score_grad = (share * (share_grad - inner)).astype(BF16)
        query_grad[head] = turn(mul(score_grad, keys) * scale, cosine[...], -sine[...]).astype(BF16)
        key_total[...] += mul_summed(score_grad, queries[:, at])
        value_total[...] += mul_summed(share.astype(BF16), attended_grad[:, at])
    key_total[...] = key_total[...] * scale
    for b in range(pairs.shape[0]):
        at = slice(b * rows, (b + 1) * rows)
        pair_grad[b, :, :side] = key_total[at].astype(BF16)
        pair_grad[b, :, side:] = value_total[at].astype(BF16)
    own = block_at(first[0], rows)
    own_pair_grad[:, :side] = key_total[own, :]
    own_pair_grad[:, side:] = value_total[own, :]


def attend_back(slots, first, full, branch, queries, pairs, own_ids, all_ids, cosine, sine):
    rows, width = branch.shape
    side = full.shape[1]
    key_rows = pairs.shape[0] * pairs.shape[1]
    V = pltpu.VMEM
    spec = pl.BlockSpec(memory_space=V)
    S = jax.ShapeDtypeStruct
    return pl.pallas_call(
        functools.partial(attend_back_kernel, side),
        grid_spec=pltpu.PrefetchScalarGridSpec(
            num_scalar_prefetch=2,
            grid=(),
            in_specs=[pl.BlockSpec(memory_space=pl.ANY)] + [spec] * 7,
            out_specs=[spec] * 3,
            scratch_shapes=[V((HEADS * side, width), BF16), V((rows, HEADS * side), BF16), V((rows, key_rows), F32),
                            V((key_rows, side), F32), V((key_rows, side), F32), pltpu.SemaphoreType.DMA((HEADS // 2,))],
        ),
        out_shape=[S((HEADS, rows, side), BF16), S(pairs.shape, BF16), S((rows, 2 * side), F32)],
        cost_estimate=cost_of(15),
        compiler_params=pltpu.CompilerParams(vmem_limit_bytes=40 * 2**20),
    )(slots, first, full, branch, queries, pairs, own_ids, all_ids, cosine, sine)


def pairs_back_kernel(pair_grad, own_grad, query_grad, branch, cosine, sine, low, query_beside, query_twin, query_far,
                      branch_beside, branch_twin, branch_far, arrived, sends, recvs, unit_sends, unit_recvs):
    replica = lax.axis_index("replica")
    member = lax.axis_index("fsdp")
    beside = ((1 - replica // 2) * 2 + replica % 2, member)
    twin = (replica // 2 * 2 + 1 - replica % 2, member)
    count = pair_grad.shape[0]
    side = cosine.shape[1]
    barrier = pltpu.get_barrier_semaphore()
    for device in [(replica, (member + step) % count) for step in range(1, count)] + [beside, twin]:
        pl.semaphore_signal(barrier, inc=1, device_id=device, device_id_type=MESH)
    pl.semaphore_wait(barrier, count + 1)

    def copy(step):
        target = (member + step) % count
        return pltpu.make_async_remote_copy(
            src_ref=pair_grad.at[target], dst_ref=arrived.at[step], send_sem=sends.at[step], recv_sem=recvs.at[step],
            device_id=(replica, target), device_id_type=MESH)

    def unit_copy(n, source, target, device):
        return pltpu.make_async_remote_copy(
            src_ref=source, dst_ref=target, send_sem=unit_sends.at[n], recv_sem=unit_recvs.at[n],
            device_id=device, device_id_type=MESH)

    moves = []
    for n, (own, from_beside, from_twin, from_far) in enumerate(
            [(branch, branch_beside, branch_twin, branch_far), (query_grad, query_beside, query_twin, query_far)]):
        moves.append((unit_copy(3 * n, own, from_beside, beside), unit_copy(3 * n + 1, own, from_twin, twin),
                      unit_copy(3 * n + 2, from_beside, from_far, twin)))
    for step in range(1, count):
        copy(step).start()
    for to_beside, to_twin, pass_on in moves:
        to_beside.start()
        to_twin.start()
    total = own_grad[...]
    for step in range(1, count):
        copy(step).wait_recv()
        total = total + arrived[step].astype(F32)
    low[0] = turn(total[:, :side], cosine[...], -sine[...]).astype(BF16)
    low[1] = total[:, side:].astype(BF16)
    for step in range(1, count):
        copy(step).wait_send()
    for to_beside, to_twin, pass_on in moves:
        to_beside.wait_recv()
        pass_on.start()
    for to_beside, to_twin, pass_on in moves:
        to_beside.wait_send()
        to_twin.wait()
        pass_on.wait()


def pairs_back(pair_grad, own_grad, query_grad, branch, cosine, sine):
    count, rows, double = pair_grad.shape
    D = pltpu.SemaphoreType.DMA
    S = jax.ShapeDtypeStruct
    spec = pl.BlockSpec(memory_space=pltpu.VMEM)
    return pl.pallas_call(
        pairs_back_kernel,
        out_shape=[S((2, rows, double // 2), BF16)] + [S(query_grad.shape, BF16)] * 3 + [S(branch.shape, BF16)] * 3,
        in_specs=[spec] * 6,
        out_specs=[spec] * 7,
        scratch_shapes=[pltpu.VMEM(pair_grad.shape, BF16), D((count,)), D((count,)), D((6,)), D((6,))],
        cost_estimate=cost_of(16),
        compiler_params=pltpu.CompilerParams(collective_id=3, has_side_effects=True),
    )(pair_grad, own_grad, query_grad, branch, cosine, sine)


def input_back_kernel(side, slots, full, query_grad, pair_grad, inputs, grad_middle, gain,
                      input_grad, gain_term, weights, joined, backward, sems):
    wide = inputs.shape[1] // side
    heads = query_grad.shape[0]

    def fetch(n, _):
        i, j = n // (heads + 2), n % (heads + 2)
        number = jnp.where(j < heads, i * heads + j, wide * j + i)
        fetch_tile(full, slots, number, weights.at[block_at(i * side, side), block_at(j * side, side)], sems.at[i // 2])
        return 0

    lax.fori_loop(0, wide * (heads + 2), fetch, 0, unroll=8)
    for h in range(heads):
        joined[:, h * side : (h + 1) * side] = query_grad[h]
    for k in range(2):
        joined[:, (heads + k) * side : (heads + k + 1) * side] = pair_grad[k]
    for c in range(wide // 2):
        view = weights.at[pl.ds(c * 2 * side, 2 * side), :]
        pltpu.make_async_copy(view, view, sems.at[c]).wait()
        backward[:, c * 2 * side : (c + 1) * 2 * side] = mul_turned(joined[...], view[...])
    back, term = norm_back(inputs[...].astype(F32), gain[...], backward[...])
    gain_term[...] = term
    input_grad[...] = (grad_middle[...] + back).astype(BF16)


def input_back(slots, full, query_grad, pair_grad, inputs, grad_middle, gain):
    rows, width = inputs.shape
    side = full.shape[1]
    V = pltpu.VMEM
    spec = pl.BlockSpec(memory_space=V)
    S = jax.ShapeDtypeStruct
    return pl.pallas_call(
        functools.partial(input_back_kernel, side),
        grid_spec=pltpu.PrefetchScalarGridSpec(
            num_scalar_prefetch=1,
            grid=(),
            in_specs=[pl.BlockSpec(memory_space=pl.ANY)] + [spec] * 5,
            out_specs=[spec] * 2,
            scratch_shapes=[V((width, (HEADS + 2) * side), BF16), V((rows, (HEADS + 2) * side), BF16), V((rows, width), F32),
                            pltpu.SemaphoreType.DMA((width // side // 2,))],
        ),
        out_shape=[S((rows, width), BF16), S((1, width), F32)],
        cost_estimate=cost_of(8),
        compiler_params=pltpu.CompilerParams(vmem_limit_bytes=40 * 2**20),
    )(slots, full, query_grad, pair_grad, inputs, grad_middle, gain)


def reduce_kernel(chunk, places, left_at, right_at, gain_part, *refs):
    count = len(places)
    sources, refs = refs[:count], refs[count:]
    (out, gain_out, left_all, right_all, x_out, x_in, z_out, z_in, z_mix, turned_out, turned_in, turned_mix, total, gain_sum, gain_in, keep_sem, gain_s, gain_r,
     x_s, x_r, z_s, z_r, ty_s, ty_r, tc_s, tc_r, tf_s, tf_r, done_sem) = refs
    quarter = x_out.shape[1]
    pieces = quarter // chunk
    replica = lax.axis_index("replica")
    member = lax.axis_index("fsdp")
    y, core = replica // 2, replica % 2
    z, x = member // 2, member % 2
    across, beside, twin = (replica, z * 2 + 1 - x), ((1 - y) * 2 + core, member), (y * 2 + 1 - core, member)
    beside_replica, twin_replica, far_replica = (1 - y) * 2 + core, y * 2 + 1 - core, (1 - y) * 2 + 1 - core
    def level(step):
        return (z + step) % 4
    def depth_device(step):
        return (replica, level(step) * 2 + x)
    def keep(n):
        is_left, block, lane = places[n]
        source = sources[n]
        if is_left:
            target = left_all.at[pl.ds(block, source.shape[0]), :, pl.ds(lane, source.shape[2])]
        else:
            target = right_all.at[pl.ds(block, source.shape[0]), pl.ds(lane, source.shape[1]), :]
        return pltpu.make_async_copy(source, target, keep_sem.at[n])
    for n in range(count):
        keep(n).start()
    left_all[left_all.shape[0] - 1] = jnp.zeros(left_all.shape[1:], left_all.dtype)
    gain_sum[...] = gain_part[...]

    barrier = pltpu.get_barrier_semaphore()
    for device in [across, beside, twin] + [depth_device(step) for step in (1, 2, 3)]:
        pl.semaphore_signal(barrier, inc=1, device_id=device, device_id_type=MESH)
    pl.semaphore_wait(barrier, 6)

    def remote(source, target, send, recv, device):
        return pltpu.make_async_remote_copy(src_ref=source, dst_ref=target, send_sem=send, recv_sem=recv, device_id=device, device_id_type=MESH)

    def gain_copy(stage, device):
        return remote(gain_sum, gain_in.at[stage], gain_s.at[stage], gain_r.at[stage], device)
    def gain_pair(stage, device):
        gain_copy(stage, device).wait()
        gain_sum[...] = gain_sum[...] + gain_in[stage]
    def gain_z(step):
        return remote(gain_sum, gain_in.at[2 + step], gain_s.at[2 + step], gain_r.at[2 + step], depth_device(step))
    def gain_finish():
        for step in (1, 2, 3):
            gain_z(step).wait()
        gain_in[0] = gain_sum[...]
        added = jnp.zeros(gain_sum.shape, F32)
        for zb in range(4):
            step = (zb - z + 4) % 4
            added = added + gain_in[jnp.where(step == 0, 0, 2 + step)]
        gain_out[...] = added
    gain_copy(0, beside).start()
    for n in range(count):
        keep(n).wait()

    def tile(owner, at):
        rank = replica * quarter + at
        return jnp.dot(left_all[left_at[owner, rank]], right_all[right_at[owner, rank]], preferred_element_type=F32)

    paired = z + 1 - 2 * (z % 2)
    levels = [z, paired, 3 - z, 3 - paired]
    middle = (z == 1) | (z == 2)
    order = (2, 3, 1, 0)
    def turned(k):
        return k % 6 == 2
    def at_level(lev):
        return (replica, lev * 2 + x)
    def x_copy(zb, k):
        at = pl.ds(k * chunk, chunk)
        return remote(x_out.at[zb, at], x_in.at[zb, at], x_s.at[zb, k], x_r.at[zb, k], across)
    def buffers(column, k):
        if column == 0:
            return z_out, z_in, z_mix, k * chunk
        return turned_out, turned_in, turned_mix, k // 6 * chunk
    def z_send(column, block, place, kind, device, k):
        out_buffer, in_buffer, mix_buffer, base = buffers(column, k)
        at = pl.ds(base, chunk)
        target = in_buffer.at[place, at] if kind < 2 else mix_buffer.at[place, at]
        return remote(out_buffer.at[block, at], target, z_s.at[column, block, k], z_r.at[column, kind, k], device)
    def pass_paired(column, k):
        z_send(column, 1, 0, 0, at_level(levels[1]), k).start()
    def pass_end(column, block, k):
        z_send(column, block, 3 - block, 5 - block, at_level(levels[1]), k).start()
    def pass_middle(column, block, k):
        z_send(column, block, 1, 1, at_level(levels[block]), k).start()
    def z_arrival(column, place, kind, k):
        z_send(column, 1, place, kind, at_level(levels[1]), k).wait_recv()
    def leave(column, block, k):
        if block == 1:
            pass_paired(column, k)
        elif block > 1:
            pl.when(jnp.logical_not(middle))(lambda: pass_end(column, block, k))
    def combine(column, k):
        @pl.when(middle)
        def _():
            out_buffer, in_buffer, mix_buffer, base = buffers(column, k)
            for place in (0, 1):
                z_arrival(column, place, 2 + place, k)
                def one(t, _):
                    at = base + t
                    out_buffer[2 + place, at] = (out_buffer[2 + place, at].astype(F32) + mix_buffer[place, at].astype(F32)).astype(BF16)
                    return 0
                lax.fori_loop(0, chunk, one, 0)
                pass_middle(column, 2 + place, k)
    def z_total(column, k, t):
        out_buffer, in_buffer, mix_buffer, base = buffers(column, k)
        at = base + t
        return out_buffer[0, at].astype(F32) + in_buffer[0, at].astype(F32) + in_buffer[1, at].astype(F32)
    def total_at(who, k):
        return total.at[pl.ds(who * quarter + k * chunk, chunk)]
    def t_beside(k):
        return remote(total_at(replica, k), total_at(replica, k), ty_s.at[k], ty_r.at[k], beside)
    def t_twin(k):
        return remote(total_at(replica, k), total_at(replica, k), tc_s.at[k], tc_r.at[k], twin)
    def t_pass(k):
        return remote(total_at(beside_replica, k), total_at(beside_replica, k), tf_s.at[k], tf_r.at[k], twin)
    def come_beside(k):
        return remote(total_at(replica, k), total_at(beside_replica, k), ty_s.at[k], ty_r.at[k], beside)
    def come_twin(k):
        return remote(total_at(replica, k), total_at(twin_replica, k), tc_s.at[k], tc_r.at[k], twin)
    def come_far(k):
        return remote(total_at(replica, k), total_at(far_replica, k), tf_s.at[k], tf_r.at[k], twin)

    def send_x(k):
        for block in order:
            lev = levels[block]
            def one(t, _):
                at = k * chunk + t
                x_out[lev, at] = tile(lev * 2 + 1 - x, at).astype(BF16)
                return 0
            lax.fori_loop(0, chunk, one, 0)
            x_copy(lev, k).start()

    def collect(k):
        for block in order:
            lev = levels[block]
            x_copy(lev, k).wait_recv()
            def one(t, _):
                at = k * chunk + t
                z_out[block, at] = (tile(lev * 2 + x, at) + x_in[lev, at].astype(F32)).astype(BF16)
                return 0
            lax.fori_loop(0, chunk, one, 0)
            leave(0, block, k)

    def turned_send(k):
        for block in order:
            for column in (0, 1):
                owner = levels[block] * 2 + (x if column == 0 else 1 - x)
                out_buffer, in_buffer, mix_buffer, base = buffers(column, k)
                def one(t, _):
                    out_buffer[block, base + t] = tile(owner, k * chunk + t).astype(BF16)
                    return 0
                lax.fori_loop(0, chunk, one, 0)
                leave(column, block, k)

    def turned_cross(k):
        for column in (0, 1):
            for place in (0, 1):
                z_arrival(column, place, place, k)
        def one(t, _):
            x_out[0, k * chunk + t] = z_total(1, k, t).astype(BF16)
            return 0
        lax.fori_loop(0, chunk, one, 0)
        x_copy(0, k).start()

    def finish(k):
        @pl.when(turned(k))
        def _():
            x_copy(0, k).wait_recv()
            def one(t, _):
                at = k * chunk + t
                total[replica * quarter + at] = (z_total(0, k, t) + x_in[0, at].astype(F32)).astype(BF16)
                return 0
            lax.fori_loop(0, chunk, one, 0)
        @pl.when(jnp.logical_not(turned(k)))
        def _():
            for place in (0, 1):
                z_arrival(0, place, place, k)
            def one(t, _):
                total[replica * quarter + k * chunk + t] = z_total(0, k, t).astype(BF16)
                return 0
            lax.fori_loop(0, chunk, one, 0)
        t_beside(k).start()
        t_twin(k).start()

    def spread(k):
        come_beside(k).wait_recv()
        t_pass(k).start()

    def beat(n, _):
        def due(behind, kind):
            k = n - behind
            here = (k >= 0) & (k < pieces)
            return here & (turned(k) if kind else jnp.logical_not(turned(k)))
        pl.when(due(0, True))(lambda: turned_send(n))
        pl.when(due(0, False))(lambda: send_x(n))
        @pl.when(due(1, True))
        def _():
            combine(0, n - 1)
            combine(1, n - 1)
        pl.when(due(2, False))(lambda: collect(n - 2))
        pl.when(due(3, False))(lambda: combine(0, n - 3))
        pl.when(due(3, True))(lambda: turned_cross(n - 3))
        pl.when((n >= 5) & (n < pieces + 5))(lambda: finish(n - 5))
        pl.when(n >= 7)(lambda: spread(n - 7))

        @pl.when(n == 2)
        def _():
            gain_pair(0, beside)
            gain_copy(1, twin).start()

        @pl.when(n == 4)
        def _():
            gain_pair(1, twin)
            gain_copy(2, across).start()

        @pl.when(n == 6)
        def _():
            gain_pair(2, across)
            for step in (1, 2, 3):
                gain_z(step).start()

        @pl.when(n == 9)
        def _():
            gain_finish()
        return 0
    lax.fori_loop(0, pieces + 7, beat, 0)

    def drain(k, _):
        come_twin(k).wait_recv()
        come_far(k).wait_recv()
        t_beside(k).wait_send()
        t_twin(k).wait_send()
        t_pass(k).wait_send()
        x_copy(0, k).wait_send()
        for block in (1, 2, 3):
            z_send(0, block, 0, 0, at_level(levels[1]), k).wait_send()
        @pl.when(turned(k))
        def _():
            for block in (1, 2, 3):
                z_send(1, block, 0, 0, at_level(levels[1]), k).wait_send()
        @pl.when(jnp.logical_not(turned(k)))
        def _():
            for zb in (1, 2, 3):
                x_copy(zb, k).wait_send()
        return 0
    lax.fori_loop(0, pieces, drain, 0)
    result = pltpu.make_async_copy(total, out, done_sem)
    result.start()
    result.wait()

def reduce_tiles(left_at, right_at, gain_part, parts, places, left_total, right_total, rows, chunk=3):
    capacity = left_at.shape[1]
    quarter = capacity // 4
    pieces = quarter // chunk
    side = parts[0].shape[1]
    D = pltpu.SemaphoreType.DMA
    V = pltpu.VMEM
    S = jax.ShapeDtypeStruct
    spec = pl.BlockSpec(memory_space=V)
    held = V((4, quarter, side, side), BF16)
    arriving = V((2, quarter, side, side), BF16)
    seldom = (pieces + 3) // 6 * chunk
    return pl.pallas_call(
        functools.partial(reduce_kernel, chunk, places),
        out_shape=[S((capacity, side, side), BF16), S(gain_part.shape, F32)],
        in_specs=[pl.BlockSpec(memory_space=pltpu.SMEM)] * 2 + [spec] + [pl.BlockSpec(memory_space=pl.ANY)] * len(parts),
        out_specs=[pl.BlockSpec(memory_space=pl.ANY), spec],
        scratch_shapes=[
            V((left_total + 1, side, rows), BF16), V((right_total, rows, side), BF16), held, held, held, arriving, arriving,
            V((4, seldom, side, side), BF16), V((2, seldom, side, side), BF16), V((2, seldom, side, side), BF16),
            V((capacity, side, side), BF16), V(gain_part.shape, F32), V((6,) + gain_part.shape, F32),
            D((len(parts),)), D((6,)), D((6,))] + [D((4, pieces))] * 2 + [D((2, 4, pieces))] * 2 + [D((pieces,))] * 6 + [D],
        compiler_params=pltpu.CompilerParams(collective_id=1, has_side_effects=True, vmem_limit_bytes=62 * 2**20),
    )(left_at, right_at, gain_part, *parts)


def shampoo_kernel(count, grads, left_old, right_old, left_root, right_root, master, grads_out, left_new, right_new, master_new, low_new):
    side = grads.shape[1]
    flips, boths = [], []
    for at in range(count):
        wide = grads[at].astype(F32)
        grads_out[at] = wide
        flips.append(wide.T.astype(BF16))
    for at in range(count):
        both = jnp.dot(grads[at], jnp.concatenate([flips[at], right_root[at].astype(BF16)], 1), preferred_element_type=F32)
        left_new[at] = STAT_DECAY * left_old[at] + (1.0 - STAT_DECAY) * both[:, :side]
        boths.append(both[:, side:].astype(BF16))
    for at in range(count):
        right_new[at] = STAT_DECAY * right_old[at] + (1.0 - STAT_DECAY) * jnp.dot(flips[at], grads[at], preferred_element_type=F32)
    for at in range(count):
        turned = jnp.dot(left_root[at].astype(BF16), boths[at], preferred_element_type=F32)
        fresh = master[at] - STEP_RATE * turned
        master_new[at] = fresh
        low_new[at] = fresh.astype(BF16)

def shampoo(grads, left_old, right_old, left_root, right_root, master, count=17):
    capacity, side = master.shape[0], master.shape[1]
    while capacity % count:
        count -= 1
    spec = pl.BlockSpec((count, side, side), lambda i: (i, 0, 0))
    wide = jax.ShapeDtypeStruct(master.shape, F32)
    return pl.pallas_call(
        functools.partial(shampoo_kernel, count),
        grid=(capacity // count,),
        in_specs=[spec] * 6,
        out_specs=[spec] * 5,
        out_shape=[wide, wide, wide, wide, jax.ShapeDtypeStruct(master.shape, BF16)],
        compiler_params=pltpu.CompilerParams(vmem_limit_bytes=60 * 2**20),
    )(grads, left_old, right_old, left_root, right_root, master)


def shifted(block, axis, distance):
    devices = range(lax.axis_size(axis))
    route = [(i - distance, i) for i in devices if i - distance in devices]
    return lax.ppermute(block, axis, route)


def normalize(values, gain_row):
    mean_square = jnp.mean(values * values, -1, keepdims=True)
    return values * lax.rsqrt(mean_square + EPSILON) * gain_row


def rotate(values, angles):
    half_dim = values.shape[-1] // 2
    cosine = jnp.cos(angles)[:, None, :]
    sine_part = jnp.sin(angles)[:, None, :]
    first_half = values[..., :half_dim]
    second = values[..., half_dim:]
    return jnp.concatenate(
        [first_half * cosine - second * sine_part, second * cosine + first_half * sine_part], -1
    )


def angles_of(positions):
    half_dim = HEAD_DIM // 2
    inverse = 10000.0 ** (-2.0 * jnp.arange(half_dim, dtype=jnp.float32) / HEAD_DIM)
    return positions[:, None] * inverse[None, :]


def slot_of_tiles(owner_table, owners, capacity):
    onehot = (owner_table[:, None] == jnp.arange(owners, dtype=jnp.int32)[None, :]).astype(
        jnp.int32
    )
    earlier = jnp.cumsum(onehot, 0) - onehot
    ranking = jnp.sum(earlier * onehot, 1)
    return owner_table * capacity + ranking


def matrix_layout(width, head_width, head_dim, hidden_width, tile_side):
    left_attended = width // tile_side
    left_second = left_attended + head_width // tile_side
    left_hidden = left_second + width // tile_side
    right_key = head_width // tile_side
    right_value = right_key + head_dim // tile_side
    right_branch = right_value + head_dim // tile_side
    right_gate = right_branch + width // tile_side
    right_up = right_gate + hidden_width // tile_side
    right_down = right_up + hidden_width // tile_side
    return [
        (width, head_width, 0, 0),
        (width, head_dim, 0, right_key),
        (width, head_dim, 0, right_value),
        (head_width, width, left_attended, right_branch),
        (width, hidden_width, left_second, right_gate),
        (width, hidden_width, left_second, right_up),
        (hidden_width, width, left_hidden, right_down),
    ]


def project(values, blocks):
    row_count = values.shape[0]
    result = jnp.einsum(
        "nar,abrc->nbc",
        values.reshape(row_count, blocks.shape[0], blocks.shape[2]),
        blocks,
        preferred_element_type=jnp.float32,
    )
    return result.reshape(row_count, blocks.shape[1] * blocks.shape[3])


def back_project(values, blocks):
    row_count = values.shape[0]
    result = jnp.einsum(
        "nbc,abrc->nar",
        values.reshape(row_count, blocks.shape[1], blocks.shape[3]),
        blocks,
        preferred_element_type=jnp.float32,
    )
    return result.reshape(row_count, blocks.shape[0] * blocks.shape[2])


def dense_tile_grads(layout, left_blocks, right_blocks, tile_side):
    pieces = []
    for row_total, column_total, left_base, right_base in layout:
        left_part = left_blocks[:, left_base : left_base + row_total // tile_side]
        right_part = right_blocks[:, right_base : right_base + column_total // tile_side]
        product = jnp.einsum(
            "nar,nbc->abrc", left_part, right_part, preferred_element_type=jnp.float32
        )
        pieces.append(product.reshape(-1, tile_side, tile_side))
    pieces.append(jnp.zeros((1, tile_side, tile_side), jnp.float32))
    return jnp.concatenate(pieces, 0)


def block_tables(layout, tile_side, left_total):
    left_of, right_of = [], []
    for row_total, column_total, left_base, right_base in layout:
        for i in range(row_total // tile_side):
            for j in range(column_total // tile_side):
                left_of.append(left_base + i)
                right_of.append(right_base + j)
    return np.array(left_of + [left_total], np.int32), np.array(right_of + [0], np.int32)


def body_anywhere(
    inputs,
    cotangent,
    segment_ids,
    gains,
    owner_table,
    master_tiles,
    left_stats,
    right_stats,
    left_roots,
    right_roots,
):
    owners = lax.axis_size("fsdp")
    replicas = lax.axis_size("replica")
    member = lax.axis_index("fsdp")
    capacity = master_tiles.shape[0]
    tile_side = master_tiles.shape[1]
    row_count = inputs.shape[0]
    width = inputs.shape[1]
    head_width = HEADS * HEAD_DIM
    tile_total = owner_table.shape[0]
    layout = matrix_layout(width, head_width, HEAD_DIM, FF, tile_side)
    slots = slot_of_tiles(owner_table, owners, capacity)
    slot_tile = (
        jnp.full((owners * capacity,), tile_total, jnp.int32)
        .at[slots]
        .set(jnp.arange(tile_total, dtype=jnp.int32))
    )
    full = lax.all_gather(master_tiles.astype(jnp.bfloat16), "fsdp", axis=0, tiled=True)
    all_tiles = jnp.take(full, slots, axis=0)
    weights = []
    offset = 0
    for row_total, column_total, left_base, right_base in layout:
        number = row_total // tile_side * (column_total // tile_side)
        weights.append(
            all_tiles[offset : offset + number].reshape(
                row_total // tile_side, column_total // tile_side, tile_side, tile_side
            )
        )
        offset = offset + number
    w_query, w_key, w_value, w_out, w_gate, w_up, w_down = weights
    base_row = member * row_count
    own_ids = lax.dynamic_slice_in_dim(segment_ids, base_row, row_count, 0)
    starts = jnp.sum((segment_ids[None, :] < own_ids[:, None]).astype(jnp.int32), 1)
    positions = (base_row + jnp.arange(row_count, dtype=jnp.int32) - starts).astype(jnp.float32)
    angles = angles_of(positions)
    inputs_wide = inputs.astype(jnp.float32)
    normed = normalize(inputs_wide, gains[0]).astype(jnp.bfloat16)
    query_pre = project(normed, w_query)
    key_pre = project(normed, w_key)
    values_own = project(normed, w_value).astype(jnp.bfloat16)
    queries = rotate(query_pre.reshape(row_count, HEADS, HEAD_DIM), angles).astype(jnp.bfloat16)
    keys_own = rotate(key_pre[:, None, :], angles)[:, 0, :].astype(jnp.bfloat16)
    reach = WINDOW // row_count
    own_pair = jnp.concatenate([keys_own, values_own], 1)
    received = [shifted(own_pair, "fsdp", distance_back) for distance_back in range(reach, 0, -1)]
    pair_rows = jnp.concatenate(received + [own_pair], 0)
    key_rows = pair_rows[:, :HEAD_DIM]
    value_rows = pair_rows[:, HEAD_DIM:]
    padded_ids = jnp.concatenate([jnp.full((reach * row_count,), -1, jnp.int32), segment_ids], 0)
    key_ids = lax.dynamic_slice_in_dim(padded_ids, base_row, (reach + 1) * row_count, 0)
    distance = (
        jnp.arange(row_count, dtype=jnp.int32)[:, None]
        + reach * row_count
        - jnp.arange((reach + 1) * row_count, dtype=jnp.int32)[None, :]
    )
    allowed = (own_ids[:, None] == key_ids[None, :]) & (distance >= 0) & (distance < WINDOW)
    score_scale = HEAD_DIM ** (-0.5)
    scores = (
        jnp.einsum("nhd,kd->hnk", queries, key_rows, preferred_element_type=jnp.float32)
        * score_scale
    )
    scores = jnp.where(allowed[None], scores, -1e30)
    row_peak = jnp.max(scores, -1, keepdims=True)
    exponent = jnp.exp(scores - row_peak)
    row_total_sum = jnp.sum(exponent, -1, keepdims=True)
    probability = (exponent / row_total_sum).astype(jnp.bfloat16)
    log_total = row_peak + jnp.log(row_total_sum)
    attended = (
        jnp.einsum("hnk,kd->nhd", probability, value_rows, preferred_element_type=jnp.float32)
        .reshape(row_count, head_width)
        .astype(jnp.bfloat16)
    )
    middle = inputs_wide + project(attended, w_out)
    normed_two = normalize(middle, gains[1]).astype(jnp.bfloat16)
    gate = project(normed_two, w_gate)
    up_part = project(normed_two, w_up)

    def geglu(gate_values, up_values):
        return jax.nn.gelu(gate_values, approximate=True) * up_values

    hidden_wide, geglu_back = jax.vjp(geglu, gate, up_part)
    hidden = hidden_wide.astype(jnp.bfloat16)
    outputs = (middle + project(hidden, w_down)).astype(jnp.bfloat16)
    grad_hidden = back_project(cotangent, w_down)
    gate_back, up_back = geglu_back(grad_hidden)
    gate_grad = gate_back.astype(jnp.bfloat16)
    up_grad = up_back.astype(jnp.bfloat16)
    grad_normed_two = back_project(gate_grad, w_gate) + back_project(up_grad, w_up)
    middle_back, norm_two_back = jax.vjp(normalize, middle, gains[1])[1](grad_normed_two)
    grad_middle = cotangent.astype(jnp.float32) + middle_back
    branch_grad = grad_middle.astype(jnp.bfloat16)
    grad_attended = (
        back_project(branch_grad, w_out).astype(jnp.bfloat16).reshape(row_count, HEADS, HEAD_DIM)
    )
    scores_again = (
        jnp.einsum("nhd,kd->hnk", queries, key_rows, preferred_element_type=jnp.float32)
        * score_scale
    )
    scores_again = jnp.where(allowed[None], scores_again, -1e30)
    exact_prob = jnp.exp(scores_again - log_total)
    grad_prob = jnp.einsum(
        "nhd,kd->hnk", grad_attended, value_rows, preferred_element_type=jnp.float32
    )
    grad_scores = (
        exact_prob * (grad_prob - jnp.sum(exact_prob * grad_prob, -1, keepdims=True))
    ).astype(jnp.bfloat16)
    grad_queries = (
        jnp.einsum("hnk,kd->nhd", grad_scores, key_rows, preferred_element_type=jnp.float32)
        * score_scale
    )
    grad_keys = (
        jnp.einsum("hnk,nhd->kd", grad_scores, queries, preferred_element_type=jnp.float32)
        * score_scale
    )
    grad_values = jnp.einsum(
        "hnk,nhd->kd", probability, grad_attended, preferred_element_type=jnp.float32
    )
    grad_pairs = jnp.concatenate([grad_keys, grad_values], 1)
    own_grad = grad_pairs[reach * row_count :]
    for distance_back in range(1, reach + 1):
        sent_rows = grad_pairs[
            (reach - distance_back) * row_count : (reach - distance_back + 1) * row_count
        ]
        own_grad = own_grad + shifted(
            sent_rows.astype(jnp.bfloat16), "fsdp", -distance_back
        ).astype(sent_rows.dtype)
    grad_query_pre = (
        rotate(grad_queries, -angles).reshape(row_count, head_width).astype(jnp.bfloat16)
    )
    grad_key_pre = rotate(own_grad[:, None, :HEAD_DIM], -angles)[:, 0, :].astype(jnp.bfloat16)
    grad_values_low = own_grad[:, HEAD_DIM:].astype(jnp.bfloat16)
    grad_normed = (
        back_project(grad_query_pre, w_query)
        + back_project(grad_key_pre, w_key)
        + back_project(grad_values_low, w_value)
    )
    inputs_back, norm_one_back = jax.vjp(normalize, inputs_wide, gains[0])[1](grad_normed)
    input_grad = (grad_middle + inputs_back).astype(jnp.bfloat16)
    gain_grads = lax.psum(jnp.stack([norm_one_back, norm_two_back]), ("replica", "fsdp"))
    gain_rate = GAIN_STEP * (row_count * owners * replicas) ** (-0.5)
    new_gains = gains - gain_rate * gain_grads
    left_parts = jnp.concatenate([normed, attended, normed_two, hidden], 1)
    right_parts = jnp.concatenate(
        [grad_query_pre, grad_key_pre, grad_values_low, branch_grad, gate_grad, up_grad, cotangent],
        1,
    )
    left_blocks = left_parts.reshape(row_count, -1, tile_side)
    right_blocks = right_parts.reshape(row_count, -1, tile_side)
    dense = dense_tile_grads(layout, left_blocks, right_blocks, tile_side)
    partial_sum = lax.psum_scatter(
        jnp.take(dense, slot_tile, axis=0), "fsdp", scatter_dimension=0, tiled=True
    )
    grads_low = lax.psum(partial_sum.astype(jnp.bfloat16), "replica")
    grads_all, left_all, right_all, master_all, low_all = shampoo(
        grads_low, left_stats, right_stats, left_roots, right_roots, master_tiles
    )
    return (
        outputs,
        input_grad,
        gain_grads,
        new_gains,
        grads_all,
        master_all,
        low_all,
        left_all,
        right_all,
    )


def body_of_units(
    inputs,
    cotangent,
    segment_ids,
    gains,
    owner_table,
    master_tiles,
    left_stats,
    right_stats,
    left_roots,
    right_roots,
):
    owners, replicas = 8, 4
    member = lax.axis_index("fsdp")
    capacity = master_tiles.shape[0]
    side = master_tiles.shape[1]
    rows, width = inputs.shape
    tile_total = owner_table.shape[0]
    layout = matrix_layout(width, HEADS * HEAD_DIM, HEAD_DIM, FF, side)
    left_of, right_of = block_tables(layout, side, 0)
    padded = -(-tile_total // 128) * 128
    block_values = np.zeros((padded, 128), np.float32)
    block_values[:tile_total, 0] = left_of[:-1] + 1
    block_values[:tile_total, 1] = right_of[:-1] + 1
    left_total, right_total = int(max(left_of)) + 1, int(max(right_of)) + 1
    owner_row = jnp.pad(owner_table, (0, padded - tile_total), constant_values=-1).reshape(1, padded)

    slots, blocks_at, normed, early = prepare(
        owners, capacity, owner_row, jnp.asarray(block_values, BF16), inputs, cotangent, gains[0:1]
    )
    slots = slots.reshape(padded)
    chosen = blocks_at[:, :capacity, :2].astype(jnp.int32) - 1
    left_at = jnp.where(chosen[..., 0] < 0, left_total, chosen[..., 0])
    right_at = jnp.maximum(chosen[..., 1], 0)
    base_row = member * rows
    own_ids = lax.dynamic_slice_in_dim(segment_ids, base_row, rows, 0)
    starts = jnp.sum((segment_ids[None, :] < own_ids[:, None]).astype(jnp.int32), 1)
    positions = (base_row + jnp.arange(rows, dtype=jnp.int32) - starts).astype(jnp.float32)
    angles = angles_of(positions)
    cosine, sine = jnp.cos(angles), jnp.sin(angles)
    cosine = jnp.concatenate([cosine, cosine], 1)
    sine = jnp.concatenate([-sine, sine], 1)
    first = base_row.astype(jnp.int32).reshape(1)
    own_column, all_row = own_ids.reshape(-1, 1), segment_ids.reshape(1, -1)

    def over_y(part):
        return lax.ppermute(part, "replica", [(0, 2), (1, 3), (2, 0), (3, 1)])

    def over_core(part):
        return lax.ppermute(part, "replica", [(0, 1), (1, 0), (2, 3), (3, 2)])

    def unit_of(part):
        beside = over_y(part)
        return [part, beside, over_core(part), over_core(beside)]

    early_unit = unit_of(early)
    full = gather(master_tiles).reshape(owners * capacity, side, side)
    queries, pair = project_heads(slots, full, normed, cosine, sine)
    pairs = gather_pairs(pair, owners)
    attended_turned, normed_two, normed_two_turned, middle = attend(
        slots, first, full, queries, pairs, own_column, all_row, inputs, gains[1:2]
    )
    two_unit = unit_of(normed_two_turned)
    attended_turned, _ = lax.optimization_barrier((attended_turned, two_unit[1]))
    attended_unit = unit_of(attended_turned)
    wide = width // side
    hidden, gate_grad, up_grad, outputs, grad_middle, branch, branch_blocks, term_two = mlp(
        slots, full, normed_two, two_unit[1], cotangent, early_unit[1][wide:], middle, gains[1:2]
    )
    hidden_far, gate_far, up_far = over_core(hidden), over_core(gate_grad), over_core(up_grad)
    query_grad, pair_grad, own_pair_grad = attend_back(
        slots, first, full, branch, queries, pairs, own_column, all_row, cosine, sine
    )
    pair_low, *others = pairs_back(pair_grad, own_pair_grad, query_grad, branch_blocks, cosine, sine)
    query_unit = [query_grad] + others[:3]
    branch_unit = [branch_blocks] + others[3:]
    pair_unit = unit_of(pair_low)
    input_grad, term_one = input_back(slots, full, query_grad, pair_low, inputs, grad_middle, gains[0:1])

    parts, places = [], []

    def place(unit, is_left, block):
        for n, part in enumerate(unit):
            parts.append(part)
            places.append((is_left, block, n * rows * (4 // len(unit))))

    place([part[:wide] for part in early_unit], True, 0)
    place(attended_unit, True, wide)
    place(two_unit, True, wide + HEADS)
    place([hidden, hidden_far], True, 2 * wide + HEADS)
    place(query_unit, False, 0)
    place(pair_unit, False, HEADS)
    place(branch_unit, False, HEADS + 2)
    place([gate_grad, gate_far], False, HEADS + 2 + wide)
    place([up_grad, up_far], False, HEADS + 2 + wide + FF // side)
    place([part[wide:] for part in early_unit], False, HEADS + 2 + wide + 2 * FF // side)
    gain_part = jnp.concatenate([term_one, term_two, jnp.zeros((6, width), F32)], 0)
    grads_low, gain_sum = reduce_tiles(
        left_at, right_at, gain_part, parts, tuple(places), left_total, right_total, replicas * rows
    )
    gain_grads = gain_sum[:2]
    gain_rate = GAIN_STEP * (rows * owners * replicas) ** (-0.5)
    grads_all, left_all, right_all, master_all, low_all = shampoo(
        grads_low, left_stats, right_stats, left_roots, right_roots, master_tiles
    )
    return (
        outputs,
        input_grad,
        gain_grads,
        gains - gain_rate * gain_grads,
        grads_all,
        master_all,
        low_all,
        left_all,
        right_all,
    )


def solution(mesh):
    units = mesh.shape["replica"] == 4 and mesh.shape["fsdp"] == 8
    return jax.shard_map(
        body_of_units if units else body_anywhere,
        mesh=mesh,
        in_specs=(
            P(("replica", "fsdp"), None),
            P(("replica", "fsdp"), None),
            P("replica"),
            P(),
            P(),
            P("fsdp", None, None),
            P("fsdp", None, None),
            P("fsdp", None, None),
            P("fsdp", None, None),
            P("fsdp", None, None),
        ),
        out_specs=(
            P(("replica", "fsdp"), None),
            P(("replica", "fsdp"), None),
            P(),
            P(),
            P("fsdp", None, None),
            P("fsdp", None, None),
            P("fsdp", None, None),
            P("fsdp", None, None),
            P("fsdp", None, None),
        ),
        check_vma=False,
    )
```

```python
import functools

import jax
import jax.numpy as jnp
import numpy as np
from jax import lax
from jax.experimental import pallas as pl
from jax.experimental.pallas import tpu as pltpu
from jax.sharding import PartitionSpec as P

HEADS = 12
HEAD_DIM = 128
FF = 4608
WINDOW = 1024


EPSILON = 1e-06
STEP_RATE = 0.02
STAT_DECAY = 0.5
GAIN_STEP = 0.1
F32, BF16 = jnp.float32, jnp.bfloat16
MESH = pl.DeviceIdType.MESH


def gather_kernel(chunk, whole, deep_most, early, patience, master, full, stage, low, stage_sem, keep_sem,
                  up_s, up_r, down_s, down_r, x_s, x_r, eu_s, eu_r, ed_s, ed_r, y_s, y_r, core_s, core_r):
    replica = lax.axis_index("replica")
    member = lax.axis_index("fsdp")
    y, core = replica // 2, replica % 2
    z, x = member // 2, member % 2
    deep = deep_most - core
    run = whole - deep
    half = whole * chunk
    mirrored = z // 2
    inner = z + mirrored * (3 - 2 * z)
    above, below = (replica, (z + 1) * 2 + x), (replica, (z - 1) * 2 + x)
    across, beside, twin = (replica, z * 2 + 1 - x), ((1 - y) * 2 + core, member), (y * 2 + 1 - core, member)

    def rows(chunk_at, owner_core):
        return pl.ds(owner_core * half + chunk_at * chunk, chunk)

    def load(c, part):
        return pltpu.make_async_copy(master.at[rows(c, part)], stage.at[pl.ds(c * chunk, chunk)], stage_sem.at[c])

    def cast(c, part):
        load(c, part).wait()
        low[rows(c, part)] = stage[pl.ds(c * chunk, chunk)].astype(BF16)

    def place(k, plane):
        return plane * (whole - 1) + k * (1 - 2 * plane)

    def load_first(k, _):
        load(place(k, y), core).start()
        return 0

    lax.fori_loop(0, whole, load_first, 0)
    barrier = pltpu.get_barrier_semaphore()

    def greet(device):
        pl.semaphore_signal(barrier, inc=1, device_id=device, device_id_type=MESH)

    pl.when(z < 3)(lambda: greet(above))
    pl.when(z > 0)(lambda: greet(below))
    greet(across)
    greet(beside)
    greet(twin)

    @pl.when((z == 0) | (z == 3))
    def _():
        pl.semaphore_wait(barrier, 4)

    @pl.when((z > 0) & (z < 3))
    def _():
        pl.semaphore_wait(barrier, 5)

    def copy(owner, chunk_at, send, recv, device, from_own=False, owner_core=None):
        at = rows(chunk_at, core if owner_core is None else owner_core)
        target = full.at[owner, at]
        source = low.at[at] if from_own else target
        return pltpu.make_async_remote_copy(src_ref=source, dst_ref=target, send_sem=send, recv_sem=recv, device_id=device, device_id_type=MESH)

    def go_up(zb, k, own=False):
        return copy(zb * 2 + x, place(k, y), up_s.at[zb, k], up_r.at[zb, k], above, own)

    def go_down(zb, k, own=False):
        return copy(zb * 2 + x, place(k, y), down_s.at[zb, k], down_r.at[zb, k], below, own)

    def early_up(zb, k):
        return copy(zb * 2 + 1 - x, place(k, y), eu_s.at[zb, k], eu_r.at[zb, k], above)

    def early_down(zb, k):
        return copy(zb * 2 + 1 - x, place(k, y), ed_s.at[zb, k], ed_r.at[zb, k], below)

    def go_x(zb, k, own=False):
        return copy(zb * 2 + x, place(k, y), x_s.at[zb, k], x_r.at[zb, k], across, own)

    def come_x(zb, k):
        return copy(zb * 2 + 1 - x, place(k, y), x_s.at[zb, k], x_r.at[zb, k], across)

    def go_y(owner, k):
        return copy(owner, place(k, y), y_s.at[owner, k], y_r.at[owner, k], beside)

    def come_y(owner, k):
        return copy(owner, place(k, 1 - y), y_s.at[owner, k], y_r.at[owner, k], beside)

    def go_core(owner, at):
        return copy(owner, at, core_s.at[owner, at], core_r.at[owner, at], twin)

    def onward(owner, k):
        go_core(owner, place(k, y)).start()
        pl.when(k < deep)(lambda: go_y(owner, k).start())

    def across_block(g):
        b = g if g >= 2 else (g + inner) % 2
        return b + mirrored * (3 - 2 * b)

    def group(g):
        def tick(k, _):
            if g == 0:
                cast(place(k, y), core)
                pl.when(z < 3)(lambda: go_up(z, k, True).start())
                pl.when(z > 0)(lambda: go_down(z, k, True).start())
                go_x(z, k, True).start()
            if 1 <= g <= 3:
                @pl.when(z - g >= 0)
                def _():
                    go_up(z - g, k).wait_recv()
                    pl.when(z < 3)(lambda: go_up(z - g, k).start())
                    onward((z - g) * 2 + x, k)

                @pl.when(z + g <= 3)
                def _():
                    go_down(z + g, k).wait_recv()
                    pl.when(z > 0)(lambda: go_down(z + g, k).start())
                    onward((z + g) * 2 + x, k)

                pl.when(k >= early)(lambda: go_x(across_block(g), k).start())
            if g == 1:
                come_x(z, k).wait_recv()
                onward(z * 2 + 1 - x, k)

                @pl.when(k < early)
                def _():
                    pl.when(z < 3)(lambda: early_up(z, k).start())
                    pl.when(z > 0)(lambda: early_down(z, k).start())

            if 2 <= g <= 4:
                @pl.when(k >= early)
                def _():
                    come_x(across_block(g - 1), k).wait_recv()
                    onward(across_block(g - 1) * 2 + 1 - x, k)

                @pl.when((k < early) & (z - (g - 1) >= 0))
                def _():
                    zb = z - (g - 1)
                    early_up(zb, k).wait_recv()
                    pl.when(z < 3)(lambda: early_up(zb, k).start())
                    onward(zb * 2 + 1 - x, k)

                @pl.when((k < early) & (z + (g - 1) <= 3))
                def _():
                    zb = z + (g - 1)
                    early_down(zb, k).wait_recv()
                    pl.when(z > 0)(lambda: early_down(zb, k).start())
                    onward(zb * 2 + 1 - x, k)
            h = g - patience
            if 1 <= h <= 4:
                def take(owner):
                    come_y(owner, k).wait_recv()
                    go_core(owner, place(k, 1 - y)).start()

                if h <= 3:
                    pl.when((k < deep) & (z - h >= 0))(lambda: take((z - h) * 2 + x))
                    pl.when((k < deep) & (z + h <= 3))(lambda: take((z + h) * 2 + x))
                if h == 1:
                    pl.when(k < deep)(lambda: take(z * 2 + 1 - x))
                else:
                    pl.when((k < deep) & (k >= early))(lambda: take(across_block(h - 1) * 2 + 1 - x))
                    pl.when((k < early) & (z - (h - 1) >= 0))(lambda: take((z - (h - 1)) * 2 + 1 - x))
                    pl.when((k < early) & (z + (h - 1) <= 3))(lambda: take((z + (h - 1)) * 2 + 1 - x))
            return 0

        lax.fori_loop(0, run, tick, 0)

    group(0)

    def rest(k, _):
        cast(place(k, y), core)
        return 0

    lax.fori_loop(run, whole, rest, 0)

    def load_other(c, _):
        load(c, 1 - core).start()
        return 0

    lax.fori_loop(0, whole, load_other, 0)

    def cast_other(c, _):
        cast(c, 1 - core)
        return 0

    group(1)
    lax.fori_loop(0, whole, cast_other, 0)
    keep = pltpu.make_async_copy(low, full.at[member], keep_sem)
    keep.start()
    for g in range(2, 5 + patience):
        group(g)

    def drain_z(zb, _):
        def one(k, _):
            pl.when((zb <= z) & (z < 3))(lambda: go_up(zb, k).wait_send())
            pl.when((zb >= z) & (z > 0))(lambda: go_down(zb, k).wait_send())
            pl.when((zb == z) | (k >= early))(lambda: go_x(zb, k).wait_send())
            pl.when((k < early) & (zb <= z) & (z < 3))(lambda: early_up(zb, k).wait_send())
            pl.when((k < early) & (zb >= z) & (z > 0))(lambda: early_down(zb, k).wait_send())
            return 0

        lax.fori_loop(0, run, one, 0)
        return 0

    lax.fori_loop(0, 4, drain_z, 0)

    def drain_owner(owner, _):
        @pl.when(owner != member)
        def _():
            def one_y(k, _):
                go_y(owner, k).wait_send()
                return 0

            lax.fori_loop(0, deep, one_y, 0)

            def one_core(k, _):
                go_core(owner, k).wait_send()
                copy(owner, k, core_s.at[owner, k], core_r.at[owner, k], twin, owner_core=1 - core).wait_recv()
                return 0

            lax.fori_loop(0, whole, one_core, 0)

        return 0

    lax.fori_loop(0, 8, drain_owner, 0)
    keep.wait()


def gather(master, chunk=6, deep=6, early=1, patience=1):
    capacity = master.shape[0]
    whole = capacity // 2 // chunk
    run = whole - deep + 1
    D = pltpu.SemaphoreType.DMA
    V = pltpu.VMEM
    return pl.pallas_call(
        functools.partial(gather_kernel, chunk, whole, deep, early, patience),
        out_shape=jax.ShapeDtypeStruct((8,) + master.shape, BF16),
        in_specs=[pl.BlockSpec(memory_space=pl.ANY)],
        out_specs=pl.BlockSpec(memory_space=pl.ANY),
        scratch_shapes=[V((capacity // 2,) + master.shape[1:], F32), V(master.shape, BF16), D((whole,)), D]
        + [D((4, run))] * 6 + [D((4, max(early, 1)))] * 4 + [D((8, deep))] * 2 + [D((8, whole))] * 2,
        compiler_params=pltpu.CompilerParams(collective_id=0, has_side_effects=True, vmem_limit_bytes=60 * 2**20),
    )(master)


def prepare_kernel(owners, capacity, owner_row, block_values, inputs, cotangent, gain, slots, blocks_at, normed, early, ranks):
    total = owner_row.shape[1]
    lanes = 128
    owner = owner_row[...]
    same = (owner == lax.broadcasted_iota(jnp.int32, (owners, total), 0)).astype(F32)
    ones_before = (lax.broadcasted_iota(jnp.int32, (lanes, lanes), 0) < lax.broadcasted_iota(jnp.int32, (lanes, lanes), 1)).astype(BF16)
    carry = jnp.zeros((owners, 1), F32)
    for c in range(total // lanes):
        at = slice(c * lanes, (c + 1) * lanes)
        piece = same[:, at]
        before = jnp.dot(piece.astype(BF16), ones_before, preferred_element_type=F32) + carry
        ranks[:, at] = jnp.sum(before * piece, 0, keepdims=True).astype(jnp.int32)
        carry = carry + jnp.sum(piece, 1, keepdims=True)
    slot = jnp.where(owner >= 0, owner * capacity + ranks[...], -1)
    slots[...] = slot
    padded = blocks_at.shape[1]
    for o in range(owners):
        here = lax.broadcasted_iota(jnp.int32, (padded, total), 0)
        here = jnp.where(here < capacity, here + o * capacity, -2)
        hit = jnp.where(here == slot, 1.0, 0.0).astype(BF16)
        blocks_at[o] = jnp.dot(hit, block_values[...], preferred_element_type=F32)
    values = inputs[...].astype(F32)
    mean_square = jnp.mean(values * values, -1, keepdims=True)
    scaled = values * lax.rsqrt(mean_square + EPSILON) * gain[...]
    normed[...] = scaled.astype(BF16)
    count = early.shape[0] // 2
    for c in range(count):
        at = slice(c * lanes, (c + 1) * lanes)
        early[c] = scaled[:, at].T.astype(BF16)
        early[count + c] = cotangent[:, at]

def prepare(owners, capacity, owner_row, block_values, inputs, cotangent, gain):
    rows, width = inputs.shape
    padded = -(-capacity // 16) * 16
    S = jax.ShapeDtypeStruct
    spec = pl.BlockSpec(memory_space=pltpu.VMEM)
    return pl.pallas_call(
        functools.partial(prepare_kernel, owners, capacity),
        in_specs=[spec] * 5,
        out_specs=[spec] * 4,
        out_shape=[S(owner_row.shape, jnp.int32), S((owners, padded, 128), F32), S((rows, width), BF16),
                   S((2 * width // 128, 128, rows), BF16)],
        scratch_shapes=[pltpu.VMEM(owner_row.shape, jnp.int32)],
        compiler_params=pltpu.CompilerParams(vmem_limit_bytes=40 * 2**20),
    )(owner_row, block_values, inputs, cotangent, gain)


BY_ROWS = (((1,), (1,)), ((), ()))
BY_COLUMNS = (((0,), (0,)), ((), ()))


def mul(a, b):
    return jnp.dot(a, b, preferred_element_type=F32)


def mul_turned(a, b):
    return lax.dot_general(a, b, BY_ROWS, preferred_element_type=F32)


def mul_summed(a, b):
    return lax.dot_general(a, b, BY_COLUMNS, preferred_element_type=F32)


def turn(part, cosine, sine):
    return part * cosine + pltpu.roll(part, HEAD_DIM // 2, 1) * sine


def cost_of(microseconds):
    return pl.CostEstimate(flops=int(microseconds * 9e8), bytes_accessed=int(microseconds * 3e6), transcendentals=0)


def fetch_tile(full, slots, number, target, sem):
    pltpu.make_async_copy(full.at[slots[number]], target, sem).start()


def block_at(start, size):
    return pl.ds(pl.multiple_of(start, size), size)


def project_kernel(side, slots, full, normed, cosine, sine, queries, pair, weights, sems):
    wide = normed.shape[1] // side
    heads = queries.shape[1] // side

    def fetch(n, _):
        j, i = n // wide, n % wide
        number = jnp.where(j < heads, i * heads + j, wide * j + i)
        fetch_tile(full, slots, number, weights.at[block_at(i * side, side), block_at(j * side, side)], sems.at[j // 2])
        return 0

    lax.fori_loop(0, wide * (heads + 2), fetch, 0, unroll=8)
    for c in range((heads + 2) // 2):
        view = weights.at[:, pl.ds(c * 2 * side, 2 * side)]
        pltpu.make_async_copy(view, view, sems.at[c]).wait()
        product = mul(normed[...], view[...])
        for k in range(2):
            part = product[:, k * side : (k + 1) * side]
            if c < heads // 2:
                queries[:, (2 * c + k) * side : (2 * c + k + 1) * side] = turn(part, cosine[...], sine[...]).astype(BF16)
            elif k == 0:
                pair[:, :side] = turn(part, cosine[...], sine[...]).astype(BF16)
            else:
                pair[:, side:] = part.astype(BF16)


def project_heads(slots, full, normed, cosine, sine):
    rows, width = normed.shape
    side = full.shape[1]
    V = pltpu.VMEM
    spec = pl.BlockSpec(memory_space=V)
    return pl.pallas_call(
        functools.partial(project_kernel, side),
        grid_spec=pltpu.PrefetchScalarGridSpec(
            num_scalar_prefetch=1,
            grid=(),
            in_specs=[pl.BlockSpec(memory_space=pl.ANY), spec, spec, spec],
            out_specs=[spec, spec],
            scratch_shapes=[V((width, (HEADS + 2) * side), BF16), pltpu.SemaphoreType.DMA(((HEADS + 2) // 2,))],
        ),
        out_shape=[jax.ShapeDtypeStruct((rows, HEADS * side), BF16), jax.ShapeDtypeStruct((rows, 2 * side), BF16)],
        cost_estimate=cost_of(6),
        compiler_params=pltpu.CompilerParams(vmem_limit_bytes=40 * 2**20),
    )(slots, full, normed, cosine, sine)


def pairs_kernel(pair, pairs, keep_sem, sends, recvs):
    replica = lax.axis_index("replica")
    member = lax.axis_index("fsdp")
    count = pairs.shape[0]
    barrier = pltpu.get_barrier_semaphore()
    others = [(member + step) % count for step in range(1, count)]
    for other in others:
        pl.semaphore_signal(barrier, inc=1, device_id=(replica, other), device_id_type=MESH)
    pl.semaphore_wait(barrier, count - 1)
    keep = pltpu.make_async_copy(pair, pairs.at[member], keep_sem)
    keep.start()

    def copy(step, owner):
        return pltpu.make_async_remote_copy(
            src_ref=pair, dst_ref=pairs.at[owner], send_sem=sends.at[step], recv_sem=recvs.at[step],
            device_id=(replica, (member + step) % count), device_id_type=MESH)

    for step in range(1, count):
        copy(step, member).start()
    for step in range(1, count):
        copy(step, (member + count - step) % count).wait_recv()
    for step in range(1, count):
        copy(step, member).wait_send()
    keep.wait()


def gather_pairs(pair, count):
    D = pltpu.SemaphoreType.DMA
    spec = pl.BlockSpec(memory_space=pltpu.VMEM)
    return pl.pallas_call(
        pairs_kernel,
        out_shape=jax.ShapeDtypeStruct((count,) + pair.shape, pair.dtype),
        in_specs=[spec],
        out_specs=spec,
        scratch_shapes=[D, D((count,)), D((count,))],
        cost_estimate=cost_of(13),
        compiler_params=pltpu.CompilerParams(collective_id=2, has_side_effects=True),
    )(pair)


def fill_bias(first, own_ids, all_ids, bias):
    shape = bias.shape
    distance = first + lax.broadcasted_iota(jnp.int32, shape, 0) - lax.broadcasted_iota(jnp.int32, shape, 1)
    allowed = (own_ids[...] == all_ids[...]) & (distance >= 0) & (distance < WINDOW)
    bias[...] = jnp.where(allowed, 0.0, -1e30)


def softmax_of(scores):
    exponent = jnp.exp(scores - jnp.max(scores, -1, keepdims=True))
    return exponent / jnp.sum(exponent, -1, keepdims=True)


def attend_kernel(side, slots, first, full, queries, pairs, own_ids, all_ids, inputs, gain,
                  attended_turned, normed_two, normed_two_turned, middle, weights, attended, bias, sems):
    heads = attended.shape[1] // side
    wide = middle.shape[1] // side

    def fetch(n, _):
        j, i = n // heads, n % heads
        number = (heads + 2) * wide + i * wide + j
        fetch_tile(full, slots, number, weights.at[block_at(i * side, side), block_at(j * side, side)], sems.at[j // 2])
        return 0

    lax.fori_loop(0, wide * heads, fetch, 0, unroll=8)
    fill_bias(first[0], own_ids, all_ids, bias)
    keys = pairs[:, :, :side].reshape(-1, side)
    values = pairs[:, :, side:].reshape(-1, side)
    scale = HEAD_DIM ** (-0.5)
    for head in range(heads):
        at = slice(head * side, (head + 1) * side)
        scores = mul_turned(queries[:, at], keys) * scale + bias[...]
        product = mul(softmax_of(scores).astype(BF16), values)
        attended[:, at] = product.astype(BF16)
        attended_turned[head] = product.T.astype(BF16)
    total = jnp.zeros((inputs.shape[0], 1), F32)
    for c in range(wide // 2):
        view = weights.at[:, pl.ds(c * 2 * side, 2 * side)]
        pltpu.make_async_copy(view, view, sems.at[c]).wait()
        at = slice(c * 2 * side, (c + 1) * 2 * side)
        part = inputs[:, at].astype(F32) + mul(attended[...], view[...])
        middle[:, at] = part
        total = total + jnp.sum(part * part, -1, keepdims=True)
    scaled = lax.rsqrt(total / middle.shape[1] + EPSILON)
    for c in range(wide):
        at = slice(c * side, (c + 1) * side)
        part = middle[:, at] * scaled * gain[:, at]
        normed_two[:, at] = part.astype(BF16)
        normed_two_turned[c] = part.T.astype(BF16)


def attend(slots, first, full, queries, pairs, own_ids, all_ids, inputs, gain):
    rows, width = inputs.shape
    side = full.shape[1]
    V = pltpu.VMEM
    spec = pl.BlockSpec(memory_space=V)
    S = jax.ShapeDtypeStruct
    return pl.pallas_call(
        functools.partial(attend_kernel, side),
        grid_spec=pltpu.PrefetchScalarGridSpec(
            num_scalar_prefetch=2,
            grid=(),
            in_specs=[pl.BlockSpec(memory_space=pl.ANY)] + [spec] * 6,
            out_specs=[spec] * 4,
            scratch_shapes=[V((HEADS * side, width), BF16), V((rows, HEADS * side), BF16),
                            V((rows, pairs.shape[0] * pairs.shape[1]), F32), pltpu.SemaphoreType.DMA((width // side // 2,))],
        ),
        out_shape=[S((HEADS, side, rows), BF16), S((rows, width), BF16), S((width // side, side, rows), BF16), S((rows, width), F32)],
        cost_estimate=cost_of(11),
        compiler_params=pltpu.CompilerParams(vmem_limit_bytes=40 * 2**20),
    )(slots, first, full, queries, pairs, own_ids, all_ids, inputs, gain)


def norm_back(values, gain, grads):
    mean_square = jnp.mean(values * values, -1, keepdims=True)
    scaled = lax.rsqrt(mean_square + EPSILON)
    weighed = grads * gain
    inner = jnp.mean(weighed * values, -1, keepdims=True)
    back = scaled * weighed - values * (scaled * scaled * scaled * inner)
    return back, jnp.sum(grads * values * scaled, 0, keepdims=True)


GELU_SCALE = 0.7978845608028654
GELU_CUBE = 0.044715


def mlp_kernel(side, ring, span, slots, full, normed_own, normed_beside, cotangent_own, cotangent_beside, middle, gain,
               hidden_turned, gate_grad, up_grad, outputs, grad_middle, branch, branch_blocks, gain_term,
               normed, cotangent, forward, backward, gate_ring, up_ring, down_ring, sems):
    rows, width = normed_own.shape
    wide = width // side
    hidden_blocks = hidden_turned.shape[0]
    steps = hidden_blocks // span
    heads = HEADS
    base = (heads + 2) * wide + heads * wide

    def pieces_of(j, slot):
        todo = []
        for i in range(wide):
            for k in range(span):
                column = span * j + k
                row, lane = pl.ds(i * side, side), pl.ds(k * side, side)
                todo.append((base + i * hidden_blocks + column, gate_ring.at[slot, row, lane]))
                todo.append((base + (wide + i) * hidden_blocks + column, up_ring.at[slot, row, lane]))
                todo.append((base + 2 * wide * hidden_blocks + column * wide + i, down_ring.at[slot, lane, row]))
        return todo

    def start(todo, slot, first, last):
        for number, target in todo[first:last]:
            fetch_tile(full, slots, number, target, sems.at[slot])

    def arrived(slot):
        for target in (gate_ring, up_ring, down_ring):
            view = target.at[slot]
            pltpu.make_async_copy(view, view, sems.at[slot]).wait()

    for j in range(ring - 1):
        todo = pieces_of(j, j)
        start(todo, j, 0, len(todo))
    normed[:rows] = normed_own[...]
    cotangent[:rows] = cotangent_own[...]
    for c in range(wide):
        at = slice(c * side, (c + 1) * side)
        normed[rows:, at] = normed_beside[c].astype(F32).T.astype(BF16)
        cotangent[rows:, at] = cotangent_beside[wide + c]
    forward[...] = jnp.zeros_like(forward)
    backward[...] = jnp.zeros_like(backward)

    def step(j, _):
        slot = j % ring
        arrived(slot)
        later = (j + ring - 1) % ring
        todo = pieces_of(jnp.minimum(j + ring - 1, steps - 1), later)
        sixth = len(todo) // 6
        start(todo, later, 0, sixth)
        gate = mul(normed[...], gate_ring[slot])
        start(todo, later, sixth, 2 * sixth)
        up = mul(normed[...], up_ring[slot])
        start(todo, later, 2 * sixth, 3 * sixth)
        grad_hidden = mul_turned(cotangent[...], down_ring[slot])
        start(todo, later, 3 * sixth, 4 * sixth)
        square = gate * gate
        bend = jnp.tanh(GELU_SCALE * gate * (1.0 + GELU_CUBE * square))
        share = 0.5 * (1.0 + bend)
        active = gate * share
        slope = share + 0.5 * gate * (1.0 - bend * bend) * (GELU_SCALE * (1.0 + 3.0 * GELU_CUBE * square))
        hidden_wide = active * up
        hidden = hidden_wide.astype(BF16)
        gate_low = (grad_hidden * up * slope).astype(BF16)
        up_low = (grad_hidden * active).astype(BF16)
        for k in range(span):
            at = slice(k * side, (k + 1) * side)
            hidden_turned[span * j + k] = hidden_wide[:, at].T.astype(BF16)
            gate_grad[span * j + k] = gate_low[:, at]
            up_grad[span * j + k] = up_low[:, at]
        forward[...] += mul(hidden[:rows], down_ring[slot])
        start(todo, later, 4 * sixth, 5 * sixth)
        start(todo, later, 5 * sixth, 6 * sixth)
        backward[...] += mul_turned(gate_low[:rows], gate_ring[slot]) + mul_turned(up_low[:rows], up_ring[slot])
        return 0

    lax.fori_loop(0, steps, step, 0)
    for j in range(steps, steps + ring - 1):
        arrived(j % ring)
    outputs[...] = (middle[...] + forward[...]).astype(BF16)
    back, term = norm_back(middle[...], gain[...], backward[...])
    gain_term[...] = term
    total = cotangent_own[...].astype(F32) + back
    grad_middle[...] = total
    low = total.astype(BF16)
    branch[...] = low
    for c in range(wide):
        branch_blocks[c] = low[:, c * side : (c + 1) * side]


def mlp(slots, full, normed_own, normed_beside, cotangent_own, cotangent_beside, middle, gain, ring=3, span=4):
    rows, width = normed_own.shape
    side = full.shape[1]
    blocks = FF // side
    V = pltpu.VMEM
    spec = pl.BlockSpec(memory_space=V)
    S = jax.ShapeDtypeStruct
    return pl.pallas_call(
        functools.partial(mlp_kernel, side, ring, span),
        grid_spec=pltpu.PrefetchScalarGridSpec(
            num_scalar_prefetch=1,
            grid=(),
            in_specs=[pl.BlockSpec(memory_space=pl.ANY)] + [spec] * 6,
            out_specs=[spec] * 8,
            scratch_shapes=[V((2 * rows, width), BF16), V((2 * rows, width), BF16), V((rows, width), F32), V((rows, width), F32),
                            V((ring, width, span * side), BF16), V((ring, width, span * side), BF16), V((ring, span * side, width), BF16),
                            pltpu.SemaphoreType.DMA((ring,))],
        ),
        out_shape=[S((blocks, side, 2 * rows), BF16), S((blocks, 2 * rows, side), BF16), S((blocks, 2 * rows, side), BF16),
                   S((rows, width), BF16), S((rows, width), F32), S((rows, width), BF16), S((width // side, rows, side), BF16),
                   S((1, width), F32)],
        cost_estimate=cost_of(37),
        compiler_params=pltpu.CompilerParams(vmem_limit_bytes=56 * 2**20),
    )(slots, full, normed_own, normed_beside, cotangent_own, cotangent_beside, middle, gain)


def attend_back_kernel(side, slots, first, full, branch, queries, pairs, own_ids, all_ids, cosine, sine,
                       query_grad, pair_grad, own_pair_grad, weights, attended_grad, bias, key_total, value_total, sems):
    rows = branch.shape[0]
    heads = queries.shape[1] // side
    wide = branch.shape[1] // side

    def fetch(n, _):
        i, j = n // wide, n % wide
        number = (heads + 2) * wide + i * wide + j
        fetch_tile(full, slots, number, weights.at[block_at(i * side, side), block_at(j * side, side)], sems.at[i // 2])
        return 0

    lax.fori_loop(0, wide * heads, fetch, 0, unroll=8)
    fill_bias(first[0], own_ids, all_ids, bias)
    keys = pairs[:, :, :side].reshape(-1, side)
    values = pairs[:, :, side:].reshape(-1, side)
    scale = HEAD_DIM ** (-0.5)
    for c in range(heads // 2):
        view = weights.at[pl.ds(c * 2 * side, 2 * side), :]
        pltpu.make_async_copy(view, view, sems.at[c]).wait()
        attended_grad[:, c * 2 * side : (c + 1) * 2 * side] = mul_turned(branch[...], view[...]).astype(BF16)
    key_total[...] = jnp.zeros_like(key_total)
    value_total[...] = jnp.zeros_like(value_total)
    for head in range(heads):
        at = slice(head * side, (head + 1) * side)
        scores = mul_turned(queries[:, at], keys) * scale + bias[...]
        share = softmax_of(scores)
        share_grad = mul_turned(attended_grad[:, at], values)
        inner = jnp.sum(share * share_grad, -1, keepdims=True)
        score_grad = (share * (share_grad - inner)).astype(BF16)
        query_grad[head] = turn(mul(score_grad, keys) * scale, cosine[...], -sine[...]).astype(BF16)
        key_total[...] += mul_summed(score_grad, queries[:, at])
        value_total[...] += mul_summed(share.astype(BF16), attended_grad[:, at])
    key_total[...] = key_total[...] * scale
    for b in range(pairs.shape[0]):
        at = slice(b * rows, (b + 1) * rows)
        pair_grad[b, :, :side] = key_total[at].astype(BF16)
        pair_grad[b, :, side:] = value_total[at].astype(BF16)
    own = block_at(first[0], rows)
    own_pair_grad[:, :side] = key_total[own, :]
    own_pair_grad[:, side:] = value_total[own, :]


def attend_back(slots, first, full, branch, queries, pairs, own_ids, all_ids, cosine, sine):
    rows, width = branch.shape
    side = full.shape[1]
    key_rows = pairs.shape[0] * pairs.shape[1]
    V = pltpu.VMEM
    spec = pl.BlockSpec(memory_space=V)
    S = jax.ShapeDtypeStruct
    return pl.pallas_call(
        functools.partial(attend_back_kernel, side),
        grid_spec=pltpu.PrefetchScalarGridSpec(
            num_scalar_prefetch=2,
            grid=(),
            in_specs=[pl.BlockSpec(memory_space=pl.ANY)] + [spec] * 7,
            out_specs=[spec] * 3,
            scratch_shapes=[V((HEADS * side, width), BF16), V((rows, HEADS * side), BF16), V((rows, key_rows), F32),
                            V((key_rows, side), F32), V((key_rows, side), F32), pltpu.SemaphoreType.DMA((HEADS // 2,))],
        ),
        out_shape=[S((HEADS, rows, side), BF16), S(pairs.shape, BF16), S((rows, 2 * side), F32)],
        cost_estimate=cost_of(15),
        compiler_params=pltpu.CompilerParams(vmem_limit_bytes=40 * 2**20),
    )(slots, first, full, branch, queries, pairs, own_ids, all_ids, cosine, sine)


def pairs_back_kernel(pair_grad, own_grad, query_grad, branch, cosine, sine, low, query_beside, query_twin, query_far,
                      branch_beside, branch_twin, branch_far, arrived, sends, recvs, unit_sends, unit_recvs):
    replica = lax.axis_index("replica")
    member = lax.axis_index("fsdp")
    beside = ((1 - replica // 2) * 2 + replica % 2, member)
    twin = (replica // 2 * 2 + 1 - replica % 2, member)
    count = pair_grad.shape[0]
    side = cosine.shape[1]
    barrier = pltpu.get_barrier_semaphore()
    for device in [(replica, (member + step) % count) for step in range(1, count)] + [beside, twin]:
        pl.semaphore_signal(barrier, inc=1, device_id=device, device_id_type=MESH)
    pl.semaphore_wait(barrier, count + 1)

    def copy(step):
        target = (member + step) % count
        return pltpu.make_async_remote_copy(
            src_ref=pair_grad.at[target], dst_ref=arrived.at[step], send_sem=sends.at[step], recv_sem=recvs.at[step],
            device_id=(replica, target), device_id_type=MESH)

    def unit_copy(n, source, target, device):
        return pltpu.make_async_remote_copy(
            src_ref=source, dst_ref=target, send_sem=unit_sends.at[n], recv_sem=unit_recvs.at[n],
            device_id=device, device_id_type=MESH)

    moves = []
    for n, (own, from_beside, from_twin, from_far) in enumerate(
            [(branch, branch_beside, branch_twin, branch_far), (query_grad, query_beside, query_twin, query_far)]):
        moves.append((unit_copy(3 * n, own, from_beside, beside), unit_copy(3 * n + 1, own, from_twin, twin),
                      unit_copy(3 * n + 2, from_beside, from_far, twin)))
    for step in range(1, count):
        copy(step).start()
    for to_beside, to_twin, pass_on in moves:
        to_beside.start()
        to_twin.start()
    total = own_grad[...]
    for step in range(1, count):
        copy(step).wait_recv()
        total = total + arrived[step].astype(F32)
    low[0] = turn(total[:, :side], cosine[...], -sine[...]).astype(BF16)
    low[1] = total[:, side:].astype(BF16)
    for step in range(1, count):
        copy(step).wait_send()
    for to_beside, to_twin, pass_on in moves:
        to_beside.wait_recv()
        pass_on.start()
    for to_beside, to_twin, pass_on in moves:
        to_beside.wait_send()
        to_twin.wait()
        pass_on.wait()


def pairs_back(pair_grad, own_grad, query_grad, branch, cosine, sine):
    count, rows, double = pair_grad.shape
    D = pltpu.SemaphoreType.DMA
    S = jax.ShapeDtypeStruct
    spec = pl.BlockSpec(memory_space=pltpu.VMEM)
    return pl.pallas_call(
        pairs_back_kernel,
        out_shape=[S((2, rows, double // 2), BF16)] + [S(query_grad.shape, BF16)] * 3 + [S(branch.shape, BF16)] * 3,
        in_specs=[spec] * 6,
        out_specs=[spec] * 7,
        scratch_shapes=[pltpu.VMEM(pair_grad.shape, BF16), D((count,)), D((count,)), D((6,)), D((6,))],
        cost_estimate=cost_of(16),
        compiler_params=pltpu.CompilerParams(collective_id=3, has_side_effects=True),
    )(pair_grad, own_grad, query_grad, branch, cosine, sine)


def input_back_kernel(side, slots, full, query_grad, pair_grad, inputs, grad_middle, gain,
                      input_grad, gain_term, weights, joined, backward, sems):
    wide = inputs.shape[1] // side
    heads = query_grad.shape[0]

    def fetch(n, _):
        i, j = n // (heads + 2), n % (heads + 2)
        number = jnp.where(j < heads, i * heads + j, wide * j + i)
        fetch_tile(full, slots, number, weights.at[block_at(i * side, side), block_at(j * side, side)], sems.at[i // 2])
        return 0

    lax.fori_loop(0, wide * (heads + 2), fetch, 0, unroll=8)
    for h in range(heads):
        joined[:, h * side : (h + 1) * side] = query_grad[h]
    for k in range(2):
        joined[:, (heads + k) * side : (heads + k + 1) * side] = pair_grad[k]
    for c in range(wide // 2):
        view = weights.at[pl.ds(c * 2 * side, 2 * side), :]
        pltpu.make_async_copy(view, view, sems.at[c]).wait()
        backward[:, c * 2 * side : (c + 1) * 2 * side] = mul_turned(joined[...], view[...])
    back, term = norm_back(inputs[...].astype(F32), gain[...], backward[...])
    gain_term[...] = term
    input_grad[...] = (grad_middle[...] + back).astype(BF16)


def input_back(slots, full, query_grad, pair_grad, inputs, grad_middle, gain):
    rows, width = inputs.shape
    side = full.shape[1]
    V = pltpu.VMEM
    spec = pl.BlockSpec(memory_space=V)
    S = jax.ShapeDtypeStruct
    return pl.pallas_call(
        functools.partial(input_back_kernel, side),
        grid_spec=pltpu.PrefetchScalarGridSpec(
            num_scalar_prefetch=1,
            grid=(),
            in_specs=[pl.BlockSpec(memory_space=pl.ANY)] + [spec] * 5,
            out_specs=[spec] * 2,
            scratch_shapes=[V((width, (HEADS + 2) * side), BF16), V((rows, (HEADS + 2) * side), BF16), V((rows, width), F32),
                            pltpu.SemaphoreType.DMA((width // side // 2,))],
        ),
        out_shape=[S((rows, width), BF16), S((1, width), F32)],
        cost_estimate=cost_of(8),
        compiler_params=pltpu.CompilerParams(vmem_limit_bytes=40 * 2**20),
    )(slots, full, query_grad, pair_grad, inputs, grad_middle, gain)


def reduce_kernel(chunk, places, left_at, right_at, gain_part, *refs):
    count = len(places)
    given = 1 + max(place[0] for place in places)
    sources, refs = refs[:given], refs[given:]
    (out, gain_out, left_all, right_all, x_out, x_in, z_out, z_in, z_mix, turned_out, turned_in, turned_mix, total, gain_sum, gain_in, keep_sem, gain_s, gain_r,
     x_s, x_r, z_s, z_r, ty_s, ty_r, tc_s, tc_r, tf_s, tf_r, done_sem) = refs
    quarter = x_out.shape[1]
    pieces = quarter // chunk
    replica = lax.axis_index("replica")
    member = lax.axis_index("fsdp")
    y, core = replica // 2, replica % 2
    z, x = member // 2, member % 2
    across, beside, twin = (replica, z * 2 + 1 - x), ((1 - y) * 2 + core, member), (y * 2 + 1 - core, member)
    beside_replica, twin_replica, far_replica = (1 - y) * 2 + core, y * 2 + 1 - core, (1 - y) * 2 + 1 - core
    def level(step):
        return (z + step) % 4
    def depth_device(step):
        return (replica, level(step) * 2 + x)
    def keep(n):
        at, is_left, block, source_block, number, lane = places[n]
        source = sources[at].at[pl.ds(source_block, number)]
        if is_left:
            target = left_all.at[pl.ds(block, number), :, pl.ds(lane, sources[at].shape[2])]
        else:
            target = right_all.at[pl.ds(block, number), pl.ds(lane, sources[at].shape[1]), :]
        return pltpu.make_async_copy(source, target, keep_sem.at[n])
    for n in range(count):
        keep(n).start()
    left_all[left_all.shape[0] - 1] = jnp.zeros(left_all.shape[1:], left_all.dtype)
    gain_sum[...] = gain_part[...]

    barrier = pltpu.get_barrier_semaphore()
    for device in [across, beside, twin] + [depth_device(step) for step in (1, 2, 3)]:
        pl.semaphore_signal(barrier, inc=1, device_id=device, device_id_type=MESH)
    pl.semaphore_wait(barrier, 6)

    def remote(source, target, send, recv, device):
        return pltpu.make_async_remote_copy(src_ref=source, dst_ref=target, send_sem=send, recv_sem=recv, device_id=device, device_id_type=MESH)

    def gain_copy(stage, device):
        return remote(gain_sum, gain_in.at[stage], gain_s.at[stage], gain_r.at[stage], device)
    def gain_pair(stage, device):
        gain_copy(stage, device).wait()
        gain_sum[...] = gain_sum[...] + gain_in[stage]
    def gain_z(step):
        return remote(gain_sum, gain_in.at[2 + step], gain_s.at[2 + step], gain_r.at[2 + step], depth_device(step))
    def gain_finish():
        for step in (1, 2, 3):
            gain_z(step).wait()
        gain_in[0] = gain_sum[...]
        added = jnp.zeros(gain_sum.shape, F32)
        for zb in range(4):
            step = (zb - z + 4) % 4
            added = added + gain_in[jnp.where(step == 0, 0, 2 + step)]
        gain_out[...] = added
    gain_copy(0, beside).start()
    for n in range(count):
        keep(n).wait()

    def tile(owner, at):
        rank = replica * quarter + at
        return jnp.dot(left_all[left_at[owner, rank]], right_all[right_at[owner, rank]], preferred_element_type=F32)

    paired = z + 1 - 2 * (z % 2)
    levels = [z, paired, 3 - z, 3 - paired]
    middle = (z == 1) | (z == 2)
    order = (2, 3, 1, 0)
    def turned(k):
        return k % 6 == 2
    def at_level(lev):
        return (replica, lev * 2 + x)
    def x_copy(zb, k):
        at = pl.ds(k * chunk, chunk)
        return remote(x_out.at[zb, at], x_in.at[zb, at], x_s.at[zb, k], x_r.at[zb, k], across)
    def buffers(column, k):
        if column == 0:
            return z_out, z_in, z_mix, k * chunk
        return turned_out, turned_in, turned_mix, k // 6 * chunk
    def z_send(column, block, place, kind, device, k):
        out_buffer, in_buffer, mix_buffer, base = buffers(column, k)
        at = pl.ds(base, chunk)
        target = in_buffer.at[place, at] if kind < 2 else mix_buffer.at[place, at]
        return remote(out_buffer.at[block, at], target, z_s.at[column, block, k], z_r.at[column, kind, k], device)
    def pass_paired(column, k):
        z_send(column, 1, 0, 0, at_level(levels[1]), k).start()
    def pass_end(column, block, k):
        z_send(column, block, 3 - block, 5 - block, at_level(levels[1]), k).start()
    def pass_middle(column, block, k):
        z_send(column, block, 1, 1, at_level(levels[block]), k).start()
    def z_arrival(column, place, kind, k):
        z_send(column, 1, place, kind, at_level(levels[1]), k).wait_recv()
    def leave(column, block, k):
        if block == 1:
            pass_paired(column, k)
        elif block > 1:
            pl.when(jnp.logical_not(middle))(lambda: pass_end(column, block, k))
    def combine(column, k):
        @pl.when(middle)
        def _():
            out_buffer, in_buffer, mix_buffer, base = buffers(column, k)
            for place in (0, 1):
                z_arrival(column, place, 2 + place, k)
                def one(t, _):
                    at = base + t
                    out_buffer[2 + place, at] = (out_buffer[2 + place, at].astype(F32) + mix_buffer[place, at].astype(F32)).astype(BF16)
                    return 0
                lax.fori_loop(0, chunk, one, 0)
                pass_middle(column, 2 + place, k)
    def z_total(column, k, t):
        out_buffer, in_buffer, mix_buffer, base = buffers(column, k)
        at = base + t
        return out_buffer[0, at].astype(F32) + in_buffer[0, at].astype(F32) + in_buffer[1, at].astype(F32)
    def total_at(who, k):
        return total.at[pl.ds(who * quarter + k * chunk, chunk)]
    def t_beside(k):
        return remote(total_at(replica, k), total_at(replica, k), ty_s.at[k], ty_r.at[k], beside)
    def t_twin(k):
        return remote(total_at(replica, k), total_at(replica, k), tc_s.at[k], tc_r.at[k], twin)
    def t_pass(k):
        return remote(total_at(beside_replica, k), total_at(beside_replica, k), tf_s.at[k], tf_r.at[k], twin)
    def come_beside(k):
        return remote(total_at(replica, k), total_at(beside_replica, k), ty_s.at[k], ty_r.at[k], beside)
    def come_twin(k):
        return remote(total_at(replica, k), total_at(twin_replica, k), tc_s.at[k], tc_r.at[k], twin)
    def come_far(k):
        return remote(total_at(replica, k), total_at(far_replica, k), tf_s.at[k], tf_r.at[k], twin)

    def send_x(k):
        for block in order:
            lev = levels[block]
            def one(t, _):
                at = k * chunk + t
                x_out[lev, at] = tile(lev * 2 + 1 - x, at).astype(BF16)
                return 0
            lax.fori_loop(0, chunk, one, 0)
            x_copy(lev, k).start()

    def collect(k):
        for block in order:
            lev = levels[block]
            x_copy(lev, k).wait_recv()
            def one(t, _):
                at = k * chunk + t
                z_out[block, at] = (tile(lev * 2 + x, at) + x_in[lev, at].astype(F32)).astype(BF16)
                return 0
            lax.fori_loop(0, chunk, one, 0)
            leave(0, block, k)

    def turned_send(k):
        for block in order:
            for column in (0, 1):
                owner = levels[block] * 2 + (x if column == 0 else 1 - x)
                out_buffer, in_buffer, mix_buffer, base = buffers(column, k)
                def one(t, _):
                    out_buffer[block, base + t] = tile(owner, k * chunk + t).astype(BF16)
                    return 0
                lax.fori_loop(0, chunk, one, 0)
                leave(column, block, k)

    def turned_cross(k):
        for column in (0, 1):
            for place in (0, 1):
                z_arrival(column, place, place, k)
        def one(t, _):
            x_out[0, k * chunk + t] = z_total(1, k, t).astype(BF16)
            return 0
        lax.fori_loop(0, chunk, one, 0)
        x_copy(0, k).start()

    def finish(k):
        @pl.when(turned(k))
        def _():
            x_copy(0, k).wait_recv()
            def one(t, _):
                at = k * chunk + t
                total[replica * quarter + at] = (z_total(0, k, t) + x_in[0, at].astype(F32)).astype(BF16)
                return 0
            lax.fori_loop(0, chunk, one, 0)
        @pl.when(jnp.logical_not(turned(k)))
        def _():
            for place in (0, 1):
                z_arrival(0, place, place, k)
            def one(t, _):
                total[replica * quarter + k * chunk + t] = z_total(0, k, t).astype(BF16)
                return 0
            lax.fori_loop(0, chunk, one, 0)
        t_beside(k).start()
        t_twin(k).start()

    def spread(k):
        come_beside(k).wait_recv()
        t_pass(k).start()

    def beat(n, _):
        def due(behind, kind):
            k = n - behind
            here = (k >= 0) & (k < pieces)
            return here & (turned(k) if kind else jnp.logical_not(turned(k)))
        pl.when(due(0, True))(lambda: turned_send(n))
        pl.when(due(0, False))(lambda: send_x(n))
        @pl.when(due(1, True))
        def _():
            combine(0, n - 1)
            combine(1, n - 1)
        pl.when(due(2, False))(lambda: collect(n - 2))
        pl.when(due(3, False))(lambda: combine(0, n - 3))
        pl.when(due(3, True))(lambda: turned_cross(n - 3))
        pl.when((n >= 5) & (n < pieces + 5))(lambda: finish(n - 5))
        pl.when(n >= 7)(lambda: spread(n - 7))

        @pl.when(n == 2)
        def _():
            gain_pair(0, beside)
            gain_copy(1, twin).start()

        @pl.when(n == 4)
        def _():
            gain_pair(1, twin)
            gain_copy(2, across).start()

        @pl.when(n == 6)
        def _():
            gain_pair(2, across)
            for step in (1, 2, 3):
                gain_z(step).start()

        @pl.when(n == 9)
        def _():
            gain_finish()
        return 0
    lax.fori_loop(0, pieces + 7, beat, 0)

    def drain(k, _):
        come_twin(k).wait_recv()
        come_far(k).wait_recv()
        t_beside(k).wait_send()
        t_twin(k).wait_send()
        t_pass(k).wait_send()
        x_copy(0, k).wait_send()
        for block in (1, 2, 3):
            z_send(0, block, 0, 0, at_level(levels[1]), k).wait_send()
        @pl.when(turned(k))
        def _():
            for block in (1, 2, 3):
                z_send(1, block, 0, 0, at_level(levels[1]), k).wait_send()
        @pl.when(jnp.logical_not(turned(k)))
        def _():
            for zb in (1, 2, 3):
                x_copy(zb, k).wait_send()
        return 0
    lax.fori_loop(0, pieces, drain, 0)
    result = pltpu.make_async_copy(total, out, done_sem)
    result.start()
    result.wait()

def reduce_tiles(left_at, right_at, gain_part, parts, places, left_total, right_total, rows, chunk=3):
    capacity = left_at.shape[1]
    quarter = capacity // 4
    pieces = quarter // chunk
    side = parts[0].shape[1]
    D = pltpu.SemaphoreType.DMA
    V = pltpu.VMEM
    S = jax.ShapeDtypeStruct
    spec = pl.BlockSpec(memory_space=V)
    held = V((4, quarter, side, side), BF16)
    arriving = V((2, quarter, side, side), BF16)
    seldom = (pieces + 3) // 6 * chunk
    return pl.pallas_call(
        functools.partial(reduce_kernel, chunk, places),
        out_shape=[S((capacity, side, side), BF16), S(gain_part.shape, F32)],
        in_specs=[pl.BlockSpec(memory_space=pltpu.SMEM)] * 2 + [spec] + [pl.BlockSpec(memory_space=pl.ANY)] * len(parts),
        out_specs=[pl.BlockSpec(memory_space=pl.ANY), spec],
        scratch_shapes=[
            V((left_total + 1, side, rows), BF16), V((right_total, rows, side), BF16), held, held, held, arriving, arriving,
            V((4, seldom, side, side), BF16), V((2, seldom, side, side), BF16), V((2, seldom, side, side), BF16),
            V((capacity, side, side), BF16), V(gain_part.shape, F32), V((6,) + gain_part.shape, F32),
            D((len(places),)), D((6,)), D((6,))] + [D((4, pieces))] * 2 + [D((2, 4, pieces))] * 2 + [D((pieces,))] * 6 + [D],
        compiler_params=pltpu.CompilerParams(collective_id=1, has_side_effects=True, vmem_limit_bytes=62 * 2**20),
    )(left_at, right_at, gain_part, *parts)


def shampoo_kernel(count, grads, left_old, right_old, left_root, right_root, master, grads_out, left_new, right_new, master_new, low_new):
    side = grads.shape[1]
    flips, boths = [], []
    for at in range(count):
        wide = grads[at].astype(F32)
        grads_out[at] = wide
        flips.append(wide.T.astype(BF16))
    for at in range(count):
        both = jnp.dot(grads[at], jnp.concatenate([flips[at], right_root[at].astype(BF16)], 1), preferred_element_type=F32)
        left_new[at] = STAT_DECAY * left_old[at] + (1.0 - STAT_DECAY) * both[:, :side]
        boths.append(both[:, side:].astype(BF16))
    for at in range(count):
        right_new[at] = STAT_DECAY * right_old[at] + (1.0 - STAT_DECAY) * jnp.dot(flips[at], grads[at], preferred_element_type=F32)
    for at in range(count):
        turned = jnp.dot(left_root[at].astype(BF16), boths[at], preferred_element_type=F32)
        fresh = master[at] - STEP_RATE * turned
        master_new[at] = fresh
        low_new[at] = fresh.astype(BF16)

def shampoo(grads, left_old, right_old, left_root, right_root, master, count=17):
    capacity, side = master.shape[0], master.shape[1]
    while capacity % count:
        count -= 1
    spec = pl.BlockSpec((count, side, side), lambda i: (i, 0, 0))
    wide = jax.ShapeDtypeStruct(master.shape, F32)
    return pl.pallas_call(
        functools.partial(shampoo_kernel, count),
        grid=(capacity // count,),
        in_specs=[spec] * 6,
        out_specs=[spec] * 5,
        out_shape=[wide, wide, wide, wide, jax.ShapeDtypeStruct(master.shape, BF16)],
        compiler_params=pltpu.CompilerParams(vmem_limit_bytes=60 * 2**20),
    )(grads, left_old, right_old, left_root, right_root, master)


def shifted(block, axis, distance):
    devices = range(lax.axis_size(axis))
    route = [(i - distance, i) for i in devices if i - distance in devices]
    return lax.ppermute(block, axis, route)


def normalize(values, gain_row):
    mean_square = jnp.mean(values * values, -1, keepdims=True)
    return values * lax.rsqrt(mean_square + EPSILON) * gain_row


def rotate(values, angles):
    half_dim = values.shape[-1] // 2
    cosine = jnp.cos(angles)[:, None, :]
    sine_part = jnp.sin(angles)[:, None, :]
    first_half = values[..., :half_dim]
    second = values[..., half_dim:]
    return jnp.concatenate(
        [first_half * cosine - second * sine_part, second * cosine + first_half * sine_part], -1
    )


def angles_of(positions):
    half_dim = HEAD_DIM // 2
    inverse = 10000.0 ** (-2.0 * jnp.arange(half_dim, dtype=jnp.float32) / HEAD_DIM)
    return positions[:, None] * inverse[None, :]


def slot_of_tiles(owner_table, owners, capacity):
    onehot = (owner_table[:, None] == jnp.arange(owners, dtype=jnp.int32)[None, :]).astype(
        jnp.int32
    )
    earlier = jnp.cumsum(onehot, 0) - onehot
    ranking = jnp.sum(earlier * onehot, 1)
    return owner_table * capacity + ranking


def matrix_layout(width, head_width, head_dim, hidden_width, tile_side):
    left_attended = width // tile_side
    left_second = left_attended + head_width // tile_side
    left_hidden = left_second + width // tile_side
    right_key = head_width // tile_side
    right_value = right_key + head_dim // tile_side
    right_branch = right_value + head_dim // tile_side
    right_gate = right_branch + width // tile_side
    right_up = right_gate + hidden_width // tile_side
    right_down = right_up + hidden_width // tile_side
    return [
        (width, head_width, 0, 0),
        (width, head_dim, 0, right_key),
        (width, head_dim, 0, right_value),
        (head_width, width, left_attended, right_branch),
        (width, hidden_width, left_second, right_gate),
        (width, hidden_width, left_second, right_up),
        (hidden_width, width, left_hidden, right_down),
    ]


def project(values, blocks):
    row_count = values.shape[0]
    result = jnp.einsum(
        "nar,abrc->nbc",
        values.reshape(row_count, blocks.shape[0], blocks.shape[2]),
        blocks,
        preferred_element_type=jnp.float32,
    )
    return result.reshape(row_count, blocks.shape[1] * blocks.shape[3])


def back_project(values, blocks):
    row_count = values.shape[0]
    result = jnp.einsum(
        "nbc,abrc->nar",
        values.reshape(row_count, blocks.shape[1], blocks.shape[3]),
        blocks,
        preferred_element_type=jnp.float32,
    )
    return result.reshape(row_count, blocks.shape[0] * blocks.shape[2])


def dense_tile_grads(layout, left_blocks, right_blocks, tile_side):
    pieces = []
    for row_total, column_total, left_base, right_base in layout:
        left_part = left_blocks[:, left_base : left_base + row_total // tile_side]
        right_part = right_blocks[:, right_base : right_base + column_total // tile_side]
        product = jnp.einsum(
            "nar,nbc->abrc", left_part, right_part, preferred_element_type=jnp.float32
        )
        pieces.append(product.reshape(-1, tile_side, tile_side))
    pieces.append(jnp.zeros((1, tile_side, tile_side), jnp.float32))
    return jnp.concatenate(pieces, 0)


def block_tables(layout, tile_side, left_total):
    left_of, right_of = [], []
    for row_total, column_total, left_base, right_base in layout:
        for i in range(row_total // tile_side):
            for j in range(column_total // tile_side):
                left_of.append(left_base + i)
                right_of.append(right_base + j)
    return np.array(left_of + [left_total], np.int32), np.array(right_of + [0], np.int32)


def body_anywhere(
    inputs,
    cotangent,
    segment_ids,
    gains,
    owner_table,
    master_tiles,
    left_stats,
    right_stats,
    left_roots,
    right_roots,
):
    owners = lax.axis_size("fsdp")
    replicas = lax.axis_size("replica")
    member = lax.axis_index("fsdp")
    capacity = master_tiles.shape[0]
    tile_side = master_tiles.shape[1]
    row_count = inputs.shape[0]
    width = inputs.shape[1]
    head_width = HEADS * HEAD_DIM
    tile_total = owner_table.shape[0]
    layout = matrix_layout(width, head_width, HEAD_DIM, FF, tile_side)
    slots = slot_of_tiles(owner_table, owners, capacity)
    slot_tile = (
        jnp.full((owners * capacity,), tile_total, jnp.int32)
        .at[slots]
        .set(jnp.arange(tile_total, dtype=jnp.int32))
    )
    full = lax.all_gather(master_tiles.astype(jnp.bfloat16), "fsdp", axis=0, tiled=True)
    all_tiles = jnp.take(full, slots, axis=0)
    weights = []
    offset = 0
    for row_total, column_total, left_base, right_base in layout:
        number = row_total // tile_side * (column_total // tile_side)
        weights.append(
            all_tiles[offset : offset + number].reshape(
                row_total // tile_side, column_total // tile_side, tile_side, tile_side
            )
        )
        offset = offset + number
    w_query, w_key, w_value, w_out, w_gate, w_up, w_down = weights
    base_row = member * row_count
    own_ids = lax.dynamic_slice_in_dim(segment_ids, base_row, row_count, 0)
    starts = jnp.sum((segment_ids[None, :] < own_ids[:, None]).astype(jnp.int32), 1)
    positions = (base_row + jnp.arange(row_count, dtype=jnp.int32) - starts).astype(jnp.float32)
    angles = angles_of(positions)
    inputs_wide = inputs.astype(jnp.float32)
    normed = normalize(inputs_wide, gains[0]).astype(jnp.bfloat16)
    query_pre = project(normed, w_query)
    key_pre = project(normed, w_key)
    values_own = project(normed, w_value).astype(jnp.bfloat16)
    queries = rotate(query_pre.reshape(row_count, HEADS, HEAD_DIM), angles).astype(jnp.bfloat16)
    keys_own = rotate(key_pre[:, None, :], angles)[:, 0, :].astype(jnp.bfloat16)
    reach = WINDOW // row_count
    own_pair = jnp.concatenate([keys_own, values_own], 1)
    received = [shifted(own_pair, "fsdp", distance_back) for distance_back in range(reach, 0, -1)]
    pair_rows = jnp.concatenate(received + [own_pair], 0)
    key_rows = pair_rows[:, :HEAD_DIM]
    value_rows = pair_rows[:, HEAD_DIM:]
    padded_ids = jnp.concatenate([jnp.full((reach * row_count,), -1, jnp.int32), segment_ids], 0)
    key_ids = lax.dynamic_slice_in_dim(padded_ids, base_row, (reach + 1) * row_count, 0)
    distance = (
        jnp.arange(row_count, dtype=jnp.int32)[:, None]
        + reach * row_count
        - jnp.arange((reach + 1) * row_count, dtype=jnp.int32)[None, :]
    )
    allowed = (own_ids[:, None] == key_ids[None, :]) & (distance >= 0) & (distance < WINDOW)
    score_scale = HEAD_DIM ** (-0.5)
    scores = (
        jnp.einsum("nhd,kd->hnk", queries, key_rows, preferred_element_type=jnp.float32)
        * score_scale
    )
    scores = jnp.where(allowed[None], scores, -1e30)
    row_peak = jnp.max(scores, -1, keepdims=True)
    exponent = jnp.exp(scores - row_peak)
    row_total_sum = jnp.sum(exponent, -1, keepdims=True)
    probability = (exponent / row_total_sum).astype(jnp.bfloat16)
    log_total = row_peak + jnp.log(row_total_sum)
    attended = (
        jnp.einsum("hnk,kd->nhd", probability, value_rows, preferred_element_type=jnp.float32)
        .reshape(row_count, head_width)
        .astype(jnp.bfloat16)
    )
    middle = inputs_wide + project(attended, w_out)
    normed_two = normalize(middle, gains[1]).astype(jnp.bfloat16)
    gate = project(normed_two, w_gate)
    up_part = project(normed_two, w_up)

    def geglu(gate_values, up_values):
        return jax.nn.gelu(gate_values, approximate=True) * up_values

    hidden_wide, geglu_back = jax.vjp(geglu, gate, up_part)
    hidden = hidden_wide.astype(jnp.bfloat16)
    outputs = (middle + project(hidden, w_down)).astype(jnp.bfloat16)
    grad_hidden = back_project(cotangent, w_down)
    gate_back, up_back = geglu_back(grad_hidden)
    gate_grad = gate_back.astype(jnp.bfloat16)
    up_grad = up_back.astype(jnp.bfloat16)
    grad_normed_two = back_project(gate_grad, w_gate) + back_project(up_grad, w_up)
    middle_back, norm_two_back = jax.vjp(normalize, middle, gains[1])[1](grad_normed_two)
    grad_middle = cotangent.astype(jnp.float32) + middle_back
    branch_grad = grad_middle.astype(jnp.bfloat16)
    grad_attended = (
        back_project(branch_grad, w_out).astype(jnp.bfloat16).reshape(row_count, HEADS, HEAD_DIM)
    )
    scores_again = (
        jnp.einsum("nhd,kd->hnk", queries, key_rows, preferred_element_type=jnp.float32)
        * score_scale
    )
    scores_again = jnp.where(allowed[None], scores_again, -1e30)
    exact_prob = jnp.exp(scores_again - log_total)
    grad_prob = jnp.einsum(
        "nhd,kd->hnk", grad_attended, value_rows, preferred_element_type=jnp.float32
    )
    grad_scores = (
        exact_prob * (grad_prob - jnp.sum(exact_prob * grad_prob, -1, keepdims=True))
    ).astype(jnp.bfloat16)
    grad_queries = (
        jnp.einsum("hnk,kd->nhd", grad_scores, key_rows, preferred_element_type=jnp.float32)
        * score_scale
    )
    grad_keys = (
        jnp.einsum("hnk,nhd->kd", grad_scores, queries, preferred_element_type=jnp.float32)
        * score_scale
    )
    grad_values = jnp.einsum(
        "hnk,nhd->kd", probability, grad_attended, preferred_element_type=jnp.float32
    )
    grad_pairs = jnp.concatenate([grad_keys, grad_values], 1)
    own_grad = grad_pairs[reach * row_count :]
    for distance_back in range(1, reach + 1):
        sent_rows = grad_pairs[
            (reach - distance_back) * row_count : (reach - distance_back + 1) * row_count
        ]
        own_grad = own_grad + shifted(
            sent_rows.astype(jnp.bfloat16), "fsdp", -distance_back
        ).astype(sent_rows.dtype)
    grad_query_pre = (
        rotate(grad_queries, -angles).reshape(row_count, head_width).astype(jnp.bfloat16)
    )
    grad_key_pre = rotate(own_grad[:, None, :HEAD_DIM], -angles)[:, 0, :].astype(jnp.bfloat16)
    grad_values_low = own_grad[:, HEAD_DIM:].astype(jnp.bfloat16)
    grad_normed = (
        back_project(grad_query_pre, w_query)
        + back_project(grad_key_pre, w_key)
        + back_project(grad_values_low, w_value)
    )
    inputs_back, norm_one_back = jax.vjp(normalize, inputs_wide, gains[0])[1](grad_normed)
    input_grad = (grad_middle + inputs_back).astype(jnp.bfloat16)
    gain_grads = lax.psum(jnp.stack([norm_one_back, norm_two_back]), ("replica", "fsdp"))
    gain_rate = GAIN_STEP * (row_count * owners * replicas) ** (-0.5)
    new_gains = gains - gain_rate * gain_grads
    left_parts = jnp.concatenate([normed, attended, normed_two, hidden], 1)
    right_parts = jnp.concatenate(
        [grad_query_pre, grad_key_pre, grad_values_low, branch_grad, gate_grad, up_grad, cotangent],
        1,
    )
    left_blocks = left_parts.reshape(row_count, -1, tile_side)
    right_blocks = right_parts.reshape(row_count, -1, tile_side)
    dense = dense_tile_grads(layout, left_blocks, right_blocks, tile_side)
    partial_sum = lax.psum_scatter(
        jnp.take(dense, slot_tile, axis=0), "fsdp", scatter_dimension=0, tiled=True
    )
    grads_low = lax.psum(partial_sum.astype(jnp.bfloat16), "replica")
    grads_all, left_all, right_all, master_all, low_all = shampoo(
        grads_low, left_stats, right_stats, left_roots, right_roots, master_tiles
    )
    return (
        outputs,
        input_grad,
        gain_grads,
        new_gains,
        grads_all,
        master_all,
        low_all,
        left_all,
        right_all,
    )


def body_of_units(
    inputs,
    cotangent,
    segment_ids,
    gains,
    owner_table,
    master_tiles,
    left_stats,
    right_stats,
    left_roots,
    right_roots,
):
    owners, replicas = 8, 4
    member = lax.axis_index("fsdp")
    capacity = master_tiles.shape[0]
    side = master_tiles.shape[1]
    rows, width = inputs.shape
    tile_total = owner_table.shape[0]
    layout = matrix_layout(width, HEADS * HEAD_DIM, HEAD_DIM, FF, side)
    left_of, right_of = block_tables(layout, side, 0)
    padded = -(-tile_total // 128) * 128
    block_values = np.zeros((padded, 128), np.float32)
    block_values[:tile_total, 0] = left_of[:-1] + 1
    block_values[:tile_total, 1] = right_of[:-1] + 1
    left_total, right_total = int(max(left_of)) + 1, int(max(right_of)) + 1
    owner_row = jnp.pad(owner_table, (0, padded - tile_total), constant_values=-1).reshape(1, padded)

    slots, blocks_at, normed, early = prepare(
        owners, capacity, owner_row, jnp.asarray(block_values, BF16), inputs, cotangent, gains[0:1]
    )
    slots = slots.reshape(padded)
    chosen = blocks_at[:, :capacity, :2].astype(jnp.int32) - 1
    left_at = jnp.where(chosen[..., 0] < 0, left_total, chosen[..., 0])
    right_at = jnp.maximum(chosen[..., 1], 0)
    base_row = member * rows
    own_ids = lax.dynamic_slice_in_dim(segment_ids, base_row, rows, 0)
    starts = jnp.sum((segment_ids[None, :] < own_ids[:, None]).astype(jnp.int32), 1)
    positions = (base_row + jnp.arange(rows, dtype=jnp.int32) - starts).astype(jnp.float32)
    angles = angles_of(positions)
    cosine, sine = jnp.cos(angles), jnp.sin(angles)
    cosine = jnp.concatenate([cosine, cosine], 1)
    sine = jnp.concatenate([-sine, sine], 1)
    first = base_row.astype(jnp.int32).reshape(1)
    own_column, all_row = own_ids.reshape(-1, 1), segment_ids.reshape(1, -1)

    def over_y(part):
        return lax.ppermute(part, "replica", [(0, 2), (1, 3), (2, 0), (3, 1)])

    def over_core(part):
        return lax.ppermute(part, "replica", [(0, 1), (1, 0), (2, 3), (3, 2)])

    def unit_of(part):
        beside = over_y(part)
        return [part, beside, over_core(part), over_core(beside)]

    early_unit = unit_of(early)
    full = gather(master_tiles).reshape(owners * capacity, side, side)
    queries, pair = project_heads(slots, full, normed, cosine, sine)
    pairs = gather_pairs(pair, owners)
    attended_turned, normed_two, normed_two_turned, middle = attend(
        slots, first, full, queries, pairs, own_column, all_row, inputs, gains[1:2]
    )
    two_unit = unit_of(normed_two_turned)
    attended_turned, _ = lax.optimization_barrier((attended_turned, two_unit[1]))
    attended_unit = unit_of(attended_turned)
    wide = width // side
    hidden, gate_grad, up_grad, outputs, grad_middle, branch, branch_blocks, term_two = mlp(
        slots, full, normed_two, two_unit[1], cotangent, early_unit[1], middle, gains[1:2]
    )
    hidden_far, gate_far, up_far = over_core(hidden), over_core(gate_grad), over_core(up_grad)
    query_grad, pair_grad, own_pair_grad = attend_back(
        slots, first, full, branch, queries, pairs, own_column, all_row, cosine, sine
    )
    pair_low, *others = pairs_back(pair_grad, own_pair_grad, query_grad, branch_blocks, cosine, sine)
    query_unit = [query_grad] + others[:3]
    branch_unit = [branch_blocks] + others[3:]
    pair_unit = unit_of(pair_low)
    input_grad, term_one = input_back(slots, full, query_grad, pair_low, inputs, grad_middle, gains[0:1])

    parts, places = [], []

    def place(unit, *spots):
        for n, part in enumerate(unit):
            for is_left, block, source_block, count in spots:
                places.append((len(parts), is_left, block, source_block, count, n * rows * (4 // len(unit))))
            parts.append(part)

    blocks = FF // side
    place(early_unit, (True, 0, 0, wide), (False, HEADS + 2 + wide + 2 * blocks, wide, wide))
    place(attended_unit, (True, wide, 0, HEADS))
    place(two_unit, (True, wide + HEADS, 0, wide))
    place([hidden, hidden_far], (True, 2 * wide + HEADS, 0, blocks))
    place(query_unit, (False, 0, 0, HEADS))
    place(pair_unit, (False, HEADS, 0, 2))
    place(branch_unit, (False, HEADS + 2, 0, wide))
    place([gate_grad, gate_far], (False, HEADS + 2 + wide, 0, blocks))
    place([up_grad, up_far], (False, HEADS + 2 + wide + blocks, 0, blocks))
    gain_part = jnp.concatenate([term_one, term_two, jnp.zeros((6, width), F32)], 0)
    grads_low, gain_sum = reduce_tiles(
        left_at, right_at, gain_part, parts, tuple(places), left_total, right_total, replicas * rows
    )
    gain_grads = gain_sum[:2]
    gain_rate = GAIN_STEP * (rows * owners * replicas) ** (-0.5)
    grads_all, left_all, right_all, master_all, low_all = shampoo(
        grads_low, left_stats, right_stats, left_roots, right_roots, master_tiles
    )
    return (
        outputs,
        input_grad,
        gain_grads,
        gains - gain_rate * gain_grads,
        grads_all,
        master_all,
        low_all,
        left_all,
        right_all,
    )


def solution(mesh):
    units = mesh.shape["replica"] == 4 and mesh.shape["fsdp"] == 8
    return jax.shard_map(
        body_of_units if units else body_anywhere,
        mesh=mesh,
        in_specs=(
            P(("replica", "fsdp"), None),
            P(("replica", "fsdp"), None),
            P("replica"),
            P(),
            P(),
            P("fsdp", None, None),
            P("fsdp", None, None),
            P("fsdp", None, None),
            P("fsdp", None, None),
            P("fsdp", None, None),
        ),
        out_specs=(
            P(("replica", "fsdp"), None),
            P(("replica", "fsdp"), None),
            P(),
            P(),
            P("fsdp", None, None),
            P("fsdp", None, None),
            P("fsdp", None, None),
            P("fsdp", None, None),
            P("fsdp", None, None),
        ),
        check_vma=False,
    )
```

```python
import functools

import jax
import jax.numpy as jnp
import numpy as np
from jax import lax
from jax.experimental import pallas as pl
from jax.experimental.pallas import tpu as pltpu
from jax.sharding import PartitionSpec as P

HEADS = 12
HEAD_DIM = 128
FF = 4608
WINDOW = 1024


EPSILON = 1e-06
STEP_RATE = 0.02
STAT_DECAY = 0.5
GAIN_STEP = 0.1
F32, BF16 = jnp.float32, jnp.bfloat16
MESH = pl.DeviceIdType.MESH


def gather_kernel(chunk, whole, deep_most, early, patience, master, full, stage, low, stage_sem, keep_sem,
                  up_s, up_r, down_s, down_r, x_s, x_r, eu_s, eu_r, ed_s, ed_r, y_s, y_r, core_s, core_r):
    replica = lax.axis_index("replica")
    member = lax.axis_index("fsdp")
    y, core = replica // 2, replica % 2
    z, x = member // 2, member % 2
    deep = deep_most - core
    run = whole - deep
    half = whole * chunk
    mirrored = z // 2
    inner = z + mirrored * (3 - 2 * z)
    above, below = (replica, (z + 1) * 2 + x), (replica, (z - 1) * 2 + x)
    across, beside, twin = (replica, z * 2 + 1 - x), ((1 - y) * 2 + core, member), (y * 2 + 1 - core, member)

    def rows(chunk_at, owner_core):
        return pl.ds(owner_core * half + chunk_at * chunk, chunk)

    def load(c, part):
        return pltpu.make_async_copy(master.at[rows(c, part)], stage.at[pl.ds(c * chunk, chunk)], stage_sem.at[c])

    def cast(c, part):
        load(c, part).wait()
        low[rows(c, part)] = stage[pl.ds(c * chunk, chunk)].astype(BF16)

    def place(k, plane):
        return plane * (whole - 1) + k * (1 - 2 * plane)

    def load_first(k, _):
        load(place(k, y), core).start()
        return 0

    lax.fori_loop(0, whole, load_first, 0)
    barrier = pltpu.get_barrier_semaphore()

    def greet(device):
        pl.semaphore_signal(barrier, inc=1, device_id=device, device_id_type=MESH)

    pl.when(z < 3)(lambda: greet(above))
    pl.when(z > 0)(lambda: greet(below))
    greet(across)
    greet(beside)
    greet(twin)

    @pl.when((z == 0) | (z == 3))
    def _():
        pl.semaphore_wait(barrier, 4)

    @pl.when((z > 0) & (z < 3))
    def _():
        pl.semaphore_wait(barrier, 5)

    def copy(owner, chunk_at, send, recv, device, from_own=False, owner_core=None):
        at = rows(chunk_at, core if owner_core is None else owner_core)
        target = full.at[owner, at]
        source = low.at[at] if from_own else target
        return pltpu.make_async_remote_copy(src_ref=source, dst_ref=target, send_sem=send, recv_sem=recv, device_id=device, device_id_type=MESH)

    def go_up(zb, k, own=False):
        return copy(zb * 2 + x, place(k, y), up_s.at[zb, k], up_r.at[zb, k], above, own)

    def go_down(zb, k, own=False):
        return copy(zb * 2 + x, place(k, y), down_s.at[zb, k], down_r.at[zb, k], below, own)

    def early_up(zb, k):
        return copy(zb * 2 + 1 - x, place(k, y), eu_s.at[zb, k], eu_r.at[zb, k], above)

    def early_down(zb, k):
        return copy(zb * 2 + 1 - x, place(k, y), ed_s.at[zb, k], ed_r.at[zb, k], below)

    def go_x(zb, k, own=False):
        return copy(zb * 2 + x, place(k, y), x_s.at[zb, k], x_r.at[zb, k], across, own)

    def come_x(zb, k):
        return copy(zb * 2 + 1 - x, place(k, y), x_s.at[zb, k], x_r.at[zb, k], across)

    def go_y(owner, k):
        return copy(owner, place(k, y), y_s.at[owner, k], y_r.at[owner, k], beside)

    def come_y(owner, k):
        return copy(owner, place(k, 1 - y), y_s.at[owner, k], y_r.at[owner, k], beside)

    def go_core(owner, at):
        return copy(owner, at, core_s.at[owner, at], core_r.at[owner, at], twin)

    def onward(owner, k):
        go_core(owner, place(k, y)).start()
        pl.when(k < deep)(lambda: go_y(owner, k).start())

    def across_block(g):
        b = g if g >= 2 else (g + inner) % 2
        return b + mirrored * (3 - 2 * b)

    def group(g):
        def tick(k, _):
            if g == 0:
                cast(place(k, y), core)
                pl.when(z < 3)(lambda: go_up(z, k, True).start())
                pl.when(z > 0)(lambda: go_down(z, k, True).start())
                go_x(z, k, True).start()
            if 1 <= g <= 3:
                @pl.when(z - g >= 0)
                def _():
                    go_up(z - g, k).wait_recv()
                    pl.when(z < 3)(lambda: go_up(z - g, k).start())
                    onward((z - g) * 2 + x, k)

                @pl.when(z + g <= 3)
                def _():
                    go_down(z + g, k).wait_recv()
                    pl.when(z > 0)(lambda: go_down(z + g, k).start())
                    onward((z + g) * 2 + x, k)

                pl.when(k >= early)(lambda: go_x(across_block(g), k).start())
            if g == 1:
                come_x(z, k).wait_recv()
                onward(z * 2 + 1 - x, k)

                @pl.when(k < early)
                def _():
                    pl.when(z < 3)(lambda: early_up(z, k).start())
                    pl.when(z > 0)(lambda: early_down(z, k).start())

            if 2 <= g <= 4:
                @pl.when(k >= early)
                def _():
                    come_x(across_block(g - 1), k).wait_recv()
                    onward(across_block(g - 1) * 2 + 1 - x, k)

                @pl.when((k < early) & (z - (g - 1) >= 0))
                def _():
                    zb = z - (g - 1)
                    early_up(zb, k).wait_recv()
                    pl.when(z < 3)(lambda: early_up(zb, k).start())
                    onward(zb * 2 + 1 - x, k)

                @pl.when((k < early) & (z + (g - 1) <= 3))
                def _():
                    zb = z + (g - 1)
                    early_down(zb, k).wait_recv()
                    pl.when(z > 0)(lambda: early_down(zb, k).start())
                    onward(zb * 2 + 1 - x, k)
            h = g - patience
            if 1 <= h <= 4:
                def take(owner):
                    come_y(owner, k).wait_recv()
                    go_core(owner, place(k, 1 - y)).start()

                if h <= 3:
                    pl.when((k < deep) & (z - h >= 0))(lambda: take((z - h) * 2 + x))
                    pl.when((k < deep) & (z + h <= 3))(lambda: take((z + h) * 2 + x))
                if h == 1:
                    pl.when(k < deep)(lambda: take(z * 2 + 1 - x))
                else:
                    pl.when((k < deep) & (k >= early))(lambda: take(across_block(h - 1) * 2 + 1 - x))
                    pl.when((k < early) & (z - (h - 1) >= 0))(lambda: take((z - (h - 1)) * 2 + 1 - x))
                    pl.when((k < early) & (z + (h - 1) <= 3))(lambda: take((z + (h - 1)) * 2 + 1 - x))
            return 0

        lax.fori_loop(0, run, tick, 0)

    group(0)

    def rest(k, _):
        cast(place(k, y), core)
        return 0

    lax.fori_loop(run, whole, rest, 0)

    def load_other(c, _):
        load(c, 1 - core).start()
        return 0

    lax.fori_loop(0, whole, load_other, 0)

    def cast_other(c, _):
        cast(c, 1 - core)
        return 0

    group(1)
    lax.fori_loop(0, whole, cast_other, 0)
    keep = pltpu.make_async_copy(low, full.at[member], keep_sem)
    keep.start()
    for g in range(2, 5 + patience):
        group(g)

    def drain_z(zb, _):
        def one(k, _):
            pl.when((zb <= z) & (z < 3))(lambda: go_up(zb, k).wait_send())
            pl.when((zb >= z) & (z > 0))(lambda: go_down(zb, k).wait_send())
            pl.when((zb == z) | (k >= early))(lambda: go_x(zb, k).wait_send())
            pl.when((k < early) & (zb <= z) & (z < 3))(lambda: early_up(zb, k).wait_send())
            pl.when((k < early) & (zb >= z) & (z > 0))(lambda: early_down(zb, k).wait_send())
            return 0

        lax.fori_loop(0, run, one, 0)
        return 0

    lax.fori_loop(0, 4, drain_z, 0)

    def drain_owner(owner, _):
        @pl.when(owner != member)
        def _():
            def one_y(k, _):
                go_y(owner, k).wait_send()
                return 0

            lax.fori_loop(0, deep, one_y, 0)

            def one_core(k, _):
                go_core(owner, k).wait_send()
                copy(owner, k, core_s.at[owner, k], core_r.at[owner, k], twin, owner_core=1 - core).wait_recv()
                return 0

            lax.fori_loop(0, whole, one_core, 0)

        return 0

    lax.fori_loop(0, 8, drain_owner, 0)
    keep.wait()


def gather(master, chunk=6, deep=6, early=1, patience=1):
    capacity = master.shape[0]
    whole = capacity // 2 // chunk
    run = whole - deep + 1
    D = pltpu.SemaphoreType.DMA
    V = pltpu.VMEM
    return pl.pallas_call(
        functools.partial(gather_kernel, chunk, whole, deep, early, patience),
        out_shape=jax.ShapeDtypeStruct((8,) + master.shape, BF16),
        in_specs=[pl.BlockSpec(memory_space=pl.ANY)],
        out_specs=pl.BlockSpec(memory_space=pl.ANY),
        scratch_shapes=[V((capacity // 2,) + master.shape[1:], F32), V(master.shape, BF16), D((whole,)), D]
        + [D((4, run))] * 6 + [D((4, max(early, 1)))] * 4 + [D((8, deep))] * 2 + [D((8, whole))] * 2,
        compiler_params=pltpu.CompilerParams(collective_id=0, has_side_effects=True, vmem_limit_bytes=60 * 2**20),
    )(master)


def prepare_kernel(owners, capacity, owner_row, block_values, inputs, cotangent, gain, slots, blocks_at, normed, early, ranks):
    total = owner_row.shape[1]
    lanes = 128
    owner = owner_row[...]
    same = (owner == lax.broadcasted_iota(jnp.int32, (owners, total), 0)).astype(F32)
    ones_before = (lax.broadcasted_iota(jnp.int32, (lanes, lanes), 0) < lax.broadcasted_iota(jnp.int32, (lanes, lanes), 1)).astype(BF16)
    carry = jnp.zeros((owners, 1), F32)
    for c in range(total // lanes):
        at = slice(c * lanes, (c + 1) * lanes)
        piece = same[:, at]
        before = jnp.dot(piece.astype(BF16), ones_before, preferred_element_type=F32) + carry
        ranks[:, at] = jnp.sum(before * piece, 0, keepdims=True).astype(jnp.int32)
        carry = carry + jnp.sum(piece, 1, keepdims=True)
    slot = jnp.where(owner >= 0, owner * capacity + ranks[...], -1)
    slots[...] = slot
    padded = blocks_at.shape[1]
    for o in range(owners):
        here = lax.broadcasted_iota(jnp.int32, (padded, total), 0)
        here = jnp.where(here < capacity, here + o * capacity, -2)
        hit = jnp.where(here == slot, 1.0, 0.0).astype(BF16)
        blocks_at[o] = jnp.dot(hit, block_values[...], preferred_element_type=F32)
    values = inputs[...].astype(F32)
    mean_square = jnp.mean(values * values, -1, keepdims=True)
    scaled = values * lax.rsqrt(mean_square + EPSILON) * gain[...]
    normed[...] = scaled.astype(BF16)
    count = early.shape[0] // 2
    for c in range(count):
        at = slice(c * lanes, (c + 1) * lanes)
        early[c] = scaled[:, at].T.astype(BF16)
        early[count + c] = cotangent[:, at]

def prepare(owners, capacity, owner_row, block_values, inputs, cotangent, gain):
    rows, width = inputs.shape
    padded = -(-capacity // 16) * 16
    S = jax.ShapeDtypeStruct
    spec = pl.BlockSpec(memory_space=pltpu.VMEM)
    return pl.pallas_call(
        functools.partial(prepare_kernel, owners, capacity),
        in_specs=[spec] * 5,
        out_specs=[spec] * 4,
        out_shape=[S(owner_row.shape, jnp.int32), S((owners, padded, 128), F32), S((rows, width), BF16),
                   S((2 * width // 128, 128, rows), BF16)],
        scratch_shapes=[pltpu.VMEM(owner_row.shape, jnp.int32)],
        compiler_params=pltpu.CompilerParams(vmem_limit_bytes=40 * 2**20),
    )(owner_row, block_values, inputs, cotangent, gain)


BY_ROWS = (((1,), (1,)), ((), ()))
BY_COLUMNS = (((0,), (0,)), ((), ()))


def mul(a, b):
    return jnp.dot(a, b, preferred_element_type=F32)


def mul_turned(a, b):
    return lax.dot_general(a, b, BY_ROWS, preferred_element_type=F32)


def mul_summed(a, b):
    return lax.dot_general(a, b, BY_COLUMNS, preferred_element_type=F32)


def turn(part, cosine, sine):
    return part * cosine + pltpu.roll(part, HEAD_DIM // 2, 1) * sine


def cost_of(microseconds):
    return pl.CostEstimate(flops=int(microseconds * 9e8), bytes_accessed=int(microseconds * 3e6), transcendentals=0)


def fetch_tile(full, slots, number, target, sem):
    pltpu.make_async_copy(full.at[slots[number]], target, sem).start()


def block_at(start, size):
    return pl.ds(pl.multiple_of(start, size), size)


def project_kernel(side, slots, full, normed, cosine, sine, queries, pair, weights, sems):
    wide = normed.shape[1] // side
    heads = queries.shape[1] // side

    def fetch(n, _):
        j, i = n // wide, n % wide
        number = jnp.where(j < heads, i * heads + j, wide * j + i)
        fetch_tile(full, slots, number, weights.at[block_at(i * side, side), block_at(j * side, side)], sems.at[j // 2])
        return 0

    lax.fori_loop(0, wide * (heads + 2), fetch, 0, unroll=8)
    for c in range((heads + 2) // 2):
        view = weights.at[:, pl.ds(c * 2 * side, 2 * side)]
        pltpu.make_async_copy(view, view, sems.at[c]).wait()
        product = mul(normed[...], view[...])
        for k in range(2):
            part = product[:, k * side : (k + 1) * side]
            if c < heads // 2:
                queries[:, (2 * c + k) * side : (2 * c + k + 1) * side] = turn(part, cosine[...], sine[...]).astype(BF16)
            elif k == 0:
                pair[:, :side] = turn(part, cosine[...], sine[...]).astype(BF16)
            else:
                pair[:, side:] = part.astype(BF16)


def project_heads(slots, full, normed, cosine, sine):
    rows, width = normed.shape
    side = full.shape[1]
    V = pltpu.VMEM
    spec = pl.BlockSpec(memory_space=V)
    return pl.pallas_call(
        functools.partial(project_kernel, side),
        grid_spec=pltpu.PrefetchScalarGridSpec(
            num_scalar_prefetch=1,
            grid=(),
            in_specs=[pl.BlockSpec(memory_space=pl.ANY), spec, spec, spec],
            out_specs=[spec, spec],
            scratch_shapes=[V((width, (HEADS + 2) * side), BF16), pltpu.SemaphoreType.DMA(((HEADS + 2) // 2,))],
        ),
        out_shape=[jax.ShapeDtypeStruct((rows, HEADS * side), BF16), jax.ShapeDtypeStruct((rows, 2 * side), BF16)],
        cost_estimate=cost_of(6),
        compiler_params=pltpu.CompilerParams(vmem_limit_bytes=40 * 2**20),
    )(slots, full, normed, cosine, sine)


def pairs_kernel(pair, pairs, keep_sem, sends, recvs, x_sends, x_recvs):
    replica = lax.axis_index("replica")
    member = lax.axis_index("fsdp")
    levels = pairs.shape[0] // 2
    z, x = member // 2, member % 2
    across = (replica, z * 2 + 1 - x)

    def level_device(step):
        return (replica, (z + step) % levels * 2 + x)

    def owner_of(step, column):
        return (z + levels - step) % levels * 2 + column

    barrier = pltpu.get_barrier_semaphore()
    for device in [across] + [level_device(step) for step in range(1, levels)]:
        pl.semaphore_signal(barrier, inc=1, device_id=device, device_id_type=MESH)
    pl.semaphore_wait(barrier, levels)
    keep = pltpu.make_async_copy(pair, pairs.at[member], keep_sem)
    keep.start()

    def copy(source, owner, send, recv, device):
        return pltpu.make_async_remote_copy(
            src_ref=source, dst_ref=pairs.at[owner], send_sem=send, recv_sem=recv, device_id=device, device_id_type=MESH)

    def along_z(step, owner):
        return copy(pair, owner, sends.at[step], recvs.at[step], level_device(step))

    def over_x(step, column):
        owner = owner_of(step, column)
        return copy(pair if step == 0 else pairs.at[owner], owner, x_sends.at[step], x_recvs.at[step], across)

    for step in range(1, levels):
        along_z(step, member).start()
    over_x(0, x).start()
    for step in range(1, levels):
        along_z(step, owner_of(step, x)).wait_recv()
        over_x(step, x).start()
    for step in range(levels):
        over_x(step, 1 - x).wait_recv()
    for step in range(1, levels):
        along_z(step, member).wait_send()
    for step in range(levels):
        over_x(step, x).wait_send()
    keep.wait()


def gather_pairs(pair, count):
    D = pltpu.SemaphoreType.DMA
    spec = pl.BlockSpec(memory_space=pltpu.VMEM)
    return pl.pallas_call(
        pairs_kernel,
        out_shape=jax.ShapeDtypeStruct((count,) + pair.shape, pair.dtype),
        in_specs=[spec],
        out_specs=spec,
        scratch_shapes=[D] + [D((count // 2,))] * 4,
        cost_estimate=cost_of(13),
        compiler_params=pltpu.CompilerParams(collective_id=2, has_side_effects=True),
    )(pair)


def fill_bias(first, own_ids, all_ids, bias):
    shape = bias.shape
    distance = first + lax.broadcasted_iota(jnp.int32, shape, 0) - lax.broadcasted_iota(jnp.int32, shape, 1)
    allowed = (own_ids[...] == all_ids[...]) & (distance >= 0) & (distance < WINDOW)
    bias[...] = jnp.where(allowed, 0.0, -1e30)


def softmax_of(scores):
    exponent = jnp.exp(scores - jnp.max(scores, -1, keepdims=True))
    return exponent / jnp.sum(exponent, -1, keepdims=True)


def attend_kernel(side, slots, first, full, queries, pairs, own_ids, all_ids, inputs, gain,
                  attended_turned, normed_two, normed_two_turned, middle, weights, attended, bias, sems):
    heads = attended.shape[1] // side
    wide = middle.shape[1] // side

    def fetch(n, _):
        j, i = n // heads, n % heads
        number = (heads + 2) * wide + i * wide + j
        fetch_tile(full, slots, number, weights.at[block_at(i * side, side), block_at(j * side, side)], sems.at[j // 2])
        return 0

    lax.fori_loop(0, wide * heads, fetch, 0, unroll=8)
    fill_bias(first[0], own_ids, all_ids, bias)
    keys = pairs[:, :, :side].reshape(-1, side)
    values = pairs[:, :, side:].reshape(-1, side)
    scale = HEAD_DIM ** (-0.5)
    for head in range(heads):
        at = slice(head * side, (head + 1) * side)
        scores = mul_turned(queries[:, at], keys) * scale + bias[...]
        product = mul(softmax_of(scores).astype(BF16), values)
        attended[:, at] = product.astype(BF16)
        attended_turned[head] = product.T.astype(BF16)
    total = jnp.zeros((inputs.shape[0], 1), F32)
    for c in range(wide // 2):
        view = weights.at[:, pl.ds(c * 2 * side, 2 * side)]
        pltpu.make_async_copy(view, view, sems.at[c]).wait()
        at = slice(c * 2 * side, (c + 1) * 2 * side)
        part = inputs[:, at].astype(F32) + mul(attended[...], view[...])
        middle[:, at] = part
        total = total + jnp.sum(part * part, -1, keepdims=True)
    scaled = lax.rsqrt(total / middle.shape[1] + EPSILON)
    for c in range(wide):
        at = slice(c * side, (c + 1) * side)
        part = middle[:, at] * scaled * gain[:, at]
        normed_two[:, at] = part.astype(BF16)
        normed_two_turned[c] = part.T.astype(BF16)


def attend(slots, first, full, queries, pairs, own_ids, all_ids, inputs, gain):
    rows, width = inputs.shape
    side = full.shape[1]
    V = pltpu.VMEM
    spec = pl.BlockSpec(memory_space=V)
    S = jax.ShapeDtypeStruct
    return pl.pallas_call(
        functools.partial(attend_kernel, side),
        grid_spec=pltpu.PrefetchScalarGridSpec(
            num_scalar_prefetch=2,
            grid=(),
            in_specs=[pl.BlockSpec(memory_space=pl.ANY)] + [spec] * 6,
            out_specs=[spec] * 4,
            scratch_shapes=[V((HEADS * side, width), BF16), V((rows, HEADS * side), BF16),
                            V((rows, pairs.shape[0] * pairs.shape[1]), F32), pltpu.SemaphoreType.DMA((width // side // 2,))],
        ),
        out_shape=[S((HEADS, side, rows), BF16), S((rows, width), BF16), S((width // side, side, rows), BF16), S((rows, width), F32)],
        cost_estimate=cost_of(11),
        compiler_params=pltpu.CompilerParams(vmem_limit_bytes=40 * 2**20),
    )(slots, first, full, queries, pairs, own_ids, all_ids, inputs, gain)


def norm_back(values, gain, grads):
    mean_square = jnp.mean(values * values, -1, keepdims=True)
    scaled = lax.rsqrt(mean_square + EPSILON)
    weighed = grads * gain
    inner = jnp.mean(weighed * values, -1, keepdims=True)
    back = scaled * weighed - values * (scaled * scaled * scaled * inner)
    return back, jnp.sum(grads * values * scaled, 0, keepdims=True)


GELU_SCALE = 0.7978845608028654
GELU_CUBE = 0.044715


def mlp_kernel(side, ring, span, slots, full, normed_own, normed_beside, cotangent_own, cotangent_beside, middle, gain,
               hidden_turned, gate_grad, up_grad, outputs, grad_middle, branch, branch_blocks, gain_term,
               normed, cotangent, forward, backward, gate_ring, up_ring, down_ring, sems):
    rows, width = normed_own.shape
    wide = width // side
    hidden_blocks = hidden_turned.shape[0]
    steps = hidden_blocks // span
    heads = HEADS
    base = (heads + 2) * wide + heads * wide

    def pieces_of(j, slot):
        todo = []
        for i in range(wide):
            for k in range(span):
                column = span * j + k
                row, lane = pl.ds(i * side, side), pl.ds(k * side, side)
                todo.append((base + i * hidden_blocks + column, gate_ring.at[slot, row, lane]))
                todo.append((base + (wide + i) * hidden_blocks + column, up_ring.at[slot, row, lane]))
                todo.append((base + 2 * wide * hidden_blocks + column * wide + i, down_ring.at[slot, lane, row]))
        return todo

    def start(todo, slot, first, last):
        for number, target in todo[first:last]:
            fetch_tile(full, slots, number, target, sems.at[slot])

    def arrived(slot):
        for target in (gate_ring, up_ring, down_ring):
            view = target.at[slot]
            pltpu.make_async_copy(view, view, sems.at[slot]).wait()

    for j in range(ring - 1):
        todo = pieces_of(j, j)
        start(todo, j, 0, len(todo))
    normed[:rows] = normed_own[...]
    cotangent[:rows] = cotangent_own[...]
    for c in range(wide):
        at = slice(c * side, (c + 1) * side)
        normed[rows:, at] = normed_beside[c].astype(F32).T.astype(BF16)
        cotangent[rows:, at] = cotangent_beside[wide + c]
    forward[...] = jnp.zeros_like(forward)
    backward[...] = jnp.zeros_like(backward)

    def step(j, _):
        slot = j % ring
        arrived(slot)
        later = (j + ring - 1) % ring
        todo = pieces_of(jnp.minimum(j + ring - 1, steps - 1), later)
        sixth = len(todo) // 6
        start(todo, later, 0, sixth)
        gate = mul(normed[...], gate_ring[slot])
        start(todo, later, sixth, 2 * sixth)
        up = mul(normed[...], up_ring[slot])
        start(todo, later, 2 * sixth, 3 * sixth)
        grad_hidden = mul_turned(cotangent[...], down_ring[slot])
        start(todo, later, 3 * sixth, 4 * sixth)
        square = gate * gate
        bend = jnp.tanh(GELU_SCALE * gate * (1.0 + GELU_CUBE * square))
        share = 0.5 * (1.0 + bend)
        active = gate * share
        slope = share + 0.5 * gate * (1.0 - bend * bend) * (GELU_SCALE * (1.0 + 3.0 * GELU_CUBE * square))
        hidden_wide = active * up
        hidden = hidden_wide.astype(BF16)
        gate_low = (grad_hidden * up * slope).astype(BF16)
        up_low = (grad_hidden * active).astype(BF16)
        for k in range(span):
            at = slice(k * side, (k + 1) * side)
            hidden_turned[span * j + k] = hidden_wide[:, at].T.astype(BF16)
            gate_grad[span * j + k] = gate_low[:, at]
            up_grad[span * j + k] = up_low[:, at]
        forward[...] += mul(hidden[:rows], down_ring[slot])
        start(todo, later, 4 * sixth, 5 * sixth)
        start(todo, later, 5 * sixth, 6 * sixth)
        backward[...] += mul_turned(gate_low[:rows], gate_ring[slot]) + mul_turned(up_low[:rows], up_ring[slot])
        return 0

    lax.fori_loop(0, steps, step, 0)
    for j in range(steps, steps + ring - 1):
        arrived(j % ring)
    outputs[...] = (middle[...] + forward[...]).astype(BF16)
    back, term = norm_back(middle[...], gain[...], backward[...])
    gain_term[...] = term
    total = cotangent_own[...].astype(F32) + back
    grad_middle[...] = total
    low = total.astype(BF16)
    branch[...] = low
    for c in range(wide):
        branch_blocks[c] = low[:, c * side : (c + 1) * side]


def mlp(slots, full, normed_own, normed_beside, cotangent_own, cotangent_beside, middle, gain, ring=3, span=4):
    rows, width = normed_own.shape
    side = full.shape[1]
    blocks = FF // side
    V = pltpu.VMEM
    spec = pl.BlockSpec(memory_space=V)
    S = jax.ShapeDtypeStruct
    return pl.pallas_call(
        functools.partial(mlp_kernel, side, ring, span),
        grid_spec=pltpu.PrefetchScalarGridSpec(
            num_scalar_prefetch=1,
            grid=(),
            in_specs=[pl.BlockSpec(memory_space=pl.ANY)] + [spec] * 6,
            out_specs=[spec] * 8,
            scratch_shapes=[V((2 * rows, width), BF16), V((2 * rows, width), BF16), V((rows, width), F32), V((rows, width), F32),
                            V((ring, width, span * side), BF16), V((ring, width, span * side), BF16), V((ring, span * side, width), BF16),
                            pltpu.SemaphoreType.DMA((ring,))],
        ),
        out_shape=[S((blocks, side, 2 * rows), BF16), S((blocks, 2 * rows, side), BF16), S((blocks, 2 * rows, side), BF16),
                   S((rows, width), BF16), S((rows, width), F32), S((rows, width), BF16), S((width // side, rows, side), BF16),
                   S((1, width), F32)],
        cost_estimate=cost_of(37),
        compiler_params=pltpu.CompilerParams(vmem_limit_bytes=56 * 2**20),
    )(slots, full, normed_own, normed_beside, cotangent_own, cotangent_beside, middle, gain)


def attend_back_kernel(side, slots, first, full, branch, queries, pairs, own_ids, all_ids, cosine, sine,
                       query_grad, pair_grad, own_pair_grad, weights, attended_grad, bias, key_total, value_total, sems):
    rows = branch.shape[0]
    heads = queries.shape[1] // side
    wide = branch.shape[1] // side

    def fetch(n, _):
        i, j = n // wide, n % wide
        number = (heads + 2) * wide + i * wide + j
        fetch_tile(full, slots, number, weights.at[block_at(i * side, side), block_at(j * side, side)], sems.at[i // 2])
        return 0

    lax.fori_loop(0, wide * heads, fetch, 0, unroll=8)
    fill_bias(first[0], own_ids, all_ids, bias)
    keys = pairs[:, :, :side].reshape(-1, side)
    values = pairs[:, :, side:].reshape(-1, side)
    scale = HEAD_DIM ** (-0.5)
    for c in range(heads // 2):
        view = weights.at[pl.ds(c * 2 * side, 2 * side), :]
        pltpu.make_async_copy(view, view, sems.at[c]).wait()
        attended_grad[:, c * 2 * side : (c + 1) * 2 * side] = mul_turned(branch[...], view[...]).astype(BF16)
    key_total[...] = jnp.zeros_like(key_total)
    value_total[...] = jnp.zeros_like(value_total)
    for head in range(heads):
        at = slice(head * side, (head + 1) * side)
        scores = mul_turned(queries[:, at], keys) * scale + bias[...]
        share = softmax_of(scores)
        share_grad = mul_turned(attended_grad[:, at], values)
        inner = jnp.sum(share * share_grad, -1, keepdims=True)
        score_grad = (share * (share_grad - inner)).astype(BF16)
        query_grad[head] = turn(mul(score_grad, keys) * scale, cosine[...], -sine[...]).astype(BF16)
        key_total[...] += mul_summed(score_grad, queries[:, at])
        value_total[...] += mul_summed(share.astype(BF16), attended_grad[:, at])
    key_total[...] = key_total[...] * scale
    for b in range(pairs.shape[0]):
        at = slice(b * rows, (b + 1) * rows)
        pair_grad[b, :, :side] = key_total[at].astype(BF16)
        pair_grad[b, :, side:] = value_total[at].astype(BF16)
    own = block_at(first[0], rows)
    own_pair_grad[:, :side] = key_total[own, :]
    own_pair_grad[:, side:] = value_total[own, :]


def attend_back(slots, first, full, branch, queries, pairs, own_ids, all_ids, cosine, sine):
    rows, width = branch.shape
    side = full.shape[1]
    key_rows = pairs.shape[0] * pairs.shape[1]
    V = pltpu.VMEM
    spec = pl.BlockSpec(memory_space=V)
    S = jax.ShapeDtypeStruct
    return pl.pallas_call(
        functools.partial(attend_back_kernel, side),
        grid_spec=pltpu.PrefetchScalarGridSpec(
            num_scalar_prefetch=2,
            grid=(),
            in_specs=[pl.BlockSpec(memory_space=pl.ANY)] + [spec] * 7,
            out_specs=[spec] * 3,
            scratch_shapes=[V((HEADS * side, width), BF16), V((rows, HEADS * side), BF16), V((rows, key_rows), F32),
                            V((key_rows, side), F32), V((key_rows, side), F32), pltpu.SemaphoreType.DMA((HEADS // 2,))],
        ),
        out_shape=[S((HEADS, rows, side), BF16), S(pairs.shape, BF16), S((rows, 2 * side), F32)],
        cost_estimate=cost_of(15),
        compiler_params=pltpu.CompilerParams(vmem_limit_bytes=40 * 2**20),
    )(slots, first, full, branch, queries, pairs, own_ids, all_ids, cosine, sine)


def pairs_back_kernel(pair_grad, own_grad, query_grad, branch, cosine, sine, low, query_beside, query_twin, query_far,
                      branch_beside, branch_twin, branch_far, arrived, sends, recvs, unit_sends, unit_recvs):
    replica = lax.axis_index("replica")
    member = lax.axis_index("fsdp")
    beside = ((1 - replica // 2) * 2 + replica % 2, member)
    twin = (replica // 2 * 2 + 1 - replica % 2, member)
    count = pair_grad.shape[0]
    side = cosine.shape[1]
    barrier = pltpu.get_barrier_semaphore()
    for device in [(replica, (member + step) % count) for step in range(1, count)] + [beside, twin]:
        pl.semaphore_signal(barrier, inc=1, device_id=device, device_id_type=MESH)
    pl.semaphore_wait(barrier, count + 1)

    def copy(step):
        target = (member + step) % count
        return pltpu.make_async_remote_copy(
            src_ref=pair_grad.at[target], dst_ref=arrived.at[step], send_sem=sends.at[step], recv_sem=recvs.at[step],
            device_id=(replica, target), device_id_type=MESH)

    def unit_copy(n, source, target, device):
        return pltpu.make_async_remote_copy(
            src_ref=source, dst_ref=target, send_sem=unit_sends.at[n], recv_sem=unit_recvs.at[n],
            device_id=device, device_id_type=MESH)

    moves = []
    for n, (own, from_beside, from_twin, from_far) in enumerate(
            [(branch, branch_beside, branch_twin, branch_far), (query_grad, query_beside, query_twin, query_far)]):
        part = own.shape[0] // 2
        for h in range(2):
            at = pl.ds(h * part, part)
            first = 6 * n + 3 * h
            moves.append((unit_copy(first, own.at[at], from_beside.at[at], beside), unit_copy(first + 1, own.at[at], from_twin.at[at], twin),
                          unit_copy(first + 2, from_beside.at[at], from_far.at[at], twin)))
    for step in range(1, count):
        copy(step).start()
    for to_beside, to_twin, pass_on in moves:
        to_beside.start()
        to_twin.start()
    total = own_grad[...]
    for step in range(1, count):
        copy(step).wait_recv()
        total = total + arrived[step].astype(F32)
    low[0] = turn(total[:, :side], cosine[...], -sine[...]).astype(BF16)
    low[1] = total[:, side:].astype(BF16)
    for step in range(1, count):
        copy(step).wait_send()
    for to_beside, to_twin, pass_on in moves:
        to_beside.wait_recv()
        pass_on.start()
    for to_beside, to_twin, pass_on in moves:
        to_beside.wait_send()
        to_twin.wait()
        pass_on.wait()


def pairs_back(pair_grad, own_grad, query_grad, branch, cosine, sine):
    count, rows, double = pair_grad.shape
    D = pltpu.SemaphoreType.DMA
    S = jax.ShapeDtypeStruct
    spec = pl.BlockSpec(memory_space=pltpu.VMEM)
    return pl.pallas_call(
        pairs_back_kernel,
        out_shape=[S((2, rows, double // 2), BF16)] + [S(query_grad.shape, BF16)] * 3 + [S(branch.shape, BF16)] * 3,
        in_specs=[spec] * 6,
        out_specs=[spec] * 7,
        scratch_shapes=[pltpu.VMEM(pair_grad.shape, BF16), D((count,)), D((count,)), D((12,)), D((12,))],
        cost_estimate=cost_of(16),
        compiler_params=pltpu.CompilerParams(collective_id=3, has_side_effects=True),
    )(pair_grad, own_grad, query_grad, branch, cosine, sine)


def input_back_kernel(side, slots, full, query_grad, pair_grad, inputs, grad_middle, gain,
                      input_grad, gain_term, weights, joined, backward, sems):
    wide = inputs.shape[1] // side
    heads = query_grad.shape[0]

    def fetch(n, _):
        i, j = n // (heads + 2), n % (heads + 2)
        number = jnp.where(j < heads, i * heads + j, wide * j + i)
        fetch_tile(full, slots, number, weights.at[block_at(i * side, side), block_at(j * side, side)], sems.at[i // 2])
        return 0

    lax.fori_loop(0, wide * (heads + 2), fetch, 0, unroll=8)
    for h in range(heads):
        joined[:, h * side : (h + 1) * side] = query_grad[h]
    for k in range(2):
        joined[:, (heads + k) * side : (heads + k + 1) * side] = pair_grad[k]
    for c in range(wide // 2):
        view = weights.at[pl.ds(c * 2 * side, 2 * side), :]
        pltpu.make_async_copy(view, view, sems.at[c]).wait()
        backward[:, c * 2 * side : (c + 1) * 2 * side] = mul_turned(joined[...], view[...])
    back, term = norm_back(inputs[...].astype(F32), gain[...], backward[...])
    gain_term[...] = term
    input_grad[...] = (grad_middle[...] + back).astype(BF16)


def input_back(slots, full, query_grad, pair_grad, inputs, grad_middle, gain):
    rows, width = inputs.shape
    side = full.shape[1]
    V = pltpu.VMEM
    spec = pl.BlockSpec(memory_space=V)
    S = jax.ShapeDtypeStruct
    return pl.pallas_call(
        functools.partial(input_back_kernel, side),
        grid_spec=pltpu.PrefetchScalarGridSpec(
            num_scalar_prefetch=1,
            grid=(),
            in_specs=[pl.BlockSpec(memory_space=pl.ANY)] + [spec] * 5,
            out_specs=[spec] * 2,
            scratch_shapes=[V((width, (HEADS + 2) * side), BF16), V((rows, (HEADS + 2) * side), BF16), V((rows, width), F32),
                            pltpu.SemaphoreType.DMA((width // side // 2,))],
        ),
        out_shape=[S((rows, width), BF16), S((1, width), F32)],
        cost_estimate=cost_of(8),
        compiler_params=pltpu.CompilerParams(vmem_limit_bytes=40 * 2**20),
    )(slots, full, query_grad, pair_grad, inputs, grad_middle, gain)


def reduce_kernel(chunk, places, left_at, right_at, gain_part, *refs):
    count = len(places)
    given = 1 + max(place[0] for place in places)
    sources, refs = refs[:given], refs[given:]
    (out, gain_out, left_all, right_all, x_out, x_in, z_out, z_in, z_mix, turned_out, turned_in, turned_mix, total, gain_sum, gain_in, keep_sem, gain_s, gain_r,
     x_s, x_r, z_s, z_r, ty_s, ty_r, tc_s, tc_r, tf_s, tf_r, done_sem) = refs
    quarter = x_out.shape[1]
    pieces = quarter // chunk
    replica = lax.axis_index("replica")
    member = lax.axis_index("fsdp")
    y, core = replica // 2, replica % 2
    z, x = member // 2, member % 2
    across, beside, twin = (replica, z * 2 + 1 - x), ((1 - y) * 2 + core, member), (y * 2 + 1 - core, member)
    beside_replica, twin_replica, far_replica = (1 - y) * 2 + core, y * 2 + 1 - core, (1 - y) * 2 + 1 - core
    def level(step):
        return (z + step) % 4
    def depth_device(step):
        return (replica, level(step) * 2 + x)
    def keep(n):
        at, is_left, block, source_block, number, lane = places[n]
        source = sources[at].at[pl.ds(source_block, number)]
        if is_left:
            target = left_all.at[pl.ds(block, number), :, pl.ds(lane, sources[at].shape[2])]
        else:
            target = right_all.at[pl.ds(block, number), pl.ds(lane, sources[at].shape[1]), :]
        return pltpu.make_async_copy(source, target, keep_sem.at[n])
    for n in range(count):
        keep(n).start()
    left_all[left_all.shape[0] - 1] = jnp.zeros(left_all.shape[1:], left_all.dtype)
    gain_sum[...] = gain_part[...]

    barrier = pltpu.get_barrier_semaphore()
    for device in [across, beside, twin] + [depth_device(step) for step in (1, 2, 3)]:
        pl.semaphore_signal(barrier, inc=1, device_id=device, device_id_type=MESH)
    pl.semaphore_wait(barrier, 6)

    def remote(source, target, send, recv, device):
        return pltpu.make_async_remote_copy(src_ref=source, dst_ref=target, send_sem=send, recv_sem=recv, device_id=device, device_id_type=MESH)

    def gain_copy(stage, device):
        return remote(gain_sum, gain_in.at[stage], gain_s.at[stage], gain_r.at[stage], device)
    def gain_pair(stage, device):
        gain_copy(stage, device).wait()
        gain_sum[...] = gain_sum[...] + gain_in[stage]
    def gain_z(step):
        return remote(gain_sum, gain_in.at[2 + step], gain_s.at[2 + step], gain_r.at[2 + step], depth_device(step))
    def gain_finish():
        for step in (1, 2, 3):
            gain_z(step).wait()
        gain_in[0] = gain_sum[...]
        added = jnp.zeros(gain_sum.shape, F32)
        for zb in range(4):
            step = (zb - z + 4) % 4
            added = added + gain_in[jnp.where(step == 0, 0, 2 + step)]
        gain_out[...] = added
    gain_copy(0, beside).start()
    for n in range(count):
        keep(n).wait()

    def tile(owner, at):
        rank = replica * quarter + at
        return jnp.dot(left_all[left_at[owner, rank]], right_all[right_at[owner, rank]], preferred_element_type=F32)

    paired = z + 1 - 2 * (z % 2)
    levels = [z, paired, 3 - z, 3 - paired]
    middle = (z == 1) | (z == 2)
    order = (2, 3, 1, 0)
    def turned(k):
        return k % 6 == 2
    def at_level(lev):
        return (replica, lev * 2 + x)
    def x_copy(zb, k):
        at = pl.ds(k * chunk, chunk)
        return remote(x_out.at[zb, at], x_in.at[zb, at], x_s.at[zb, k], x_r.at[zb, k], across)
    def buffers(column, k):
        if column == 0:
            return z_out, z_in, z_mix, k * chunk
        return turned_out, turned_in, turned_mix, k // 6 * chunk
    def z_send(column, block, place, kind, device, k):
        out_buffer, in_buffer, mix_buffer, base = buffers(column, k)
        at = pl.ds(base, chunk)
        target = in_buffer.at[place, at] if kind < 2 else mix_buffer.at[place, at]
        return remote(out_buffer.at[block, at], target, z_s.at[column, block, k], z_r.at[column, kind, k], device)
    def pass_paired(column, k):
        z_send(column, 1, 0, 0, at_level(levels[1]), k).start()
    def pass_end(column, block, k):
        z_send(column, block, 3 - block, 5 - block, at_level(levels[1]), k).start()
    def pass_middle(column, block, k):
        z_send(column, block, 1, 1, at_level(levels[block]), k).start()
    def z_arrival(column, place, kind, k):
        z_send(column, 1, place, kind, at_level(levels[1]), k).wait_recv()
    def leave(column, block, k):
        if block == 1:
            pass_paired(column, k)
        elif block > 1:
            pl.when(jnp.logical_not(middle))(lambda: pass_end(column, block, k))
    def combine(column, k):
        @pl.when(middle)
        def _():
            out_buffer, in_buffer, mix_buffer, base = buffers(column, k)
            for place in (0, 1):
                z_arrival(column, place, 2 + place, k)
                def one(t, _):
                    at = base + t
                    out_buffer[2 + place, at] = (out_buffer[2 + place, at].astype(F32) + mix_buffer[place, at].astype(F32)).astype(BF16)
                    return 0
                lax.fori_loop(0, chunk, one, 0)
                pass_middle(column, 2 + place, k)
    def z_total(column, k, t):
        out_buffer, in_buffer, mix_buffer, base = buffers(column, k)
        at = base + t
        return out_buffer[0, at].astype(F32) + in_buffer[0, at].astype(F32) + in_buffer[1, at].astype(F32)
    def total_at(who, k):
        return total.at[pl.ds(who * quarter + k * chunk, chunk)]
    def t_beside(k):
        return remote(total_at(replica, k), total_at(replica, k), ty_s.at[k], ty_r.at[k], beside)
    def t_twin(k):
        return remote(total_at(replica, k), total_at(replica, k), tc_s.at[k], tc_r.at[k], twin)
    def t_pass(k):
        return remote(total_at(beside_replica, k), total_at(beside_replica, k), tf_s.at[k], tf_r.at[k], twin)
    def come_beside(k):
        return remote(total_at(replica, k), total_at(beside_replica, k), ty_s.at[k], ty_r.at[k], beside)
    def come_twin(k):
        return remote(total_at(replica, k), total_at(twin_replica, k), tc_s.at[k], tc_r.at[k], twin)
    def come_far(k):
        return remote(total_at(replica, k), total_at(far_replica, k), tf_s.at[k], tf_r.at[k], twin)

    def send_x(k):
        for block in order:
            lev = levels[block]
            def one(t, _):
                at = k * chunk + t
                x_out[lev, at] = tile(lev * 2 + 1 - x, at).astype(BF16)
                return 0
            lax.fori_loop(0, chunk, one, 0)
            x_copy(lev, k).start()

    def collect(k):
        for block in order:
            lev = levels[block]
            x_copy(lev, k).wait_recv()
            def one(t, _):
                at = k * chunk + t
                z_out[block, at] = (tile(lev * 2 + x, at) + x_in[lev, at].astype(F32)).astype(BF16)
                return 0
            lax.fori_loop(0, chunk, one, 0)
            leave(0, block, k)

    def turned_send(k):
        for block in order:
            for column in (0, 1):
                owner = levels[block] * 2 + (x if column == 0 else 1 - x)
                out_buffer, in_buffer, mix_buffer, base = buffers(column, k)
                def one(t, _):
                    out_buffer[block, base + t] = tile(owner, k * chunk + t).astype(BF16)
                    return 0
                lax.fori_loop(0, chunk, one, 0)
                leave(column, block, k)

    def turned_cross(k):
        for column in (0, 1):
            for place in (0, 1):
                z_arrival(column, place, place, k)
        def one(t, _):
            x_out[0, k * chunk + t] = z_total(1, k, t).astype(BF16)
            return 0
        lax.fori_loop(0, chunk, one, 0)
        x_copy(0, k).start()

    def finish(k):
        @pl.when(turned(k))
        def _():
            x_copy(0, k).wait_recv()
            def one(t, _):
                at = k * chunk + t
                total[replica * quarter + at] = (z_total(0, k, t) + x_in[0, at].astype(F32)).astype(BF16)
                return 0
            lax.fori_loop(0, chunk, one, 0)
        @pl.when(jnp.logical_not(turned(k)))
        def _():
            for place in (0, 1):
                z_arrival(0, place, place, k)
            def one(t, _):
                total[replica * quarter + k * chunk + t] = z_total(0, k, t).astype(BF16)
                return 0
            lax.fori_loop(0, chunk, one, 0)
        t_beside(k).start()
        t_twin(k).start()

    def spread(k):
        come_beside(k).wait_recv()
        t_pass(k).start()

    def beat(n, _):
        def due(behind, kind):
            k = n - behind
            here = (k >= 0) & (k < pieces)
            return here & (turned(k) if kind else jnp.logical_not(turned(k)))
        pl.when(due(0, True))(lambda: turned_send(n))
        pl.when(due(0, False))(lambda: send_x(n))
        @pl.when(due(1, True))
        def _():
            combine(0, n - 1)
            combine(1, n - 1)
        pl.when(due(2, False))(lambda: collect(n - 2))
        pl.when(due(3, False))(lambda: combine(0, n - 3))
        pl.when(due(3, True))(lambda: turned_cross(n - 3))
        pl.when((n >= 5) & (n < pieces + 5))(lambda: finish(n - 5))
        pl.when(n >= 7)(lambda: spread(n - 7))

        @pl.when(n == 2)
        def _():
            gain_pair(0, beside)
            gain_copy(1, twin).start()

        @pl.when(n == 4)
        def _():
            gain_pair(1, twin)
            gain_copy(2, across).start()

        @pl.when(n == 6)
        def _():
            gain_pair(2, across)
            for step in (1, 2, 3):
                gain_z(step).start()

        @pl.when(n == 9)
        def _():
            gain_finish()
        return 0
    lax.fori_loop(0, pieces + 7, beat, 0)

    def drain(k, _):
        come_twin(k).wait_recv()
        come_far(k).wait_recv()
        t_beside(k).wait_send()
        t_twin(k).wait_send()
        t_pass(k).wait_send()
        x_copy(0, k).wait_send()
        for block in (1, 2, 3):
            z_send(0, block, 0, 0, at_level(levels[1]), k).wait_send()
        @pl.when(turned(k))
        def _():
            for block in (1, 2, 3):
                z_send(1, block, 0, 0, at_level(levels[1]), k).wait_send()
        @pl.when(jnp.logical_not(turned(k)))
        def _():
            for zb in (1, 2, 3):
                x_copy(zb, k).wait_send()
        return 0
    lax.fori_loop(0, pieces, drain, 0)
    result = pltpu.make_async_copy(total, out, done_sem)
    result.start()
    result.wait()

def reduce_tiles(left_at, right_at, gain_part, parts, places, left_total, right_total, rows, chunk=3):
    capacity = left_at.shape[1]
    quarter = capacity // 4
    pieces = quarter // chunk
    side = parts[0].shape[1]
    D = pltpu.SemaphoreType.DMA
    V = pltpu.VMEM
    S = jax.ShapeDtypeStruct
    spec = pl.BlockSpec(memory_space=V)
    held = V((4, quarter, side, side), BF16)
    arriving = V((2, quarter, side, side), BF16)
    seldom = (pieces + 3) // 6 * chunk
    return pl.pallas_call(
        functools.partial(reduce_kernel, chunk, places),
        out_shape=[S((capacity, side, side), BF16), S(gain_part.shape, F32)],
        in_specs=[pl.BlockSpec(memory_space=pltpu.SMEM)] * 2 + [spec] + [pl.BlockSpec(memory_space=pl.ANY)] * len(parts),
        out_specs=[pl.BlockSpec(memory_space=pl.ANY), spec],
        scratch_shapes=[
            V((left_total + 1, side, rows), BF16), V((right_total, rows, side), BF16), held, held, held, arriving, arriving,
            V((4, seldom, side, side), BF16), V((2, seldom, side, side), BF16), V((2, seldom, side, side), BF16),
            V((capacity, side, side), BF16), V(gain_part.shape, F32), V((6,) + gain_part.shape, F32),
            D((len(places),)), D((6,)), D((6,))] + [D((4, pieces))] * 2 + [D((2, 4, pieces))] * 2 + [D((pieces,))] * 6 + [D],
        compiler_params=pltpu.CompilerParams(collective_id=1, has_side_effects=True, vmem_limit_bytes=62 * 2**20),
    )(left_at, right_at, gain_part, *parts)


def shampoo_kernel(count, grads, left_old, right_old, left_root, right_root, master, grads_out, left_new, right_new, master_new, low_new):
    side = grads.shape[1]
    flips, boths = [], []
    for at in range(count):
        wide = grads[at].astype(F32)
        grads_out[at] = wide
        flips.append(wide.T.astype(BF16))
    for at in range(count):
        both = jnp.dot(grads[at], jnp.concatenate([flips[at], right_root[at].astype(BF16)], 1), preferred_element_type=F32)
        left_new[at] = STAT_DECAY * left_old[at] + (1.0 - STAT_DECAY) * both[:, :side]
        boths.append(both[:, side:].astype(BF16))
    for at in range(count):
        right_new[at] = STAT_DECAY * right_old[at] + (1.0 - STAT_DECAY) * jnp.dot(flips[at], grads[at], preferred_element_type=F32)
    for at in range(count):
        turned = jnp.dot(left_root[at].astype(BF16), boths[at], preferred_element_type=F32)
        fresh = master[at] - STEP_RATE * turned
        master_new[at] = fresh
        low_new[at] = fresh.astype(BF16)

def shampoo(grads, left_old, right_old, left_root, right_root, master, count=17):
    capacity, side = master.shape[0], master.shape[1]
    while capacity % count:
        count -= 1
    spec = pl.BlockSpec((count, side, side), lambda i: (i, 0, 0))
    wide = jax.ShapeDtypeStruct(master.shape, F32)
    return pl.pallas_call(
        functools.partial(shampoo_kernel, count),
        grid=(capacity // count,),
        in_specs=[spec] * 6,
        out_specs=[spec] * 5,
        out_shape=[wide, wide, wide, wide, jax.ShapeDtypeStruct(master.shape, BF16)],
        compiler_params=pltpu.CompilerParams(vmem_limit_bytes=60 * 2**20),
    )(grads, left_old, right_old, left_root, right_root, master)


def shifted(block, axis, distance):
    devices = range(lax.axis_size(axis))
    route = [(i - distance, i) for i in devices if i - distance in devices]
    return lax.ppermute(block, axis, route)


def normalize(values, gain_row):
    mean_square = jnp.mean(values * values, -1, keepdims=True)
    return values * lax.rsqrt(mean_square + EPSILON) * gain_row


def rotate(values, angles):
    half_dim = values.shape[-1] // 2
    cosine = jnp.cos(angles)[:, None, :]
    sine_part = jnp.sin(angles)[:, None, :]
    first_half = values[..., :half_dim]
    second = values[..., half_dim:]
    return jnp.concatenate(
        [first_half * cosine - second * sine_part, second * cosine + first_half * sine_part], -1
    )


def angles_of(positions):
    half_dim = HEAD_DIM // 2
    inverse = 10000.0 ** (-2.0 * jnp.arange(half_dim, dtype=jnp.float32) / HEAD_DIM)
    return positions[:, None] * inverse[None, :]


def slot_of_tiles(owner_table, owners, capacity):
    onehot = (owner_table[:, None] == jnp.arange(owners, dtype=jnp.int32)[None, :]).astype(
        jnp.int32
    )
    earlier = jnp.cumsum(onehot, 0) - onehot
    ranking = jnp.sum(earlier * onehot, 1)
    return owner_table * capacity + ranking


def matrix_layout(width, head_width, head_dim, hidden_width, tile_side):
    left_attended = width // tile_side
    left_second = left_attended + head_width // tile_side
    left_hidden = left_second + width // tile_side
    right_key = head_width // tile_side
    right_value = right_key + head_dim // tile_side
    right_branch = right_value + head_dim // tile_side
    right_gate = right_branch + width // tile_side
    right_up = right_gate + hidden_width // tile_side
    right_down = right_up + hidden_width // tile_side
    return [
        (width, head_width, 0, 0),
        (width, head_dim, 0, right_key),
        (width, head_dim, 0, right_value),
        (head_width, width, left_attended, right_branch),
        (width, hidden_width, left_second, right_gate),
        (width, hidden_width, left_second, right_up),
        (hidden_width, width, left_hidden, right_down),
    ]


def project(values, blocks):
    row_count = values.shape[0]
    result = jnp.einsum(
        "nar,abrc->nbc",
        values.reshape(row_count, blocks.shape[0], blocks.shape[2]),
        blocks,
        preferred_element_type=jnp.float32,
    )
    return result.reshape(row_count, blocks.shape[1] * blocks.shape[3])


def back_project(values, blocks):
    row_count = values.shape[0]
    result = jnp.einsum(
        "nbc,abrc->nar",
        values.reshape(row_count, blocks.shape[1], blocks.shape[3]),
        blocks,
        preferred_element_type=jnp.float32,
    )
    return result.reshape(row_count, blocks.shape[0] * blocks.shape[2])


def dense_tile_grads(layout, left_blocks, right_blocks, tile_side):
    pieces = []
    for row_total, column_total, left_base, right_base in layout:
        left_part = left_blocks[:, left_base : left_base + row_total // tile_side]
        right_part = right_blocks[:, right_base : right_base + column_total // tile_side]
        product = jnp.einsum(
            "nar,nbc->abrc", left_part, right_part, preferred_element_type=jnp.float32
        )
        pieces.append(product.reshape(-1, tile_side, tile_side))
    pieces.append(jnp.zeros((1, tile_side, tile_side), jnp.float32))
    return jnp.concatenate(pieces, 0)


def block_tables(layout, tile_side, left_total):
    left_of, right_of = [], []
    for row_total, column_total, left_base, right_base in layout:
        for i in range(row_total // tile_side):
            for j in range(column_total // tile_side):
                left_of.append(left_base + i)
                right_of.append(right_base + j)
    return np.array(left_of + [left_total], np.int32), np.array(right_of + [0], np.int32)


def body_anywhere(
    inputs,
    cotangent,
    segment_ids,
    gains,
    owner_table,
    master_tiles,
    left_stats,
    right_stats,
    left_roots,
    right_roots,
):
    owners = lax.axis_size("fsdp")
    replicas = lax.axis_size("replica")
    member = lax.axis_index("fsdp")
    capacity = master_tiles.shape[0]
    tile_side = master_tiles.shape[1]
    row_count = inputs.shape[0]
    width = inputs.shape[1]
    head_width = HEADS * HEAD_DIM
    tile_total = owner_table.shape[0]
    layout = matrix_layout(width, head_width, HEAD_DIM, FF, tile_side)
    slots = slot_of_tiles(owner_table, owners, capacity)
    slot_tile = (
        jnp.full((owners * capacity,), tile_total, jnp.int32)
        .at[slots]
        .set(jnp.arange(tile_total, dtype=jnp.int32))
    )
    full = lax.all_gather(master_tiles.astype(jnp.bfloat16), "fsdp", axis=0, tiled=True)
    all_tiles = jnp.take(full, slots, axis=0)
    weights = []
    offset = 0
    for row_total, column_total, left_base, right_base in layout:
        number = row_total // tile_side * (column_total // tile_side)
        weights.append(
            all_tiles[offset : offset + number].reshape(
                row_total // tile_side, column_total // tile_side, tile_side, tile_side
            )
        )
        offset = offset + number
    w_query, w_key, w_value, w_out, w_gate, w_up, w_down = weights
    base_row = member * row_count
    own_ids = lax.dynamic_slice_in_dim(segment_ids, base_row, row_count, 0)
    starts = jnp.sum((segment_ids[None, :] < own_ids[:, None]).astype(jnp.int32), 1)
    positions = (base_row + jnp.arange(row_count, dtype=jnp.int32) - starts).astype(jnp.float32)
    angles = angles_of(positions)
    inputs_wide = inputs.astype(jnp.float32)
    normed = normalize(inputs_wide, gains[0]).astype(jnp.bfloat16)
    query_pre = project(normed, w_query)
    key_pre = project(normed, w_key)
    values_own = project(normed, w_value).astype(jnp.bfloat16)
    queries = rotate(query_pre.reshape(row_count, HEADS, HEAD_DIM), angles).astype(jnp.bfloat16)
    keys_own = rotate(key_pre[:, None, :], angles)[:, 0, :].astype(jnp.bfloat16)
    reach = WINDOW // row_count
    own_pair = jnp.concatenate([keys_own, values_own], 1)
    received = [shifted(own_pair, "fsdp", distance_back) for distance_back in range(reach, 0, -1)]
    pair_rows = jnp.concatenate(received + [own_pair], 0)
    key_rows = pair_rows[:, :HEAD_DIM]
    value_rows = pair_rows[:, HEAD_DIM:]
    padded_ids = jnp.concatenate([jnp.full((reach * row_count,), -1, jnp.int32), segment_ids], 0)
    key_ids = lax.dynamic_slice_in_dim(padded_ids, base_row, (reach + 1) * row_count, 0)
    distance = (
        jnp.arange(row_count, dtype=jnp.int32)[:, None]
        + reach * row_count
        - jnp.arange((reach + 1) * row_count, dtype=jnp.int32)[None, :]
    )
    allowed = (own_ids[:, None] == key_ids[None, :]) & (distance >= 0) & (distance < WINDOW)
    score_scale = HEAD_DIM ** (-0.5)
    scores = (
        jnp.einsum("nhd,kd->hnk", queries, key_rows, preferred_element_type=jnp.float32)
        * score_scale
    )
    scores = jnp.where(allowed[None], scores, -1e30)
    row_peak = jnp.max(scores, -1, keepdims=True)
    exponent = jnp.exp(scores - row_peak)
    row_total_sum = jnp.sum(exponent, -1, keepdims=True)
    probability = (exponent / row_total_sum).astype(jnp.bfloat16)
    log_total = row_peak + jnp.log(row_total_sum)
    attended = (
        jnp.einsum("hnk,kd->nhd", probability, value_rows, preferred_element_type=jnp.float32)
        .reshape(row_count, head_width)
        .astype(jnp.bfloat16)
    )
    middle = inputs_wide + project(attended, w_out)
    normed_two = normalize(middle, gains[1]).astype(jnp.bfloat16)
    gate = project(normed_two, w_gate)
    up_part = project(normed_two, w_up)

    def geglu(gate_values, up_values):
        return jax.nn.gelu(gate_values, approximate=True) * up_values

    hidden_wide, geglu_back = jax.vjp(geglu, gate, up_part)
    hidden = hidden_wide.astype(jnp.bfloat16)
    outputs = (middle + project(hidden, w_down)).astype(jnp.bfloat16)
    grad_hidden = back_project(cotangent, w_down)
    gate_back, up_back = geglu_back(grad_hidden)
    gate_grad = gate_back.astype(jnp.bfloat16)
    up_grad = up_back.astype(jnp.bfloat16)
    grad_normed_two = back_project(gate_grad, w_gate) + back_project(up_grad, w_up)
    middle_back, norm_two_back = jax.vjp(normalize, middle, gains[1])[1](grad_normed_two)
    grad_middle = cotangent.astype(jnp.float32) + middle_back
    branch_grad = grad_middle.astype(jnp.bfloat16)
    grad_attended = (
        back_project(branch_grad, w_out).astype(jnp.bfloat16).reshape(row_count, HEADS, HEAD_DIM)
    )
    scores_again = (
        jnp.einsum("nhd,kd->hnk", queries, key_rows, preferred_element_type=jnp.float32)
        * score_scale
    )
    scores_again = jnp.where(allowed[None], scores_again, -1e30)
    exact_prob = jnp.exp(scores_again - log_total)
    grad_prob = jnp.einsum(
        "nhd,kd->hnk", grad_attended, value_rows, preferred_element_type=jnp.float32
    )
    grad_scores = (
        exact_prob * (grad_prob - jnp.sum(exact_prob * grad_prob, -1, keepdims=True))
    ).astype(jnp.bfloat16)
    grad_queries = (
        jnp.einsum("hnk,kd->nhd", grad_scores, key_rows, preferred_element_type=jnp.float32)
        * score_scale
    )
    grad_keys = (
        jnp.einsum("hnk,nhd->kd", grad_scores, queries, preferred_element_type=jnp.float32)
        * score_scale
    )
    grad_values = jnp.einsum(
        "hnk,nhd->kd", probability, grad_attended, preferred_element_type=jnp.float32
    )
    grad_pairs = jnp.concatenate([grad_keys, grad_values], 1)
    own_grad = grad_pairs[reach * row_count :]
    for distance_back in range(1, reach + 1):
        sent_rows = grad_pairs[
            (reach - distance_back) * row_count : (reach - distance_back + 1) * row_count
        ]
        own_grad = own_grad + shifted(
            sent_rows.astype(jnp.bfloat16), "fsdp", -distance_back
        ).astype(sent_rows.dtype)
    grad_query_pre = (
        rotate(grad_queries, -angles).reshape(row_count, head_width).astype(jnp.bfloat16)
    )
    grad_key_pre = rotate(own_grad[:, None, :HEAD_DIM], -angles)[:, 0, :].astype(jnp.bfloat16)
    grad_values_low = own_grad[:, HEAD_DIM:].astype(jnp.bfloat16)
    grad_normed = (
        back_project(grad_query_pre, w_query)
        + back_project(grad_key_pre, w_key)
        + back_project(grad_values_low, w_value)
    )
    inputs_back, norm_one_back = jax.vjp(normalize, inputs_wide, gains[0])[1](grad_normed)
    input_grad = (grad_middle + inputs_back).astype(jnp.bfloat16)
    gain_grads = lax.psum(jnp.stack([norm_one_back, norm_two_back]), ("replica", "fsdp"))
    gain_rate = GAIN_STEP * (row_count * owners * replicas) ** (-0.5)
    new_gains = gains - gain_rate * gain_grads
    left_parts = jnp.concatenate([normed, attended, normed_two, hidden], 1)
    right_parts = jnp.concatenate(
        [grad_query_pre, grad_key_pre, grad_values_low, branch_grad, gate_grad, up_grad, cotangent],
        1,
    )
    left_blocks = left_parts.reshape(row_count, -1, tile_side)
    right_blocks = right_parts.reshape(row_count, -1, tile_side)
    dense = dense_tile_grads(layout, left_blocks, right_blocks, tile_side)
    partial_sum = lax.psum_scatter(
        jnp.take(dense, slot_tile, axis=0), "fsdp", scatter_dimension=0, tiled=True
    )
    grads_low = lax.psum(partial_sum.astype(jnp.bfloat16), "replica")
    grads_all, left_all, right_all, master_all, low_all = shampoo(
        grads_low, left_stats, right_stats, left_roots, right_roots, master_tiles
    )
    return (
        outputs,
        input_grad,
        gain_grads,
        new_gains,
        grads_all,
        master_all,
        low_all,
        left_all,
        right_all,
    )


def body_of_units(
    inputs,
    cotangent,
    segment_ids,
    gains,
    owner_table,
    master_tiles,
    left_stats,
    right_stats,
    left_roots,
    right_roots,
):
    owners, replicas = 8, 4
    member = lax.axis_index("fsdp")
    capacity = master_tiles.shape[0]
    side = master_tiles.shape[1]
    rows, width = inputs.shape
    tile_total = owner_table.shape[0]
    layout = matrix_layout(width, HEADS * HEAD_DIM, HEAD_DIM, FF, side)
    left_of, right_of = block_tables(layout, side, 0)
    padded = -(-tile_total // 128) * 128
    block_values = np.zeros((padded, 128), np.float32)
    block_values[:tile_total, 0] = left_of[:-1] + 1
    block_values[:tile_total, 1] = right_of[:-1] + 1
    left_total, right_total = int(max(left_of)) + 1, int(max(right_of)) + 1
    owner_row = jnp.pad(owner_table, (0, padded - tile_total), constant_values=-1).reshape(1, padded)

    slots, blocks_at, normed, early = prepare(
        owners, capacity, owner_row, jnp.asarray(block_values, BF16), inputs, cotangent, gains[0:1]
    )
    slots = slots.reshape(padded)
    chosen = blocks_at[:, :capacity, :2].astype(jnp.int32) - 1
    left_at = jnp.where(chosen[..., 0] < 0, left_total, chosen[..., 0])
    right_at = jnp.maximum(chosen[..., 1], 0)
    base_row = member * rows
    own_ids = lax.dynamic_slice_in_dim(segment_ids, base_row, rows, 0)
    starts = jnp.sum((segment_ids[None, :] < own_ids[:, None]).astype(jnp.int32), 1)
    positions = (base_row + jnp.arange(rows, dtype=jnp.int32) - starts).astype(jnp.float32)
    angles = angles_of(positions)
    cosine, sine = jnp.cos(angles), jnp.sin(angles)
    cosine = jnp.concatenate([cosine, cosine], 1)
    sine = jnp.concatenate([-sine, sine], 1)
    first = base_row.astype(jnp.int32).reshape(1)
    own_column, all_row = own_ids.reshape(-1, 1), segment_ids.reshape(1, -1)

    def over_y(part):
        return lax.ppermute(part, "replica", [(0, 2), (1, 3), (2, 0), (3, 1)])

    def over_core(part):
        return lax.ppermute(part, "replica", [(0, 1), (1, 0), (2, 3), (3, 2)])

    def unit_of(part):
        beside = over_y(part)
        return [part, beside, over_core(part), over_core(beside)]

    early_unit = unit_of(early)
    full = gather(master_tiles).reshape(owners * capacity, side, side)
    queries, pair = project_heads(slots, full, normed, cosine, sine)
    pairs = gather_pairs(pair, owners)
    attended_turned, normed_two, normed_two_turned, middle = attend(
        slots, first, full, queries, pairs, own_column, all_row, inputs, gains[1:2]
    )
    two_unit = unit_of(normed_two_turned)
    attended_turned, _ = lax.optimization_barrier((attended_turned, two_unit[1]))
    attended_unit = unit_of(attended_turned)
    wide = width // side
    hidden, gate_grad, up_grad, outputs, grad_middle, branch, branch_blocks, term_two = mlp(
        slots, full, normed_two, two_unit[1], cotangent, early_unit[1], middle, gains[1:2]
    )
    hidden_far, gate_far, up_far = over_core(hidden), over_core(gate_grad), over_core(up_grad)
    query_grad, pair_grad, own_pair_grad = attend_back(
        slots, first, full, branch, queries, pairs, own_column, all_row, cosine, sine
    )
    pair_low, *others = pairs_back(pair_grad, own_pair_grad, query_grad, branch_blocks, cosine, sine)
    query_unit = [query_grad] + others[:3]
    branch_unit = [branch_blocks] + others[3:]
    pair_unit = unit_of(pair_low)
    input_grad, term_one = input_back(slots, full, query_grad, pair_low, inputs, grad_middle, gains[0:1])

    parts, places = [], []

    def place(unit, *spots):
        for n, part in enumerate(unit):
            for is_left, block, source_block, count in spots:
                places.append((len(parts), is_left, block, source_block, count, n * rows * (4 // len(unit))))
            parts.append(part)

    blocks = FF // side
    place(early_unit, (True, 0, 0, wide), (False, HEADS + 2 + wide + 2 * blocks, wide, wide))
    place(attended_unit, (True, wide, 0, HEADS))
    place(two_unit, (True, wide + HEADS, 0, wide))
    place([hidden, hidden_far], (True, 2 * wide + HEADS, 0, blocks))
    place(query_unit, (False, 0, 0, HEADS))
    place(pair_unit, (False, HEADS, 0, 2))
    place(branch_unit, (False, HEADS + 2, 0, wide))
    place([gate_grad, gate_far], (False, HEADS + 2 + wide, 0, blocks))
    place([up_grad, up_far], (False, HEADS + 2 + wide + blocks, 0, blocks))
    gain_part = jnp.concatenate([term_one, term_two, jnp.zeros((6, width), F32)], 0)
    grads_low, gain_sum = reduce_tiles(
        left_at, right_at, gain_part, parts, tuple(places), left_total, right_total, replicas * rows
    )
    gain_grads = gain_sum[:2]
    gain_rate = GAIN_STEP * (rows * owners * replicas) ** (-0.5)
    grads_all, left_all, right_all, master_all, low_all = shampoo(
        grads_low, left_stats, right_stats, left_roots, right_roots, master_tiles
    )
    return (
        outputs,
        input_grad,
        gain_grads,
        gains - gain_rate * gain_grads,
        grads_all,
        master_all,
        low_all,
        left_all,
        right_all,
    )


def solution(mesh):
    units = mesh.shape["replica"] == 4 and mesh.shape["fsdp"] == 8
    return jax.shard_map(
        body_of_units if units else body_anywhere,
        mesh=mesh,
        in_specs=(
            P(("replica", "fsdp"), None),
            P(("replica", "fsdp"), None),
            P("replica"),
            P(),
            P(),
            P("fsdp", None, None),
            P("fsdp", None, None),
            P("fsdp", None, None),
            P("fsdp", None, None),
            P("fsdp", None, None),
        ),
        out_specs=(
            P(("replica", "fsdp"), None),
            P(("replica", "fsdp"), None),
            P(),
            P(),
            P("fsdp", None, None),
            P("fsdp", None, None),
            P("fsdp", None, None),
            P("fsdp", None, None),
            P("fsdp", None, None),
        ),
        check_vma=False,
    )
```

```python
import functools

import jax
import jax.numpy as jnp
import numpy as np
from jax import lax
from jax.experimental import pallas as pl
from jax.experimental.pallas import tpu as pltpu
from jax.sharding import PartitionSpec as P

HEADS = 12
HEAD_DIM = 128
FF = 4608
WINDOW = 1024


EPSILON = 1e-06
STEP_RATE = 0.02
STAT_DECAY = 0.5
GAIN_STEP = 0.1
F32, BF16 = jnp.float32, jnp.bfloat16
MESH = pl.DeviceIdType.MESH


def gather_kernel(chunk, whole, deep_most, early, patience, master, full, stage, low, stage_sem, keep_sem,
                  up_s, up_r, down_s, down_r, x_s, x_r, eu_s, eu_r, ed_s, ed_r, y_s, y_r, core_s, core_r):
    replica = lax.axis_index("replica")
    member = lax.axis_index("fsdp")
    y, core = replica // 2, replica % 2
    z, x = member // 2, member % 2
    deep = deep_most - core
    run = whole - deep
    half = whole * chunk
    mirrored = z // 2
    inner = z + mirrored * (3 - 2 * z)
    above, below = (replica, (z + 1) * 2 + x), (replica, (z - 1) * 2 + x)
    across, beside, twin = (replica, z * 2 + 1 - x), ((1 - y) * 2 + core, member), (y * 2 + 1 - core, member)

    def rows(chunk_at, owner_core):
        return pl.ds(owner_core * half + chunk_at * chunk, chunk)

    def load(c, part):
        return pltpu.make_async_copy(master.at[rows(c, part)], stage.at[pl.ds(c * chunk, chunk)], stage_sem.at[c])

    def cast(c, part):
        load(c, part).wait()
        low[rows(c, part)] = stage[pl.ds(c * chunk, chunk)].astype(BF16)

    def place(k, plane):
        return plane * (whole - 1) + k * (1 - 2 * plane)

    def load_first(k, _):
        load(place(k, y), core).start()
        return 0

    lax.fori_loop(0, whole, load_first, 0)
    barrier = pltpu.get_barrier_semaphore()

    def greet(device):
        pl.semaphore_signal(barrier, inc=1, device_id=device, device_id_type=MESH)

    pl.when(z < 3)(lambda: greet(above))
    pl.when(z > 0)(lambda: greet(below))
    greet(across)
    greet(beside)
    greet(twin)

    @pl.when((z == 0) | (z == 3))
    def _():
        pl.semaphore_wait(barrier, 4)

    @pl.when((z > 0) & (z < 3))
    def _():
        pl.semaphore_wait(barrier, 5)

    def copy(owner, chunk_at, send, recv, device, from_own=False, owner_core=None):
        at = rows(chunk_at, core if owner_core is None else owner_core)
        target = full.at[owner, at]
        source = low.at[at] if from_own else target
        return pltpu.make_async_remote_copy(src_ref=source, dst_ref=target, send_sem=send, recv_sem=recv, device_id=device, device_id_type=MESH)

    def go_up(zb, k, own=False):
        return copy(zb * 2 + x, place(k, y), up_s.at[zb, k], up_r.at[zb, k], above, own)

    def go_down(zb, k, own=False):
        return copy(zb * 2 + x, place(k, y), down_s.at[zb, k], down_r.at[zb, k], below, own)

    def early_up(zb, k):
        return copy(zb * 2 + 1 - x, place(k, y), eu_s.at[zb, k], eu_r.at[zb, k], above)

    def early_down(zb, k):
        return copy(zb * 2 + 1 - x, place(k, y), ed_s.at[zb, k], ed_r.at[zb, k], below)

    def go_x(zb, k, own=False):
        return copy(zb * 2 + x, place(k, y), x_s.at[zb, k], x_r.at[zb, k], across, own)

    def come_x(zb, k):
        return copy(zb * 2 + 1 - x, place(k, y), x_s.at[zb, k], x_r.at[zb, k], across)

    def go_y(owner, k):
        return copy(owner, place(k, y), y_s.at[owner, k], y_r.at[owner, k], beside)

    def come_y(owner, k):
        return copy(owner, place(k, 1 - y), y_s.at[owner, k], y_r.at[owner, k], beside)

    def go_core(owner, at):
        return copy(owner, at, core_s.at[owner, at], core_r.at[owner, at], twin)

    def onward(owner, k):
        go_core(owner, place(k, y)).start()
        pl.when(k < deep)(lambda: go_y(owner, k).start())

    def across_block(g):
        b = g if g >= 2 else (g + inner) % 2
        return b + mirrored * (3 - 2 * b)

    def group(g):
        def tick(k, _):
            if g == 0:
                cast(place(k, y), core)
                pl.when(z < 3)(lambda: go_up(z, k, True).start())
                pl.when(z > 0)(lambda: go_down(z, k, True).start())
                go_x(z, k, True).start()
            if 1 <= g <= 3:
                @pl.when(z - g >= 0)
                def _():
                    go_up(z - g, k).wait_recv()
                    pl.when(z < 3)(lambda: go_up(z - g, k).start())
                    onward((z - g) * 2 + x, k)

                @pl.when(z + g <= 3)
                def _():
                    go_down(z + g, k).wait_recv()
                    pl.when(z > 0)(lambda: go_down(z + g, k).start())
                    onward((z + g) * 2 + x, k)

                pl.when(k >= early)(lambda: go_x(across_block(g), k).start())
            if g == 1:
                come_x(z, k).wait_recv()
                onward(z * 2 + 1 - x, k)

                @pl.when(k < early)
                def _():
                    pl.when(z < 3)(lambda: early_up(z, k).start())
                    pl.when(z > 0)(lambda: early_down(z, k).start())

            if 2 <= g <= 4:
                @pl.when(k >= early)
                def _():
                    come_x(across_block(g - 1), k).wait_recv()
                    onward(across_block(g - 1) * 2 + 1 - x, k)

                @pl.when((k < early) & (z - (g - 1) >= 0))
                def _():
                    zb = z - (g - 1)
                    early_up(zb, k).wait_recv()
                    pl.when(z < 3)(lambda: early_up(zb, k).start())
                    onward(zb * 2 + 1 - x, k)

                @pl.when((k < early) & (z + (g - 1) <= 3))
                def _():
                    zb = z + (g - 1)
                    early_down(zb, k).wait_recv()
                    pl.when(z > 0)(lambda: early_down(zb, k).start())
                    onward(zb * 2 + 1 - x, k)
            h = g - patience
            if 1 <= h <= 4:
                def take(owner):
                    come_y(owner, k).wait_recv()
                    go_core(owner, place(k, 1 - y)).start()

                if h <= 3:
                    pl.when((k < deep) & (z - h >= 0))(lambda: take((z - h) * 2 + x))
                    pl.when((k < deep) & (z + h <= 3))(lambda: take((z + h) * 2 + x))
                if h == 1:
                    pl.when(k < deep)(lambda: take(z * 2 + 1 - x))
                else:
                    pl.when((k < deep) & (k >= early))(lambda: take(across_block(h - 1) * 2 + 1 - x))
                    pl.when((k < early) & (z - (h - 1) >= 0))(lambda: take((z - (h - 1)) * 2 + 1 - x))
                    pl.when((k < early) & (z + (h - 1) <= 3))(lambda: take((z + (h - 1)) * 2 + 1 - x))
            return 0

        lax.fori_loop(0, run, tick, 0)

    group(0)

    def rest(k, _):
        cast(place(k, y), core)
        return 0

    lax.fori_loop(run, whole, rest, 0)

    def load_other(c, _):
        load(c, 1 - core).start()
        return 0

    lax.fori_loop(0, whole, load_other, 0)

    def cast_other(c, _):
        cast(c, 1 - core)
        return 0

    group(1)
    lax.fori_loop(0, whole, cast_other, 0)
    keep = pltpu.make_async_copy(low, full.at[member], keep_sem)
    keep.start()
    for g in range(2, 5 + patience):
        group(g)

    def drain_z(zb, _):
        def one(k, _):
            pl.when((zb <= z) & (z < 3))(lambda: go_up(zb, k).wait_send())
            pl.when((zb >= z) & (z > 0))(lambda: go_down(zb, k).wait_send())
            pl.when((zb == z) | (k >= early))(lambda: go_x(zb, k).wait_send())
            pl.when((k < early) & (zb <= z) & (z < 3))(lambda: early_up(zb, k).wait_send())
            pl.when((k < early) & (zb >= z) & (z > 0))(lambda: early_down(zb, k).wait_send())
            return 0

        lax.fori_loop(0, run, one, 0)
        return 0

    lax.fori_loop(0, 4, drain_z, 0)

    def drain_owner(owner, _):
        @pl.when(owner != member)
        def _():
            def one_y(k, _):
                go_y(owner, k).wait_send()
                return 0

            lax.fori_loop(0, deep, one_y, 0)

            def one_core(k, _):
                go_core(owner, k).wait_send()
                copy(owner, k, core_s.at[owner, k], core_r.at[owner, k], twin, owner_core=1 - core).wait_recv()
                return 0

            lax.fori_loop(0, whole, one_core, 0)

        return 0

    lax.fori_loop(0, 8, drain_owner, 0)
    keep.wait()


def gather(master, chunk=6, deep=6, early=1, patience=1):
    capacity = master.shape[0]
    whole = capacity // 2 // chunk
    run = whole - deep + 1
    D = pltpu.SemaphoreType.DMA
    V = pltpu.VMEM
    return pl.pallas_call(
        functools.partial(gather_kernel, chunk, whole, deep, early, patience),
        out_shape=jax.ShapeDtypeStruct((8,) + master.shape, BF16),
        in_specs=[pl.BlockSpec(memory_space=pl.ANY)],
        out_specs=pl.BlockSpec(memory_space=pl.ANY),
        scratch_shapes=[V((capacity // 2,) + master.shape[1:], F32), V(master.shape, BF16), D((whole,)), D]
        + [D((4, run))] * 6 + [D((4, max(early, 1)))] * 4 + [D((8, deep))] * 2 + [D((8, whole))] * 2,
        compiler_params=pltpu.CompilerParams(collective_id=0, has_side_effects=True, vmem_limit_bytes=60 * 2**20),
    )(master)


def prepare_kernel(owners, capacity, owner_row, block_values, inputs, cotangent, gain, slots, blocks_at, normed, early, ranks):
    total = owner_row.shape[1]
    lanes = 128
    owner = owner_row[...]
    same = (owner == lax.broadcasted_iota(jnp.int32, (owners, total), 0)).astype(F32)
    ones_before = (lax.broadcasted_iota(jnp.int32, (lanes, lanes), 0) < lax.broadcasted_iota(jnp.int32, (lanes, lanes), 1)).astype(BF16)
    carry = jnp.zeros((owners, 1), F32)
    for c in range(total // lanes):
        at = slice(c * lanes, (c + 1) * lanes)
        piece = same[:, at]
        before = jnp.dot(piece.astype(BF16), ones_before, preferred_element_type=F32) + carry
        ranks[:, at] = jnp.sum(before * piece, 0, keepdims=True).astype(jnp.int32)
        carry = carry + jnp.sum(piece, 1, keepdims=True)
    slot = jnp.where(owner >= 0, owner * capacity + ranks[...], -1)
    slots[...] = slot
    padded = blocks_at.shape[1]
    for o in range(owners):
        here = lax.broadcasted_iota(jnp.int32, (padded, total), 0)
        here = jnp.where(here < capacity, here + o * capacity, -2)
        hit = jnp.where(here == slot, 1.0, 0.0).astype(BF16)
        blocks_at[o] = jnp.dot(hit, block_values[...], preferred_element_type=F32)
    values = inputs[...].astype(F32)
    mean_square = jnp.mean(values * values, -1, keepdims=True)
    scaled = values * lax.rsqrt(mean_square + EPSILON) * gain[...]
    normed[...] = scaled.astype(BF16)
    count = early.shape[0] // 2
    for c in range(count):
        at = slice(c * lanes, (c + 1) * lanes)
        early[c] = scaled[:, at].T.astype(BF16)
        early[count + c] = cotangent[:, at]

def prepare(owners, capacity, owner_row, block_values, inputs, cotangent, gain):
    rows, width = inputs.shape
    padded = -(-capacity // 16) * 16
    S = jax.ShapeDtypeStruct
    spec = pl.BlockSpec(memory_space=pltpu.VMEM)
    return pl.pallas_call(
        functools.partial(prepare_kernel, owners, capacity),
        in_specs=[spec] * 5,
        out_specs=[spec] * 4,
        out_shape=[S(owner_row.shape, jnp.int32), S((owners, padded, 128), F32), S((rows, width), BF16),
                   S((2 * width // 128, 128, rows), BF16)],
        scratch_shapes=[pltpu.VMEM(owner_row.shape, jnp.int32)],
        compiler_params=pltpu.CompilerParams(vmem_limit_bytes=40 * 2**20),
    )(owner_row, block_values, inputs, cotangent, gain)


BY_ROWS = (((1,), (1,)), ((), ()))
BY_COLUMNS = (((0,), (0,)), ((), ()))


def mul(a, b):
    return jnp.dot(a, b, preferred_element_type=F32)


def mul_turned(a, b):
    return lax.dot_general(a, b, BY_ROWS, preferred_element_type=F32)


def mul_summed(a, b):
    return lax.dot_general(a, b, BY_COLUMNS, preferred_element_type=F32)


def turn(part, cosine, sine):
    return part * cosine + pltpu.roll(part, HEAD_DIM // 2, 1) * sine


def cost_of(microseconds):
    return pl.CostEstimate(flops=int(microseconds * 9e8), bytes_accessed=int(microseconds * 3e6), transcendentals=0)


def fetch_tile(full, slots, number, target, sem):
    pltpu.make_async_copy(full.at[slots[number]], target, sem).start()


def block_at(start, size):
    return pl.ds(pl.multiple_of(start, size), size)


def project_kernel(side, slots, full, normed, cosine, sine, queries, pair, weights, sems):
    wide = normed.shape[1] // side
    heads = queries.shape[1] // side

    def fetch(n, _):
        j, i = n // wide, n % wide
        number = jnp.where(j < heads, i * heads + j, wide * j + i)
        fetch_tile(full, slots, number, weights.at[block_at(i * side, side), block_at(j * side, side)], sems.at[j // 2])
        return 0

    lax.fori_loop(0, wide * (heads + 2), fetch, 0, unroll=8)
    for c in range((heads + 2) // 2):
        view = weights.at[:, pl.ds(c * 2 * side, 2 * side)]
        pltpu.make_async_copy(view, view, sems.at[c]).wait()
        product = mul(normed[...], view[...])
        for k in range(2):
            part = product[:, k * side : (k + 1) * side]
            if c < heads // 2:
                queries[:, (2 * c + k) * side : (2 * c + k + 1) * side] = turn(part, cosine[...], sine[...]).astype(BF16)
            elif k == 0:
                pair[:, :side] = turn(part, cosine[...], sine[...]).astype(BF16)
            else:
                pair[:, side:] = part.astype(BF16)


def project_heads(slots, full, normed, cosine, sine):
    rows, width = normed.shape
    side = full.shape[1]
    V = pltpu.VMEM
    spec = pl.BlockSpec(memory_space=V)
    return pl.pallas_call(
        functools.partial(project_kernel, side),
        grid_spec=pltpu.PrefetchScalarGridSpec(
            num_scalar_prefetch=1,
            grid=(),
            in_specs=[pl.BlockSpec(memory_space=pl.ANY), spec, spec, spec],
            out_specs=[spec, spec],
            scratch_shapes=[V((width, (HEADS + 2) * side), BF16), pltpu.SemaphoreType.DMA(((HEADS + 2) // 2,))],
        ),
        out_shape=[jax.ShapeDtypeStruct((rows, HEADS * side), BF16), jax.ShapeDtypeStruct((rows, 2 * side), BF16)],
        cost_estimate=cost_of(6),
        compiler_params=pltpu.CompilerParams(vmem_limit_bytes=40 * 2**20),
    )(slots, full, normed, cosine, sine)


def pairs_kernel(pair, pairs, keep_sem, sends, recvs):
    replica = lax.axis_index("replica")
    member = lax.axis_index("fsdp")
    count = pairs.shape[0]
    barrier = pltpu.get_barrier_semaphore()
    others = [(member + step) % count for step in range(1, count)]
    for other in others:
        pl.semaphore_signal(barrier, inc=1, device_id=(replica, other), device_id_type=MESH)
    pl.semaphore_wait(barrier, count - 1)
    keep = pltpu.make_async_copy(pair, pairs.at[member], keep_sem)
    keep.start()

    def copy(step, owner):
        return pltpu.make_async_remote_copy(
            src_ref=pair, dst_ref=pairs.at[owner], send_sem=sends.at[step], recv_sem=recvs.at[step],
            device_id=(replica, (member + step) % count), device_id_type=MESH)

    for step in range(1, count):
        copy(step, member).start()
    for step in range(1, count):
        copy(step, (member + count - step) % count).wait_recv()
    for step in range(1, count):
        copy(step, member).wait_send()
    keep.wait()


def gather_pairs(pair, count):
    D = pltpu.SemaphoreType.DMA
    spec = pl.BlockSpec(memory_space=pltpu.VMEM)
    return pl.pallas_call(
        pairs_kernel,
        out_shape=jax.ShapeDtypeStruct((count,) + pair.shape, pair.dtype),
        in_specs=[spec],
        out_specs=spec,
        scratch_shapes=[D, D((count,)), D((count,))],
        cost_estimate=cost_of(13),
        compiler_params=pltpu.CompilerParams(collective_id=2, has_side_effects=True),
    )(pair)


def fill_bias(first, own_ids, all_ids, bias):
    shape = bias.shape
    distance = first + lax.broadcasted_iota(jnp.int32, shape, 0) - lax.broadcasted_iota(jnp.int32, shape, 1)
    allowed = (own_ids[...] == all_ids[...]) & (distance >= 0) & (distance < WINDOW)
    bias[...] = jnp.where(allowed, 0.0, -1e30)


def softmax_of(scores):
    exponent = jnp.exp(scores - jnp.max(scores, -1, keepdims=True))
    return exponent / jnp.sum(exponent, -1, keepdims=True)


def attend_kernel(side, slots, first, full, queries, pairs, own_ids, all_ids, inputs, gain,
                  attended_turned, normed_two, normed_two_turned, middle, weights, attended, bias, sems):
    heads = attended.shape[1] // side
    wide = middle.shape[1] // side

    def fetch(n, _):
        j, i = n // heads, n % heads
        number = (heads + 2) * wide + i * wide + j
        fetch_tile(full, slots, number, weights.at[block_at(i * side, side), block_at(j * side, side)], sems.at[j // 2])
        return 0

    lax.fori_loop(0, wide * heads, fetch, 0, unroll=8)
    fill_bias(first[0], own_ids, all_ids, bias)
    keys = pairs[:, :, :side].reshape(-1, side)
    values = pairs[:, :, side:].reshape(-1, side)
    scale = HEAD_DIM ** (-0.5)
    for head in range(heads):
        at = slice(head * side, (head + 1) * side)
        scores = mul_turned(queries[:, at], keys) * scale + bias[...]
        product = mul(softmax_of(scores).astype(BF16), values)
        attended[:, at] = product.astype(BF16)
        attended_turned[head] = product.T.astype(BF16)
    total = jnp.zeros((inputs.shape[0], 1), F32)
    for c in range(wide // 2):
        view = weights.at[:, pl.ds(c * 2 * side, 2 * side)]
        pltpu.make_async_copy(view, view, sems.at[c]).wait()
        at = slice(c * 2 * side, (c + 1) * 2 * side)
        part = inputs[:, at].astype(F32) + mul(attended[...], view[...])
        middle[:, at] = part
        total = total + jnp.sum(part * part, -1, keepdims=True)
    scaled = lax.rsqrt(total / middle.shape[1] + EPSILON)
    for c in range(wide):
        at = slice(c * side, (c + 1) * side)
        part = middle[:, at] * scaled * gain[:, at]
        normed_two[:, at] = part.astype(BF16)
        normed_two_turned[c] = part.T.astype(BF16)


def attend(slots, first, full, queries, pairs, own_ids, all_ids, inputs, gain):
    rows, width = inputs.shape
    side = full.shape[1]
    V = pltpu.VMEM
    spec = pl.BlockSpec(memory_space=V)
    S = jax.ShapeDtypeStruct
    return pl.pallas_call(
        functools.partial(attend_kernel, side),
        grid_spec=pltpu.PrefetchScalarGridSpec(
            num_scalar_prefetch=2,
            grid=(),
            in_specs=[pl.BlockSpec(memory_space=pl.ANY)] + [spec] * 6,
            out_specs=[spec] * 4,
            scratch_shapes=[V((HEADS * side, width), BF16), V((rows, HEADS * side), BF16),
                            V((rows, pairs.shape[0] * pairs.shape[1]), F32), pltpu.SemaphoreType.DMA((width // side // 2,))],
        ),
        out_shape=[S((HEADS, side, rows), BF16), S((rows, width), BF16), S((width // side, side, rows), BF16), S((rows, width), F32)],
        cost_estimate=cost_of(11),
        compiler_params=pltpu.CompilerParams(vmem_limit_bytes=40 * 2**20),
    )(slots, first, full, queries, pairs, own_ids, all_ids, inputs, gain)


def norm_back(values, gain, grads):
    mean_square = jnp.mean(values * values, -1, keepdims=True)
    scaled = lax.rsqrt(mean_square + EPSILON)
    weighed = grads * gain
    inner = jnp.mean(weighed * values, -1, keepdims=True)
    back = scaled * weighed - values * (scaled * scaled * scaled * inner)
    return back, jnp.sum(grads * values * scaled, 0, keepdims=True)


GELU_SCALE = 0.7978845608028654
GELU_CUBE = 0.044715


def mlp_kernel(side, ring, span, slots, full, normed_own, normed_beside, cotangent_own, cotangent_beside, middle, gain,
               hidden_turned, gate_grad, up_grad, outputs, grad_middle, branch, branch_blocks, gain_term,
               normed, cotangent, forward, backward, gate_ring, up_ring, down_ring, sems):
    rows, width = normed_own.shape
    wide = width // side
    hidden_blocks = hidden_turned.shape[0]
    steps = hidden_blocks // span
    heads = HEADS
    base = (heads + 2) * wide + heads * wide

    def pieces_of(j, slot):
        todo = []
        for i in range(wide):
            for k in range(span):
                column = span * j + k
                row, lane = pl.ds(i * side, side), pl.ds(k * side, side)
                todo.append((base + i * hidden_blocks + column, gate_ring.at[slot, row, lane]))
                todo.append((base + (wide + i) * hidden_blocks + column, up_ring.at[slot, row, lane]))
                todo.append((base + 2 * wide * hidden_blocks + column * wide + i, down_ring.at[slot, lane, row]))
        return todo

    def start(todo, slot, first, last):
        for number, target in todo[first:last]:
            fetch_tile(full, slots, number, target, sems.at[slot])

    def arrived(slot):
        for target in (gate_ring, up_ring, down_ring):
            view = target.at[slot]
            pltpu.make_async_copy(view, view, sems.at[slot]).wait()

    for j in range(ring - 1):
        todo = pieces_of(j, j)
        start(todo, j, 0, len(todo))
    normed[:rows] = normed_own[...]
    cotangent[:rows] = cotangent_own[...]
    for c in range(wide):
        at = slice(c * side, (c + 1) * side)
        normed[rows:, at] = normed_beside[c].astype(F32).T.astype(BF16)
        cotangent[rows:, at] = cotangent_beside[wide + c]
    forward[...] = jnp.zeros_like(forward)
    backward[...] = jnp.zeros_like(backward)

    def step(j, _):
        slot = j % ring
        arrived(slot)
        later = (j + ring - 1) % ring
        todo = pieces_of(jnp.minimum(j + ring - 1, steps - 1), later)
        sixth = len(todo) // 6
        start(todo, later, 0, sixth)
        gate = mul(normed[...], gate_ring[slot])
        start(todo, later, sixth, 2 * sixth)
        up = mul(normed[...], up_ring[slot])
        start(todo, later, 2 * sixth, 3 * sixth)
        grad_hidden = mul_turned(cotangent[...], down_ring[slot])
        start(todo, later, 3 * sixth, 4 * sixth)
        square = gate * gate
        bend = jnp.tanh(GELU_SCALE * gate * (1.0 + GELU_CUBE * square))
        share = 0.5 * (1.0 + bend)
        active = gate * share
        slope = share + 0.5 * gate * (1.0 - bend * bend) * (GELU_SCALE * (1.0 + 3.0 * GELU_CUBE * square))
        hidden_wide = active * up
        hidden = hidden_wide.astype(BF16)
        gate_low = (grad_hidden * up * slope).astype(BF16)
        up_low = (grad_hidden * active).astype(BF16)
        for k in range(span):
            at = slice(k * side, (k + 1) * side)
            hidden_turned[span * j + k] = hidden_wide[:, at].T.astype(BF16)
            gate_grad[span * j + k] = gate_low[:, at]
            up_grad[span * j + k] = up_low[:, at]
        forward[...] += mul(hidden[:rows], down_ring[slot])
        start(todo, later, 4 * sixth, 5 * sixth)
        start(todo, later, 5 * sixth, 6 * sixth)
        backward[...] += mul_turned(gate_low[:rows], gate_ring[slot]) + mul_turned(up_low[:rows], up_ring[slot])
        return 0

    lax.fori_loop(0, steps, step, 0)
    for j in range(steps, steps + ring - 1):
        arrived(j % ring)
    outputs[...] = (middle[...] + forward[...]).astype(BF16)
    back, term = norm_back(middle[...], gain[...], backward[...])
    gain_term[...] = term
    total = cotangent_own[...].astype(F32) + back
    grad_middle[...] = total
    low = total.astype(BF16)
    branch[...] = low
    for c in range(wide):
        branch_blocks[c] = low[:, c * side : (c + 1) * side]


def mlp(slots, full, normed_own, normed_beside, cotangent_own, cotangent_beside, middle, gain, ring=3, span=4):
    rows, width = normed_own.shape
    side = full.shape[1]
    blocks = FF // side
    V = pltpu.VMEM
    spec = pl.BlockSpec(memory_space=V)
    S = jax.ShapeDtypeStruct
    return pl.pallas_call(
        functools.partial(mlp_kernel, side, ring, span),
        grid_spec=pltpu.PrefetchScalarGridSpec(
            num_scalar_prefetch=1,
            grid=(),
            in_specs=[pl.BlockSpec(memory_space=pl.ANY)] + [spec] * 6,
            out_specs=[spec] * 8,
            scratch_shapes=[V((2 * rows, width), BF16), V((2 * rows, width), BF16), V((rows, width), F32), V((rows, width), F32),
                            V((ring, width, span * side), BF16), V((ring, width, span * side), BF16), V((ring, span * side, width), BF16),
                            pltpu.SemaphoreType.DMA((ring,))],
        ),
        out_shape=[S((blocks, side, 2 * rows), BF16), S((blocks, 2 * rows, side), BF16), S((blocks, 2 * rows, side), BF16),
                   S((rows, width), BF16), S((rows, width), F32), S((rows, width), BF16), S((width // side, rows, side), BF16),
                   S((1, width), F32)],
        cost_estimate=cost_of(37),
        compiler_params=pltpu.CompilerParams(vmem_limit_bytes=56 * 2**20),
    )(slots, full, normed_own, normed_beside, cotangent_own, cotangent_beside, middle, gain)


def attend_back_kernel(side, slots, first, full, branch, queries, pairs, own_ids, all_ids, cosine, sine,
                       query_grad, pair_grad, own_pair_grad, weights, attended_grad, bias, key_total, value_total, sems):
    rows = branch.shape[0]
    heads = queries.shape[1] // side
    wide = branch.shape[1] // side

    def fetch(n, _):
        i, j = n // wide, n % wide
        number = (heads + 2) * wide + i * wide + j
        fetch_tile(full, slots, number, weights.at[block_at(i * side, side), block_at(j * side, side)], sems.at[i // 2])
        return 0

    lax.fori_loop(0, wide * heads, fetch, 0, unroll=8)
    fill_bias(first[0], own_ids, all_ids, bias)
    keys = pairs[:, :, :side].reshape(-1, side)
    values = pairs[:, :, side:].reshape(-1, side)
    scale = HEAD_DIM ** (-0.5)
    for c in range(heads // 2):
        view = weights.at[pl.ds(c * 2 * side, 2 * side), :]
        pltpu.make_async_copy(view, view, sems.at[c]).wait()
        attended_grad[:, c * 2 * side : (c + 1) * 2 * side] = mul_turned(branch[...], view[...]).astype(BF16)
    key_total[...] = jnp.zeros_like(key_total)
    value_total[...] = jnp.zeros_like(value_total)
    for head in range(heads):
        at = slice(head * side, (head + 1) * side)
        scores = mul_turned(queries[:, at], keys) * scale + bias[...]
        share = softmax_of(scores)
        share_grad = mul_turned(attended_grad[:, at], values)
        inner = jnp.sum(share * share_grad, -1, keepdims=True)
        score_grad = (share * (share_grad - inner)).astype(BF16)
        query_grad[head] = turn(mul(score_grad, keys) * scale, cosine[...], -sine[...]).astype(BF16)
        key_total[...] += mul_summed(score_grad, queries[:, at])
        value_total[...] += mul_summed(share.astype(BF16), attended_grad[:, at])
    key_total[...] = key_total[...] * scale
    for b in range(pairs.shape[0]):
        at = slice(b * rows, (b + 1) * rows)
        pair_grad[b, :, :side] = key_total[at].astype(BF16)
        pair_grad[b, :, side:] = value_total[at].astype(BF16)
    own = block_at(first[0], rows)
    own_pair_grad[:, :side] = key_total[own, :]
    own_pair_grad[:, side:] = value_total[own, :]


def attend_back(slots, first, full, branch, queries, pairs, own_ids, all_ids, cosine, sine):
    rows, width = branch.shape
    side = full.shape[1]
    key_rows = pairs.shape[0] * pairs.shape[1]
    V = pltpu.VMEM
    spec = pl.BlockSpec(memory_space=V)
    S = jax.ShapeDtypeStruct
    return pl.pallas_call(
        functools.partial(attend_back_kernel, side),
        grid_spec=pltpu.PrefetchScalarGridSpec(
            num_scalar_prefetch=2,
            grid=(),
            in_specs=[pl.BlockSpec(memory_space=pl.ANY)] + [spec] * 7,
            out_specs=[spec] * 3,
            scratch_shapes=[V((HEADS * side, width), BF16), V((rows, HEADS * side), BF16), V((rows, key_rows), F32),
                            V((key_rows, side), F32), V((key_rows, side), F32), pltpu.SemaphoreType.DMA((HEADS // 2,))],
        ),
        out_shape=[S((HEADS, rows, side), BF16), S(pairs.shape, BF16), S((rows, 2 * side), F32)],
        cost_estimate=cost_of(15),
        compiler_params=pltpu.CompilerParams(vmem_limit_bytes=40 * 2**20),
    )(slots, first, full, branch, queries, pairs, own_ids, all_ids, cosine, sine)


def pairs_back_kernel(pair_grad, own_grad, query_grad, branch, cosine, sine, low, query_beside, query_twin, query_far,
                      branch_beside, branch_twin, branch_far, arrived, sends, recvs, unit_sends, unit_recvs):
    replica = lax.axis_index("replica")
    member = lax.axis_index("fsdp")
    beside = ((1 - replica // 2) * 2 + replica % 2, member)
    twin = (replica // 2 * 2 + 1 - replica % 2, member)
    count = pair_grad.shape[0]
    side = cosine.shape[1]
    barrier = pltpu.get_barrier_semaphore()
    for device in [(replica, (member + step) % count) for step in range(1, count)] + [beside, twin]:
        pl.semaphore_signal(barrier, inc=1, device_id=device, device_id_type=MESH)
    pl.semaphore_wait(barrier, count + 1)

    def copy(step):
        target = (member + step) % count
        return pltpu.make_async_remote_copy(
            src_ref=pair_grad.at[target], dst_ref=arrived.at[step], send_sem=sends.at[step], recv_sem=recvs.at[step],
            device_id=(replica, target), device_id_type=MESH)

    def unit_copy(n, source, target, device):
        return pltpu.make_async_remote_copy(
            src_ref=source, dst_ref=target, send_sem=unit_sends.at[n], recv_sem=unit_recvs.at[n],
            device_id=device, device_id_type=MESH)

    moves = []
    for n, (own, from_beside, from_twin, from_far) in enumerate(
            [(branch, branch_beside, branch_twin, branch_far), (query_grad, query_beside, query_twin, query_far)]):
        part = own.shape[0] // 2
        for h in range(2):
            at = pl.ds(h * part, part)
            first = 6 * n + 3 * h
            moves.append((unit_copy(first, own.at[at], from_beside.at[at], beside), unit_copy(first + 1, own.at[at], from_twin.at[at], twin),
                          unit_copy(first + 2, from_beside.at[at], from_far.at[at], twin)))
    for step in range(1, count):
        copy(step).start()
    for to_beside, to_twin, pass_on in moves:
        to_beside.start()
        to_twin.start()
    total = own_grad[...]
    for step in range(1, count):
        copy(step).wait_recv()
        total = total + arrived[step].astype(F32)
    low[0] = turn(total[:, :side], cosine[...], -sine[...]).astype(BF16)
    low[1] = total[:, side:].astype(BF16)
    for step in range(1, count):
        copy(step).wait_send()
    for to_beside, to_twin, pass_on in moves:
        to_beside.wait_recv()
        pass_on.start()
    for to_beside, to_twin, pass_on in moves:
        to_beside.wait_send()
        to_twin.wait()
        pass_on.wait()


def pairs_back(pair_grad, own_grad, query_grad, branch, cosine, sine):
    count, rows, double = pair_grad.shape
    D = pltpu.SemaphoreType.DMA
    S = jax.ShapeDtypeStruct
    spec = pl.BlockSpec(memory_space=pltpu.VMEM)
    return pl.pallas_call(
        pairs_back_kernel,
        out_shape=[S((2, rows, double // 2), BF16)] + [S(query_grad.shape, BF16)] * 3 + [S(branch.shape, BF16)] * 3,
        in_specs=[spec] * 6,
        out_specs=[spec] * 7,
        scratch_shapes=[pltpu.VMEM(pair_grad.shape, BF16), D((count,)), D((count,)), D((12,)), D((12,))],
        cost_estimate=cost_of(16),
        compiler_params=pltpu.CompilerParams(collective_id=3, has_side_effects=True),
    )(pair_grad, own_grad, query_grad, branch, cosine, sine)


def input_back_kernel(side, slots, full, query_grad, pair_grad, inputs, grad_middle, gain,
                      input_grad, gain_term, weights, joined, backward, sems):
    wide = inputs.shape[1] // side
    heads = query_grad.shape[0]

    def fetch(n, _):
        i, j = n // (heads + 2), n % (heads + 2)
        number = jnp.where(j < heads, i * heads + j, wide * j + i)
        fetch_tile(full, slots, number, weights.at[block_at(i * side, side), block_at(j * side, side)], sems.at[i // 2])
        return 0

    lax.fori_loop(0, wide * (heads + 2), fetch, 0, unroll=8)
    for h in range(heads):
        joined[:, h * side : (h + 1) * side] = query_grad[h]
    for k in range(2):
        joined[:, (heads + k) * side : (heads + k + 1) * side] = pair_grad[k]
    for c in range(wide // 2):
        view = weights.at[pl.ds(c * 2 * side, 2 * side), :]
        pltpu.make_async_copy(view, view, sems.at[c]).wait()
        backward[:, c * 2 * side : (c + 1) * 2 * side] = mul_turned(joined[...], view[...])
    back, term = norm_back(inputs[...].astype(F32), gain[...], backward[...])
    gain_term[...] = term
    input_grad[...] = (grad_middle[...] + back).astype(BF16)


def input_back(slots, full, query_grad, pair_grad, inputs, grad_middle, gain):
    rows, width = inputs.shape
    side = full.shape[1]
    V = pltpu.VMEM
    spec = pl.BlockSpec(memory_space=V)
    S = jax.ShapeDtypeStruct
    return pl.pallas_call(
        functools.partial(input_back_kernel, side),
        grid_spec=pltpu.PrefetchScalarGridSpec(
            num_scalar_prefetch=1,
            grid=(),
            in_specs=[pl.BlockSpec(memory_space=pl.ANY)] + [spec] * 5,
            out_specs=[spec] * 2,
            scratch_shapes=[V((width, (HEADS + 2) * side), BF16), V((rows, (HEADS + 2) * side), BF16), V((rows, width), F32),
                            pltpu.SemaphoreType.DMA((width // side // 2,))],
        ),
        out_shape=[S((rows, width), BF16), S((1, width), F32)],
        cost_estimate=cost_of(8),
        compiler_params=pltpu.CompilerParams(vmem_limit_bytes=40 * 2**20),
    )(slots, full, query_grad, pair_grad, inputs, grad_middle, gain)


def reduce_kernel(chunk, places, left_at, right_at, gain_part, *refs):
    count = len(places)
    given = 1 + max(place[0] for place in places)
    sources, refs = refs[:given], refs[given:]
    (out, gain_out, left_all, right_all, x_out, x_in, z_out, z_in, z_mix, turned_out, turned_in, turned_mix, total, gain_sum, gain_in, keep_sem, gain_s, gain_r,
     x_s, x_r, z_s, z_r, ty_s, ty_r, tc_s, tc_r, tf_s, tf_r, done_sem) = refs
    quarter = x_out.shape[1]
    pieces = quarter // chunk
    replica = lax.axis_index("replica")
    member = lax.axis_index("fsdp")
    y, core = replica // 2, replica % 2
    z, x = member // 2, member % 2
    across, beside, twin = (replica, z * 2 + 1 - x), ((1 - y) * 2 + core, member), (y * 2 + 1 - core, member)
    beside_replica, twin_replica, far_replica = (1 - y) * 2 + core, y * 2 + 1 - core, (1 - y) * 2 + 1 - core
    def level(step):
        return (z + step) % 4
    def depth_device(step):
        return (replica, level(step) * 2 + x)
    def keep(n):
        at, is_left, block, source_block, number, lane = places[n]
        source = sources[at].at[pl.ds(source_block, number)]
        if is_left:
            target = left_all.at[pl.ds(block, number), :, pl.ds(lane, sources[at].shape[2])]
        else:
            target = right_all.at[pl.ds(block, number), pl.ds(lane, sources[at].shape[1]), :]
        return pltpu.make_async_copy(source, target, keep_sem.at[n])
    for n in range(count):
        keep(n).start()
    left_all[left_all.shape[0] - 1] = jnp.zeros(left_all.shape[1:], left_all.dtype)
    gain_sum[...] = gain_part[...]

    barrier = pltpu.get_barrier_semaphore()
    for device in [across, beside, twin] + [depth_device(step) for step in (1, 2, 3)]:
        pl.semaphore_signal(barrier, inc=1, device_id=device, device_id_type=MESH)
    pl.semaphore_wait(barrier, 6)

    def remote(source, target, send, recv, device):
        return pltpu.make_async_remote_copy(src_ref=source, dst_ref=target, send_sem=send, recv_sem=recv, device_id=device, device_id_type=MESH)

    def gain_copy(stage, device):
        return remote(gain_sum, gain_in.at[stage], gain_s.at[stage], gain_r.at[stage], device)
    def gain_pair(stage, device):
        gain_copy(stage, device).wait()
        gain_sum[...] = gain_sum[...] + gain_in[stage]
    def gain_z(step):
        return remote(gain_sum, gain_in.at[2 + step], gain_s.at[2 + step], gain_r.at[2 + step], depth_device(step))
    def gain_finish():
        for step in (1, 2, 3):
            gain_z(step).wait()
        gain_in[0] = gain_sum[...]
        added = jnp.zeros(gain_sum.shape, F32)
        for zb in range(4):
            step = (zb - z + 4) % 4
            added = added + gain_in[jnp.where(step == 0, 0, 2 + step)]
        gain_out[...] = added
    gain_copy(0, beside).start()
    for n in range(count):
        keep(n).wait()

    def tile(owner, at):
        rank = replica * quarter + at
        return jnp.dot(left_all[left_at[owner, rank]], right_all[right_at[owner, rank]], preferred_element_type=F32)

    paired = z + 1 - 2 * (z % 2)
    levels = [z, paired, 3 - z, 3 - paired]
    middle = (z == 1) | (z == 2)
    order = (2, 3, 1, 0)
    def turned(k):
        return k % 6 == 2
    def at_level(lev):
        return (replica, lev * 2 + x)
    def x_copy(zb, k):
        at = pl.ds(k * chunk, chunk)
        return remote(x_out.at[zb, at], x_in.at[zb, at], x_s.at[zb, k], x_r.at[zb, k], across)
    def buffers(column, k):
        if column == 0:
            return z_out, z_in, z_mix, k * chunk
        return turned_out, turned_in, turned_mix, k // 6 * chunk
    def z_send(column, block, place, kind, device, k):
        out_buffer, in_buffer, mix_buffer, base = buffers(column, k)
        at = pl.ds(base, chunk)
        target = in_buffer.at[place, at] if kind < 2 else mix_buffer.at[place, at]
        return remote(out_buffer.at[block, at], target, z_s.at[column, block, k], z_r.at[column, kind, k], device)
    def pass_paired(column, k):
        z_send(column, 1, 0, 0, at_level(levels[1]), k).start()
    def pass_end(column, block, k):
        z_send(column, block, 3 - block, 5 - block, at_level(levels[1]), k).start()
    def pass_middle(column, block, k):
        z_send(column, block, 1, 1, at_level(levels[block]), k).start()
    def z_arrival(column, place, kind, k):
        z_send(column, 1, place, kind, at_level(levels[1]), k).wait_recv()
    def leave(column, block, k):
        if block == 1:
            pass_paired(column, k)
        elif block > 1:
            pl.when(jnp.logical_not(middle))(lambda: pass_end(column, block, k))
    def combine(column, k):
        @pl.when(middle)
        def _():
            out_buffer, in_buffer, mix_buffer, base = buffers(column, k)
            for place in (0, 1):
                z_arrival(column, place, 2 + place, k)
                def one(t, _):
                    at = base + t
                    out_buffer[2 + place, at] = (out_buffer[2 + place, at].astype(F32) + mix_buffer[place, at].astype(F32)).astype(BF16)
                    return 0
                lax.fori_loop(0, chunk, one, 0)
                pass_middle(column, 2 + place, k)
    def z_total(column, k, t):
        out_buffer, in_buffer, mix_buffer, base = buffers(column, k)
        at = base + t
        return out_buffer[0, at].astype(F32) + in_buffer[0, at].astype(F32) + in_buffer[1, at].astype(F32)
    def total_at(who, k):
        return total.at[pl.ds(who * quarter + k * chunk, chunk)]
    def t_beside(k):
        return remote(total_at(replica, k), total_at(replica, k), ty_s.at[k], ty_r.at[k], beside)
    def t_twin(k):
        return remote(total_at(replica, k), total_at(replica, k), tc_s.at[k], tc_r.at[k], twin)
    def t_pass(k):
        return remote(total_at(beside_replica, k), total_at(beside_replica, k), tf_s.at[k], tf_r.at[k], twin)
    def come_beside(k):
        return remote(total_at(replica, k), total_at(beside_replica, k), ty_s.at[k], ty_r.at[k], beside)
    def come_twin(k):
        return remote(total_at(replica, k), total_at(twin_replica, k), tc_s.at[k], tc_r.at[k], twin)
    def come_far(k):
        return remote(total_at(replica, k), total_at(far_replica, k), tf_s.at[k], tf_r.at[k], twin)

    def send_x(k):
        for block in order:
            lev = levels[block]
            def one(t, _):
                at = k * chunk + t
                x_out[lev, at] = tile(lev * 2 + 1 - x, at).astype(BF16)
                return 0
            lax.fori_loop(0, chunk, one, 0)
            x_copy(lev, k).start()

    def collect(k):
        for block in order:
            lev = levels[block]
            x_copy(lev, k).wait_recv()
            def one(t, _):
                at = k * chunk + t
                z_out[block, at] = (tile(lev * 2 + x, at) + x_in[lev, at].astype(F32)).astype(BF16)
                return 0
            lax.fori_loop(0, chunk, one, 0)
            leave(0, block, k)

    def turned_send(k):
        for block in order:
            for column in (0, 1):
                owner = levels[block] * 2 + (x if column == 0 else 1 - x)
                out_buffer, in_buffer, mix_buffer, base = buffers(column, k)
                def one(t, _):
                    out_buffer[block, base + t] = tile(owner, k * chunk + t).astype(BF16)
                    return 0
                lax.fori_loop(0, chunk, one, 0)
                leave(column, block, k)

    def turned_cross(k):
        for column in (0, 1):
            for place in (0, 1):
                z_arrival(column, place, place, k)
        def one(t, _):
            x_out[0, k * chunk + t] = z_total(1, k, t).astype(BF16)
            return 0
        lax.fori_loop(0, chunk, one, 0)
        x_copy(0, k).start()

    def finish(k):
        @pl.when(turned(k))
        def _():
            x_copy(0, k).wait_recv()
            def one(t, _):
                at = k * chunk + t
                total[replica * quarter + at] = (z_total(0, k, t) + x_in[0, at].astype(F32)).astype(BF16)
                return 0
            lax.fori_loop(0, chunk, one, 0)
        @pl.when(jnp.logical_not(turned(k)))
        def _():
            for place in (0, 1):
                z_arrival(0, place, place, k)
            def one(t, _):
                total[replica * quarter + k * chunk + t] = z_total(0, k, t).astype(BF16)
                return 0
            lax.fori_loop(0, chunk, one, 0)
        t_beside(k).start()
        t_twin(k).start()

    def spread(k):
        come_beside(k).wait_recv()
        t_pass(k).start()

    def beat(n, _):
        def due(behind, kind):
            k = n - behind
            here = (k >= 0) & (k < pieces)
            return here & (turned(k) if kind else jnp.logical_not(turned(k)))
        pl.when(due(0, True))(lambda: turned_send(n))
        pl.when(due(0, False))(lambda: send_x(n))
        @pl.when(due(2, True))
        def _():
            combine(0, n - 2)
            combine(1, n - 2)
        pl.when(due(3, False))(lambda: collect(n - 3))
        pl.when(due(5, False))(lambda: combine(0, n - 5))
        pl.when(due(4, True))(lambda: turned_cross(n - 4))
        pl.when((n >= 7) & (n < pieces + 7))(lambda: finish(n - 7))
        pl.when(n >= 9)(lambda: spread(n - 9))

        @pl.when(n == 2)
        def _():
            gain_pair(0, beside)
            gain_copy(1, twin).start()

        @pl.when(n == 4)
        def _():
            gain_pair(1, twin)
            gain_copy(2, across).start()

        @pl.when(n == 6)
        def _():
            gain_pair(2, across)
            for step in (1, 2, 3):
                gain_z(step).start()

        @pl.when(n == 9)
        def _():
            gain_finish()
        return 0
    lax.fori_loop(0, pieces + 9, beat, 0)

    def drain(k, _):
        come_twin(k).wait_recv()
        come_far(k).wait_recv()
        t_beside(k).wait_send()
        t_twin(k).wait_send()
        t_pass(k).wait_send()
        x_copy(0, k).wait_send()
        for block in (1, 2, 3):
            z_send(0, block, 0, 0, at_level(levels[1]), k).wait_send()
        @pl.when(turned(k))
        def _():
            for block in (1, 2, 3):
                z_send(1, block, 0, 0, at_level(levels[1]), k).wait_send()
        @pl.when(jnp.logical_not(turned(k)))
        def _():
            for zb in (1, 2, 3):
                x_copy(zb, k).wait_send()
        return 0
    lax.fori_loop(0, pieces, drain, 0)
    result = pltpu.make_async_copy(total, out, done_sem)
    result.start()
    result.wait()

def reduce_tiles(left_at, right_at, gain_part, parts, places, left_total, right_total, rows, chunk=3):
    capacity = left_at.shape[1]
    quarter = capacity // 4
    pieces = quarter // chunk
    side = parts[0].shape[1]
    D = pltpu.SemaphoreType.DMA
    V = pltpu.VMEM
    S = jax.ShapeDtypeStruct
    spec = pl.BlockSpec(memory_space=V)
    held = V((4, quarter, side, side), BF16)
    arriving = V((2, quarter, side, side), BF16)
    seldom = (pieces + 3) // 6 * chunk
    return pl.pallas_call(
        functools.partial(reduce_kernel, chunk, places),
        out_shape=[S((capacity, side, side), BF16), S(gain_part.shape, F32)],
        in_specs=[pl.BlockSpec(memory_space=pltpu.SMEM)] * 2 + [spec] + [pl.BlockSpec(memory_space=pl.ANY)] * len(parts),
        out_specs=[pl.BlockSpec(memory_space=pl.ANY), spec],
        scratch_shapes=[
            V((left_total + 1, side, rows), BF16), V((right_total, rows, side), BF16), held, held, held, arriving, arriving,
            V((4, seldom, side, side), BF16), V((2, seldom, side, side), BF16), V((2, seldom, side, side), BF16),
            V((capacity, side, side), BF16), V(gain_part.shape, F32), V((6,) + gain_part.shape, F32),
            D((len(places),)), D((6,)), D((6,))] + [D((4, pieces))] * 2 + [D((2, 4, pieces))] * 2 + [D((pieces,))] * 6 + [D],
        compiler_params=pltpu.CompilerParams(collective_id=1, has_side_effects=True, vmem_limit_bytes=62 * 2**20),
    )(left_at, right_at, gain_part, *parts)


def shampoo_kernel(count, grads, left_old, right_old, left_root, right_root, master, grads_out, left_new, right_new, master_new, low_new):
    side = grads.shape[1]
    flips, boths = [], []
    for at in range(count):
        wide = grads[at].astype(F32)
        grads_out[at] = wide
        flips.append(wide.T.astype(BF16))
    for at in range(count):
        both = jnp.dot(grads[at], jnp.concatenate([flips[at], right_root[at].astype(BF16)], 1), preferred_element_type=F32)
        left_new[at] = STAT_DECAY * left_old[at] + (1.0 - STAT_DECAY) * both[:, :side]
        boths.append(both[:, side:].astype(BF16))
    for at in range(count):
        right_new[at] = STAT_DECAY * right_old[at] + (1.0 - STAT_DECAY) * jnp.dot(flips[at], grads[at], preferred_element_type=F32)
    for at in range(count):
        turned = jnp.dot(left_root[at].astype(BF16), boths[at], preferred_element_type=F32)
        fresh = master[at] - STEP_RATE * turned
        master_new[at] = fresh
        low_new[at] = fresh.astype(BF16)

def shampoo(grads, left_old, right_old, left_root, right_root, master, count=17):
    capacity, side = master.shape[0], master.shape[1]
    while capacity % count:
        count -= 1
    spec = pl.BlockSpec((count, side, side), lambda i: (i, 0, 0))
    wide = jax.ShapeDtypeStruct(master.shape, F32)
    return pl.pallas_call(
        functools.partial(shampoo_kernel, count),
        grid=(capacity // count,),
        in_specs=[spec] * 6,
        out_specs=[spec] * 5,
        out_shape=[wide, wide, wide, wide, jax.ShapeDtypeStruct(master.shape, BF16)],
        compiler_params=pltpu.CompilerParams(vmem_limit_bytes=60 * 2**20),
    )(grads, left_old, right_old, left_root, right_root, master)


def shifted(block, axis, distance):
    devices = range(lax.axis_size(axis))
    route = [(i - distance, i) for i in devices if i - distance in devices]
    return lax.ppermute(block, axis, route)


def normalize(values, gain_row):
    mean_square = jnp.mean(values * values, -1, keepdims=True)
    return values * lax.rsqrt(mean_square + EPSILON) * gain_row


def rotate(values, angles):
    half_dim = values.shape[-1] // 2
    cosine = jnp.cos(angles)[:, None, :]
    sine_part = jnp.sin(angles)[:, None, :]
    first_half = values[..., :half_dim]
    second = values[..., half_dim:]
    return jnp.concatenate(
        [first_half * cosine - second * sine_part, second * cosine + first_half * sine_part], -1
    )


def angles_of(positions):
    half_dim = HEAD_DIM // 2
    inverse = 10000.0 ** (-2.0 * jnp.arange(half_dim, dtype=jnp.float32) / HEAD_DIM)
    return positions[:, None] * inverse[None, :]


def slot_of_tiles(owner_table, owners, capacity):
    onehot = (owner_table[:, None] == jnp.arange(owners, dtype=jnp.int32)[None, :]).astype(
        jnp.int32
    )
    earlier = jnp.cumsum(onehot, 0) - onehot
    ranking = jnp.sum(earlier * onehot, 1)
    return owner_table * capacity + ranking


def matrix_layout(width, head_width, head_dim, hidden_width, tile_side):
    left_attended = width // tile_side
    left_second = left_attended + head_width // tile_side
    left_hidden = left_second + width // tile_side
    right_key = head_width // tile_side
    right_value = right_key + head_dim // tile_side
    right_branch = right_value + head_dim // tile_side
    right_gate = right_branch + width // tile_side
    right_up = right_gate + hidden_width // tile_side
    right_down = right_up + hidden_width // tile_side
    return [
        (width, head_width, 0, 0),
        (width, head_dim, 0, right_key),
        (width, head_dim, 0, right_value),
        (head_width, width, left_attended, right_branch),
        (width, hidden_width, left_second, right_gate),
        (width, hidden_width, left_second, right_up),
        (hidden_width, width, left_hidden, right_down),
    ]


def project(values, blocks):
    row_count = values.shape[0]
    result = jnp.einsum(
        "nar,abrc->nbc",
        values.reshape(row_count, blocks.shape[0], blocks.shape[2]),
        blocks,
        preferred_element_type=jnp.float32,
    )
    return result.reshape(row_count, blocks.shape[1] * blocks.shape[3])


def back_project(values, blocks):
    row_count = values.shape[0]
    result = jnp.einsum(
        "nbc,abrc->nar",
        values.reshape(row_count, blocks.shape[1], blocks.shape[3]),
        blocks,
        preferred_element_type=jnp.float32,
    )
    return result.reshape(row_count, blocks.shape[0] * blocks.shape[2])


def dense_tile_grads(layout, left_blocks, right_blocks, tile_side):
    pieces = []
    for row_total, column_total, left_base, right_base in layout:
        left_part = left_blocks[:, left_base : left_base + row_total // tile_side]
        right_part = right_blocks[:, right_base : right_base + column_total // tile_side]
        product = jnp.einsum(
            "nar,nbc->abrc", left_part, right_part, preferred_element_type=jnp.float32
        )
        pieces.append(product.reshape(-1, tile_side, tile_side))
    pieces.append(jnp.zeros((1, tile_side, tile_side), jnp.float32))
    return jnp.concatenate(pieces, 0)


def block_tables(layout, tile_side, left_total):
    left_of, right_of = [], []
    for row_total, column_total, left_base, right_base in layout:
        for i in range(row_total // tile_side):
            for j in range(column_total // tile_side):
                left_of.append(left_base + i)
                right_of.append(right_base + j)
    return np.array(left_of + [left_total], np.int32), np.array(right_of + [0], np.int32)


def body_anywhere(
    inputs,
    cotangent,
    segment_ids,
    gains,
    owner_table,
    master_tiles,
    left_stats,
    right_stats,
    left_roots,
    right_roots,
):
    owners = lax.axis_size("fsdp")
    replicas = lax.axis_size("replica")
    member = lax.axis_index("fsdp")
    capacity = master_tiles.shape[0]
    tile_side = master_tiles.shape[1]
    row_count = inputs.shape[0]
    width = inputs.shape[1]
    head_width = HEADS * HEAD_DIM
    tile_total = owner_table.shape[0]
    layout = matrix_layout(width, head_width, HEAD_DIM, FF, tile_side)
    slots = slot_of_tiles(owner_table, owners, capacity)
    slot_tile = (
        jnp.full((owners * capacity,), tile_total, jnp.int32)
        .at[slots]
        .set(jnp.arange(tile_total, dtype=jnp.int32))
    )
    full = lax.all_gather(master_tiles.astype(jnp.bfloat16), "fsdp", axis=0, tiled=True)
    all_tiles = jnp.take(full, slots, axis=0)
    weights = []
    offset = 0
    for row_total, column_total, left_base, right_base in layout:
        number = row_total // tile_side * (column_total // tile_side)
        weights.append(
            all_tiles[offset : offset + number].reshape(
                row_total // tile_side, column_total // tile_side, tile_side, tile_side
            )
        )
        offset = offset + number
    w_query, w_key, w_value, w_out, w_gate, w_up, w_down = weights
    base_row = member * row_count
    own_ids = lax.dynamic_slice_in_dim(segment_ids, base_row, row_count, 0)
    starts = jnp.sum((segment_ids[None, :] < own_ids[:, None]).astype(jnp.int32), 1)
    positions = (base_row + jnp.arange(row_count, dtype=jnp.int32) - starts).astype(jnp.float32)
    angles = angles_of(positions)
    inputs_wide = inputs.astype(jnp.float32)
    normed = normalize(inputs_wide, gains[0]).astype(jnp.bfloat16)
    query_pre = project(normed, w_query)
    key_pre = project(normed, w_key)
    values_own = project(normed, w_value).astype(jnp.bfloat16)
    queries = rotate(query_pre.reshape(row_count, HEADS, HEAD_DIM), angles).astype(jnp.bfloat16)
    keys_own = rotate(key_pre[:, None, :], angles)[:, 0, :].astype(jnp.bfloat16)
    reach = WINDOW // row_count
    own_pair = jnp.concatenate([keys_own, values_own], 1)
    received = [shifted(own_pair, "fsdp", distance_back) for distance_back in range(reach, 0, -1)]
    pair_rows = jnp.concatenate(received + [own_pair], 0)
    key_rows = pair_rows[:, :HEAD_DIM]
    value_rows = pair_rows[:, HEAD_DIM:]
    padded_ids = jnp.concatenate([jnp.full((reach * row_count,), -1, jnp.int32), segment_ids], 0)
    key_ids = lax.dynamic_slice_in_dim(padded_ids, base_row, (reach + 1) * row_count, 0)
    distance = (
        jnp.arange(row_count, dtype=jnp.int32)[:, None]
        + reach * row_count
        - jnp.arange((reach + 1) * row_count, dtype=jnp.int32)[None, :]
    )
    allowed = (own_ids[:, None] == key_ids[None, :]) & (distance >= 0) & (distance < WINDOW)
    score_scale = HEAD_DIM ** (-0.5)
    scores = (
        jnp.einsum("nhd,kd->hnk", queries, key_rows, preferred_element_type=jnp.float32)
        * score_scale
    )
    scores = jnp.where(allowed[None], scores, -1e30)
    row_peak = jnp.max(scores, -1, keepdims=True)
    exponent = jnp.exp(scores - row_peak)
    row_total_sum = jnp.sum(exponent, -1, keepdims=True)
    probability = (exponent / row_total_sum).astype(jnp.bfloat16)
    log_total = row_peak + jnp.log(row_total_sum)
    attended = (
        jnp.einsum("hnk,kd->nhd", probability, value_rows, preferred_element_type=jnp.float32)
        .reshape(row_count, head_width)
        .astype(jnp.bfloat16)
    )
    middle = inputs_wide + project(attended, w_out)
    normed_two = normalize(middle, gains[1]).astype(jnp.bfloat16)
    gate = project(normed_two, w_gate)
    up_part = project(normed_two, w_up)

    def geglu(gate_values, up_values):
        return jax.nn.gelu(gate_values, approximate=True) * up_values

    hidden_wide, geglu_back = jax.vjp(geglu, gate, up_part)
    hidden = hidden_wide.astype(jnp.bfloat16)
    outputs = (middle + project(hidden, w_down)).astype(jnp.bfloat16)
    grad_hidden = back_project(cotangent, w_down)
    gate_back, up_back = geglu_back(grad_hidden)
    gate_grad = gate_back.astype(jnp.bfloat16)
    up_grad = up_back.astype(jnp.bfloat16)
    grad_normed_two = back_project(gate_grad, w_gate) + back_project(up_grad, w_up)
    middle_back, norm_two_back = jax.vjp(normalize, middle, gains[1])[1](grad_normed_two)
    grad_middle = cotangent.astype(jnp.float32) + middle_back
    branch_grad = grad_middle.astype(jnp.bfloat16)
    grad_attended = (
        back_project(branch_grad, w_out).astype(jnp.bfloat16).reshape(row_count, HEADS, HEAD_DIM)
    )
    scores_again = (
        jnp.einsum("nhd,kd->hnk", queries, key_rows, preferred_element_type=jnp.float32)
        * score_scale
    )
    scores_again = jnp.where(allowed[None], scores_again, -1e30)
    exact_prob = jnp.exp(scores_again - log_total)
    grad_prob = jnp.einsum(
        "nhd,kd->hnk", grad_attended, value_rows, preferred_element_type=jnp.float32
    )
    grad_scores = (
        exact_prob * (grad_prob - jnp.sum(exact_prob * grad_prob, -1, keepdims=True))
    ).astype(jnp.bfloat16)
    grad_queries = (
        jnp.einsum("hnk,kd->nhd", grad_scores, key_rows, preferred_element_type=jnp.float32)
        * score_scale
    )
    grad_keys = (
        jnp.einsum("hnk,nhd->kd", grad_scores, queries, preferred_element_type=jnp.float32)
        * score_scale
    )
    grad_values = jnp.einsum(
        "hnk,nhd->kd", probability, grad_attended, preferred_element_type=jnp.float32
    )
    grad_pairs = jnp.concatenate([grad_keys, grad_values], 1)
    own_grad = grad_pairs[reach * row_count :]
    for distance_back in range(1, reach + 1):
        sent_rows = grad_pairs[
            (reach - distance_back) * row_count : (reach - distance_back + 1) * row_count
        ]
        own_grad = own_grad + shifted(
            sent_rows.astype(jnp.bfloat16), "fsdp", -distance_back
        ).astype(sent_rows.dtype)
    grad_query_pre = (
        rotate(grad_queries, -angles).reshape(row_count, head_width).astype(jnp.bfloat16)
    )
    grad_key_pre = rotate(own_grad[:, None, :HEAD_DIM], -angles)[:, 0, :].astype(jnp.bfloat16)
    grad_values_low = own_grad[:, HEAD_DIM:].astype(jnp.bfloat16)
    grad_normed = (
        back_project(grad_query_pre, w_query)
        + back_project(grad_key_pre, w_key)
        + back_project(grad_values_low, w_value)
    )
    inputs_back, norm_one_back = jax.vjp(normalize, inputs_wide, gains[0])[1](grad_normed)
    input_grad = (grad_middle + inputs_back).astype(jnp.bfloat16)
    gain_grads = lax.psum(jnp.stack([norm_one_back, norm_two_back]), ("replica", "fsdp"))
    gain_rate = GAIN_STEP * (row_count * owners * replicas) ** (-0.5)
    new_gains = gains - gain_rate * gain_grads
    left_parts = jnp.concatenate([normed, attended, normed_two, hidden], 1)
    right_parts = jnp.concatenate(
        [grad_query_pre, grad_key_pre, grad_values_low, branch_grad, gate_grad, up_grad, cotangent],
        1,
    )
    left_blocks = left_parts.reshape(row_count, -1, tile_side)
    right_blocks = right_parts.reshape(row_count, -1, tile_side)
    dense = dense_tile_grads(layout, left_blocks, right_blocks, tile_side)
    partial_sum = lax.psum_scatter(
        jnp.take(dense, slot_tile, axis=0), "fsdp", scatter_dimension=0, tiled=True
    )
    grads_low = lax.psum(partial_sum.astype(jnp.bfloat16), "replica")
    grads_all, left_all, right_all, master_all, low_all = shampoo(
        grads_low, left_stats, right_stats, left_roots, right_roots, master_tiles
    )
    return (
        outputs,
        input_grad,
        gain_grads,
        new_gains,
        grads_all,
        master_all,
        low_all,
        left_all,
        right_all,
    )


def body_of_units(
    inputs,
    cotangent,
    segment_ids,
    gains,
    owner_table,
    master_tiles,
    left_stats,
    right_stats,
    left_roots,
    right_roots,
):
    owners, replicas = 8, 4
    member = lax.axis_index("fsdp")
    capacity = master_tiles.shape[0]
    side = master_tiles.shape[1]
    rows, width = inputs.shape
    tile_total = owner_table.shape[0]
    layout = matrix_layout(width, HEADS * HEAD_DIM, HEAD_DIM, FF, side)
    left_of, right_of = block_tables(layout, side, 0)
    padded = -(-tile_total // 128) * 128
    block_values = np.zeros((padded, 128), np.float32)
    block_values[:tile_total, 0] = left_of[:-1] + 1
    block_values[:tile_total, 1] = right_of[:-1] + 1
    left_total, right_total = int(max(left_of)) + 1, int(max(right_of)) + 1
    owner_row = jnp.pad(owner_table, (0, padded - tile_total), constant_values=-1).reshape(1, padded)

    slots, blocks_at, normed, early = prepare(
        owners, capacity, owner_row, jnp.asarray(block_values, BF16), inputs, cotangent, gains[0:1]
    )
    slots = slots.reshape(padded)
    chosen = blocks_at[:, :capacity, :2].astype(jnp.int32) - 1
    left_at = jnp.where(chosen[..., 0] < 0, left_total, chosen[..., 0])
    right_at = jnp.maximum(chosen[..., 1], 0)
    base_row = member * rows
    own_ids = lax.dynamic_slice_in_dim(segment_ids, base_row, rows, 0)
    starts = jnp.sum((segment_ids[None, :] < own_ids[:, None]).astype(jnp.int32), 1)
    positions = (base_row + jnp.arange(rows, dtype=jnp.int32) - starts).astype(jnp.float32)
    angles = angles_of(positions)
    cosine, sine = jnp.cos(angles), jnp.sin(angles)
    cosine = jnp.concatenate([cosine, cosine], 1)
    sine = jnp.concatenate([-sine, sine], 1)
    first = base_row.astype(jnp.int32).reshape(1)
    own_column, all_row = own_ids.reshape(-1, 1), segment_ids.reshape(1, -1)

    def over_y(part):
        return lax.ppermute(part, "replica", [(0, 2), (1, 3), (2, 0), (3, 1)])

    def over_core(part):
        return lax.ppermute(part, "replica", [(0, 1), (1, 0), (2, 3), (3, 2)])

    def unit_of(part):
        beside = over_y(part)
        return [part, beside, over_core(part), over_core(beside)]

    early_unit = unit_of(early)
    full = gather(master_tiles).reshape(owners * capacity, side, side)
    queries, pair = project_heads(slots, full, normed, cosine, sine)
    pairs = gather_pairs(pair, owners)
    attended_turned, normed_two, normed_two_turned, middle = attend(
        slots, first, full, queries, pairs, own_column, all_row, inputs, gains[1:2]
    )
    two_unit = unit_of(normed_two_turned)
    attended_turned, _ = lax.optimization_barrier((attended_turned, two_unit[1]))
    attended_unit = unit_of(attended_turned)
    wide = width // side
    hidden, gate_grad, up_grad, outputs, grad_middle, branch, branch_blocks, term_two = mlp(
        slots, full, normed_two, two_unit[1], cotangent, early_unit[1], middle, gains[1:2]
    )
    hidden_far, gate_far, up_far = over_core(hidden), over_core(gate_grad), over_core(up_grad)
    query_grad, pair_grad, own_pair_grad = attend_back(
        slots, first, full, branch, queries, pairs, own_column, all_row, cosine, sine
    )
    pair_low, *others = pairs_back(pair_grad, own_pair_grad, query_grad, branch_blocks, cosine, sine)
    query_unit = [query_grad] + others[:3]
    branch_unit = [branch_blocks] + others[3:]
    pair_unit = unit_of(pair_low)
    input_grad, term_one = input_back(slots, full, query_grad, pair_low, inputs, grad_middle, gains[0:1])

    parts, places = [], []

    def place(unit, *spots):
        for n, part in enumerate(unit):
            for is_left, block, source_block, count in spots:
                places.append((len(parts), is_left, block, source_block, count, n * rows * (4 // len(unit))))
            parts.append(part)

    blocks = FF // side
    place(early_unit, (True, 0, 0, wide), (False, HEADS + 2 + wide + 2 * blocks, wide, wide))
    place(attended_unit, (True, wide, 0, HEADS))
    place(two_unit, (True, wide + HEADS, 0, wide))
    place([hidden, hidden_far], (True, 2 * wide + HEADS, 0, blocks))
    place(query_unit, (False, 0, 0, HEADS))
    place(pair_unit, (False, HEADS, 0, 2))
    place(branch_unit, (False, HEADS + 2, 0, wide))
    place([gate_grad, gate_far], (False, HEADS + 2 + wide, 0, blocks))
    place([up_grad, up_far], (False, HEADS + 2 + wide + blocks, 0, blocks))
    gain_part = jnp.concatenate([term_one, term_two, jnp.zeros((6, width), F32)], 0)
    grads_low, gain_sum = reduce_tiles(
        left_at, right_at, gain_part, parts, tuple(places), left_total, right_total, replicas * rows
    )
    gain_grads = gain_sum[:2]
    gain_rate = GAIN_STEP * (rows * owners * replicas) ** (-0.5)
    grads_all, left_all, right_all, master_all, low_all = shampoo(
        grads_low, left_stats, right_stats, left_roots, right_roots, master_tiles
    )
    return (
        outputs,
        input_grad,
        gain_grads,
        gains - gain_rate * gain_grads,
        grads_all,
        master_all,
        low_all,
        left_all,
        right_all,
    )


def solution(mesh):
    units = mesh.shape["replica"] == 4 and mesh.shape["fsdp"] == 8
    return jax.shard_map(
        body_of_units if units else body_anywhere,
        mesh=mesh,
        in_specs=(
            P(("replica", "fsdp"), None),
            P(("replica", "fsdp"), None),
            P("replica"),
            P(),
            P(),
            P("fsdp", None, None),
            P("fsdp", None, None),
            P("fsdp", None, None),
            P("fsdp", None, None),
            P("fsdp", None, None),
        ),
        out_specs=(
            P(("replica", "fsdp"), None),
            P(("replica", "fsdp"), None),
            P(),
            P(),
            P("fsdp", None, None),
            P("fsdp", None, None),
            P("fsdp", None, None),
            P("fsdp", None, None),
            P("fsdp", None, None),
        ),
        check_vma=False,
    )
```
